32 devices in a mesh: canvas: 8 (over z, x), band: 4 (over y, core).
Axes of the slice: x: 2, y: 2, z: 4, core: 2. Of those that a mesh axis runs over, the one named last changes fastest.
Arguments:
- latents: bfloat16 [2, 8, 32, 34, 1152], P(None, 'canvas', 'band'), may hold values from -6 to 6
- segment_ids: int32 [2, 8, 32, 34], P(None, 'canvas', 'band'), may hold values from -1 to 4, as said below
- time_embed: bfloat16 [2, 8, 5, 1152], P(None, 'canvas'), may hold values from -6 to 6
- norm_gains: float32 [1152, 2], replicated, may hold values from 0.1 to 1.9
- attn_in: bfloat16 [1152, 3456], P('canvas'), may hold values from -0.1875 to 0.1875
- time_in: bfloat16 [1152, 2304], P('canvas'), may hold values from -0.1875 to 0.1875
- rel_bias: float32 [25, 16], replicated, may hold values from -4 to 4
- out_proj: bfloat16 [1152, 1152], P('canvas'), may hold values from -0.5 to 0.5
- mlp_in: bfloat16 [1152, 4608], P('canvas'), may hold values from -0.1875 to 0.1875
- mlp_out: bfloat16 [4608, 1152], P('canvas'), may hold values from -0.125 to 0.125
- cotangent: bfloat16 [2, 8, 32, 34, 1152], P(None, 'canvas', 'band'), may hold values from -6 to 6
Outputs:
- layer_out: bfloat16 [2, 8, 32, 34, 1152], P(None, 'canvas', 'band')
- grad_latents: float32 [2, 8, 32, 34, 1152], P(None, 'canvas', 'band')
- grad_time: float32 [2, 8, 5, 1152], P(None, 'canvas')
- grad_norm_gains: float32 [1152, 2], P(('canvas', 'band'))
- grad_attn_in: float32 [1152, 3456], P(('canvas', 'band'))
- grad_time_in: float32 [1152, 2304], P(('canvas', 'band'))
- grad_rel_bias: float32 [25, 16], replicated
- grad_out_proj: float32 [1152, 1152], P(('canvas', 'band'))
- grad_mlp_in: float32 [1152, 4608], P(('canvas', 'band'))
- grad_mlp_out: float32 [4608, 1152], P(('canvas', 'band'))
The draws below stay inside these ranges and needn't reach their ends.
Inputs may be any that keep to these rules, and one draw needn't show every extreme that they name: `segment_ids`: in every canvas slot 0 covers whole columns over all 32 rows; slots 1 to 4 are runs of rows beside it, each with some empty tokens; every value from -1 to 4 occurs in every canvas.
All inputs are finite; a program needn't handle non-finite values.
Results may differ from the reference program's by a relative error of at most 0.02.
Values may be sent and summed in bfloat16 or wider, within the bound.
A program may use at most 384 MiB of HBM per device.

```python
import jax
import jax.numpy as jnp
from jax import lax

D = 1152
H = 16
FF = 4608
HEAD_SIZE = 72
WIN = 5
ROWS = 32
COLS = 34
SEGS = 5
MICRO = 2
CANV = 8


def canvas_layout(key):
    keys = jax.random.split(key, 4)
    left = jax.random.randint(keys[0], (), COLS // 4, COLS - 2)
    cuts = jnp.sort(jax.random.permutation(keys[1], ROWS - 1)[:SEGS - 2] + 1)
    spans = jax.random.randint(keys[2], (SEGS - 1,), 2, COLS - left)
    mirror = jax.random.randint(keys[3], (), 0, 2)
    row_ids = jnp.arange(ROWS)[:, None]
    col_ids = jnp.arange(COLS)[None, :]
    pieces = jnp.sum((row_ids[:, :, None] >= cuts[None, None, :]).astype(jnp.int32), -1)
    span_here = spans[pieces]
    inner = col_ids - left
    layout = jnp.where(col_ids < left, 0, jnp.where(inner < span_here, pieces + 1, -1))
    layout = jnp.where(mirror == 1, layout[:, ::-1], layout)
    return layout.astype(jnp.int32)


def draw_segment_ids(key, part):
    keys = jax.random.split(key, MICRO * CANV)
    return jax.vmap(canvas_layout)(keys).reshape(MICRO, CANV, ROWS, COLS)


def block_scale(own_key, dims, shards, smallest, high):
    def one(position, blocks):
        heights = jax.random.uniform(jax.random.fold_in(jax.random.fold_in(own_key, 6), position), (blocks,), jnp.float32, smallest / len(shards), high / len(shards))
        return jnp.repeat(jnp.exp(heights), dims[position] // blocks).reshape((-1,) + (1,) * (len(dims) - position - 1))

    level = one(*shards[0])
    for cut in shards[1:]:
        level = level * one(*cut)
    return level


def bell_draw(stream_key, extent, scale, limit, cuts=(), held_as=jnp.bfloat16):
    drawn = scale * jax.random.normal(stream_key, extent, jnp.float32)
    if cuts:
        drawn = drawn * block_scale(stream_key, extent, cuts, -0.22, 0.18)
    return jnp.clip(drawn, -limit, limit).astype(held_as)


def setup_inputs(seed: int = 0) -> dict:
    key_of = jax.random.split(jax.random.key(seed), 12)
    latents = bell_draw(key_of[0], (MICRO, CANV, ROWS, COLS, D), 1.0, 6.0, ((1, 8), (2, 4)))
    segment_ids = draw_segment_ids(jax.random.fold_in(key_of[11], 71), 0)
    time_embed = bell_draw(key_of[2], (MICRO, CANV, SEGS, D), 1.0, 6.0, ((1, 8),))
    norm_gains = jnp.clip(1.0 + 0.18 * jax.random.normal(key_of[3], (D, 2), jnp.float32), 0.1, 1.9)
    attn_in = bell_draw(key_of[4], (D, 3 * D), D ** -0.5, 0.1875, ((0, 8),))
    time_in = bell_draw(key_of[5], (D, 2 * D), D ** -0.5, 0.1875, ((0, 8),))
    rel_bias = bell_draw(key_of[6], (WIN * WIN, H), 1.0, 4.0, (), jnp.float32)
    out_proj = bell_draw(key_of[7], (D, D), (D // 8) ** -0.5, 0.5, ((0, 8),))
    mlp_in = bell_draw(key_of[8], (D, FF), D ** -0.5, 0.1875, ((0, 8),))
    mlp_out = bell_draw(key_of[9], (FF, D), (FF // 2) ** -0.5, 0.125, ((0, 8),))
    cotangent = bell_draw(key_of[10], (MICRO, CANV, ROWS, COLS, D), 1.0, 6.0, ((1, 8), (2, 4)))
    return {"latents": latents, "segment_ids": segment_ids, "time_embed": time_embed, "norm_gains": norm_gains, "attn_in": attn_in, "time_in": time_in, "rel_bias": rel_bias, "out_proj": out_proj, "mlp_in": mlp_in, "mlp_out": mlp_out, "cotangent": cotangent}


@jax.custom_vjp
def low(v):
    return lax.optimization_barrier(v.astype(jnp.bfloat16)).astype(jnp.float32)

@jax.custom_vjp
def low_back(v):
    return v

def low_keep(v):
    return (low(v), None)

def low_pass(kept, grad):
    return (grad,)

def back_keep(v):
    return (v, None)

def back_low(kept, grad):
    return (low(grad),)
low.defvjp(low_keep, low_pass)
low_back.defvjp(back_keep, back_low)
EPSILON = 1e-05
HIGH_PRECISION = lax.Precision.HIGHEST

def layer_norm(value, gain):
    center = value - lax.optimization_barrier(jnp.mean(value, -1, keepdims=True))
    return center * lax.rsqrt(lax.optimization_barrier(jnp.mean(center * center, -1, keepdims=True)) + EPSILON) * gain

def windows(padded, rows_count, cols_count):
    return jnp.stack([padded[i:i + rows_count, j:j + cols_count] for i in range(WIN) for j in range(WIN)])

def canvas_attention(query, keys, values, seg_code, score_bias):
    reach = WIN // 2
    rows_count = query.shape[0]
    cols_count = query.shape[1]
    key_pad = jnp.pad(keys, ((reach, reach), (reach, reach), (0, 0)))
    value_pad = jnp.pad(values, ((reach, reach), (reach, reach), (0, 0)))
    code_pad = jnp.pad(seg_code, ((reach, reach), (reach, reach)))
    key_window = windows(key_pad, rows_count, cols_count).reshape(WIN * WIN, rows_count, cols_count, H, HEAD_SIZE)
    value_window = windows(value_pad, rows_count, cols_count).reshape(WIN * WIN, rows_count, cols_count, H, HEAD_SIZE)
    code_win = windows(code_pad, rows_count, cols_count)
    query_head_rows = query.reshape(rows_count, cols_count, H, HEAD_SIZE)
    logit_scores = jnp.einsum('alxf,balxf->balx', query_head_rows, key_window, precision=HIGH_PRECISION) * HEAD_SIZE ** (-0.5) + score_bias[:, None, None, :]
    logit_scores = low_back(logit_scores)
    allowed = (code_win == seg_code[None])[..., None]
    masked = jnp.where(allowed, logit_scores, -1e+30)
    peak = lax.optimization_barrier(jnp.max(masked, 0))
    raised = jnp.where(allowed, jnp.exp(masked - peak), 0.0)
    attention_probabilities = low(raised / lax.optimization_barrier(jnp.sum(raised, 0)))
    mixed_values = jnp.einsum('wsyi,wsyib->syib', attention_probabilities, value_window, precision=HIGH_PRECISION)
    return mixed_values.reshape(rows_count, cols_count, H * HEAD_SIZE)

def flatten_lead(value):
    return value.reshape((value.shape[0] * value.shape[1],) + value.shape[2:])

def layer(inputs, time_emb, gain_cols, attn_in, time_in, rel_bias, out_proj, mlp_in, mlp_out, segment_ids):
    width = inputs.shape[-1]
    normed = low(layer_norm(inputs, gain_cols[:, 0]))
    time_rows = low(time_emb)
    time_proj = low_back(jnp.einsum('mksd,de->mkse', time_rows, time_in, precision=HIGH_PRECISION))
    member = (segment_ids[..., None] == jnp.arange(SEGS)).astype(inputs.dtype)
    token_time = jnp.einsum('mkrcs,mkse->mkrce', member, time_proj, precision=HIGH_PRECISION)
    qkv = jnp.einsum('mkrcd,de->mkrce', normed, attn_in, precision=HIGH_PRECISION)
    query = low_back(low(qkv[..., :width] + token_time[..., :width]))
    keys = low_back(low(qkv[..., width:2 * width]))
    values = low_back(low(qkv[..., 2 * width:] + token_time[..., width:]))
    attend = jax.checkpoint(canvas_attention)

    def one_canvas(item):
        return attend(item[0], item[1], item[2], item[3], rel_bias)
    mixed_values = lax.map(one_canvas, (flatten_lead(query), flatten_lead(keys), flatten_lead(values), flatten_lead(segment_ids + 2)))
    mixed_values = low_back(low(mixed_values.reshape(inputs.shape)))
    branch = low_back(jnp.einsum('mkrcd,de->mkrce', mixed_values, out_proj, precision=HIGH_PRECISION))
    resid = inputs + branch
    hidden_in = low(layer_norm(resid, gain_cols[:, 1]))
    pre_act = low_back(jnp.einsum('mkrcd,de->mkrce', hidden_in, mlp_in, precision=HIGH_PRECISION))
    activated = low(jax.nn.gelu(pre_act, approximate=False))
    mlp_y = jnp.einsum('mkrce,ed->mkrcd', activated, mlp_out, precision=HIGH_PRECISION)
    filled = (segment_ids >= 0)[..., None].astype(inputs.dtype)
    return filled * (resid + mlp_y)

def reference(latents, segment_ids, time_embed, norm_gains, attn_in, time_in, rel_bias, out_proj, mlp_in, mlp_out, cotangent):
    floats = (latents.astype(jnp.float32), time_embed.astype(jnp.float32), norm_gains.astype(jnp.float32), attn_in.astype(jnp.float32), time_in.astype(jnp.float32), rel_bias.astype(jnp.float32), out_proj.astype(jnp.float32), mlp_in.astype(jnp.float32), mlp_out.astype(jnp.float32))

    def forward(inputs, time_emb, gain_cols, w_attn, w_time, score_bias, w_out, w_in, w_back):
        return layer(inputs, time_emb, gain_cols, w_attn, w_time, score_bias, w_out, w_in, w_back, segment_ids)
    result, pull = jax.vjp(forward, *floats)
    grads = pull(cotangent.astype(jnp.float32))
    return (result.astype(jnp.bfloat16), grads[0], grads[1], grads[2], grads[3], grads[4], grads[5], grads[6], grads[7], grads[8])
```

```python
from functools import partial
import jax
import jax.numpy as jnp
from jax import lax
from jax.experimental import pallas as pl
from jax.experimental.pallas import tpu as pltpu

from jax.sharding import PartitionSpec as P

WIN = 5


EPSILON = 1e-05


def padded_2(shard, sides, width):
    for axis, dim in sides:
        devices, length = (lax.axis_size(axis), shard.shape[dim])
        up = [(i, (i + 1) % devices) for i in range(devices - 1)]
        down = [(j, i) for i, j in up]
        last = lax.slice_in_dim(shard, length - width, length, axis=dim)
        first = lax.slice_in_dim(shard, 0, width, axis=dim)
        before = lax.ppermute(last, axis, up)
        after = lax.ppermute(first, axis, down)
        shard = jnp.concatenate([before, shard, after], axis=dim)
    return shard


def shifted(shard, axis, by):
    devices = lax.axis_size(axis)
    pairs = [(i, i + by) for i in range(devices) if 0 <= i + by < devices]
    return lax.ppermute(shard, axis, pairs)


def shortened(shard):

    def short(part):
        return part.astype(jnp.bfloat16) if part.dtype == jnp.float32 else part

    return jax.tree.map(short, shard)


def normalize(value, gain):
    center = value - jnp.mean(value, -1, keepdims=True)
    scaled = lax.rsqrt(jnp.mean(center * center, -1, keepdims=True) + EPSILON)
    unit = center * scaled
    return (unit, scaled, unit * gain)


def normalize_back(unit, scaled, gain, grad_out):
    part = grad_out * gain
    return scaled * (
        part - jnp.mean(part, -1, keepdims=True) - unit * jnp.mean(part * unit, -1, keepdims=True)
    )


def rows_dot(left, right):
    return lax.dot_general(
        left, right, (((0,), (0,)), ((), ())), preferred_element_type=jnp.float32
    )


def back_dot(left, weight):
    return lax.dot_general(
        left, weight, (((1,), (1,)), ((), ())), preferred_element_type=jnp.float32
    )


def neighbour_stack(padded, band_rows, columns):
    pieces = [padded[:, i : i + band_rows, j : j + columns] for i in range(WIN) for j in range(WIN)]
    stacked = jnp.stack(pieces)
    return stacked.reshape((WIN * WIN, -1) + padded.shape[3:])


def spread_back(terms, canvases, band_rows, columns):
    reach = WIN // 2
    shaped = terms.reshape((WIN * WIN, canvases, band_rows, columns, terms.shape[-1]))
    summed = None
    for i in range(WIN):
        for j in range(WIN):
            placed = jnp.pad(
                shaped[i * WIN + j], ((0, 0), (i, 2 * reach - i), (j, 2 * reach - j), (0, 0))
            )
            summed = placed if summed is None else summed + placed
    return summed


def head_total(terms, head_sum):
    flat = terms.reshape(-1, terms.shape[-1])
    return jnp.dot(flat, head_sum, precision=lax.Precision.HIGHEST).reshape(
        terms.shape[:-1] + (head_sum.shape[1],)
    )


def head_widen(values, head_spread):
    flat = values.reshape(-1, values.shape[-1])
    return jnp.dot(flat, head_spread, preferred_element_type=jnp.bfloat16).reshape(
        values.shape[:-1] + (head_spread.shape[1],)
    )


def local(
    latents,
    segment_ids,
    time_embed,
    norm_gains,
    attn_in,
    time_in,
    rel_bias,
    out_proj,
    mlp_in,
    mlp_out,
    cotangent,
):
    micro_count, canvases, band_rows, columns, width = latents.shape
    slots = time_embed.shape[2]
    heads = rel_bias.shape[1]
    head_dim = width // heads
    reach = WIN // 2
    tokens = canvases * band_rows * columns
    score_scale = head_dim ** (-0.5)
    head_sum = (jnp.arange(width)[:, None] // head_dim == jnp.arange(heads)[None, :]).astype(
        jnp.float32
    )
    head_spread = head_sum.T.astype(jnp.bfloat16)
    owned = (attn_in, time_in, out_proj, mlp_in, mlp_out)
    seg_code = segment_ids + 2
    seg_rims = padded_2(seg_code, (("band", 2),), reach)
    seg_rims = jnp.pad(seg_rims, ((0, 0), (0, 0), (0, 0), (reach, reach)))
    band_share = 1.0 / lax.axis_size("band")
    outputs = []
    input_grads = []
    time_grads = []
    accum = None
    shards = None
    bias_accum = jnp.zeros(rel_bias.shape, jnp.float32)
    for batch_index in range(micro_count):
        full_weights = (
            lax.all_gather(owned[0], "canvas", axis=0, tiled=True),
            lax.all_gather(owned[1], "canvas", axis=0, tiled=True),
            lax.all_gather(owned[2], "canvas", axis=0, tiled=True),
            lax.all_gather(owned[3], "canvas", axis=0, tiled=True),
            lax.all_gather(owned[4], "canvas", axis=0, tiled=True),
        )
        w_attn, w_time, w_out, w_in, w_back = full_weights
        inputs = latents[batch_index].astype(jnp.float32).reshape(tokens, width)
        unit_one, scaled_one, normed_one = normalize(inputs, norm_gains[:, 0])
        normed = normed_one.astype(jnp.bfloat16)
        time_rows = time_embed[batch_index].reshape(canvases * slots, width)
        time_proj = jnp.dot(time_rows, w_time, preferred_element_type=jnp.float32).reshape(
            canvases, slots, 2 * width
        )
        seg_here = segment_ids[batch_index]
        member = (seg_here[..., None] == jnp.arange(slots)).astype(jnp.float32)
        token_time = jnp.einsum(
            "krcs,kse->krce", member, time_proj, precision=lax.Precision.HIGHEST
        ).reshape(tokens, 2 * width)
        qkv = jnp.dot(normed, w_attn, preferred_element_type=jnp.float32)
        query = (qkv[:, :width] + token_time[:, :width]).astype(jnp.bfloat16)
        keys = qkv[:, width : 2 * width].astype(jnp.bfloat16)
        values = (qkv[:, 2 * width :] + token_time[:, width:]).astype(jnp.bfloat16)
        paired = jnp.stack([keys, values]).reshape(2, canvases, band_rows, columns, width)
        paired = padded_2(paired, (("band", 2),), reach)
        paired = jnp.pad(paired, ((0, 0), (0, 0), (0, 0), (reach, reach), (0, 0)))
        key_win = neighbour_stack(paired[0], band_rows, columns)
        value_win = neighbour_stack(paired[1], band_rows, columns)
        seg_win = neighbour_stack(seg_rims[batch_index], band_rows, columns)
        allowed = (seg_win == seg_code[batch_index].reshape(1, tokens))[..., None]
        query_wide = query.astype(jnp.float32)
        raw = head_total(query_wide[None] * key_win.astype(jnp.float32), head_sum)
        logit_scores = raw * score_scale + rel_bias[:, None, :]
        masked = jnp.where(allowed, logit_scores, -1e30)
        peak = jnp.max(masked, 0)
        raised = jnp.where(allowed, jnp.exp(masked - peak), 0.0)
        probs_full = raised / jnp.sum(raised, 0)
        attention_probabilities = probs_full.astype(jnp.bfloat16)
        probs_wide = head_widen(attention_probabilities, head_spread)
        mixed_values = jnp.sum(probs_wide.astype(jnp.float32) * value_win.astype(jnp.float32), 0)
        attended = mixed_values.astype(jnp.bfloat16)
        branch = jnp.dot(attended, w_out, preferred_element_type=jnp.float32)
        resid = inputs + branch
        unit_two, scaled_two, normed_two = normalize(resid, norm_gains[:, 1])
        hidden_in = normed_two.astype(jnp.bfloat16)
        pre_act = jnp.dot(hidden_in, w_in, preferred_element_type=jnp.float32)
        activated = jax.nn.gelu(pre_act, approximate=False).astype(jnp.bfloat16)
        mlp_y = jnp.dot(activated, w_back, preferred_element_type=jnp.float32)
        filled = (seg_here >= 0).reshape(tokens, 1)
        outputs.append(
            jnp.where(filled, resid + mlp_y, 0.0)
            .astype(jnp.bfloat16)
            .reshape(canvases, band_rows, columns, width)
        )
        grad_y = cotangent[batch_index].reshape(tokens, width)
        grad_f = jnp.where(filled, grad_y, jnp.zeros_like(grad_y))
        grad_back = rows_dot(activated, grad_f)
        grad_act = back_dot(grad_f, w_back)
        gelu_out, gelu_pull = jax.vjp(partial(jax.nn.gelu, approximate=False), pre_act)
        grad_pre = gelu_pull(grad_act)[0].astype(jnp.bfloat16)
        grad_in = rows_dot(hidden_in, grad_pre)
        grad_hidden = back_dot(grad_pre, w_in)
        grad_resid = jnp.where(filled, grad_y.astype(jnp.float32), 0.0) + normalize_back(
            unit_two, scaled_two, norm_gains[:, 1], grad_hidden
        )
        gain_two = jnp.sum(grad_hidden * unit_two, 0)
        grad_branch = grad_resid.astype(jnp.bfloat16)
        grad_out = rows_dot(attended, grad_branch)
        grad_att = back_dot(grad_branch, w_out).astype(jnp.bfloat16)
        grad_att_wide = grad_att.astype(jnp.float32)
        grad_probs = head_total(grad_att_wide[None] * value_win.astype(jnp.float32), head_sum)
        centered = jnp.sum(probs_full * grad_probs, 0)
        grad_scores = (probs_full * (grad_probs - centered)).astype(jnp.bfloat16)
        bias_accum = bias_accum + jnp.sum(grad_scores.astype(jnp.float32), axis=1)
        scores_wide = head_widen(grad_scores, head_spread).astype(jnp.float32)
        grad_query = jnp.sum(scores_wide * key_win.astype(jnp.float32), 0) * score_scale
        key_summed = (
            spread_back(scores_wide * query_wide[None], canvases, band_rows, columns) * score_scale
        )
        value_summed = spread_back(
            probs_wide.astype(jnp.float32) * grad_att_wide[None], canvases, band_rows, columns
        )
        pair_grad = jnp.stack([key_summed, value_summed])[:, :, :, reach : reach + columns]
        upper_rim = pair_grad[:, :, :reach]
        lower_rim = pair_grad[:, :, band_rows + reach :]
        owned_rows = pair_grad[:, :, reach : reach + band_rows]
        from_below = shifted(upper_rim.astype(jnp.bfloat16), "band", -1).astype(upper_rim.dtype)
        from_above = shifted(lower_rim.astype(jnp.bfloat16), "band", 1).astype(lower_rim.dtype)
        owned_rows = owned_rows.at[:, :, band_rows - reach :].add(from_below)
        owned_rows = owned_rows.at[:, :, :reach].add(from_above)
        grad_keys = owned_rows[0].reshape(tokens, width).astype(jnp.bfloat16)
        grad_values = owned_rows[1].reshape(tokens, width).astype(jnp.bfloat16)
        grad_q_low = grad_query.astype(jnp.bfloat16)
        member_low = member.astype(jnp.bfloat16).reshape(canvases, band_rows * columns, slots)
        slot_query = jnp.einsum(
            "kns,knd->ksd",
            member_low,
            grad_q_low.reshape(canvases, band_rows * columns, width),
            preferred_element_type=jnp.float32,
        )
        slot_value = jnp.einsum(
            "kns,knd->ksd",
            member_low,
            grad_values.reshape(canvases, band_rows * columns, width),
            preferred_element_type=jnp.float32,
        )
        slot_part = jnp.concatenate([slot_query, slot_value], -1)
        slot_total = lax.psum(slot_part.astype(jnp.bfloat16), "band")
        slot_low = slot_total.reshape(canvases * slots, 2 * width)
        time_grads.append(back_dot(slot_low, w_time).reshape(canvases, slots, width))
        grad_time_in = rows_dot(time_rows, slot_low) * band_share
        grad_qkv = jnp.concatenate([grad_q_low, grad_keys, grad_values], -1)
        grad_attn = rows_dot(normed, grad_qkv)
        grad_normed = back_dot(grad_qkv, w_attn)
        grad_inputs = grad_resid + normalize_back(
            unit_one, scaled_one, norm_gains[:, 0], grad_normed
        )
        gain_one = jnp.sum(grad_normed * unit_one, 0)
        input_grads.append(grad_inputs.reshape(canvases, band_rows, columns, width))
        micro_grads = (
            grad_attn,
            grad_time_in,
            grad_out,
            grad_in,
            grad_back,
            jnp.stack([gain_one, gain_two], 1),
        )
        accum = micro_grads if accum is None else jax.tree.map(jnp.add, accum, micro_grads)
    wide_sums = jax.tree.map(
        lambda part: part.astype(jnp.float32),
        lax.psum_scatter(shortened(accum), "canvas", scatter_dimension=0, tiled=True),
    )
    shards = jax.tree.map(
        lambda part: part.astype(jnp.float32),
        lax.psum_scatter(shortened(wide_sums), "band", scatter_dimension=0, tiled=True),
    )
    bias_grad = lax.psum(bias_accum, ("canvas", "band"))
    return (
        jnp.stack(outputs),
        jnp.stack(input_grads),
        jnp.stack(time_grads),
        shards[5],
        shards[0],
        shards[1],
        bias_grad,
        shards[2],
        shards[3],
        shards[4],
    )


MESH = pl.DeviceIdType.MESH
BF, F32 = jnp.bfloat16, jnp.float32
EPS = 1e-5
TOK, HALF, D, QC, FH = 544, 272, 1152, 640, 2304
KEYS, KW, PADK = 784, 512, 80
SCALE = 72 ** -0.5
NEG = -1e30


def dot(a, b):
    return jnp.dot(a, b, preferred_element_type=F32)


def dot_nt(a, b):
    return lax.dot_general(a, b, (((1,), (1,)), ((), ())), preferred_element_type=F32)


def dot_tn(a, b):
    return lax.dot_general(a, b, (((0,), (0,)), ((), ())), preferred_element_type=F32)


def norm(v):
    center = v - jnp.mean(v, -1, keepdims=True)
    r = lax.rsqrt(jnp.mean(center * center, -1, keepdims=True) + EPS)
    return center * r, r


def norm_back(n, r, e):
    return r * (e - jnp.mean(e, -1, keepdims=True) - n * jnp.mean(e * n, -1, keepdims=True))


def place():
    c, b = lax.axis_index("canvas"), lax.axis_index("band")
    return c, b, b // 2, lax.rem(b, 2)


def greet(devs):
    bar = pltpu.get_barrier_semaphore()
    for dev in devs:
        pl.semaphore_signal(bar, 1, device_id=dev, device_id_type=MESH)
    pl.semaphore_wait(bar, len(devs))


def remote(src, dst, ss, rs, dev):
    return pltpu.make_async_remote_copy(src, dst, ss, rs, device_id=dev, device_id_type=MESH)


def head_window(h):
    ws = pl.multiple_of(jnp.minimum(80 * h // 128, 3) * 128, 128)
    lane = lax.broadcasted_iota(jnp.int32, (1, 256), 1) + ws - 80 * h
    hm = jnp.where((lane >= 0) & (lane < 80), 1.0, 0.0).astype(BF)
    return pl.ds(ws, 256), hm


def build_masks(segq, segk, colq, colk, mask):
    for m in range(2):
        for j in range(2):
            ok = (segq[m, j] == segk[m, j]) & (jnp.abs(colq[...] - colk[...]) < 2.5)
            mask[m, j] = jnp.where(ok, 0.0, NEG).astype(mask.dtype)


def toeplitz(base, h):
    row = jnp.broadcast_to(base[pl.ds(h, 1)], (HALF, KW))
    return pltpu.roll(row, 0, 1, stride=1, stride_axis=0)


def forward_kernel(lat, gains, WA, WO, WI, WB, te, ti, segq, segk, colq, colk, base, onehot, filled,
                   out, xn, q, kb, vb, lse, o, hres, hn, g, gp,
                   tp_send, tp_recv, tmix, mask, toep, of, x_send, x_recv, fo,
                   xs, xr, ts, tr, ks, kr, as_, ar, hs, hr, fs, fr):
    c, b, y, k = place()
    sib = {"band": b + 1 - 2 * k}
    ynb = {"band": b + 2 - 4 * y}
    peers = [lax.rem(c + d, 8) for d in range(1, 8)]
    greet([sib, ynb] + [{"canvas": p} for p in peers])
    pend = []

    tp_send[...] = dot(te[...], ti[...]).astype(BF)
    for i, p in enumerate(peers):
        cp = remote(tp_send.at[pl.ds(pl.multiple_of(16 * p, 16), 16)], tp_recv.at[7 - 1 - i], ts.at[i], tr.at[6 - i], {"canvas": p})
        cp.start()
        pend.append(cp)
    mine = pl.ds(pl.multiple_of(HALF * k, 16), HALF)
    other = pl.ds(pl.multiple_of(HALF * (1 - k), 16), HALF)
    for m in range(2):
        n, _ = norm(lat[m].astype(F32))
        xn[m, mine] = (n * gains[0:1]).astype(BF)
        cp = remote(xn.at[m, mine], xn.at[m, mine], xs.at[m], xr.at[m], sib)
        cp.start()
        pend.append(cp)
    build_masks(segq, segk, colq, colk, mask)
    for i in range(7):
        pltpu.make_async_copy(tp_recv.at[i], tp_recv.at[i], tr.at[i]).wait()
    tproj = tp_send[pl.ds(pl.multiple_of(16 * c, 16), 16)].astype(F32)
    for i in range(7):
        tproj = tproj + tp_recv[i].astype(F32)
    hi = tproj.astype(BF)
    tmix[0:16] = hi
    tmix[16:32] = (tproj - hi.astype(F32)).astype(BF)

    dead = pl.ds(pl.multiple_of(y * 624, 16), 80)
    for m in range(2):
        for ref in (kb, vb):
            ref[m, dead] = jnp.zeros((80, QC), BF)
            ref[m, 704:784] = jnp.zeros((80, QC), BF)
    edge = pl.ds(pl.multiple_of(544 - 464 * y, 16), 80)
    land = pl.ds(pl.multiple_of(624 * y, 16), 80)
    land_here = pl.ds(pl.multiple_of(624 * (1 - y), 16), 80)
    for m in range(2):
        pltpu.make_async_copy(xn.at[m, other], xn.at[m, other], xr.at[m]).wait()
        x = xn[m]
        kb[m, 80:624] = dot(x, WA[:, QC:2 * QC]).astype(BF)
        vb[m, 80:624] = (dot(x, WA[:, 2 * QC:]) + dot(onehot[m], tmix[:, QC:])).astype(BF)
        for i, ref in enumerate((kb, vb)):
            cp = remote(ref.at[m, edge], ref.at[m, land], ks.at[m, i], kr.at[m, i], ynb)
            cp.start()
            pend.append(cp)
        q[m] = (dot(x, WA[:, :QC]) + dot(onehot[m], tmix[:, :QC])).astype(BF)
    for m in range(2):
        for i, ref in enumerate((kb, vb)):
            pltpu.make_async_copy(ref.at[m, land_here], ref.at[m, land_here], kr.at[m, i]).wait()

    of[...] = jnp.zeros_like(of)
    lse[...] = jnp.zeros_like(lse)

    def head(h, _):
        win, hm = head_window(h)
        toep[...] = toeplitz(base, h)
        lane_h = lax.broadcasted_iota(jnp.int32, (1, 128), 1) == h

        def tile(t, _):
            m, j = t // 2, lax.rem(t, 2)
            rows = pl.ds(pl.multiple_of(HALF * j, 16), HALF)
            krows = pl.ds(pl.multiple_of(HALF * j, 16), KW)
            s = dot_nt(q[m, rows, win] * hm, kb[m, krows, win])
            s = s * SCALE + (toep[...] + mask[m, j])
            peak = jnp.max(s, -1, keepdims=True)
            e = jnp.exp(s - peak)
            total = jnp.sum(e, -1, keepdims=True)
            p = (e * (1.0 / total)).astype(BF)
            of[m, rows, win] += dot(p, vb[m, krows, win] * hm)
            lse[m, rows] = jnp.where(lane_h, peak + jnp.log(total), lse[m, rows])
            return 0

        return lax.fori_loop(0, 4, tile, 0)

    lax.fori_loop(0, 8, head, 0)
    for m in range(2):
        o[m] = of[m].astype(BF)

    for m in range(2):
        x_send[0, m] = dot(o[m, other], WO[...]).astype(BF)
        cp = remote(x_send.at[0, m], x_recv.at[0, m], as_.at[m], ar.at[m], sib)
        cp.start()
        pend.append(cp)
    for m in range(2):
        hres[m] = lat[m].astype(F32) + dot(o[m, mine], WO[...])
    for m in range(2):
        pltpu.make_async_copy(x_recv.at[0, m], x_recv.at[0, m], ar.at[m]).wait()
        hv = hres[m] + x_recv[0, m].astype(F32)
        hres[m] = hv
        n, _ = norm(hv)
        hn[m, mine] = (n * gains[1:2]).astype(BF)
        cp = remote(hn.at[m, mine], hn.at[m, mine], hs.at[m], hr.at[m], sib)
        cp.start()
        pend.append(cp)
    for m in range(2):
        pltpu.make_async_copy(hn.at[m, other], hn.at[m, other], hr.at[m]).wait()

        def up(i, _):
            cols = pl.ds(pl.multiple_of(i * 384, 128), 384)
            u = dot(hn[m], WI[:, cols])
            phi = 0.5 + 0.5 * lax.erf(u * (0.5 ** 0.5))
            g[m, :, cols] = (u * phi).astype(BF)
            gp[m, :, cols] = (phi + u * (jnp.exp(-0.5 * u * u) * 0.3989422804014327)).astype(BF)
            return 0

        lax.fori_loop(0, 6, up, 0)
    for m in range(2):
        def down_other(i, _):
            cols = pl.ds(pl.multiple_of(i * 384, 128), 384)
            x_send[1, m, :, cols] = dot(g[m, other], WB[:, cols]).astype(BF)
            return 0

        lax.fori_loop(0, 3, down_other, 0)
        cp = remote(x_send.at[1, m], x_recv.at[1, m], fs.at[m], fr.at[m], sib)
        cp.start()
        pend.append(cp)

        def down(i, _):
            cols = pl.ds(pl.multiple_of(i * 384, 128), 384)
            fo[m, :, cols] = dot(g[m, mine], WB[:, cols])
            return 0

        lax.fori_loop(0, 3, down, 0)
    for m in range(2):
        pltpu.make_async_copy(x_recv.at[1, m], x_recv.at[1, m], fr.at[m]).wait()
        out[m] = ((hres[m] + (fo[m] + x_recv[1, m].astype(F32))) * filled[m]).astype(BF)
    for cp in pend:
        cp.wait_send()


def forward(lat, gains, WA, WO, WI, WB, te, ti, segq, segk, colq, colk, base, onehot, filled):
    S = jax.ShapeDtypeStruct
    dma = pltpu.SemaphoreType.DMA
    V = pl.BlockSpec(memory_space=pltpu.VMEM)
    return pl.pallas_call(
        forward_kernel,
        out_shape=[S((2, HALF, D), BF), S((2, TOK, D), BF), S((2, TOK, QC), BF), S((2, KEYS, QC), BF), S((2, KEYS, QC), BF),
                   S((2, TOK, 128), F32), S((2, TOK, QC), BF), S((2, HALF, D), F32), S((2, TOK, D), BF), S((2, TOK, FH), BF), S((2, TOK, FH), BF)],
        in_specs=[V] * 15, out_specs=[V] * 11,
        scratch_shapes=[pltpu.VMEM((128, 2 * QC), BF), pltpu.VMEM((7, 16, 2 * QC), BF), pltpu.VMEM((32, 2 * QC), BF), pltpu.VMEM((2, 2, HALF, KW), F32),
                        pltpu.VMEM((HALF, KW), F32), pltpu.VMEM((2, TOK, QC), F32), pltpu.VMEM((2, 2, HALF, D), BF), pltpu.VMEM((2, 2, HALF, D), BF),
                        pltpu.VMEM((2, HALF, D), F32),
                        dma((2,)), dma((2,)), dma((7,)), dma((7,)), dma((2, 2)), dma((2, 2)), dma((2,)), dma((2,)), dma((2,)), dma((2,)), dma((2,)), dma((2,))],
        compiler_params=pltpu.CompilerParams(collective_id=1, has_side_effects=True, vmem_limit_bytes=62 * 2 ** 20),
        name="forward")(lat, gains, WA, WO, WI, WB, te, ti, segq, segk, colq, colk, base, onehot, filled)
SPEC = {"A": (144, 640, 640), "O": (80, 384, 384), "I": (144, 896, 512), "B": (288, 512, 128)}
NAMES = "AOIB"


def gather_kernel(*refs):
    own = dict(zip(NAMES, refs[:4]))
    full = dict(zip(NAMES, refs[4:8]))
    s_sem, r_sem, y_sem, l_sem = refs[8:]
    c, b, y, k = place()
    z, x = c // 2, lax.rem(c, 2)
    zp = [lax.rem(z + d, 4) for d in (1, 3, 2)]
    xdev, ydev = {"canvas": c + 1 - 2 * x}, {"band": b + 2 - 4 * y}
    greet([{"canvas": p * 2 + x} for p in zp] + [xdev, ydev])
    pend, count = [], dict.fromkeys(NAMES, 0)

    def part(name, src, plane, side):
        rows, wide, mid = SPEC[name]
        at = pl.ds(pl.multiple_of(src * rows, 16), rows)
        if plane:
            return at, pl.ds(pl.multiple_of(wide * side, 128), wide + mid)
        return at, pl.ds(pl.multiple_of((wide + mid) * side, 128), wide)

    def send(name, src, dev, plane, first=False):
        n = NAMES.index(name)
        at, cols = part(name, src, plane, y)
        cp = remote(own[name].at[:, cols] if first else full[name].at[at, cols], full[name].at[at, cols],
                    s_sem.at[n, count[name]], (r_sem if plane else y_sem).at[n, src], dev)
        count[name] += 1
        cp.start()
        pend.append(cp)

    def own_sends(name):
        for p in zp:
            send(name, c, {"canvas": p * 2 + x}, True, True)
        send(name, c, xdev, True, True)

    def wait(name, src, plane):
        at, cols = part(name, src, plane, y if plane else 1 - y)
        view = full[name].at[at, cols]
        pltpu.make_async_copy(view, view, (r_sem if plane else y_sem).at[NAMES.index(name), src]).wait()

    local = []
    for n, name in enumerate(NAMES):
        rows = SPEC[name][0]
        cp = pltpu.make_async_copy(own[name], full[name].at[pl.ds(pl.multiple_of(c * rows, 16), rows)], l_sem.at[n])
        cp.start()
        local.append(cp)
    own_sends("A")
    own_sends("O")
    following = {"A": "I", "I": "B"}
    for name in NAMES:
        if name in following:
            own_sends(following[name])
        for i, p in enumerate(zp):
            src = p * 2 + x
            wait(name, src, True)
            send(name, src, xdev, True)
            send(name, src, ydev, False)
            if i == 0:
                src = z * 2 + 1 - x
                wait(name, src, True)
                send(name, src, ydev, False)
        for p in zp:
            src = p * 2 + 1 - x
            wait(name, src, True)
            send(name, src, ydev, False)
    for name in NAMES:
        for d in range(1, 8):
            wait(name, lax.rem(c + d, 8), False)
    for cp in pend:
        cp.wait_send()
    for cp in local:
        cp.wait()


def gather(*own):
    anyspace = pl.BlockSpec(memory_space=pl.ANY)
    dma = pltpu.SemaphoreType.DMA
    return pl.pallas_call(
        gather_kernel,
        out_shape=[jax.ShapeDtypeStruct((8 * SPEC[n][0], 2 * SPEC[n][1] + SPEC[n][2]), BF) for n in NAMES],
        in_specs=[anyspace] * 4, out_specs=[anyspace] * 4,
        scratch_shapes=[dma((4, 14)), dma((4, 8)), dma((4, 8)), dma((4,))],
        compiler_params=pltpu.CompilerParams(collective_id=0, has_side_effects=True),
        name="gather")(*own)


def prologue(latents, segment_ids, time_embed, norm_gains, attn_in, time_in, rel_bias, out_proj, mlp_in, mlp_out, cotangent):
    c, b, y, k = place()

    def pick(v, axis):
        return lax.dynamic_index_in_dim(v, k, axis, keepdims=False)

    def pad_heads(v, n):
        v = pick(v.reshape(144, n, 8, 2, 72), 3)
        return jnp.pad(v, ((0, 0), (0, 0), (0, 0), (0, 8))).reshape(144, n * QC)

    own = (pad_heads(attn_in, 3),
           jnp.pad(pick(out_proj.reshape(2, 72, D), 0), ((0, 8), (0, 0))),
           pick(mlp_in.reshape(144, 8, 2, 288), 2).reshape(144, FH),
           pick(mlp_out.reshape(2, 288, D), 0))
    ti = pad_heads(time_in, 2)
    seg = lax.all_gather(segment_ids, "band", axis=2, tiled=True).reshape(2, 32 * 34) + 2
    te_all = lax.all_gather(jnp.pad(time_embed.reshape(10, D), ((0, 6), (0, 0))), "canvas", axis=0, tiled=True)
    te = lax.dynamic_slice_in_dim(te_all, 144 * c, 144, 1)
    segp = jnp.pad(seg, ((0, 0), (80, 240))).astype(F32)
    start = TOK * y
    chip = lax.dynamic_slice_in_dim(seg, start, TOK, 1)
    live = jnp.arange(KW) < 432
    segk = jnp.stack([jnp.where(live, lax.dynamic_slice_in_dim(segp, start + HALF * j, KW, 1), 0.0) for j in range(2)], 1)
    segq = chip.astype(F32).reshape(2, 2, HALF)
    slot = jnp.arange(32) % 16
    onehot = jnp.stack([(chip[m][:, None] - 2 + 5 * m == slot[None]) & (chip[m][:, None] >= 2) for m in range(2)]).astype(BF)
    colq = (jnp.arange(HALF) % 34).astype(F32)[:, None]
    colk = ((jnp.arange(KW) - 80 + 34 * 3) % 34).astype(F32)[None]
    bias = pick(rel_bias.reshape(25, 8, 2), 2)
    base = jnp.full((8, KW), NEG, F32)
    places = [80 + 34 * dr + dc for dr in range(-2, 3) for dc in range(-2, 3)]
    base = base.at[:, jnp.array(places)].set(bias.T)
    filled = (segment_ids.reshape(2, HALF, 1) >= 0).astype(F32)
    return dict(own=own, ti=ti, te=te, te_all=te_all, segq=segq[..., None], segk=segk[:, :, None], onehot=onehot, colq=colq, colk=colk,
                base=base, filled=filled, lat=latents.reshape(2, HALF, D), gains=norm_gains.T)
RSPEC = {"A": (144, 640, 640), "O": (80, 384, 384), "I": (144, 768, 768), "B": (288, 384, 384)}


def scatter_scratch(name):
    rows, wide, mid = RSPEC[name]
    slab = wide + mid
    dma = pltpu.SemaphoreType.DMA
    short = name in "OB"
    frows, sources = (((48 if name == "O" else 144), 2) if short else (48, 4))
    return [pltpu.VMEM((8 * rows, wide), BF), pltpu.VMEM((4 * rows, slab), BF), pltpu.VMEM((3 * rows, slab), BF),
            pltpu.VMEM((2 if short else 4, frows, slab), BF), pltpu.VMEM((sources, frows, slab), BF),
            dma((4,)), dma((4,)), dma((8,)), dma((8,)), dma((3,)), dma((3,)), dma((4,)), dma((4,))]


N_SCATTER = 13


class Scatter:
    def __init__(self, name, grad, total, scratch, pend):
        self.name, self.grad, self.total, self.pend = name, grad, total, pend
        (self.yr, self.xr, self.zr, self.stage, self.fr, self.ys, self.yw, self.xs, self.xw, self.zs, self.zw, self.fs, self.fw) = scratch
        self.rows, self.wide, self.mid = RSPEC[name]
        self.c, self.b, self.y, self.k = place()
        self.z, self.x = self.c // 2, lax.rem(self.c, 2)
        y, w, l = self.y, self.wide, self.mid
        self.slab = pl.ds(pl.multiple_of(w * y, 128), w + l)
        self.mids = pl.ds(w, l)
        self.side = pl.ds(pl.multiple_of((w + l) * y, 128), w)
        self.away = pl.ds(pl.multiple_of((w + l) * (1 - y), 128), w)
        self.slab_mid = pl.ds(pl.multiple_of(w * (1 - y), 128), l)
        self.slab_side = pl.ds(pl.multiple_of(l * y, 128), w)
        self.xdev, self.ydev = {"canvas": self.c + 1 - 2 * self.x}, {"band": self.b + 2 - 4 * self.y}

    def at(self, group):
        return pl.ds(pl.multiple_of(group * self.rows, 16), self.rows)

    def go(self, src, dst, ss, rs, dev):
        cp = remote(src, dst, ss, rs, dev)
        cp.start()
        self.pend.append(cp)

    def parts(self):
        return (self.away, self.wide), (self.mids, self.mid), (self.side, self.wide)

    def send_y(self):
        for i in range(4):
            rows = pl.ds(2 * self.rows * i, 2 * self.rows)
            self.go(self.grad.at[rows, self.away], self.yr.at[rows], self.ys.at[i], self.yw.at[i], self.ydev)

    def send_mid(self):
        for i in range(4):
            self.go(self.grad.at[self.at(2 * i + 1 - self.x), self.mids], self.xr.at[pl.ds(self.rows * i, self.rows), self.slab_mid],
                    self.xs.at[i], self.xw.at[i], self.xdev)

    def side_x(self, i):
        rows2 = pl.ds(2 * self.rows * i, 2 * self.rows)
        pltpu.make_async_copy(self.yr.at[rows2], self.yr.at[rows2], self.yw.at[i]).wait()
        self.grad[rows2, self.side] = (self.grad[rows2, self.side].astype(F32) + self.yr[rows2].astype(F32)).astype(BF)
        self.go(self.grad.at[self.at(2 * i + 1 - self.x), self.side], self.xr.at[pl.ds(self.rows * i, self.rows), self.slab_side],
                self.xs.at[4 + i], self.xw.at[4 + i], self.xdev)

    def sum_x(self, i):
        rows = pl.ds(pl.multiple_of(self.rows * i, 16), self.rows)
        for view, sem in ((self.xr.at[rows, self.slab_mid], i), (self.xr.at[rows, self.slab_side], 4 + i)):
            pltpu.make_async_copy(view, view, self.xw.at[sem]).wait()
        return self.grad[self.at(2 * i + self.x), self.slab].astype(F32) + self.xr[rows].astype(F32)

    def send_z(self, d):
        i = lax.rem(self.z + d, 4)
        rows = self.at(2 * i + self.x)
        self.grad[rows, self.slab] = self.sum_x(i).astype(BF)
        self.go(self.grad.at[rows, self.slab], self.zr.at[pl.ds((3 - d) * self.rows, self.rows)], self.zs.at[d - 1], self.zw.at[3 - d],
                {"canvas": 2 * i + self.x})

    def finish(self):
        acc = self.sum_x(self.z)
        for i in range(3):
            rows = pl.ds(i * self.rows, self.rows)
            pltpu.make_async_copy(self.zr.at[rows], self.zr.at[rows], self.zw.at[i]).wait()
            acc = acc + self.zr[rows].astype(F32)
        self.total[0:self.rows, 0:self.wide + self.mid] = acc
        n = {"A": 36, "I": 36, "O": 36, "B": 144}[self.name]
        dests = [(i, i) for i in range(4)] if self.name in "AI" else [(i, 2 * self.k + i) for i in range(2)]
        slot = self.b if self.name in "AI" else self.y
        for i, dest in dests:
            piece = self.total[n * i:n * i + n, 0:self.wide + self.mid].astype(BF)
            self.stage[i, 0:n] = piece
            if n == 36:
                self.stage[i, 36:48] = jnp.zeros((12, self.wide + self.mid), BF)

            @pl.when(self.b == dest)
            def _():
                self.fr[slot] = self.stage[i]

            @pl.when(self.b != dest)
            def _():
                remote(self.stage.at[i], self.fr.at[slot], self.fs.at[i], self.fw.at[slot], {"band": dest}).start()
        self.dests = dests

    def collect(self, out):
        if self.name in "AI":
            slots = [(i, i) for i in range(4)]
        else:
            slots = [(i, 2 * i + self.y) for i in range(2)]
        for i, src in slots:
            @pl.when(self.b != src)
            def _():
                pltpu.make_async_copy(self.fr.at[i], self.fr.at[i], self.fw.at[i]).wait()
        n = 144 if self.name == "B" else 36
        w, l = self.wide, self.mid
        for half in range(2 if self.name in "AI" else 1):
            lo, hi = (self.fr[half], self.fr[2 + half]) if self.name in "AI" else (self.fr[0], self.fr[1])
            lo, hi = lo.astype(F32)[:n], hi.astype(F32)[:n]
            dst = out.at[half] if self.name in "AI" else out
            dst[:, 0:w] = lo[:, :w]
            dst[:, w:w + l] = lo[:, w:] + hi[:, :l]
            dst[:, w + l:] = hi[:, l:]
        for i, dest in self.dests:
            @pl.when(self.b != dest)
            def _():
                remote(self.stage.at[i], self.fr.at[0], self.fs.at[i], self.fw.at[0], {"band": dest}).wait_send()


def everyone():
    c, b, y, k = place()
    z, x = c // 2, lax.rem(c, 2)
    return ([{"band": lax.rem(b + d, 4)} for d in (1, 2, 3)] + [{"canvas": c + 1 - 2 * x}]
            + [{"canvas": 2 * lax.rem(z + d, 4) + x} for d in (1, 2, 3)])


def mlp_back_kernel(cot, filled, gains, WI, WB, hres, hn, g, gp,
                    dh, da, gain, out_b, out_i,
                    grad_b, grad_i, du, x_send, x_recv, dn, total, ds_, dr_, xs, xr, as_, ar, ls, *scratch):
    c, b, y, k = place()
    sib = {"band": b + 1 - 2 * k}
    df = da
    loads = [pltpu.make_async_copy(gp, du, ls.at[0]), pltpu.make_async_copy(hres, dh, ls.at[1])]
    for cp in loads:
        cp.start()
    greet(everyone())
    pend = []
    rs_b = Scatter("B", grad_b, total, scratch[:N_SCATTER], pend)
    rs_i = Scatter("I", grad_i, total, scratch[N_SCATTER:], pend)

    def half(m, which):
        return pl.ds(pl.multiple_of(TOK * m + HALF * which, 16), HALF)

    for m in range(2):
        df[half(m, k)] = (cot[m].astype(F32) * filled[m]).astype(BF)
        cp = remote(df.at[half(m, k)], df.at[half(m, k)], ds_.at[m], dr_.at[m], sib)
        cp.start()
        loads.append(cp)
    for m in range(2):
        v = df.at[half(m, 1 - k)]
        pltpu.make_async_copy(v, v, dr_.at[m]).wait()

    def grad_part(rs, left, right, part):
        cols, _ = part

        def step(i, _):
            r = pl.ds(pl.multiple_of(i * 384, 128), 384)
            rs.grad[r, cols] = dot_tn(left[:, r], right[:, cols]).astype(BF)
            return 0

        lax.fori_loop(0, left.shape[1] // 384, step, 0)

    for i, part in enumerate(rs_b.parts()):
        grad_part(rs_b, g, df, part)
        if i == 0:
            rs_b.send_y()
        if i == 1:
            rs_b.send_mid()

    def back_act(m):
        def step(i, _):
            cols = pl.ds(pl.multiple_of(i * 384, 128), 384)
            rows = pl.ds(TOK * m, TOK)
            du[rows, cols] = (dot_nt(df[rows], WB[cols]) * du[rows, cols].astype(F32)).astype(BF)
            return 0

        lax.fori_loop(0, 6, step, 0)

    loads[0].wait()
    back_act(0)
    for i in range(4):
        rs_b.side_x(i)
    back_act(1)
    parts = rs_i.parts()
    grad_part(rs_i, hn, du, parts[0])
    rs_i.send_y()
    for d in (1, 3, 2):
        rs_b.send_z(d)
    grad_part(rs_i, hn, du, parts[1])
    rs_i.send_mid()
    grad_part(rs_i, hn, du, parts[2])

    for m in range(2):
        def hid(i, _):
            cols = pl.ds(pl.multiple_of(i * 384, 128), 384)
            x_send[m, :, cols] = dot_nt(du[half(m, 1 - k)], WI[cols]).astype(BF)
            return 0

        lax.fori_loop(0, 3, hid, 0)
        cp = remote(x_send.at[m], x_recv.at[m], xs.at[m], xr.at[m], sib)
        cp.start()
        pend.append(cp)

        def hid_own(i, _):
            cols = pl.ds(pl.multiple_of(i * 384, 128), 384)
            dn[m, :, cols] = dot_nt(du[half(m, k)], WI[cols])
            return 0

        lax.fori_loop(0, 3, hid_own, 0)
    for i in range(4):
        rs_i.side_x(i)
    rs_b.finish()
    gain_two = jnp.zeros((1, D), F32)
    loads[1].wait()
    for m in range(2):
        pltpu.make_async_copy(x_recv.at[m], x_recv.at[m], xr.at[m]).wait()
        grad = dn[m] + x_recv[m].astype(F32)
        n, r = norm(dh[m])
        gain_two = gain_two + jnp.sum(grad * n, 0, keepdims=True)
        v = cot[m].astype(F32) * filled[m] + norm_back(n, r, grad * gains[1:2])
        dh[m] = v
        loads[2 + m].wait_send()
        da[half(m, k)] = v.astype(BF)
        cp = remote(da.at[half(m, k)], da.at[half(m, k)], as_.at[m], ar.at[m], sib)
        cp.start()
        pend.append(cp)
    gain[...] = jnp.broadcast_to(gain_two, (8, D))
    for d in (1, 3, 2):
        rs_i.send_z(d)
    rs_b.collect(out_b)
    rs_i.finish()
    for m in range(2):
        v = da.at[half(m, 1 - k)]
        pltpu.make_async_copy(v, v, ar.at[m]).wait()
    rs_i.collect(out_i)
    for cp in pend:
        cp.wait_send()


def mlp_back(*args):
    S = jax.ShapeDtypeStruct
    dma = pltpu.SemaphoreType.DMA
    V = pl.BlockSpec(memory_space=pltpu.VMEM)
    return pl.pallas_call(
        mlp_back_kernel,
        out_shape=[S((2, HALF, D), F32), S((2 * TOK, D), BF), S((8, D), F32), S((144, D), F32), S((2, 36, FH), F32)],
        in_specs=[V] * 5 + [pl.BlockSpec(memory_space=pl.ANY), V, V, pl.BlockSpec(memory_space=pl.ANY)], out_specs=[V] * 5,
        scratch_shapes=[pltpu.VMEM((FH, D), BF), pltpu.VMEM((D, FH), BF), pltpu.VMEM((2 * TOK, FH), BF),
                        pltpu.VMEM((2, HALF, D), BF), pltpu.VMEM((2, HALF, D), BF), pltpu.VMEM((2, HALF, D), F32), pltpu.VMEM((288, 1536), F32)]
        + [dma((2,))] * 7 + scatter_scratch("B") + scatter_scratch("I"),
        compiler_params=pltpu.CompilerParams(collective_id=2, has_side_effects=True, vmem_limit_bytes=127 * 2 ** 19),
        name="mlp_back")(*args)


def attn_back_kernel(WA, WO, ti, gains, lat, xn, q, kb, vb, lse, o, da, dh, segq, segk, colq, colk, base, onehot,
                     dlat, gain, dbias, dt_all, gt, out_o, out_a,
                     grad_o, grad_a, do, dqf, dkf, dvf, dqkv, mask, toep, dsum, rim, rim_in, tsum, tsum_in, gt_send, gt_in, x_send, x_recv, total,
                     ks, kr, ts, tr, ps, pr, us, ur, vs, vr, ls, wr, xs, xr, *scratch):
    load = pltpu.make_async_copy(dh, dlat, ls.at[0])
    load.start()
    c, b, y, k = place()
    sib, ynb = {"band": b + 1 - 2 * k}, {"band": b + 2 - 4 * y}
    peers = [lax.rem(c + d, 8) for d in range(1, 8)]
    z, x = c // 2, lax.rem(c, 2)
    greet([{"band": lax.rem(b + d, 4)} for d in (1, 2, 3)] + [{"canvas": p} for p in peers])
    pend = []
    rs_o = Scatter("O", grad_o, total, scratch[:N_SCATTER], pend)
    rs_a = Scatter("A", grad_a, total, scratch[N_SCATTER:], pend)

    def go(src, dst, ss, rs, dev):
        cp = remote(src, dst, ss, rs, dev)
        cp.start()
        pend.append(cp)

    def arrive(view, sem):
        pltpu.make_async_copy(view, view, sem).wait()

    for i, (cols, _) in enumerate(rs_o.parts()):
        grad_o[:, cols] = dot_tn(o[...], da[:, cols]).astype(BF)
        if i == 0:
            rs_o.send_y()
        if i == 1:
            rs_o.send_mid()
    for m in range(2):
        do[m] = dot_nt(da[pl.ds(TOK * m, TOK)], WO[...]).astype(BF)
    build_masks(segq, segk, colq, colk, mask)
    dqf[...] = jnp.zeros_like(dqf)
    dkf[...] = jnp.zeros_like(dkf)
    dvf[...] = jnp.zeros_like(dvf)

    def head(h, _):
        win, hm = head_window(h)
        toep[...] = toeplitz(base, h)
        dsum[...] = jnp.zeros_like(dsum)
        lane_h = lax.broadcasted_iota(jnp.int32, (1, 128), 1) == h

        def tile(t, _):
            m, j = t // 2, lax.rem(t, 2)
            rows = pl.ds(pl.multiple_of(HALF * j, 16), HALF)
            krows = pl.ds(pl.multiple_of(HALF * j, 16), KW)
            qm, dm = q[m, rows, win] * hm, do[m, rows, win] * hm
            kw = kb[m, krows, win]
            level = jnp.sum(jnp.where(lane_h, lse[m, rows], 0.0), -1, keepdims=True)
            p = jnp.exp(dot_nt(qm, kw) * SCALE + (toep[...] + mask[m, j]) - level)
            dp = dot_nt(dm, vb[m, krows, win])
            delta = jnp.sum(p * dp, -1, keepdims=True)
            ds = (p * (dp - delta)).astype(BF)
            dsum[...] += ds.astype(F32)
            dqf[m, rows, win] += dot(ds, kw * hm)
            dkf[m, krows, win] += dot_tn(ds, qm)
            dvf[m, krows, win] += dot_tn(p.astype(BF), dm)
            return 0

        lax.fori_loop(0, 4, tile, 0)
        strip = dsum[0:8]
        for n in range(8, HALF, 8):
            strip = strip + pltpu.roll(dsum[n:n + 8], KW - n, 1)
        line = strip[0:1]
        for n in range(1, 8):
            line = line + pltpu.roll(strip, KW - n, 1)[n:n + 1]
        dbias[pl.ds(h, 1)] = line
        return 0

    lax.fori_loop(0, 4, head, 0)
    for i in range(4):
        rs_o.side_x(i)
    lax.fori_loop(4, 8, head, 0)
    for d in (1, 3, 2):
        rs_o.send_z(d)

    away = pl.ds(pl.multiple_of(624 * (1 - y), 16), 80)
    edge = pl.ds(pl.multiple_of(544 - 464 * y, 16), 80)
    for m in range(2):
        rim[m, 0] = (dkf[m, away] * SCALE).astype(BF)
        rim[m, 1] = dvf[m, away].astype(BF)
        go(rim.at[m], rim_in.at[m], ks.at[m], kr.at[m], ynb)
    for m in range(2):
        tok = pl.ds(TOK * m, TOK)
        dqkv[tok, 0:QC] = (dqf[m] * SCALE).astype(BF)
    for m in range(2):
        arrive(rim_in.at[m], kr.at[m])
        tok = pl.ds(TOK * m, TOK)
        dkf[m, edge] += rim_in[m, 0].astype(F32) * (1.0 / SCALE)
        dvf[m, edge] += rim_in[m, 1].astype(F32)
        dqkv[tok, QC:2 * QC] = (dkf[m, 80:624] * SCALE).astype(BF)
        dqkv[tok, 2 * QC:] = dvf[m, 80:624].astype(BF)
    rs_o.finish()
    tq = dot_tn(onehot[0], dqkv[0:TOK, 0:QC]) + dot_tn(onehot[1], dqkv[TOK:, 0:QC])
    tv = dot_tn(onehot[0], dqkv[0:TOK, 2 * QC:]) + dot_tn(onehot[1], dqkv[TOK:, 2 * QC:])
    tsum[:, 0:QC] = tq[0:16].astype(BF)
    tsum[:, QC:] = tv[0:16].astype(BF)
    go(tsum, tsum_in, ts.at[0], tr.at[0], ynb)

    for i, (cols, wide) in enumerate(rs_a.parts()):
        def step(n, _):
            r = pl.ds(pl.multiple_of(n * 384, 128), 384)
            grad_a[r, cols] = dot_tn(xn[:, r], dqkv[:, cols]).astype(BF)
            return 0

        lax.fori_loop(0, 3, step, 0)
        if i == 0:
            rs_a.send_y()
            arrive(tsum_in, tr.at[0])
            slots = pl.ds(pl.multiple_of(16 * c, 16), 16)
            dt_all[k, slots] = (tsum[...].astype(F32) + tsum_in[...].astype(F32)).astype(BF)
            for n, p in enumerate(peers):
                go(dt_all.at[k, slots], dt_all.at[k, slots], ps.at[n], pr.at[6 - n], {"canvas": p})
        if i == 1:
            rs_a.send_mid()
    for m in range(2):
        rows = pl.ds(pl.multiple_of(TOK * m + HALF * (1 - k), 16), HALF)
        rows_own = pl.ds(pl.multiple_of(TOK * m + HALF * k, 16), HALF)

        def back(n, _):
            cols = pl.ds(pl.multiple_of(n * 384, 128), 384)
            x_send[m, :, cols] = dot_nt(dqkv[rows], WA[cols]).astype(BF)
            return 0

        lax.fori_loop(0, 3, back, 0)
        go(x_send.at[m], x_recv.at[m], xs.at[m], xr.at[m], sib)

        dqf[m, 0:HALF] = dot_nt(dqkv[rows_own], WA[0:QC])
        dqf[m, HALF:, 0:D - QC] = dot_nt(dqkv[rows_own], WA[QC:])
    rs_o.collect(out_o)
    load.wait()
    for n in range(7):
        slots = pl.ds(pl.multiple_of(16 * lax.rem(c + n + 1, 8), 16), 16)
        arrive(dt_all.at[k, slots], pr.at[n])
    go(dt_all.at[k], dt_all.at[k], us.at[0], ur.at[0], sib)
    gt_send[...] = dot_nt(dt_all[k], ti[...])
    go(gt_send, gt_in, us.at[1], ur.at[1], sib)
    for i in range(4):
        rs_a.side_x(i)
    gain_one = jnp.zeros((1, D), F32)
    for m in range(2):
        arrive(x_recv.at[m], xr.at[m])
        grad = jnp.concatenate([dqf[m, 0:HALF], dqf[m, HALF:, 0:D - QC]], 1) + x_recv[m].astype(F32)
        n, r = norm(lat[m].astype(F32))
        gain_one = gain_one + jnp.sum(grad * n, 0, keepdims=True)
        dlat[m] = dlat[m] + norm_back(n, r, grad * gains[0:1])
    gain[...] = jnp.broadcast_to(gain_one, (8, D))
    arrive(gt_in, ur.at[1])
    gt_in[...] = gt_in[...] + gt_send[...]
    for n, p in enumerate(peers):
        go(gt_in.at[pl.ds(pl.multiple_of(16 * p, 16), 16)], gt.at[c], vs.at[n], vr.at[6 - n], {"canvas": p})
    gt[c] = gt_in[pl.ds(pl.multiple_of(16 * c, 16), 16)]
    for d in (1, 3, 2):
        rs_a.send_z(d)
    rs_a.finish()
    for n in range(7):
        arrive(gt.at[lax.rem(c + n + 1, 8)], vr.at[n])
    arrive(dt_all.at[1 - k], ur.at[0])
    rs_a.collect(out_a)
    for cp in pend:
        cp.wait_send()


def attn_back(*args):
    S = jax.ShapeDtypeStruct
    dma = pltpu.SemaphoreType.DMA
    V = pl.BlockSpec(memory_space=pltpu.VMEM)
    return pl.pallas_call(
        attn_back_kernel,
        out_shape=[S((2, HALF, D), F32), S((8, D), F32), S((8, KW), F32), S((2, 128, 2 * QC), BF), S((8, 16, 144), F32), S((36, D), F32), S((2, 36, 3 * QC), F32)],
        in_specs=[V] * 12 + [pl.BlockSpec(memory_space=pl.ANY)] + [V] * 6, out_specs=[V] * 7,
        scratch_shapes=[pltpu.VMEM((QC, D), BF), pltpu.VMEM((D, 3 * QC), BF), pltpu.VMEM((2, TOK, QC), BF),
                        pltpu.VMEM((2, TOK, QC), F32), pltpu.VMEM((2, KEYS, QC), F32), pltpu.VMEM((2, KEYS, QC), F32), pltpu.VMEM((2 * TOK, 3 * QC), BF),
                        pltpu.VMEM((2, 2, HALF, KW), BF), pltpu.VMEM((HALF, KW), F32), pltpu.VMEM((HALF, KW), F32),
                        pltpu.VMEM((2, 2, 80, QC), BF), pltpu.VMEM((2, 2, 80, QC), BF), pltpu.VMEM((16, 2 * QC), BF), pltpu.VMEM((16, 2 * QC), BF),
                        pltpu.VMEM((128, 144), F32), pltpu.VMEM((128, 144), F32),
                        pltpu.VMEM((2, HALF, D), BF), pltpu.VMEM((2, HALF, D), BF), pltpu.VMEM((144, 1280), F32),
                        dma((2,)), dma((2,)), dma((1,)), dma((1,)), dma((7,)), dma((7,)), dma((2,)), dma((2,)), dma((7,)), dma((7,)), dma((1,)), dma((1,)), dma((2,)), dma((2,))]
        + scatter_scratch("O") + scatter_scratch("A"),
        compiler_params=pltpu.CompilerParams(collective_id=3, has_side_effects=True, vmem_limit_bytes=127 * 2 ** 19),
        name="attn_back")(*args)


def local_fast(*args):
    p = prologue(*args)
    c, b, y, k = place()
    WA, WO, WI, WB = gather(*p["own"])
    (out, xn, q, kb, vb, lse, o, hres, hn, g, gp) = forward(
        p["lat"], p["gains"], WA, WO, WI, WB, p["te"], p["ti"], p["segq"], p["segk"], p["colq"], p["colk"], p["base"], p["onehot"], p["filled"])
    cot = args[10].reshape(2, HALF, D)
    dh, da, gain_two, out_b, out_i = mlp_back(cot, p["filled"], p["gains"], WI, WB, hres, hn.reshape(2 * TOK, D), g.reshape(2 * TOK, FH), gp.reshape(2 * TOK, FH))
    dlat, gain_one, dbias, dt_all, gt, out_o, out_a = attn_back(
        WA, WO, p["ti"], p["gains"], p["lat"], xn.reshape(2 * TOK, D), q, kb, vb, lse, o.reshape(2 * TOK, QC), da, dh,
        p["segq"], p["segk"], p["colq"], p["colk"], p["base"], p["onehot"])
    shape = (2, 1, 8, 34, D)
    places = jnp.array([80 + 34 * dr + dc for dr in range(-2, 3) for dc in range(-2, 3)])
    bias = dbias[:, places].T
    both = jnp.zeros((25, 8, 2), F32)
    both = lax.dynamic_update_slice(both, bias[..., None], (0, 0, k))
    gains = jnp.stack([gain_one[0], gain_two[0]], 1)
    flat = lax.psum(jnp.concatenate([both.reshape(-1), gains.reshape(-1)]), ("canvas", "band"))
    grad_bias = flat[:400].reshape(25, 16)
    grad_gains = lax.dynamic_slice_in_dim(flat[400:].reshape(D, 2), 144 * c + 36 * b, 36, 0)
    grad_a = out_a.reshape(2, 36, 3, 8, 80)[..., :72].transpose(1, 2, 3, 0, 4).reshape(36, 3 * D)
    grad_i = out_i.reshape(2, 36, 8, 288).transpose(1, 2, 0, 3).reshape(36, 2 * FH)
    dt = dt_all.reshape(2, 128, 2, 8, 80)[..., :72].transpose(1, 2, 3, 0, 4).reshape(128, 2 * D)
    mine = lax.dynamic_slice_in_dim(p["te_all"], 144 * c + 36 * b, 36, 1)
    grad_time_in = dot_tn(mine, dt)
    grad_time = gt.transpose(1, 0, 2).reshape(16, D)[:10].reshape(2, 1, 5, D)
    return (out.reshape(shape), dlat.reshape(shape), grad_time, grad_gains, grad_a, grad_time_in, grad_bias, out_o, grad_i, out_b)


def solution(mesh):
    return jax.shard_map(
        local_fast if mesh.shape["canvas"] == 8 and mesh.shape["band"] == 4 else local,
        mesh=mesh,
        in_specs=(
            P(None, "canvas", "band", None, None),
            P(None, "canvas", "band", None),
            P(None, "canvas", None, None),
            P(),
            P("canvas", None),
            P("canvas", None),
            P(),
            P("canvas", None),
            P("canvas", None),
            P("canvas", None),
            P(None, "canvas", "band", None, None),
        ),
        out_specs=(
            P(None, "canvas", "band", None, None),
            P(None, "canvas", "band", None, None),
            P(None, "canvas", None, None),
            P(("canvas", "band"), None),
            P(("canvas", "band"), None),
            P(("canvas", "band"), None),
            P(),
            P(("canvas", "band"), None),
            P(("canvas", "band"), None),
            P(("canvas", "band"), None),
        ),
        check_vma=False,
    )
```

```python
from functools import partial
import jax
import jax.numpy as jnp
from jax import lax
from jax.experimental import pallas as pl
from jax.experimental.pallas import tpu as pltpu

from jax.sharding import PartitionSpec as P

WIN = 5


EPSILON = 1e-05


def padded_2(shard, sides, width):
    for axis, dim in sides:
        devices, length = (lax.axis_size(axis), shard.shape[dim])
        up = [(i, (i + 1) % devices) for i in range(devices - 1)]
        down = [(j, i) for i, j in up]
        last = lax.slice_in_dim(shard, length - width, length, axis=dim)
        first = lax.slice_in_dim(shard, 0, width, axis=dim)
        before = lax.ppermute(last, axis, up)
        after = lax.ppermute(first, axis, down)
        shard = jnp.concatenate([before, shard, after], axis=dim)
    return shard


def shifted(shard, axis, by):
    devices = lax.axis_size(axis)
    pairs = [(i, i + by) for i in range(devices) if 0 <= i + by < devices]
    return lax.ppermute(shard, axis, pairs)


def shortened(shard):

    def short(part):
        return part.astype(jnp.bfloat16) if part.dtype == jnp.float32 else part

    return jax.tree.map(short, shard)


def normalize(value, gain):
    center = value - jnp.mean(value, -1, keepdims=True)
    scaled = lax.rsqrt(jnp.mean(center * center, -1, keepdims=True) + EPSILON)
    unit = center * scaled
    return (unit, scaled, unit * gain)


def normalize_back(unit, scaled, gain, grad_out):
    part = grad_out * gain
    return scaled * (
        part - jnp.mean(part, -1, keepdims=True) - unit * jnp.mean(part * unit, -1, keepdims=True)
    )


def rows_dot(left, right):
    return lax.dot_general(
        left, right, (((0,), (0,)), ((), ())), preferred_element_type=jnp.float32
    )


def back_dot(left, weight):
    return lax.dot_general(
        left, weight, (((1,), (1,)), ((), ())), preferred_element_type=jnp.float32
    )


def neighbour_stack(padded, band_rows, columns):
    pieces = [padded[:, i : i + band_rows, j : j + columns] for i in range(WIN) for j in range(WIN)]
    stacked = jnp.stack(pieces)
    return stacked.reshape((WIN * WIN, -1) + padded.shape[3:])


def spread_back(terms, canvases, band_rows, columns):
    reach = WIN // 2
    shaped = terms.reshape((WIN * WIN, canvases, band_rows, columns, terms.shape[-1]))
    summed = None
    for i in range(WIN):
        for j in range(WIN):
            placed = jnp.pad(
                shaped[i * WIN + j], ((0, 0), (i, 2 * reach - i), (j, 2 * reach - j), (0, 0))
            )
            summed = placed if summed is None else summed + placed
    return summed


def head_total(terms, head_sum):
    flat = terms.reshape(-1, terms.shape[-1])
    return jnp.dot(flat, head_sum, precision=lax.Precision.HIGHEST).reshape(
        terms.shape[:-1] + (head_sum.shape[1],)
    )


def head_widen(values, head_spread):
    flat = values.reshape(-1, values.shape[-1])
    return jnp.dot(flat, head_spread, preferred_element_type=jnp.bfloat16).reshape(
        values.shape[:-1] + (head_spread.shape[1],)
    )


def local(
    latents,
    segment_ids,
    time_embed,
    norm_gains,
    attn_in,
    time_in,
    rel_bias,
    out_proj,
    mlp_in,
    mlp_out,
    cotangent,
):
    micro_count, canvases, band_rows, columns, width = latents.shape
    slots = time_embed.shape[2]
    heads = rel_bias.shape[1]
    head_dim = width // heads
    reach = WIN // 2
    tokens = canvases * band_rows * columns
    score_scale = head_dim ** (-0.5)
    head_sum = (jnp.arange(width)[:, None] // head_dim == jnp.arange(heads)[None, :]).astype(
        jnp.float32
    )
    head_spread = head_sum.T.astype(jnp.bfloat16)
    owned = (attn_in, time_in, out_proj, mlp_in, mlp_out)
    seg_code = segment_ids + 2
    seg_rims = padded_2(seg_code, (("band", 2),), reach)
    seg_rims = jnp.pad(seg_rims, ((0, 0), (0, 0), (0, 0), (reach, reach)))
    band_share = 1.0 / lax.axis_size("band")
    outputs = []
    input_grads = []
    time_grads = []
    accum = None
    shards = None
    bias_accum = jnp.zeros(rel_bias.shape, jnp.float32)
    for batch_index in range(micro_count):
        full_weights = (
            lax.all_gather(owned[0], "canvas", axis=0, tiled=True),
            lax.all_gather(owned[1], "canvas", axis=0, tiled=True),
            lax.all_gather(owned[2], "canvas", axis=0, tiled=True),
            lax.all_gather(owned[3], "canvas", axis=0, tiled=True),
            lax.all_gather(owned[4], "canvas", axis=0, tiled=True),
        )
        w_attn, w_time, w_out, w_in, w_back = full_weights
        inputs = latents[batch_index].astype(jnp.float32).reshape(tokens, width)
        unit_one, scaled_one, normed_one = normalize(inputs, norm_gains[:, 0])
        normed = normed_one.astype(jnp.bfloat16)
        time_rows = time_embed[batch_index].reshape(canvases * slots, width)
        time_proj = jnp.dot(time_rows, w_time, preferred_element_type=jnp.float32).reshape(
            canvases, slots, 2 * width
        )
        seg_here = segment_ids[batch_index]
        member = (seg_here[..., None] == jnp.arange(slots)).astype(jnp.float32)
        token_time = jnp.einsum(
            "krcs,kse->krce", member, time_proj, precision=lax.Precision.HIGHEST
        ).reshape(tokens, 2 * width)
        qkv = jnp.dot(normed, w_attn, preferred_element_type=jnp.float32)
        query = (qkv[:, :width] + token_time[:, :width]).astype(jnp.bfloat16)
        keys = qkv[:, width : 2 * width].astype(jnp.bfloat16)
        values = (qkv[:, 2 * width :] + token_time[:, width:]).astype(jnp.bfloat16)
        paired = jnp.stack([keys, values]).reshape(2, canvases, band_rows, columns, width)
        paired = padded_2(paired, (("band", 2),), reach)
        paired = jnp.pad(paired, ((0, 0), (0, 0), (0, 0), (reach, reach), (0, 0)))
        key_win = neighbour_stack(paired[0], band_rows, columns)
        value_win = neighbour_stack(paired[1], band_rows, columns)
        seg_win = neighbour_stack(seg_rims[batch_index], band_rows, columns)
        allowed = (seg_win == seg_code[batch_index].reshape(1, tokens))[..., None]
        query_wide = query.astype(jnp.float32)
        raw = head_total(query_wide[None] * key_win.astype(jnp.float32), head_sum)
        logit_scores = raw * score_scale + rel_bias[:, None, :]
        masked = jnp.where(allowed, logit_scores, -1e30)
        peak = jnp.max(masked, 0)
        raised = jnp.where(allowed, jnp.exp(masked - peak), 0.0)
        probs_full = raised / jnp.sum(raised, 0)
        attention_probabilities = probs_full.astype(jnp.bfloat16)
        probs_wide = head_widen(attention_probabilities, head_spread)
        mixed_values = jnp.sum(probs_wide.astype(jnp.float32) * value_win.astype(jnp.float32), 0)
        attended = mixed_values.astype(jnp.bfloat16)
        branch = jnp.dot(attended, w_out, preferred_element_type=jnp.float32)
        resid = inputs + branch
        unit_two, scaled_two, normed_two = normalize(resid, norm_gains[:, 1])
        hidden_in = normed_two.astype(jnp.bfloat16)
        pre_act = jnp.dot(hidden_in, w_in, preferred_element_type=jnp.float32)
        activated = jax.nn.gelu(pre_act, approximate=False).astype(jnp.bfloat16)
        mlp_y = jnp.dot(activated, w_back, preferred_element_type=jnp.float32)
        filled = (seg_here >= 0).reshape(tokens, 1)
        outputs.append(
            jnp.where(filled, resid + mlp_y, 0.0)
            .astype(jnp.bfloat16)
            .reshape(canvases, band_rows, columns, width)
        )
        grad_y = cotangent[batch_index].reshape(tokens, width)
        grad_f = jnp.where(filled, grad_y, jnp.zeros_like(grad_y))
        grad_back = rows_dot(activated, grad_f)
        grad_act = back_dot(grad_f, w_back)
        gelu_out, gelu_pull = jax.vjp(partial(jax.nn.gelu, approximate=False), pre_act)
        grad_pre = gelu_pull(grad_act)[0].astype(jnp.bfloat16)
        grad_in = rows_dot(hidden_in, grad_pre)
        grad_hidden = back_dot(grad_pre, w_in)
        grad_resid = jnp.where(filled, grad_y.astype(jnp.float32), 0.0) + normalize_back(
            unit_two, scaled_two, norm_gains[:, 1], grad_hidden
        )
        gain_two = jnp.sum(grad_hidden * unit_two, 0)
        grad_branch = grad_resid.astype(jnp.bfloat16)
        grad_out = rows_dot(attended, grad_branch)
        grad_att = back_dot(grad_branch, w_out).astype(jnp.bfloat16)
        grad_att_wide = grad_att.astype(jnp.float32)
        grad_probs = head_total(grad_att_wide[None] * value_win.astype(jnp.float32), head_sum)
        centered = jnp.sum(probs_full * grad_probs, 0)
        grad_scores = (probs_full * (grad_probs - centered)).astype(jnp.bfloat16)
        bias_accum = bias_accum + jnp.sum(grad_scores.astype(jnp.float32), axis=1)
        scores_wide = head_widen(grad_scores, head_spread).astype(jnp.float32)
        grad_query = jnp.sum(scores_wide * key_win.astype(jnp.float32), 0) * score_scale
        key_summed = (
            spread_back(scores_wide * query_wide[None], canvases, band_rows, columns) * score_scale
        )
        value_summed = spread_back(
            probs_wide.astype(jnp.float32) * grad_att_wide[None], canvases, band_rows, columns
        )
        pair_grad = jnp.stack([key_summed, value_summed])[:, :, :, reach : reach + columns]
        upper_rim = pair_grad[:, :, :reach]
        lower_rim = pair_grad[:, :, band_rows + reach :]
        owned_rows = pair_grad[:, :, reach : reach + band_rows]
        from_below = shifted(upper_rim.astype(jnp.bfloat16), "band", -1).astype(upper_rim.dtype)
        from_above = shifted(lower_rim.astype(jnp.bfloat16), "band", 1).astype(lower_rim.dtype)
        owned_rows = owned_rows.at[:, :, band_rows - reach :].add(from_below)
        owned_rows = owned_rows.at[:, :, :reach].add(from_above)
        grad_keys = owned_rows[0].reshape(tokens, width).astype(jnp.bfloat16)
        grad_values = owned_rows[1].reshape(tokens, width).astype(jnp.bfloat16)
        grad_q_low = grad_query.astype(jnp.bfloat16)
        member_low = member.astype(jnp.bfloat16).reshape(canvases, band_rows * columns, slots)
        slot_query = jnp.einsum(
            "kns,knd->ksd",
            member_low,
            grad_q_low.reshape(canvases, band_rows * columns, width),
            preferred_element_type=jnp.float32,
        )
        slot_value = jnp.einsum(
            "kns,knd->ksd",
            member_low,
            grad_values.reshape(canvases, band_rows * columns, width),
            preferred_element_type=jnp.float32,
        )
        slot_part = jnp.concatenate([slot_query, slot_value], -1)
        slot_total = lax.psum(slot_part.astype(jnp.bfloat16), "band")
        slot_low = slot_total.reshape(canvases * slots, 2 * width)
        time_grads.append(back_dot(slot_low, w_time).reshape(canvases, slots, width))
        grad_time_in = rows_dot(time_rows, slot_low) * band_share
        grad_qkv = jnp.concatenate([grad_q_low, grad_keys, grad_values], -1)
        grad_attn = rows_dot(normed, grad_qkv)
        grad_normed = back_dot(grad_qkv, w_attn)
        grad_inputs = grad_resid + normalize_back(
            unit_one, scaled_one, norm_gains[:, 0], grad_normed
        )
        gain_one = jnp.sum(grad_normed * unit_one, 0)
        input_grads.append(grad_inputs.reshape(canvases, band_rows, columns, width))
        micro_grads = (
            grad_attn,
            grad_time_in,
            grad_out,
            grad_in,
            grad_back,
            jnp.stack([gain_one, gain_two], 1),
        )
        accum = micro_grads if accum is None else jax.tree.map(jnp.add, accum, micro_grads)
    wide_sums = jax.tree.map(
        lambda part: part.astype(jnp.float32),
        lax.psum_scatter(shortened(accum), "canvas", scatter_dimension=0, tiled=True),
    )
    shards = jax.tree.map(
        lambda part: part.astype(jnp.float32),
        lax.psum_scatter(shortened(wide_sums), "band", scatter_dimension=0, tiled=True),
    )
    bias_grad = lax.psum(bias_accum, ("canvas", "band"))
    return (
        jnp.stack(outputs),
        jnp.stack(input_grads),
        jnp.stack(time_grads),
        shards[5],
        shards[0],
        shards[1],
        bias_grad,
        shards[2],
        shards[3],
        shards[4],
    )


MESH = pl.DeviceIdType.MESH
BF, F32 = jnp.bfloat16, jnp.float32
EPS = 1e-5
TOK, HALF, D, QC, FH = 544, 272, 1152, 640, 2304
KEYS, KW, PADK = 784, 512, 80
SCALE = 72 ** -0.5
NEG = -1e30


def dot(a, b):
    return jnp.dot(a, b, preferred_element_type=F32)


def dot_nt(a, b):
    return lax.dot_general(a, b, (((1,), (1,)), ((), ())), preferred_element_type=F32)


def dot_tn(a, b):
    return lax.dot_general(a, b, (((0,), (0,)), ((), ())), preferred_element_type=F32)


def norm(v):
    center = v - jnp.mean(v, -1, keepdims=True)
    r = lax.rsqrt(jnp.mean(center * center, -1, keepdims=True) + EPS)
    return center * r, r


def norm_back(n, r, e):
    return r * (e - jnp.mean(e, -1, keepdims=True) - n * jnp.mean(e * n, -1, keepdims=True))


def place():
    c, b = lax.axis_index("canvas"), lax.axis_index("band")
    return c, b, b // 2, lax.rem(b, 2)


def greet(devs):
    bar = pltpu.get_barrier_semaphore()
    for dev in devs:
        pl.semaphore_signal(bar, 1, device_id=dev, device_id_type=MESH)
    pl.semaphore_wait(bar, len(devs))


def remote(src, dst, ss, rs, dev):
    return pltpu.make_async_remote_copy(src, dst, ss, rs, device_id=dev, device_id_type=MESH)


def head_window(h):
    ws = pl.multiple_of(jnp.minimum(80 * h // 128, 3) * 128, 128)
    lane = lax.broadcasted_iota(jnp.int32, (1, 256), 1) + ws - 80 * h
    hm = jnp.where((lane >= 0) & (lane < 80), 1.0, 0.0).astype(BF)
    return pl.ds(ws, 256), hm


def toeplitz(base, h):
    row = jnp.broadcast_to(base[pl.ds(h, 1)], (HALF, KW))
    return pltpu.roll(row, 0, 1, stride=1, stride_axis=0)


GSPEC = {"A": (144, 640, 640), "O": (80, 384, 384), "I0": (144, 512, 128), "I1": (144, 384, 384), "B0": (144, 512, 128), "B1": (144, 384, 384)}
GNAMES = list(GSPEC)


class Gather:
    def __init__(self, own, full, s_sem, r_sem, y_sem, l_sem, pend):
        self.own, self.full, self.pend = dict(zip(GNAMES, own)), dict(zip(GNAMES, full)), pend
        self.s_sem, self.r_sem, self.y_sem, self.l_sem = s_sem, r_sem, y_sem, l_sem
        self.c, self.b, self.y, _ = place()
        self.z, self.x = self.c // 2, lax.rem(self.c, 2)
        self.zp = [lax.rem(self.z + d, 4) for d in (1, 3, 2)]
        self.xdev, self.ydev = {"canvas": self.c + 1 - 2 * self.x}, {"band": self.b + 2 - 4 * self.y}
        self.count = dict.fromkeys(GNAMES, 0)

    def part(self, name, src, plane, side):
        rows, wide, mid = GSPEC[name]
        at = pl.ds(pl.multiple_of(src * rows, 16), rows)
        if plane:
            return at, pl.ds(pl.multiple_of(wide * side, 128), wide + mid)
        return at, pl.ds(pl.multiple_of((wide + mid) * side, 128), wide)

    def send(self, name, src, dev, plane, first=False):
        n = GNAMES.index(name)
        at, cols = self.part(name, src, plane, self.y)
        cp = remote(self.own[name].at[:, cols] if first else self.full[name].at[at, cols], self.full[name].at[at, cols],
                    self.s_sem.at[n, self.count[name]], (self.r_sem if plane else self.y_sem).at[n, src], dev)
        self.count[name] += 1
        cp.start()
        self.pend.append(cp)

    def own_sends(self, name):
        rows = GSPEC[name][0]
        for p in self.zp:
            self.send(name, self.c, {"canvas": p * 2 + self.x}, True, True)
        self.send(name, self.c, self.xdev, True, True)
        pltpu.make_async_copy(self.own[name], self.full[name].at[pl.ds(pl.multiple_of(self.c * rows, 16), rows)],
                              self.l_sem.at[GNAMES.index(name)]).start()

    def wait(self, name, src, plane):
        at, cols = self.part(name, src, plane, self.y if plane else 1 - self.y)
        view = self.full[name].at[at, cols]
        pltpu.make_async_copy(view, view, (self.r_sem if plane else self.y_sem).at[GNAMES.index(name), src]).wait()

    def from_z(self, name, i):
        src = self.zp[i] * 2 + self.x
        self.wait(name, src, True)
        self.send(name, src, self.xdev, True)
        self.send(name, src, self.ydev, False)

    def from_x(self, name, i):
        src = (self.z if i == 0 else self.zp[i - 1]) * 2 + 1 - self.x
        self.wait(name, src, True)
        self.send(name, src, self.ydev, False)

    def complete(self, name):
        rows = GSPEC[name][0]
        for d in range(1, 8):
            self.wait(name, lax.rem(self.c + d, 8), False)
        pltpu.make_async_copy(self.own[name], self.full[name].at[pl.ds(pl.multiple_of(self.c * rows, 16), rows)],
                              self.l_sem.at[GNAMES.index(name)]).wait()

    def events(self, name):
        return [partial(self.from_z, name, 0), partial(self.from_x, name, 0), partial(self.from_z, name, 1), partial(self.from_x, name, 1),
                partial(self.from_z, name, 2), partial(self.from_x, name, 2), partial(self.from_x, name, 3)]


def gather_forward_kernel(A, O, I0, I1, B0, B1, lat, gains, te, ti, seg_row, seg_col, colq, colk, base,
                          out, xn_o, q_o, kb_o, vb_o, lse_o, o_o, hres_o, hn_o, g_o, gp_o, WA_o, WO_o, WI0_o, WI1_o, WB0_o, WB1_o, te_o, mask_o, onehot_o,
                          WA, WO, WI0, WI1, WB0, WB1, xn, q, kb, vb, lse, o, hres, hn, g, gp, te_in, seg_in, col_in, onehot,
                          tp_send, tp_recv, tmix, mask, toep, of, x_send, x_recv, fo, layer,
                          s_sem, r_sem, y_sem, l_sem, es, er, gs, gr, cs, cr,
                          xs, xr, ts, tr, ks, kr, as_, ar, hs, hr, fs, fr, outs):
    c, b, y, k = place()
    sib, ynb = {"band": b + 1 - 2 * k}, {"band": b + 2 - 4 * y}
    peers = [lax.rem(c + d, 8) for d in range(1, 8)]
    pend, saves = [], []

    def go(src, dst, ss, rs, dev):
        cp = remote(src, dst, ss, rs, dev)
        cp.start()
        pend.append(cp)

    def arrive(view, sem):
        pltpu.make_async_copy(view, view, sem).wait()

    def save(src, dst):
        cp = pltpu.make_async_copy(src, dst, outs.at[len(saves)])
        cp.start()
        saves.append(cp)

    gat = Gather((A, O, I0.at[0], I0.at[1], B0.at[0], B0.at[1]), (WA, WO, WI0, WI1, WB0, WB1), s_sem, r_sem, y_sem, l_sem, pend)
    queue = []
    for name, nxt in (("A", "I0"), ("O", "I1"), ("I0", "B0"), ("I1", "B1"), ("B0", None), ("B1", None)):
        steps = gat.events(name)
        if nxt:
            steps.insert(1, partial(gat.own_sends, nxt))
        queue += steps

    def pump(n):
        for _ in range(min(n, len(queue))):
            queue.pop(0)()

    greet([{"band": lax.rem(b + d, 4)} for d in (1, 2, 3)] + [{"canvas": p} for p in peers])
    for i, p in enumerate(peers):
        go(te.at[p], te_in.at[c], es.at[i], er.at[6 - i], {"canvas": p})
    te_in[c] = te[c]
    for i in range(3):
        go(seg_row, seg_in.at[b], gs.at[i], gr.at[2 - i], {"band": lax.rem(b + i + 1, 4)})
    seg_in[b] = seg_row[...]
    go(seg_col, col_in.at[k], cs.at[0], cr.at[0], sib)
    col_in[k] = seg_col[...]
    gat.own_sends("A")
    gat.own_sends("O")

    mine = pl.ds(pl.multiple_of(HALF * k, 16), HALF)
    other = pl.ds(pl.multiple_of(HALF * (1 - k), 16), HALF)
    for m in range(2):
        n, _ = norm(lat[m].astype(F32))
        xn[m, mine] = (n * gains[0:1]).astype(BF)
        go(xn.at[m, mine], xn.at[m, mine], xs.at[m], xr.at[m], sib)
        if m == 0:
            for i in range(7):
                arrive(te_in.at[lax.rem(c + i + 1, 8)], er.at[i])
            for p in range(8):
                tp_send[16 * p:16 * p + 16] = dot(te_in[p], ti[...]).astype(BF)
            for i, p in enumerate(peers):
                go(tp_send.at[pl.ds(pl.multiple_of(16 * p, 16), 16)], tp_recv.at[6 - i], ts.at[i], tr.at[6 - i], {"canvas": p})
    save(te_in, te_o)
    arrive(col_in.at[1 - k], cr.at[0])
    for i in range(3):
        arrive(seg_in.at[lax.rem(b + i + 1, 4)], gr.at[i])
    slot = lax.rem(lax.broadcasted_iota(jnp.int32, (1, 32), 1), 16)
    lane = lax.broadcasted_iota(jnp.int32, (1, KW), 1)
    near = jnp.abs(colq[...] - colk[...]) < 2.5
    for j in range(2):
        at = 2 * y + j
        before, here, after = seg_in[jnp.maximum(at - 1, 0)], seg_in[at], seg_in[jnp.minimum(at + 1, 3)]
        before = pltpu.roll(jnp.where(at > 0, before, 0.0), KW - HALF, 1)
        after = pltpu.roll(jnp.where(at < 3, after, 0.0), HALF, 1)
        keys = jnp.where(lane < 80, before, jnp.where(lane < 352, here, jnp.where(lane < 432, after, 0.0)))
        for m in range(2):
            code = col_in[j, m, :, 0:1]
            mask[m, j] = jnp.where((code == keys[m:m + 1]) & near, 0.0, NEG).astype(BF)
            hit = (code.astype(jnp.int32) + (5 * m - 2) == slot) & (code >= 1.5)
            onehot[m, HALF * j:HALF * j + HALF] = jnp.where(hit, 1.0, 0.0).astype(BF)
    save(mask, mask_o)
    save(onehot, onehot_o)
    pump(5)
    for i in range(7):
        arrive(tp_recv.at[i], tr.at[i])
    tproj = tp_send[pl.ds(pl.multiple_of(16 * c, 16), 16)].astype(F32)
    for i in range(7):
        tproj = tproj + tp_recv[i].astype(F32)
    hi = tproj.astype(BF)
    tmix[0:16] = hi
    tmix[16:32] = (tproj - hi.astype(F32)).astype(BF)
    dead = pl.ds(pl.multiple_of(y * 624, 16), 80)
    for m in range(2):
        for ref in (kb, vb):
            ref[m, dead] = jnp.zeros((80, QC), BF)
            ref[m, 704:784] = jnp.zeros((80, QC), BF)
    of[...] = jnp.zeros_like(of)
    lse[...] = jnp.zeros_like(lse)
    pump(3)
    gat.complete("A")
    save(WA, WA_o)

    edge = pl.ds(pl.multiple_of(544 - 464 * y, 16), 80)
    land = pl.ds(pl.multiple_of(624 * y, 16), 80)
    land_here = pl.ds(pl.multiple_of(624 * (1 - y), 16), 80)
    for m in range(2):
        arrive(xn.at[m, other], xr.at[m])
        x = xn[m]
        kb[m, 80:624] = dot(x, WA[:, QC:2 * QC]).astype(BF)
        vb[m, 80:624] = (dot(x, WA[:, 2 * QC:]) + dot(onehot[m], tmix[:, QC:])).astype(BF)
        for i, ref in enumerate((kb, vb)):
            go(ref.at[m, edge], ref.at[m, land], ks.at[m, i], kr.at[m, i], ynb)
        q[m] = (dot(x, WA[:, :QC]) + dot(onehot[m], tmix[:, :QC])).astype(BF)
        pump(2)
    save(xn, xn_o)
    save(q, q_o)
    for m in range(2):
        for i, ref in enumerate((kb, vb)):
            arrive(ref.at[m, land_here], kr.at[m, i])
    save(kb, kb_o)
    save(vb, vb_o)

    def head(h, _):
        win, hm = head_window(h)
        toep[...] = toeplitz(base, h)
        lane_h = lax.broadcasted_iota(jnp.int32, (1, 128), 1) == h

        def tile(t, _):
            m, j = t // 2, lax.rem(t, 2)
            rows = pl.ds(pl.multiple_of(HALF * j, 16), HALF)
            krows = pl.ds(pl.multiple_of(HALF * j, 16), KW)
            s = dot_nt(q[m, rows, win] * hm, kb[m, krows, win])
            s = s * SCALE + (toep[...] + mask[m, j])
            peak = jnp.max(s, -1, keepdims=True)
            e = jnp.exp(s - peak)
            total = jnp.sum(e, -1, keepdims=True)
            p = (e * (1.0 / total)).astype(BF)
            of[m, rows, win] += dot(p, vb[m, krows, win] * hm)
            lse[m, rows] = jnp.where(lane_h, peak + jnp.log(total), lse[m, rows])
            return 0

        return lax.fori_loop(0, 4, tile, 0)

    for n in range(4):
        lax.fori_loop(2 * n, 2 * n + 2, head, 0)
        pump((3, 2, 2, 2)[n])
    save(lse, lse_o)
    for m in range(2):
        o[m] = of[m].astype(BF)
    save(o, o_o)
    gat.complete("O")
    save(WO, WO_o)

    for m in range(2):
        x_send[0, m] = dot(o[m, other], WO[...]).astype(BF)
        go(x_send.at[0, m], x_recv.at[0, m], as_.at[m], ar.at[m], sib)
    for m in range(2):
        hres[m] = lat[m].astype(F32) + dot(o[m, mine], WO[...])
    pump(2)
    for m in range(2):
        arrive(x_recv.at[0, m], ar.at[m])
        hv = hres[m] + x_recv[0, m].astype(F32)
        hres[m] = hv
        n, _ = norm(hv)
        hn[m, mine] = (n * gains[1:2]).astype(BF)
        go(hn.at[m, mine], hn.at[m, mine], hs.at[m], hr.at[m], sib)
    save(hres, hres_o)
    pump(2)
    for m in range(2):
        arrive(hn.at[m, other], hr.at[m])
    save(hn, hn_o)
    for s, W in enumerate((WI0, WI1)):
        while len(queue) > (21 if s == 0 else 14):
            pump(1)
        gat.complete("I0" if s == 0 else "I1")
        save(W, (WI0_o, WI1_o)[s])
        for m in range(2):
            def up(i, _):
                cols = pl.ds(pl.multiple_of(i * 384, 128), 384)
                put = pl.ds(pl.multiple_of(i * 384 + D * s, 128), 384)
                u = dot(hn[m], W[:, cols])
                phi = 0.5 + 0.5 * lax.erf(u * (0.5 ** 0.5))
                g[m, :, put] = (u * phi).astype(BF)
                gp[m, :, put] = (phi + u * (jnp.exp(-0.5 * u * u) * 0.3989422804014327)).astype(BF)
                return 0

            lax.fori_loop(0, 3, up, 0)
            pump(2)
    save(g, g_o)
    save(gp, gp_o)
    for s, W in enumerate((WB0, WB1)):
        while len(queue) > (7 if s == 0 else 0):
            pump(1)
        gat.complete("B0" if s == 0 else "B1")
        save(W, (WB0_o, WB1_o)[s])
        for m in range(2):
            if s == 0:
                fo[1, m] = dot(g[m, other, 0:D], W[...])
                fo[0, m] = dot(g[m, mine, 0:D], W[...])
            else:
                x_send[1, m] = (fo[1, m] + dot(g[m, other, D:], W[...])).astype(BF)
                go(x_send.at[1, m], x_recv.at[1, m], fs.at[m], fr.at[m], sib)
                fo[0, m] += dot(g[m, mine, D:], W[...])
    for m in range(2):
        arrive(x_recv.at[1, m], fr.at[m])
        filled = jnp.where(col_in[k, m, :, 0:1] >= 1.5, 1.0, 0.0)
        layer[m] = ((hres[m] + (fo[0, m] + x_recv[1, m].astype(F32))) * filled).astype(BF)
    save(layer, out)
    for cp in saves:
        cp.wait()
    for cp in pend:
        cp.wait_send()


def gather_forward(own, p):
    S = jax.ShapeDtypeStruct
    dma = pltpu.SemaphoreType.DMA
    V, anyspace = pl.BlockSpec(memory_space=pltpu.VMEM), pl.BlockSpec(memory_space=pl.ANY)
    weights = [(D, 3 * QC), (QC, D), (D, D), (D, D), (D, D), (D, D)]
    kept = [((2, TOK, D), BF), ((2, TOK, QC), BF), ((2, KEYS, QC), BF), ((2, KEYS, QC), BF), ((2, TOK, 128), F32), ((2, TOK, QC), BF),
            ((2, HALF, D), F32), ((2, TOK, D), BF), ((2, TOK, FH), BF), ((2, TOK, FH), BF)]
    A, O, I, B = own
    return pl.pallas_call(
        gather_forward_kernel,
        out_shape=[S((2, HALF, D), BF)] + [S(s, t) for s, t in kept] + [S(s, BF) for s in weights]
        + [S((8, 16, 144), BF), S((2, 2, HALF, KW), BF), S((2, TOK, 32), BF)],
        in_specs=[anyspace] * 6 + [V] * 9, out_specs=[anyspace] * 20,
        scratch_shapes=[pltpu.VMEM(s, BF) for s in weights] + [pltpu.VMEM(s, t) for s, t in kept]
        + [pltpu.VMEM((8, 16, 144), BF), pltpu.VMEM((4, 8, KW), F32), pltpu.VMEM((2, 2, HALF, 128), F32), pltpu.VMEM((2, TOK, 32), BF),
           pltpu.VMEM((128, 2 * QC), BF), pltpu.VMEM((7, 16, 2 * QC), BF), pltpu.VMEM((32, 2 * QC), BF), pltpu.VMEM((2, 2, HALF, KW), BF),
           pltpu.VMEM((HALF, KW), F32), pltpu.VMEM((2, TOK, QC), F32), pltpu.VMEM((2, 2, HALF, D), BF), pltpu.VMEM((2, 2, HALF, D), BF),
           pltpu.VMEM((2, 2, HALF, D), F32), pltpu.VMEM((2, HALF, D), BF),
           dma((6, 14)), dma((6, 8)), dma((6, 8)), dma((6,)), dma((7,)), dma((7,)), dma((3,)), dma((3,)), dma((1,)), dma((1,)),
           dma((2,)), dma((2,)), dma((7,)), dma((7,)), dma((2, 2)), dma((2, 2)), dma((2,)), dma((2,)), dma((2,)), dma((2,)), dma((2,)), dma((2,)), dma((20,))],
        compiler_params=pltpu.CompilerParams(collective_id=1, has_side_effects=True, vmem_limit_bytes=127 * 2 ** 19),
        name="gather_forward")(A, O, I, I, B, B, p["lat"], p["gains"], p["te"], p["ti"], p["seg_row"], p["seg_col"], p["colq"], p["colk"], p["base"])


def prologue(latents, segment_ids, time_embed, norm_gains, attn_in, time_in, rel_bias, out_proj, mlp_in, mlp_out, cotangent):
    c, b, y, k = place()

    def pick(v, axis):
        return lax.dynamic_index_in_dim(v, k, axis, keepdims=False)

    def pad_heads(v, n):
        v = pick(v.reshape(144, n, 8, 2, 72), 3)
        return jnp.pad(v, ((0, 0), (0, 0), (0, 0), (0, 8))).reshape(144, n * QC)

    own = (pad_heads(attn_in, 3),
           jnp.pad(pick(out_proj.reshape(2, 72, D), 0), ((0, 8), (0, 0))),
           pick(mlp_in.reshape(144, 8, 2, 2, 144), 2).transpose(2, 0, 1, 3).reshape(2, 144, D),
           pick(mlp_out.reshape(2, 2, 144, D), 0))
    code = (segment_ids.reshape(2, HALF) + 2).astype(F32)
    seg_row = jnp.pad(code, ((0, 6), (80, KW - 80 - HALF)))
    seg_col = jnp.broadcast_to(code[..., None], (2, HALF, 128))
    te = jnp.pad(time_embed.reshape(10, D), ((0, 6), (0, 0))).reshape(16, 8, 144).transpose(1, 0, 2)
    colq = (jnp.arange(HALF) % 34).astype(F32)[:, None]
    colk = ((jnp.arange(KW) - 80 + 34 * 3) % 34).astype(F32)[None]
    bias = pick(rel_bias.reshape(25, 8, 2), 2)
    base = jnp.full((8, KW), NEG, F32)
    places = [80 + 34 * dr + dc for dr in range(-2, 3) for dc in range(-2, 3)]
    base = base.at[:, jnp.array(places)].set(bias.T)
    filled = (segment_ids.reshape(2, HALF, 1) >= 0).astype(F32)
    return dict(own=own, ti=pad_heads(time_in, 2), te=te, seg_row=seg_row, seg_col=seg_col, colq=colq, colk=colk,
                base=base, filled=filled, lat=latents.reshape(2, HALF, D), gains=norm_gains.T)


RSPEC = {"A": (144, 640, 640), "O": (80, 384, 384), "I0": (144, 384, 384), "I1": (144, 384, 384), "B0": (144, 384, 384), "B1": (144, 384, 384)}
KEEP = {"A": (36, 48, 4), "I0": (36, 48, 4), "I1": (36, 48, 4), "O": (36, 48, 2), "B0": (144, 144, 2), "B1": (144, 144, 2)}
ORDER = (1, 3, 2, 0)


def scatter_scratch(name):
    rows, wide, mid = RSPEC[name]
    slab = wide + mid
    dma = pltpu.SemaphoreType.DMA
    _, held, sources = KEEP[name]
    sends = {"A": 4, "I": 4, "O": 2, "B": 1}[name[0]]
    return [pltpu.VMEM((8 * rows, wide), BF), pltpu.VMEM((4 * rows, slab), BF), pltpu.VMEM((3 * rows, slab), BF),
            pltpu.VMEM((sends, held, slab), BF), pltpu.VMEM((sources, held, slab), BF),
            dma((4,)), dma((4,)), dma((8,)), dma((8,)), dma((3,)), dma((3,)), dma((4,)), dma((4,))]


N_SCATTER = 13


class Scatter:
    def __init__(self, name, grad, total, scratch, pend):
        self.name, self.grad, self.total, self.pend = name, grad, total, pend
        (self.yr, self.xr, self.zr, self.stage, self.fr, self.ys, self.yw, self.xs, self.xw, self.zs, self.zw, self.fs, self.fw) = scratch
        self.rows, self.wide, self.mid = RSPEC[name]
        self.c, self.b, self.y, self.k = place()
        self.z, self.x = self.c // 2, lax.rem(self.c, 2)
        y, w, l = self.y, self.wide, self.mid
        self.slab = pl.ds(pl.multiple_of(w * y, 128), w + l)
        self.mids = pl.ds(w, l)
        self.side = pl.ds(pl.multiple_of((w + l) * y, 128), w)
        self.away = pl.ds(pl.multiple_of((w + l) * (1 - y), 128), w)
        self.slab_mid = pl.ds(pl.multiple_of(w * (1 - y), 128), l)
        self.slab_side = pl.ds(pl.multiple_of(l * y, 128), w)
        self.xdev, self.ydev = {"canvas": self.c + 1 - 2 * self.x}, {"band": self.b + 2 - 4 * self.y}

    def at(self, group):
        return pl.ds(pl.multiple_of(group * self.rows, 16), self.rows)

    def pair(self, d):
        return pl.ds(pl.multiple_of(lax.rem(self.z + d, 4) * (2 * self.rows), 16), 2 * self.rows)

    def go(self, make):
        make().start()
        self.pend.append(make)

    def parts(self):
        return self.away, self.mids, self.side

    def group(self, d, x):
        return self.at(2 * lax.rem(self.z + d, 4) + x)

    def send_y(self):
        for d in ORDER:
            self.go(lambda d=d: remote(self.grad.at[self.pair(d), self.away], self.yr.at[self.pair(d)], self.ys.at[d], self.yw.at[d], self.ydev))

    def send_mid(self):
        for d in ORDER:
            self.go(lambda d=d: remote(self.grad.at[self.group(d, 1 - self.x), self.mids], self.xr.at[pl.ds(self.rows * d, self.rows), self.slab_mid],
                                       self.xs.at[d], self.xw.at[d], self.xdev))

    def side_x(self, d):
        rows2 = self.pair(d)
        pltpu.make_async_copy(self.yr.at[rows2], self.yr.at[rows2], self.yw.at[d]).wait()
        self.grad[rows2, self.side] = (self.grad[rows2, self.side].astype(F32) + self.yr[rows2].astype(F32)).astype(BF)
        self.go(lambda: remote(self.grad.at[self.group(d, 1 - self.x), self.side], self.xr.at[pl.ds(self.rows * d, self.rows), self.slab_side],
                               self.xs.at[4 + d], self.xw.at[4 + d], self.xdev))

    def sum_x(self, d):
        rows = pl.ds(self.rows * d, self.rows)
        for view, sem in ((self.xr.at[rows, self.slab_mid], d), (self.xr.at[rows, self.slab_side], 4 + d)):
            pltpu.make_async_copy(view, view, self.xw.at[sem]).wait()
        return self.grad[self.group(d, self.x), self.slab].astype(F32) + self.xr[rows].astype(F32)

    def send_z(self, d):
        self.grad[self.group(d, self.x), self.slab] = self.sum_x(d).astype(BF)
        self.go(lambda: remote(self.grad.at[self.group(d, self.x), self.slab], self.zr.at[pl.ds((3 - d) * self.rows, self.rows)], self.zs.at[d - 1],
                               self.zw.at[3 - d], {"canvas": 2 * lax.rem(self.z + d, 4) + self.x}))

    def dests(self):
        sources = KEEP[self.name][2]
        if self.name[0] == "B":
            return [(0, 2 * self.k + int(self.name[1]))]
        return [(i, 2 * self.k + i if sources == 2 else i) for i in range(sources)]

    def finish(self):
        acc = self.sum_x(0)
        for i in (2, 0, 1):
            rows = pl.ds(i * self.rows, self.rows)
            pltpu.make_async_copy(self.zr.at[rows], self.zr.at[rows], self.zw.at[i]).wait()
            acc = acc + self.zr[rows].astype(F32)
        n, held, sources = KEEP[self.name]
        slab = self.wide + self.mid
        if self.name[0] == "B":
            self.stage[0] = acc.astype(BF)
        else:
            self.total[0:self.rows, 0:slab] = acc
            for i in range(sources):
                self.stage[i, 0:n] = self.total[n * i:n * i + n, 0:slab].astype(BF)
                self.stage[i, n:held] = jnp.zeros((held - n, slab), BF)
        slot = self.b if sources == 4 else self.y
        for i, dest in self.dests():
            @pl.when(self.b == dest)
            def _():
                self.fr[slot] = self.stage[i]

            @pl.when(self.b != dest)
            def _():
                remote(self.stage.at[i], self.fr.at[slot], self.fs.at[i], self.fw.at[slot], {"band": dest}).start()

    def sent(self):
        for i, dest in self.dests():
            @pl.when(self.b != dest)
            def _():
                remote(self.stage.at[i], self.fr.at[0], self.fs.at[i], self.fw.at[0], {"band": dest}).wait_send()

    def collect(self, out):
        n, held, sources = KEEP[self.name]
        for i in range(sources):
            src = i if sources == 4 else 2 * i + self.y

            @pl.when(self.b != src)
            def _():
                pltpu.make_async_copy(self.fr.at[i], self.fr.at[i], self.fw.at[i]).wait()
        w, l = self.wide, self.mid
        for half in range(sources // 2):
            lo, hi = self.fr[half].astype(F32)[:n], self.fr[half + sources // 2].astype(F32)[:n]
            dst = out.at[half] if sources == 4 else out
            dst[:, 0:w] = lo[:, :w]
            dst[:, w:w + l] = lo[:, w:] + hi[:, :l]
            dst[:, w + l:] = hi[:, l:]


def everyone():
    c, b, y, k = place()
    return [{"band": lax.rem(b + d, 4)} for d in (1, 2, 3)] + [{"canvas": lax.rem(c + d, 8)} for d in range(1, 8)]


def fill_part(grad, left, right, cols, lefts, rights):
    def step(i, _):
        r = pl.multiple_of(i * 384, 128)
        grad[pl.ds(r, 384), cols] = dot_tn(left[:, pl.ds(r + lefts, 384)], right[:, rights]).astype(BF)
        return 0

    lax.fori_loop(0, grad.shape[0] // 384, step, 0)


def mlp_back_kernel(cot, filled, gains, WI0, WI1, WB0, WB1, hres, hn, g, gp,
                    dh, da, gain, out_b, grad_i0, grad_i1,
                    grad_b0, grad_b1, du, gi, x_send, x_recv, dn, ds_, dr_, xs, xr, as_, ar, ls, gs, *scratch):
    c, b, y, k = place()
    sib = {"band": b + 1 - 2 * k}
    df = da
    loads = [pltpu.make_async_copy(gp, du, ls.at[0]), pltpu.make_async_copy(hres, dh, ls.at[1])]
    for cp in loads:
        cp.start()
    greet([{"band": lax.rem(b + d, 4)} for d in (1, 2, 3)] + [{"canvas": c + 1 - 2 * lax.rem(c, 2)}] + [{"canvas": lax.rem(c + d, 8)} for d in (2, 4, 6)])
    pend = []
    rs = [Scatter("B0", grad_b0, None, scratch[:N_SCATTER], pend), Scatter("B1", grad_b1, None, scratch[N_SCATTER:], pend)]
    rs[1].fr, rs[1].fw = rs[0].fr, rs[0].fw

    def half(m, which):
        return pl.ds(pl.multiple_of(TOK * m + HALF * which, 16), HALF)

    for m in range(2):
        df[half(m, k)] = (cot[m].astype(F32) * filled[m]).astype(BF)
        cp = remote(df.at[half(m, k)], df.at[half(m, k)], ds_.at[m], dr_.at[m], sib)
        cp.start()
        loads.append(cp)
    for m in range(2):
        v = df.at[half(m, 1 - k)]
        pltpu.make_async_copy(v, v, dr_.at[m]).wait()
    for s in range(2):
        for i, cols in enumerate(rs[s].parts()):
            fill_part(rs[s].grad, g, df, cols, D * s, cols)
            if i == 0:
                rs[s].send_y()
            if i == 1:
                rs[s].send_mid()
    loads[0].wait()

    def back_act(m, s):
        def step(i, _):
            r = pl.multiple_of(i * 384, 128)
            cols = pl.ds(pl.multiple_of(r + D * s, 128), 384)
            rows = pl.ds(TOK * m, TOK)
            du[rows, cols] = (dot_nt(df[rows], (WB0, WB1)[s][pl.ds(r, 384)]) * du[rows, cols].astype(F32)).astype(BF)
            return 0

        lax.fori_loop(0, 3, step, 0)

    back_act(0, 0)
    rs[0].side_x(1)
    back_act(1, 0)
    rs[0].side_x(3)
    back_act(0, 1)
    rs[0].side_x(2)
    back_act(1, 1)
    rs[0].side_x(0)
    rs[0].send_z(1)
    saves = []
    for s in range(2):
        def step(i, _):
            r = pl.multiple_of(i * 384, 128)
            gi[s, pl.ds(r, 384)] = dot_tn(hn[:, pl.ds(r, 384)], du[:, D * s:D * s + D]).astype(BF)
            return 0

        lax.fori_loop(0, 3, step, 0)
        cp = pltpu.make_async_copy(gi.at[s], (grad_i0, grad_i1)[s], gs.at[s])
        cp.start()
        saves.append(cp)
        if s == 0:
            rs[0].send_z(3)
            rs[0].send_z(2)
            rs[1].side_x(1)
        else:
            rs[1].side_x(3)
            rs[1].side_x(2)

    for m in range(2):
        def hid(i, _):
            r = pl.multiple_of(i * 384, 128)
            rows = pl.ds(r, 384)
            v = dot_nt(du[half(m, 1 - k), 0:D], WI0[rows]) + dot_nt(du[half(m, 1 - k), D:], WI1[rows])
            x_send[m, :, rows] = v.astype(BF)
            return 0

        lax.fori_loop(0, 3, hid, 0)
        cp = remote(x_send.at[m], x_recv.at[m], xs.at[m], xr.at[m], sib)
        cp.start()
        loads.append(cp)

        def hid_own(i, _):
            r = pl.multiple_of(i * 384, 128)
            rows = pl.ds(r, 384)
            dn[m, :, rows] = dot_nt(du[half(m, k), 0:D], WI0[rows]) + dot_nt(du[half(m, k), D:], WI1[rows])
            return 0

        lax.fori_loop(0, 3, hid_own, 0)
        if m == 0:
            rs[1].side_x(0)
            rs[1].send_z(1)
    rs[0].finish()
    rs[1].send_z(3)
    gain_two = jnp.zeros((1, D), F32)
    loads[1].wait()
    for m in range(2):
        pltpu.make_async_copy(x_recv.at[m], x_recv.at[m], xr.at[m]).wait()
        grad = dn[m] + x_recv[m].astype(F32)
        n, r = norm(dh[m])
        gain_two = gain_two + jnp.sum(grad * n, 0, keepdims=True)
        v = cot[m].astype(F32) * filled[m] + norm_back(n, r, grad * gains[1:2])
        dh[m] = v
        loads[2 + m].wait_send()
        da[half(m, k)] = v.astype(BF)
        cp = remote(da.at[half(m, k)], da.at[half(m, k)], as_.at[m], ar.at[m], sib)
        cp.start()
        loads.append(cp)
    gain[...] = jnp.broadcast_to(gain_two, (8, D))
    rs[1].send_z(2)
    for m in range(2):
        v = da.at[half(m, 1 - k)]
        pltpu.make_async_copy(v, v, ar.at[m]).wait()
    rs[1].finish()
    rs[0].collect(out_b)
    rs[0].sent()
    rs[1].sent()
    for cp in saves:
        cp.wait()
    for cp in loads[4:]:
        cp.wait_send()
    for make in pend:
        make().wait_send()


def mlp_back(*args):
    S = jax.ShapeDtypeStruct
    dma = pltpu.SemaphoreType.DMA
    V, anyspace = pl.BlockSpec(memory_space=pltpu.VMEM), pl.BlockSpec(memory_space=pl.ANY)
    return pl.pallas_call(
        mlp_back_kernel,
        out_shape=[S((2, HALF, D), F32), S((2 * TOK, D), BF), S((8, D), F32), S((144, D), F32), S((D, D), BF), S((D, D), BF)],
        in_specs=[V] * 7 + [anyspace, V, V, anyspace], out_specs=[V] * 4 + [anyspace] * 2,
        scratch_shapes=[pltpu.VMEM((D, D), BF), pltpu.VMEM((D, D), BF), pltpu.VMEM((2 * TOK, FH), BF), pltpu.VMEM((2, D, D), BF),
                        pltpu.VMEM((2, HALF, D), BF), pltpu.VMEM((2, HALF, D), BF), pltpu.VMEM((2, HALF, D), F32)]
        + [dma((2,))] * 8 + scatter_scratch("B0") + scatter_scratch("B1"),
        compiler_params=pltpu.CompilerParams(collective_id=2, has_side_effects=True, vmem_limit_bytes=127 * 2 ** 19),
        name="mlp_back")(*args)


def attn_back_kernel(WA, WO, ti, gains, lat, xn, q, kb, vb, lse, o, da, dh, mask, base, onehot, gain_two, gi0, gi1,
                     dlat, dt_all, gt, small, out_o, out_a, out_i0, out_i1,
                     grad_o, grad_a, grad_i0, grad_i1, do, dqkv, rim, rim_in, tsum, tsum_in, gt_send, gt_in, x_send, x_recv, dbias, sm_send, sm_in, total,
                     ks, kr, ts, tr, ps, pr, us, ur, vs, vr, ls, xs, xr, ss, sr, bs, br, *scratch):
    c, b, y, k = place()
    sib, ynb = {"band": b + 1 - 2 * k}, {"band": b + 2 - 4 * y}
    peers = [lax.rem(c + d, 8) for d in range(1, 8)]
    pend, waits = [], iter(range(20))

    def load(src, dst):
        cp = pltpu.make_async_copy(src, dst, ls.at[next(waits)])
        cp.start()
        return cp

    loads_i = [load(gi0, grad_i0), load(gi1, grad_i1)]
    load_dh = load(dh, dlat)
    greet(everyone())
    n = N_SCATTER
    rs_o = Scatter("O", grad_o, total, scratch[:n], pend)
    rs_a = Scatter("A", grad_a, total, scratch[n:2 * n], pend)
    rs_i = [Scatter("I0", grad_i0, total, scratch[2 * n:3 * n], pend), Scatter("I1", grad_i1, total, scratch[3 * n:], pend)]

    def go(make):
        make().start()
        pend.append(make)

    def arrive(view, sem):
        pltpu.make_async_copy(view, view, sem).wait()

    slots = pl.ds(pl.multiple_of(16 * c, 16), 16)
    for s in range(2):
        loads_i[s].wait()
        rs_i[s].send_y()
        rs_i[s].send_mid()

    def first(o_v, da_v, wo_v):
        parts = [load(o, o_v), load(da, da_v), load(WO, wo_v)]
        for cp in parts:
            cp.wait()
        for i, cols in enumerate(rs_o.parts()):
            grad_o[:, cols] = dot_tn(o_v[...], da_v[:, cols]).astype(BF)
            if i == 0:
                rs_o.send_y()
            if i == 1:
                rs_o.send_mid()
        for m in range(2):
            do[m] = dot_nt(da_v[pl.ds(TOK * m, TOK)], wo_v[...]).astype(BF)

    pl.run_scoped(first, pltpu.VMEM((2 * TOK, QC), BF), pltpu.VMEM((2 * TOK, D), BF), pltpu.VMEM((QC, D), BF))

    def second(q_v, kb_v, vb_v, dqf, dkf, dvf, toep, dsum):
        parts = [load(q, q_v), load(kb, kb_v), load(vb, vb_v)]
        dqf[...] = jnp.zeros_like(dqf)
        dkf[...] = jnp.zeros_like(dkf)
        dvf[...] = jnp.zeros_like(dvf)
        for cp in parts:
            cp.wait()

        def head(h, _):
            win, hm = head_window(h)
            toep[...] = toeplitz(base, h)
            dsum[...] = jnp.zeros_like(dsum)
            lane_h = lax.broadcasted_iota(jnp.int32, (1, 128), 1) == h

            def tile(t, _):
                m, j = t // 2, lax.rem(t, 2)
                rows = pl.ds(pl.multiple_of(HALF * j, 16), HALF)
                krows = pl.ds(pl.multiple_of(HALF * j, 16), KW)
                qm, dm = q_v[m, rows, win] * hm, do[m, rows, win] * hm
                kw = kb_v[m, krows, win]
                level = jnp.sum(jnp.where(lane_h, lse[m, rows], 0.0), -1, keepdims=True)
                p = jnp.exp(dot_nt(qm, kw) * SCALE + (toep[...] + mask[m, j]) - level)
                dp = dot_nt(dm, vb_v[m, krows, win])
                delta = jnp.sum(p * dp, -1, keepdims=True)
                ds = (p * (dp - delta)).astype(BF)
                dsum[...] += ds.astype(F32)
                dqf[m, rows, win] += dot(ds, kw * hm)
                dkf[m, krows, win] += dot_tn(ds, qm)
                dvf[m, krows, win] += dot_tn(p.astype(BF), dm)
                return 0

            lax.fori_loop(0, 4, tile, 0)
            strip = dsum[0:8]
            for r in range(8, HALF, 8):
                strip = strip + pltpu.roll(dsum[r:r + 8], KW - r, 1)
            line = strip[0:1]
            for r in range(1, 8):
                line = line + pltpu.roll(strip, KW - r, 1)[r:r + 1]
            dbias[pl.ds(h, 1)] = line
            return 0

        for i in range(4):
            lax.fori_loop(2 * i, 2 * i + 2, head, 0)
            if i == 0:
                for d in (1, 3, 2):
                    rs_i[0].side_x(d)
            elif i == 1:
                rs_i[0].side_x(0)
                for d in (1, 3, 2):
                    rs_i[0].send_z(d)
                rs_i[1].side_x(1)
            elif i == 2:
                for d in (3, 2, 0):
                    rs_i[1].side_x(d)
                rs_i[1].send_z(1)
        away = pl.ds(pl.multiple_of(624 * (1 - y), 16), 80)
        edge = pl.ds(pl.multiple_of(544 - 464 * y, 16), 80)
        for m in range(2):
            rim[m, 0] = (dkf[m, away] * SCALE).astype(BF)
            rim[m, 1] = dvf[m, away].astype(BF)
            go(lambda m=m: remote(rim.at[m], rim_in.at[m], ks.at[m], kr.at[m], ynb))
        for m in range(2):
            tok = pl.ds(TOK * m, TOK)
            dqkv[tok, 0:QC] = (dqf[m] * SCALE).astype(BF)
        for d in ORDER:
            rs_o.side_x(d)
        rs_i[1].send_z(3)
        rs_i[1].send_z(2)
        for m in range(2):
            arrive(rim_in.at[m], kr.at[m])
            tok = pl.ds(TOK * m, TOK)
            dkf[m, edge] += rim_in[m, 0].astype(F32) * (1.0 / SCALE)
            dvf[m, edge] += rim_in[m, 1].astype(F32)
            dqkv[tok, QC:2 * QC] = (dkf[m, 80:624] * SCALE).astype(BF)
            dqkv[tok, 2 * QC:] = dvf[m, 80:624].astype(BF)

    pl.run_scoped(second, pltpu.VMEM((2, TOK, QC), BF), pltpu.VMEM((2, KEYS, QC), BF), pltpu.VMEM((2, KEYS, QC), BF),
                  pltpu.VMEM((2, TOK, QC), F32), pltpu.VMEM((2, KEYS, QC), F32), pltpu.VMEM((2, KEYS, QC), F32),
                  pltpu.VMEM((HALF, KW), F32), pltpu.VMEM((HALF, KW), F32))

    def third(xn_v, wa_v, dn):
        loads = [load(xn, xn_v), load(WA, wa_v)]
        tq = dot_tn(onehot[0], dqkv[0:TOK, 0:QC]) + dot_tn(onehot[1], dqkv[TOK:, 0:QC])
        tv = dot_tn(onehot[0], dqkv[0:TOK, 2 * QC:]) + dot_tn(onehot[1], dqkv[TOK:, 2 * QC:])
        tsum[:, 0:QC] = tq[0:16].astype(BF)
        tsum[:, QC:] = tv[0:16].astype(BF)
        go(lambda: remote(tsum, tsum_in, ts.at[0], tr.at[0], ynb))
        loads[0].wait()
        for i, cols in enumerate(rs_a.parts()):
            fill_part(grad_a, xn_v, dqkv, cols, 0, cols)
            if i == 0:
                rs_a.send_y()
                arrive(tsum_in, tr.at[0])
                dt_all[k, slots] = (tsum[...].astype(F32) + tsum_in[...].astype(F32)).astype(BF)
                for n, p in enumerate(peers):
                    go(lambda n=n, p=p: remote(dt_all.at[k, slots], dt_all.at[k, slots], ps.at[n], pr.at[6 - n], {"canvas": p}))
            if i == 1:
                rs_a.send_mid()
        for d in (1, 3, 2):
            rs_o.send_z(d)
        rs_i[0].finish()
        loads[1].wait()
        for m in range(2):
            rows = pl.ds(pl.multiple_of(TOK * m + HALF * (1 - k), 16), HALF)
            rows_own = pl.ds(pl.multiple_of(TOK * m + HALF * k, 16), HALF)

            def back(n, _):
                cols = pl.ds(pl.multiple_of(n * 384, 128), 384)
                x_send[m, :, cols] = dot_nt(dqkv[rows], wa_v[cols]).astype(BF)
                return 0

            lax.fori_loop(0, 3, back, 0)
            go(lambda m=m: remote(x_send.at[m], x_recv.at[m], xs.at[m], xr.at[m], sib))

            def back_own(n, _):
                cols = pl.ds(pl.multiple_of(n * 384, 128), 384)
                dn[m, :, cols] = dot_nt(dqkv[rows_own], wa_v[cols])
                return 0

            lax.fori_loop(0, 3, back_own, 0)
        rs_i[1].finish()
        rs_a.side_x(1)
        for n in range(7):
            arrive(dt_all.at[k, pl.ds(pl.multiple_of(16 * lax.rem(c + n + 1, 8), 16), 16)], pr.at[n])
        go(lambda: remote(dt_all.at[k], dt_all.at[k], us.at[0], ur.at[0], sib))
        gt_send[...] = dot_nt(dt_all[k], ti[...])
        go(lambda: remote(gt_send, gt_in, us.at[1], ur.at[1], sib))
        rs_a.side_x(3)
        rs_a.send_z(1)
        load_dh.wait()
        gain_one = jnp.zeros((1, D), F32)
        for m in range(2):
            arrive(x_recv.at[m], xr.at[m])
            grad = dn[m] + x_recv[m].astype(F32)
            n, r = norm(lat[m].astype(F32))
            gain_one = gain_one + jnp.sum(grad * n, 0, keepdims=True)
            dlat[m] = dlat[m] + norm_back(n, r, grad * gains[0:1])
            if m == 0:
                rs_a.side_x(2)
                rs_a.send_z(3)
        first_row = lax.broadcasted_iota(jnp.int32, (8, 1), 0) == 0
        both = jnp.where(first_row, jnp.broadcast_to(gain_one, (8, D)), gain_two[...])
        for p in range(8):
            sm_send[p, 0:8] = dbias[...]
            sm_send[p, 8:16] = (pltpu.roll(both, D - 144 * p, 1) if p else both)[:, 0:KW]

    pl.run_scoped(third, pltpu.VMEM((2 * TOK, D), BF), pltpu.VMEM((D, 3 * QC), BF), pltpu.VMEM((2, HALF, D), F32))
    for n, p in enumerate(peers):
        go(lambda n=n, p=p: remote(sm_send.at[p], sm_in.at[6 - n], ss.at[n], sr.at[6 - n], {"canvas": p}))
    rs_o.finish()
    arrive(gt_in, ur.at[1])
    gt_in[...] = gt_in[...] + gt_send[...]
    for n, p in enumerate(peers):
        go(lambda n=n, p=p: remote(gt_in.at[pl.ds(pl.multiple_of(16 * p, 16), 16)], gt.at[c], vs.at[n], vr.at[6 - n], {"canvas": p}))
    gt[c] = gt_in[pl.ds(pl.multiple_of(16 * c, 16), 16)]
    rs_a.side_x(0)
    rs_a.send_z(2)
    acc = sm_send[c]
    for n in range(7):
        arrive(sm_in.at[n], sr.at[n])
        acc = acc + sm_in[n]
    small[b] = acc
    for i in range(3):
        go(lambda i=i: remote(small.at[b], small.at[b], bs.at[i], br.at[2 - i], {"band": lax.rem(b + i + 1, 4)}))
    rs_i[0].collect(out_i0)
    rs_i[1].collect(out_i1)
    rs_o.collect(out_o)
    for n in range(7):
        arrive(gt.at[lax.rem(c + n + 1, 8)], vr.at[n])
    arrive(dt_all.at[1 - k], ur.at[0])
    for i in range(3):
        arrive(small.at[lax.rem(b + i + 1, 4)], br.at[i])
    rs_a.finish()
    rs_a.collect(out_a)
    for rs in (rs_o, rs_a, *rs_i):
        rs.sent()
    for make in pend:
        make().wait_send()


def attn_back(*args):
    S = jax.ShapeDtypeStruct
    dma = pltpu.SemaphoreType.DMA
    V, anyspace = pl.BlockSpec(memory_space=pltpu.VMEM), pl.BlockSpec(memory_space=pl.ANY)
    return pl.pallas_call(
        attn_back_kernel,
        out_shape=[S((2, HALF, D), F32), S((2, 128, 2 * QC), BF), S((8, 16, 144), F32), S((4, 16, KW), F32),
                   S((36, D), F32), S((2, 36, 3 * QC), F32), S((2, 36, D), F32), S((2, 36, D), F32)],
        in_specs=[anyspace, anyspace, V, V, V] + [anyspace] * 4 + [V] + [anyspace] * 3 + [V] * 4 + [anyspace] * 2, out_specs=[V] * 8,
        scratch_shapes=[pltpu.VMEM((QC, D), BF), pltpu.VMEM((D, 3 * QC), BF), pltpu.VMEM((D, D), BF), pltpu.VMEM((D, D), BF), pltpu.VMEM((2, TOK, QC), BF),
                        pltpu.VMEM((2 * TOK, 3 * QC), BF),
                        pltpu.VMEM((2, 2, 80, QC), BF), pltpu.VMEM((2, 2, 80, QC), BF), pltpu.VMEM((16, 2 * QC), BF), pltpu.VMEM((16, 2 * QC), BF),
                        pltpu.VMEM((128, 144), F32), pltpu.VMEM((128, 144), F32),
                        pltpu.VMEM((2, HALF, D), BF), pltpu.VMEM((2, HALF, D), BF), pltpu.VMEM((8, KW), F32), pltpu.VMEM((8, 16, KW), F32), pltpu.VMEM((7, 16, KW), F32),
                        pltpu.VMEM((144, 1280), F32),
                        dma((2,)), dma((2,)), dma((1,)), dma((1,)), dma((7,)), dma((7,)), dma((2,)), dma((2,)), dma((7,)), dma((7,)), dma((20,)), dma((2,)), dma((2,)),
                        dma((7,)), dma((7,)), dma((3,)), dma((3,))]
        + scatter_scratch("O") + scatter_scratch("A") + scatter_scratch("I0") + scatter_scratch("I1"),
        compiler_params=pltpu.CompilerParams(collective_id=3, has_side_effects=True, vmem_limit_bytes=127 * 2 ** 19),
        name="attn_back")(*args)


def local_fast(*args):
    p = prologue(*args)
    c, b, y, k = place()
    (out, xn, q, kb, vb, lse, o, hres, hn, g, gp, WA, WO, WI0, WI1, WB0, WB1, te_all, mask, onehot) = gather_forward(p["own"], p)
    cot = args[10].reshape(2, HALF, D)
    dh, da, gain_two, out_b, gi0, gi1 = mlp_back(cot, p["filled"], p["gains"], WI0, WI1, WB0, WB1, hres, hn.reshape(2 * TOK, D),
                                                 g.reshape(2 * TOK, FH), gp.reshape(2 * TOK, FH))
    dlat, dt_all, gt, small, out_o, out_a, out_i0, out_i1 = attn_back(
        WA, WO, p["ti"], p["gains"], p["lat"], xn.reshape(2 * TOK, D), q, kb, vb, lse, o.reshape(2 * TOK, QC), da, dh,
        mask, p["base"], onehot, gain_two, gi0, gi1)
    shape = (2, 1, 8, 34, D)
    places = [80 + 34 * dr + dc for dr in range(-2, 3) for dc in range(-2, 3)]
    bias = small[0:2, 0:8] + small[2:4, 0:8]
    grad_bias = bias[:, :, jnp.array(places)].transpose(2, 1, 0).reshape(25, 16)
    mine = lax.dynamic_slice_in_dim(small[:, 8:10, 0:144].sum(0), 36 * b, 36, 1)
    grad_a = out_a.reshape(2, 36, 3, 8, 80)[..., :72].transpose(1, 2, 3, 0, 4).reshape(36, 3 * D)
    grad_i = jnp.stack([out_i0, out_i1]).reshape(2, 2, 36, 8, 144).transpose(2, 3, 1, 0, 4).reshape(36, 2 * FH)
    dt = dt_all.reshape(2, 128, 2, 8, 80)[..., :72].transpose(1, 2, 3, 0, 4).reshape(128, 2 * D)
    te_mine = lax.dynamic_slice_in_dim(te_all.reshape(128, 144), 36 * b, 36, 1)
    grad_time_in = dot_tn(te_mine, dt)
    grad_time = gt.transpose(1, 0, 2).reshape(16, D)[:10].reshape(2, 1, 5, D)
    return (out.reshape(shape), dlat.reshape(shape), grad_time, mine.T, grad_a, grad_time_in, grad_bias, out_o, grad_i, out_b)


def solution(mesh):
    return jax.shard_map(
        local_fast if mesh.shape["canvas"] == 8 and mesh.shape["band"] == 4 else local,
        mesh=mesh,
        in_specs=(
            P(None, "canvas", "band", None, None),
            P(None, "canvas", "band", None),
            P(None, "canvas", None, None),
            P(),
            P("canvas", None),
            P("canvas", None),
            P(),
            P("canvas", None),
            P("canvas", None),
            P("canvas", None),
            P(None, "canvas", "band", None, None),
        ),
        out_specs=(
            P(None, "canvas", "band", None, None),
            P(None, "canvas", "band", None, None),
            P(None, "canvas", None, None),
            P(("canvas", "band"), None),
            P(("canvas", "band"), None),
            P(("canvas", "band"), None),
            P(),
            P(("canvas", "band"), None),
            P(("canvas", "band"), None),
            P(("canvas", "band"), None),
        ),
        check_vma=False,
    )
```

```python
from functools import partial
import jax
import jax.numpy as jnp
from jax import lax
from jax.experimental import pallas as pl
from jax.experimental.pallas import tpu as pltpu

from jax.sharding import PartitionSpec as P

WIN = 5


EPSILON = 1e-05


def padded_2(shard, sides, width):
    for axis, dim in sides:
        devices, length = (lax.axis_size(axis), shard.shape[dim])
        up = [(i, (i + 1) % devices) for i in range(devices - 1)]
        down = [(j, i) for i, j in up]
        last = lax.slice_in_dim(shard, length - width, length, axis=dim)
        first = lax.slice_in_dim(shard, 0, width, axis=dim)
        before = lax.ppermute(last, axis, up)
        after = lax.ppermute(first, axis, down)
        shard = jnp.concatenate([before, shard, after], axis=dim)
    return shard


def shifted(shard, axis, by):
    devices = lax.axis_size(axis)
    pairs = [(i, i + by) for i in range(devices) if 0 <= i + by < devices]
    return lax.ppermute(shard, axis, pairs)


def shortened(shard):

    def short(part):
        return part.astype(jnp.bfloat16) if part.dtype == jnp.float32 else part

    return jax.tree.map(short, shard)


def normalize(value, gain):
    center = value - jnp.mean(value, -1, keepdims=True)
    scaled = lax.rsqrt(jnp.mean(center * center, -1, keepdims=True) + EPSILON)
    unit = center * scaled
    return (unit, scaled, unit * gain)


def normalize_back(unit, scaled, gain, grad_out):
    part = grad_out * gain
    return scaled * (
        part - jnp.mean(part, -1, keepdims=True) - unit * jnp.mean(part * unit, -1, keepdims=True)
    )


def rows_dot(left, right):
    return lax.dot_general(
        left, right, (((0,), (0,)), ((), ())), preferred_element_type=jnp.float32
    )


def back_dot(left, weight):
    return lax.dot_general(
        left, weight, (((1,), (1,)), ((), ())), preferred_element_type=jnp.float32
    )


def neighbour_stack(padded, band_rows, columns):
    pieces = [padded[:, i : i + band_rows, j : j + columns] for i in range(WIN) for j in range(WIN)]
    stacked = jnp.stack(pieces)
    return stacked.reshape((WIN * WIN, -1) + padded.shape[3:])


def spread_back(terms, canvases, band_rows, columns):
    reach = WIN // 2
    shaped = terms.reshape((WIN * WIN, canvases, band_rows, columns, terms.shape[-1]))
    summed = None
    for i in range(WIN):
        for j in range(WIN):
            placed = jnp.pad(
                shaped[i * WIN + j], ((0, 0), (i, 2 * reach - i), (j, 2 * reach - j), (0, 0))
            )
            summed = placed if summed is None else summed + placed
    return summed


def head_total(terms, head_sum):
    flat = terms.reshape(-1, terms.shape[-1])
    return jnp.dot(flat, head_sum, precision=lax.Precision.HIGHEST).reshape(
        terms.shape[:-1] + (head_sum.shape[1],)
    )


def head_widen(values, head_spread):
    flat = values.reshape(-1, values.shape[-1])
    return jnp.dot(flat, head_spread, preferred_element_type=jnp.bfloat16).reshape(
        values.shape[:-1] + (head_spread.shape[1],)
    )


def local(
    latents,
    segment_ids,
    time_embed,
    norm_gains,
    attn_in,
    time_in,
    rel_bias,
    out_proj,
    mlp_in,
    mlp_out,
    cotangent,
):
    micro_count, canvases, band_rows, columns, width = latents.shape
    slots = time_embed.shape[2]
    heads = rel_bias.shape[1]
    head_dim = width // heads
    reach = WIN // 2
    tokens = canvases * band_rows * columns
    score_scale = head_dim ** (-0.5)
    head_sum = (jnp.arange(width)[:, None] // head_dim == jnp.arange(heads)[None, :]).astype(
        jnp.float32
    )
    head_spread = head_sum.T.astype(jnp.bfloat16)
    owned = (attn_in, time_in, out_proj, mlp_in, mlp_out)
    seg_code = segment_ids + 2
    seg_rims = padded_2(seg_code, (("band", 2),), reach)
    seg_rims = jnp.pad(seg_rims, ((0, 0), (0, 0), (0, 0), (reach, reach)))
    band_share = 1.0 / lax.axis_size("band")
    outputs = []
    input_grads = []
    time_grads = []
    accum = None
    shards = None
    bias_accum = jnp.zeros(rel_bias.shape, jnp.float32)
    for batch_index in range(micro_count):
        full_weights = (
            lax.all_gather(owned[0], "canvas", axis=0, tiled=True),
            lax.all_gather(owned[1], "canvas", axis=0, tiled=True),
            lax.all_gather(owned[2], "canvas", axis=0, tiled=True),
            lax.all_gather(owned[3], "canvas", axis=0, tiled=True),
            lax.all_gather(owned[4], "canvas", axis=0, tiled=True),
        )
        w_attn, w_time, w_out, w_in, w_back = full_weights
        inputs = latents[batch_index].astype(jnp.float32).reshape(tokens, width)
        unit_one, scaled_one, normed_one = normalize(inputs, norm_gains[:, 0])
        normed = normed_one.astype(jnp.bfloat16)
        time_rows = time_embed[batch_index].reshape(canvases * slots, width)
        time_proj = jnp.dot(time_rows, w_time, preferred_element_type=jnp.float32).reshape(
            canvases, slots, 2 * width
        )
        seg_here = segment_ids[batch_index]
        member = (seg_here[..., None] == jnp.arange(slots)).astype(jnp.float32)
        token_time = jnp.einsum(
            "krcs,kse->krce", member, time_proj, precision=lax.Precision.HIGHEST
        ).reshape(tokens, 2 * width)
        qkv = jnp.dot(normed, w_attn, preferred_element_type=jnp.float32)
        query = (qkv[:, :width] + token_time[:, :width]).astype(jnp.bfloat16)
        keys = qkv[:, width : 2 * width].astype(jnp.bfloat16)
        values = (qkv[:, 2 * width :] + token_time[:, width:]).astype(jnp.bfloat16)
        paired = jnp.stack([keys, values]).reshape(2, canvases, band_rows, columns, width)
        paired = padded_2(paired, (("band", 2),), reach)
        paired = jnp.pad(paired, ((0, 0), (0, 0), (0, 0), (reach, reach), (0, 0)))
        key_win = neighbour_stack(paired[0], band_rows, columns)
        value_win = neighbour_stack(paired[1], band_rows, columns)
        seg_win = neighbour_stack(seg_rims[batch_index], band_rows, columns)
        allowed = (seg_win == seg_code[batch_index].reshape(1, tokens))[..., None]
        query_wide = query.astype(jnp.float32)
        raw = head_total(query_wide[None] * key_win.astype(jnp.float32), head_sum)
        logit_scores = raw * score_scale + rel_bias[:, None, :]
        masked = jnp.where(allowed, logit_scores, -1e30)
        peak = jnp.max(masked, 0)
        raised = jnp.where(allowed, jnp.exp(masked - peak), 0.0)
        probs_full = raised / jnp.sum(raised, 0)
        attention_probabilities = probs_full.astype(jnp.bfloat16)
        probs_wide = head_widen(attention_probabilities, head_spread)
        mixed_values = jnp.sum(probs_wide.astype(jnp.float32) * value_win.astype(jnp.float32), 0)
        attended = mixed_values.astype(jnp.bfloat16)
        branch = jnp.dot(attended, w_out, preferred_element_type=jnp.float32)
        resid = inputs + branch
        unit_two, scaled_two, normed_two = normalize(resid, norm_gains[:, 1])
        hidden_in = normed_two.astype(jnp.bfloat16)
        pre_act = jnp.dot(hidden_in, w_in, preferred_element_type=jnp.float32)
        activated = jax.nn.gelu(pre_act, approximate=False).astype(jnp.bfloat16)
        mlp_y = jnp.dot(activated, w_back, preferred_element_type=jnp.float32)
        filled = (seg_here >= 0).reshape(tokens, 1)
        outputs.append(
            jnp.where(filled, resid + mlp_y, 0.0)
            .astype(jnp.bfloat16)
            .reshape(canvases, band_rows, columns, width)
        )
        grad_y = cotangent[batch_index].reshape(tokens, width)
        grad_f = jnp.where(filled, grad_y, jnp.zeros_like(grad_y))
        grad_back = rows_dot(activated, grad_f)
        grad_act = back_dot(grad_f, w_back)
        gelu_out, gelu_pull = jax.vjp(partial(jax.nn.gelu, approximate=False), pre_act)
        grad_pre = gelu_pull(grad_act)[0].astype(jnp.bfloat16)
        grad_in = rows_dot(hidden_in, grad_pre)
        grad_hidden = back_dot(grad_pre, w_in)
        grad_resid = jnp.where(filled, grad_y.astype(jnp.float32), 0.0) + normalize_back(
            unit_two, scaled_two, norm_gains[:, 1], grad_hidden
        )
        gain_two = jnp.sum(grad_hidden * unit_two, 0)
        grad_branch = grad_resid.astype(jnp.bfloat16)
        grad_out = rows_dot(attended, grad_branch)
        grad_att = back_dot(grad_branch, w_out).astype(jnp.bfloat16)
        grad_att_wide = grad_att.astype(jnp.float32)
        grad_probs = head_total(grad_att_wide[None] * value_win.astype(jnp.float32), head_sum)
        centered = jnp.sum(probs_full * grad_probs, 0)
        grad_scores = (probs_full * (grad_probs - centered)).astype(jnp.bfloat16)
        bias_accum = bias_accum + jnp.sum(grad_scores.astype(jnp.float32), axis=1)
        scores_wide = head_widen(grad_scores, head_spread).astype(jnp.float32)
        grad_query = jnp.sum(scores_wide * key_win.astype(jnp.float32), 0) * score_scale
        key_summed = (
            spread_back(scores_wide * query_wide[None], canvases, band_rows, columns) * score_scale
        )
        value_summed = spread_back(
            probs_wide.astype(jnp.float32) * grad_att_wide[None], canvases, band_rows, columns
        )
        pair_grad = jnp.stack([key_summed, value_summed])[:, :, :, reach : reach + columns]
        upper_rim = pair_grad[:, :, :reach]
        lower_rim = pair_grad[:, :, band_rows + reach :]
        owned_rows = pair_grad[:, :, reach : reach + band_rows]
        from_below = shifted(upper_rim.astype(jnp.bfloat16), "band", -1).astype(upper_rim.dtype)
        from_above = shifted(lower_rim.astype(jnp.bfloat16), "band", 1).astype(lower_rim.dtype)
        owned_rows = owned_rows.at[:, :, band_rows - reach :].add(from_below)
        owned_rows = owned_rows.at[:, :, :reach].add(from_above)
        grad_keys = owned_rows[0].reshape(tokens, width).astype(jnp.bfloat16)
        grad_values = owned_rows[1].reshape(tokens, width).astype(jnp.bfloat16)
        grad_q_low = grad_query.astype(jnp.bfloat16)
        member_low = member.astype(jnp.bfloat16).reshape(canvases, band_rows * columns, slots)
        slot_query = jnp.einsum(
            "kns,knd->ksd",
            member_low,
            grad_q_low.reshape(canvases, band_rows * columns, width),
            preferred_element_type=jnp.float32,
        )
        slot_value = jnp.einsum(
            "kns,knd->ksd",
            member_low,
            grad_values.reshape(canvases, band_rows * columns, width),
            preferred_element_type=jnp.float32,
        )
        slot_part = jnp.concatenate([slot_query, slot_value], -1)
        slot_total = lax.psum(slot_part.astype(jnp.bfloat16), "band")
        slot_low = slot_total.reshape(canvases * slots, 2 * width)
        time_grads.append(back_dot(slot_low, w_time).reshape(canvases, slots, width))
        grad_time_in = rows_dot(time_rows, slot_low) * band_share
        grad_qkv = jnp.concatenate([grad_q_low, grad_keys, grad_values], -1)
        grad_attn = rows_dot(normed, grad_qkv)
        grad_normed = back_dot(grad_qkv, w_attn)
        grad_inputs = grad_resid + normalize_back(
            unit_one, scaled_one, norm_gains[:, 0], grad_normed
        )
        gain_one = jnp.sum(grad_normed * unit_one, 0)
        input_grads.append(grad_inputs.reshape(canvases, band_rows, columns, width))
        micro_grads = (
            grad_attn,
            grad_time_in,
            grad_out,
            grad_in,
            grad_back,
            jnp.stack([gain_one, gain_two], 1),
        )
        accum = micro_grads if accum is None else jax.tree.map(jnp.add, accum, micro_grads)
    wide_sums = jax.tree.map(
        lambda part: part.astype(jnp.float32),
        lax.psum_scatter(shortened(accum), "canvas", scatter_dimension=0, tiled=True),
    )
    shards = jax.tree.map(
        lambda part: part.astype(jnp.float32),
        lax.psum_scatter(shortened(wide_sums), "band", scatter_dimension=0, tiled=True),
    )
    bias_grad = lax.psum(bias_accum, ("canvas", "band"))
    return (
        jnp.stack(outputs),
        jnp.stack(input_grads),
        jnp.stack(time_grads),
        shards[5],
        shards[0],
        shards[1],
        bias_grad,
        shards[2],
        shards[3],
        shards[4],
    )


MESH = pl.DeviceIdType.MESH
BF, F32 = jnp.bfloat16, jnp.float32
EPS = 1e-5
TOK, HALF, D, QC, FH = 544, 272, 1152, 640, 2304
KEYS, KW, PADK = 784, 512, 80
SCALE = 72 ** -0.5
NEG = -1e30


def dot(a, b):
    return jnp.dot(a, b, preferred_element_type=F32)


def dot_nt(a, b):
    return lax.dot_general(a, b, (((1,), (1,)), ((), ())), preferred_element_type=F32)


def dot_tn(a, b):
    return lax.dot_general(a, b, (((0,), (0,)), ((), ())), preferred_element_type=F32)


def norm(v):
    center = v - jnp.mean(v, -1, keepdims=True)
    r = lax.rsqrt(jnp.mean(center * center, -1, keepdims=True) + EPS)
    return center * r, r


def norm_back(n, r, e):
    return r * (e - jnp.mean(e, -1, keepdims=True) - n * jnp.mean(e * n, -1, keepdims=True))


def place():
    c, b = lax.axis_index("canvas"), lax.axis_index("band")
    return c, b, b // 2, lax.rem(b, 2)


def greet(devs):
    bar = pltpu.get_barrier_semaphore()
    for dev in devs:
        pl.semaphore_signal(bar, 1, device_id=dev, device_id_type=MESH)
    pl.semaphore_wait(bar, len(devs))


def remote(src, dst, ss, rs, dev):
    return pltpu.make_async_remote_copy(src, dst, ss, rs, device_id=dev, device_id_type=MESH)


def head_window(h):
    ws = pl.multiple_of(jnp.minimum(80 * h // 128, 3) * 128, 128)
    lane = lax.broadcasted_iota(jnp.int32, (1, 256), 1) + ws - 80 * h
    hm = jnp.where((lane >= 0) & (lane < 80), 1.0, 0.0).astype(BF)
    return pl.ds(ws, 256), hm


def toeplitz(base, h):
    row = jnp.broadcast_to(base[pl.ds(h, 1)], (HALF, KW))
    return pltpu.roll(row, 0, 1, stride=1, stride_axis=0)


GSPEC = {"A": (144, 640, 640), "O": (80, 384, 384), "I0": (144, 384, 384), "I1": (144, 384, 384), "B0": (144, 384, 384), "B1": (144, 384, 384)}
GNAMES = list(GSPEC)


FIRST, STEP, SPARE = 4.0, 2.2, -4


class Gather:
    def __init__(self, own, full, s_sem, r_sem, y_sem, l_sem, pend):
        self.own, self.full, self.pend = dict(zip(GNAMES, own)), dict(zip(GNAMES, full)), pend
        self.s_sem, self.r_sem, self.y_sem, self.l_sem = s_sem, r_sem, y_sem, l_sem
        self.c, self.b, self.y, _ = place()
        self.z, self.x = self.c // 2, lax.rem(self.c, 2)
        z = self.z
        self.zp = [jnp.where(z == 0, t[0], jnp.where(z == 1, t[1], jnp.where(z == 2, t[2], t[3]))) for t in ((1, 0, 3, 2), (2, 2, 1, 1), (3, 3, 0, 0))]
        self.xdev, self.ydev = {"canvas": self.c + 1 - 2 * self.x}, {"band": self.b + 2 - 4 * self.y}
        self.count = dict.fromkeys(GNAMES, 0)

    def part(self, name, src, plane, side):
        rows, wide, mid = GSPEC[name]
        at = pl.ds(pl.multiple_of(src * rows, 16), rows)
        if plane:
            return at, pl.ds(pl.multiple_of(wide * side, 128), wide + mid)
        return at, pl.ds(pl.multiple_of((wide + mid) * side, 128), wide)

    def send(self, name, src, dev, plane, first=False, when=None):
        n = GNAMES.index(name)
        at, cols = self.part(name, src, plane, self.y)
        cp = remote(self.own[name].at[:, cols] if first else self.full[name].at[at, cols], self.full[name].at[at, cols],
                    self.s_sem.at[n, self.count[name]], (self.r_sem if plane else self.y_sem).at[n, src], dev)
        self.count[name] += 1
        if when is None:
            cp.start()
            self.pend.append(cp.wait_send)
        else:
            pl.when(when)(cp.start)
            self.pend.append(lambda: pl.when(when)(cp.wait_send))

    def own_sends(self, name):
        rows = GSPEC[name][0]
        for up in (1, -1):
            to = self.z + up
            self.send(name, self.c, {"canvas": jnp.clip(to, 0, 3) * 2 + self.x}, True, True, (to >= 0) & (to <= 3))
        self.send(name, self.c, self.xdev, True, True)
        pltpu.make_async_copy(self.own[name], self.full[name].at[pl.ds(pl.multiple_of(self.c * rows, 16), rows)],
                              self.l_sem.at[GNAMES.index(name)]).start()

    def wait(self, name, src, plane):
        at, cols = self.part(name, src, plane, self.y if plane else 1 - self.y)
        view = self.full[name].at[at, cols]
        pltpu.make_async_copy(view, view, (self.r_sem if plane else self.y_sem).at[GNAMES.index(name), src]).wait()

    def from_z(self, name, i):
        src = self.zp[i] * 2 + self.x
        self.wait(name, src, True)
        to = jnp.where(self.zp[i] < self.z, self.z + 1, self.z - 1)
        self.send(name, src, {"canvas": jnp.clip(to, 0, 3) * 2 + self.x}, True, False, (to >= 0) & (to <= 3))
        self.send(name, src, self.xdev, True)
        self.send(name, src, self.ydev, False)

    def from_x(self, name, i):
        src = (self.z if i == 0 else self.zp[i - 1]) * 2 + 1 - self.x
        self.wait(name, src, True)
        self.send(name, src, self.ydev, False)

    def complete(self, name):
        rows = GSPEC[name][0]
        for d in range(1, 8):
            self.wait(name, lax.rem(self.c + d, 8), False)
        pltpu.make_async_copy(self.own[name], self.full[name].at[pl.ds(pl.multiple_of(self.c * rows, 16), rows)],
                              self.l_sem.at[GNAMES.index(name)]).wait()

    def events(self, name):
        return [partial(self.from_z, name, 0), partial(self.from_x, name, 0), partial(self.from_z, name, 1), partial(self.from_x, name, 1),
                partial(self.from_z, name, 2), partial(self.from_x, name, 2), partial(self.from_x, name, 3)]


def gather_forward_kernel(A, O, I0, I1, B0, B1, lat_in, cot_in, gains, te, ti, seg_row, seg_col, colq, colk, base,
                          xn_o, q_o, kb_o, vb_o, lse_o, o_o, hres_o, hn_o, g_o, gp_o, df_o, gb0_o, gb1_o,
                          WA_o, WO_o, WI0_o, WI1_o, WB0_o, WB1_o, te_o, mask_o, onehot_o,
                          WA, WO, WI0, WI1, WB0, WB1, xn, q, kb, vb, lse, o, hres, hn, g, gp, df, gb0, gb1, te_in, seg_in, col_in, onehot,
                          tp_send, tp_recv, tmix, mask, toep, of, x_send, x_recv, lat, cot,
                          s_sem, r_sem, y_sem, l_sem, es, er, gs, gr, cs, cr,
                          xs, xr, ts, tr, ks, kr, as_, ar, hs, hr, fs, fr, ls, outs):
    loads = [pltpu.make_async_copy(lat_in, lat, ls.at[0]), pltpu.make_async_copy(cot_in, cot, ls.at[1])]
    for cp in loads:
        cp.start()
    c, b, y, k = place()
    sib, ynb = {"band": b + 1 - 2 * k}, {"band": b + 2 - 4 * y}
    peers = [lax.rem(c + d, 8) for d in range(1, 8)]
    pend, saves = [], []

    def go(src, dst, ss, rs, dev):
        cp = remote(src, dst, ss, rs, dev)
        cp.start()
        pend.append(cp.wait_send)

    def arrive(view, sem):
        pltpu.make_async_copy(view, view, sem).wait()

    def save(src, dst):
        cp = pltpu.make_async_copy(src, dst, outs.at[len(saves)])
        cp.start()
        saves.append(cp)

    gat = Gather((A, O, I0.at[0], I0.at[1], B0.at[0], B0.at[1]), (WA, WO, WI0, WI1, WB0, WB1), s_sem, r_sem, y_sem, l_sem, pend)
    queue, ends = [], {}
    for name, nxt in (("A", "I0"), ("O", "I1"), ("I0", "B0"), ("I1", "B1"), ("B0", None), ("B1", None)):
        steps = gat.events(name)
        if nxt:
            steps.insert(1, partial(gat.own_sends, nxt))
        queue += steps
        ends[name] = len(queue)

    total, clock = len(queue), [0.0]

    def tick(us):
        clock[0] += us
        while queue and FIRST + STEP * (total - len(queue)) <= clock[0]:
            queue.pop(0)()

    def complete(name):
        left = total - ends[name]
        while len(queue) > max(left + SPARE, 0):
            queue.pop(0)()
        gat.complete(name)
        clock[0] = max(clock[0], FIRST + STEP * (total - left))

    greet([{"band": lax.rem(b + d, 4)} for d in (1, 2, 3)] + [{"canvas": p} for p in peers])
    for i, p in enumerate(peers):
        go(te.at[p], te_in.at[c], es.at[i], er.at[6 - i], {"canvas": p})
    te_in[c] = te[c]
    for i in range(3):
        go(seg_row, seg_in.at[b], gs.at[i], gr.at[2 - i], {"band": lax.rem(b + i + 1, 4)})
    seg_in[b] = seg_row[...]
    go(seg_col, col_in.at[k], cs.at[0], cr.at[0], sib)
    col_in[k] = seg_col[...]
    gat.own_sends("A")
    gat.own_sends("O")

    loads[0].wait()
    mine = pl.ds(pl.multiple_of(HALF * k, 16), HALF)
    other = pl.ds(pl.multiple_of(HALF * (1 - k), 16), HALF)
    for m in range(2):
        n, _ = norm(lat[m].astype(F32))
        xn[m, mine] = (n * gains[0:1]).astype(BF)
        go(xn.at[m, mine], xn.at[m, mine], xs.at[m], xr.at[m], sib)
        if m == 0:
            for i in range(7):
                arrive(te_in.at[lax.rem(c + i + 1, 8)], er.at[i])
            for p in range(8):
                tp_send[16 * p:16 * p + 16] = dot(te_in[p], ti[...]).astype(BF)
            for i, p in enumerate(peers):
                go(tp_send.at[pl.ds(pl.multiple_of(16 * p, 16), 16)], tp_recv.at[6 - i], ts.at[i], tr.at[6 - i], {"canvas": p})
    save(te_in, te_o)
    arrive(col_in.at[1 - k], cr.at[0])
    for i in range(3):
        arrive(seg_in.at[lax.rem(b + i + 1, 4)], gr.at[i])
    slot = lax.rem(lax.broadcasted_iota(jnp.int32, (1, 32), 1), 16)
    lane = lax.broadcasted_iota(jnp.int32, (1, KW), 1)
    near = jnp.abs(colq[...] - colk[...]) < 2.5
    for j in range(2):
        at = 2 * y + j
        before, here, after = seg_in[jnp.maximum(at - 1, 0)], seg_in[at], seg_in[jnp.minimum(at + 1, 3)]
        before = pltpu.roll(jnp.where(at > 0, before, 0.0), KW - HALF, 1)
        after = pltpu.roll(jnp.where(at < 3, after, 0.0), HALF, 1)
        keys = jnp.where(lane < 80, before, jnp.where(lane < 352, here, jnp.where(lane < 432, after, 0.0)))
        for m in range(2):
            code = col_in[j, m, :, 0:1]
            mask[m, j] = jnp.where((code == keys[m:m + 1]) & near, 0.0, NEG).astype(BF)
            hit = (code.astype(jnp.int32) + (5 * m - 2) == slot) & (code >= 1.5)
            onehot[m, HALF * j:HALF * j + HALF] = jnp.where(hit, 1.0, 0.0).astype(BF)
    loads[1].wait()
    for m in range(2):
        filled = jnp.where(col_in[k, m, :, 0:1] >= 1.5, 1.0, 0.0)
        rows = pl.ds(pl.multiple_of(TOK * m + HALF * k, 16), HALF)
        df[rows] = (cot[m].astype(F32) * filled).astype(BF)
        go(df.at[rows], df.at[rows], fs.at[m], fr.at[m], sib)
    save(mask, mask_o)
    save(onehot, onehot_o)
    tick(13.0)
    for i in range(7):
        arrive(tp_recv.at[i], tr.at[i])
    tproj = tp_send[pl.ds(pl.multiple_of(16 * c, 16), 16)].astype(F32)
    for i in range(7):
        tproj = tproj + tp_recv[i].astype(F32)
    hi = tproj.astype(BF)
    tmix[0:16] = hi
    tmix[16:32] = (tproj - hi.astype(F32)).astype(BF)
    dead = pl.ds(pl.multiple_of(y * 624, 16), 80)
    for m in range(2):
        for ref in (kb, vb):
            ref[m, dead] = jnp.zeros((80, QC), BF)
            ref[m, 704:784] = jnp.zeros((80, QC), BF)
    of[...] = jnp.zeros_like(of)
    lse[...] = jnp.zeros_like(lse)
    complete("A")
    save(WA, WA_o)

    edge = pl.ds(pl.multiple_of(544 - 464 * y, 16), 80)
    land = pl.ds(pl.multiple_of(624 * y, 16), 80)
    land_here = pl.ds(pl.multiple_of(624 * (1 - y), 16), 80)
    for m in range(2):
        arrive(xn.at[m, other], xr.at[m])
        x = xn[m]
        kb[m, 80:624] = dot(x, WA[:, QC:2 * QC]).astype(BF)
        tick(1.2)
        vb[m, 80:624] = (dot(x, WA[:, 2 * QC:]) + dot(onehot[m], tmix[:, QC:])).astype(BF)
        for i, ref in enumerate((kb, vb)):
            go(ref.at[m, edge], ref.at[m, land], ks.at[m, i], kr.at[m, i], ynb)
        q[m] = (dot(x, WA[:, :QC]) + dot(onehot[m], tmix[:, :QC])).astype(BF)
        tick(2.5)
    save(xn, xn_o)
    save(q, q_o)
    for m in range(2):
        for i, ref in enumerate((kb, vb)):
            arrive(ref.at[m, land_here], kr.at[m, i])
    save(kb, kb_o)
    save(vb, vb_o)

    def head(h, _):
        win, hm = head_window(h)
        toep[...] = toeplitz(base, h)
        lane_h = lax.broadcasted_iota(jnp.int32, (1, 128), 1) == h

        def tile(t, _):
            m, j = t // 2, lax.rem(t, 2)
            rows = pl.ds(pl.multiple_of(HALF * j, 16), HALF)
            krows = pl.ds(pl.multiple_of(HALF * j, 16), KW)
            s = dot_nt(q[m, rows, win] * hm, kb[m, krows, win])
            s = s * SCALE + (toep[...] + mask[m, j])
            peak = jnp.max(s, -1, keepdims=True)
            e = jnp.exp(s - peak)
            total = jnp.sum(e, -1, keepdims=True)
            p = (e * (1.0 / total)).astype(BF)
            of[m, rows, win] += dot(p, vb[m, krows, win] * hm)
            lse[m, rows] = jnp.where(lane_h, peak + jnp.log(total), lse[m, rows])
            return 0

        return lax.fori_loop(0, 4, tile, 0)

    for n in range(8):
        lax.fori_loop(n, n + 1, head, 0)
        tick(3.1)
    save(lse, lse_o)
    for m in range(2):
        o[m] = of[m].astype(BF)
    save(o, o_o)
    complete("O")
    save(WO, WO_o)

    for m in range(2):
        x_send[m] = dot(o[m, other], WO[...]).astype(BF)
        go(x_send.at[m], x_recv.at[m], as_.at[m], ar.at[m], sib)
    for m in range(2):
        hres[m] = lat[m].astype(F32) + dot(o[m, mine], WO[...])
    tick(4.0)
    for m in range(2):
        arrive(x_recv.at[m], ar.at[m])
        hv = hres[m] + x_recv[m].astype(F32)
        hres[m] = hv
        n, _ = norm(hv)
        hn[m, mine] = (n * gains[1:2]).astype(BF)
        go(hn.at[m, mine], hn.at[m, mine], hs.at[m], hr.at[m], sib)
        tick(2.5)
    save(hres, hres_o)
    for m in range(2):
        arrive(hn.at[m, other], hr.at[m])
    save(hn, hn_o)
    for s, W in enumerate((WI0, WI1)):
        complete("I0" if s == 0 else "I1")
        save(W, (WI0_o, WI1_o)[s])
        for m in range(2):
            def up(i, _):
                cols = pl.ds(pl.multiple_of(i * 384, 128), 384)
                put = pl.ds(pl.multiple_of(i * 384 + D * s, 128), 384)
                u = dot(hn[m], W[:, cols])
                phi = 0.5 + 0.5 * lax.erf(u * (0.5 ** 0.5))
                g[pl.ds(TOK * m, TOK), put] = (u * phi).astype(BF)
                gp[pl.ds(TOK * m, TOK), put] = (phi + u * (jnp.exp(-0.5 * u * u) * 0.3989422804014327)).astype(BF)
                return 0

            lax.fori_loop(0, 3, up, 0)
            tick(3.3)
    save(g, g_o)
    save(gp, gp_o)
    for m in range(2):
        rows = pl.ds(pl.multiple_of(TOK * m + HALF * (1 - k), 16), HALF)
        arrive(df.at[rows], fr.at[m])
    save(df, df_o)
    for s, grad in enumerate((gb0, gb1)):
        for i in range(3):
            cols = pl.ds(384 * i, 384)
            fill_part(grad, g, df, cols, D * s, cols)
            tick(1.3)
        save(grad, (gb0_o, gb1_o)[s])
    for s, W in enumerate((WB0, WB1)):
        complete("B0" if s == 0 else "B1")
        save(W, (WB0_o, WB1_o)[s])
    for cp in saves:
        cp.wait()
    for wait in pend:
        wait()


def gather_forward(own, p, cot):
    S = jax.ShapeDtypeStruct
    dma = pltpu.SemaphoreType.DMA
    V, anyspace = pl.BlockSpec(memory_space=pltpu.VMEM), pl.BlockSpec(memory_space=pl.ANY)
    weights = [(D, 3 * QC), (QC, D), (D, D), (D, D), (D, D), (D, D)]
    kept = [((2, TOK, D), BF), ((2, TOK, QC), BF), ((2, KEYS, QC), BF), ((2, KEYS, QC), BF), ((2, TOK, 128), F32), ((2, TOK, QC), BF),
            ((2, HALF, D), F32), ((2, TOK, D), BF), ((2 * TOK, FH), BF), ((2 * TOK, FH), BF), ((2 * TOK, D), BF), ((D, D), BF), ((D, D), BF)]
    A, O, I, B = own
    return pl.pallas_call(
        gather_forward_kernel,
        out_shape=[S(s, t) for s, t in kept] + [S(s, BF) for s in weights]
        + [S((8, 16, 144), BF), S((2, 2, HALF, KW), BF), S((2, TOK, 32), BF)],
        in_specs=[anyspace] * 8 + [V] * 8, out_specs=[anyspace] * 22,
        scratch_shapes=[pltpu.VMEM(s, BF) for s in weights] + [pltpu.VMEM(s, t) for s, t in kept]
        + [pltpu.VMEM((8, 16, 144), BF), pltpu.VMEM((4, 8, KW), F32), pltpu.VMEM((2, 2, HALF, 128), F32), pltpu.VMEM((2, TOK, 32), BF),
           pltpu.VMEM((128, 2 * QC), BF), pltpu.VMEM((7, 16, 2 * QC), BF), pltpu.VMEM((32, 2 * QC), BF), pltpu.VMEM((2, 2, HALF, KW), BF),
           pltpu.VMEM((HALF, KW), F32), pltpu.VMEM((2, TOK, QC), F32), pltpu.VMEM((2, HALF, D), BF), pltpu.VMEM((2, HALF, D), BF),
           pltpu.VMEM((2, HALF, D), BF), pltpu.VMEM((2, HALF, D), BF),
           dma((6, 16)), dma((6, 8)), dma((6, 8)), dma((6,)), dma((7,)), dma((7,)), dma((3,)), dma((3,)), dma((1,)), dma((1,)),
           dma((2,)), dma((2,)), dma((7,)), dma((7,)), dma((2, 2)), dma((2, 2)), dma((2,)), dma((2,)), dma((2,)), dma((2,)), dma((2,)), dma((2,)), dma((2,)), dma((22,))],
        compiler_params=pltpu.CompilerParams(collective_id=1, has_side_effects=True, vmem_limit_bytes=127 * 2 ** 19),
        name="gather_forward")(A, O, I, I, B, B, p["lat"], cot, p["gains"], p["te"], p["ti"], p["seg_row"], p["seg_col"], p["colq"], p["colk"], p["base"])


def prologue(latents, segment_ids, time_embed, norm_gains, attn_in, time_in, rel_bias, out_proj, mlp_in, mlp_out, cotangent):
    c, b, y, k = place()

    def pick(v, axis):
        return lax.dynamic_index_in_dim(v, k, axis, keepdims=False)

    def pad_heads(v, n):
        v = pick(v.reshape(144, n, 8, 2, 72), 3)
        return jnp.pad(v, ((0, 0), (0, 0), (0, 0), (0, 8))).reshape(144, n * QC)

    own = (pad_heads(attn_in, 3),
           jnp.pad(pick(out_proj.reshape(2, 72, D), 0), ((0, 8), (0, 0))),
           pick(mlp_in.reshape(144, 8, 2, 2, 144), 2).transpose(2, 0, 1, 3).reshape(2, 144, D),
           pick(mlp_out.reshape(2, 2, 144, D), 0))
    code = (segment_ids.reshape(2, HALF) + 2).astype(F32)
    seg_row = jnp.pad(code, ((0, 6), (80, KW - 80 - HALF)))
    seg_col = jnp.broadcast_to(code[..., None], (2, HALF, 128))
    te = jnp.pad(time_embed.reshape(10, D), ((0, 6), (0, 0))).reshape(16, 8, 144).transpose(1, 0, 2)
    colq = (jnp.arange(HALF) % 34).astype(F32)[:, None]
    colk = ((jnp.arange(KW) - 80 + 34 * 3) % 34).astype(F32)[None]
    bias = pick(rel_bias.reshape(25, 8, 2), 2)
    base = jnp.full((8, KW), NEG, F32)
    places = [80 + 34 * dr + dc for dr in range(-2, 3) for dc in range(-2, 3)]
    base = base.at[:, jnp.array(places)].set(bias.T)
    filled = (segment_ids.reshape(2, HALF, 1) >= 0).astype(F32)
    return dict(own=own, ti=pad_heads(time_in, 2), te=te, seg_row=seg_row, seg_col=seg_col, colq=colq, colk=colk,
                base=base, filled=filled, lat=latents.reshape(2, HALF, D), gains=norm_gains.T)


RSPEC = {"A": (144, 640, 640), "O": (80, 384, 384), "I0": (144, 384, 384), "I1": (144, 384, 384), "B0": (144, 384, 384), "B1": (144, 384, 384)}
KEEP = {"A": (36, 48, 4), "I0": (36, 48, 4), "I1": (36, 48, 4), "O": (36, 48, 2), "B0": (144, 144, 2), "B1": (144, 144, 2)}
ORDER = (1, 3, 2, 0)


def scatter_scratch(name):
    rows, wide, mid = RSPEC[name]
    slab = wide + mid
    dma = pltpu.SemaphoreType.DMA
    _, held, sources = KEEP[name]
    sends = {"A": 4, "I": 4, "O": 2, "B": 1}[name[0]]
    return [pltpu.VMEM((8 * rows, wide), BF), pltpu.VMEM((4 * rows, slab), BF), pltpu.VMEM((3 * rows, slab), BF),
            pltpu.VMEM((sends, held, slab), BF), pltpu.VMEM((sources, held, slab), BF),
            dma((4,)), dma((4,)), dma((8,)), dma((8,)), dma((3,)), dma((3,)), dma((4,)), dma((4,))]


N_SCATTER = 13


class Scatter:
    def __init__(self, name, grad, total, scratch, pend):
        self.name, self.grad, self.total, self.pend = name, grad, total, pend
        (self.yr, self.xr, self.zr, self.stage, self.fr, self.ys, self.yw, self.xs, self.xw, self.zs, self.zw, self.fs, self.fw) = scratch
        self.rows, self.wide, self.mid = RSPEC[name]
        self.c, self.b, self.y, self.k = place()
        self.z, self.x = self.c // 2, lax.rem(self.c, 2)
        y, w, l = self.y, self.wide, self.mid
        self.slab = pl.ds(pl.multiple_of(w * y, 128), w + l)
        self.mids = pl.ds(w, l)
        self.side = pl.ds(pl.multiple_of((w + l) * y, 128), w)
        self.away = pl.ds(pl.multiple_of((w + l) * (1 - y), 128), w)
        self.slab_mid = pl.ds(pl.multiple_of(w * (1 - y), 128), l)
        self.slab_side = pl.ds(pl.multiple_of(l * y, 128), w)
        self.xdev, self.ydev = {"canvas": self.c + 1 - 2 * self.x}, {"band": self.b + 2 - 4 * self.y}

    def at(self, group):
        return pl.ds(pl.multiple_of(group * self.rows, 16), self.rows)

    def pair(self, d):
        return pl.ds(pl.multiple_of(lax.rem(self.z + d, 4) * (2 * self.rows), 16), 2 * self.rows)

    def go(self, make):
        make().start()
        self.pend.append(make)

    def parts(self):
        return self.away, self.mids, self.side

    def group(self, d, x):
        return self.at(2 * lax.rem(self.z + d, 4) + x)

    def send_y(self):
        for d in ORDER:
            self.go(lambda d=d: remote(self.grad.at[self.pair(d), self.away], self.yr.at[self.pair(d)], self.ys.at[d], self.yw.at[d], self.ydev))

    def send_mid(self):
        for d in ORDER:
            self.go(lambda d=d: remote(self.grad.at[self.group(d, 1 - self.x), self.mids], self.xr.at[pl.ds(self.rows * d, self.rows), self.slab_mid],
                                       self.xs.at[d], self.xw.at[d], self.xdev))

    def side_x(self, d):
        rows2 = self.pair(d)
        pltpu.make_async_copy(self.yr.at[rows2], self.yr.at[rows2], self.yw.at[d]).wait()
        self.grad[rows2, self.side] += self.yr[rows2]
        self.go(lambda: remote(self.grad.at[self.group(d, 1 - self.x), self.side], self.xr.at[pl.ds(self.rows * d, self.rows), self.slab_side],
                               self.xs.at[4 + d], self.xw.at[4 + d], self.xdev))

    def sum_x(self, d):
        rows = pl.ds(self.rows * d, self.rows)
        for view, sem in ((self.xr.at[rows, self.slab_mid], d), (self.xr.at[rows, self.slab_side], 4 + d)):
            pltpu.make_async_copy(view, view, self.xw.at[sem]).wait()
        return self.grad[self.group(d, self.x), self.slab] + self.xr[rows]

    def send_z(self, d):
        self.grad[self.group(d, self.x), self.slab] = self.sum_x(d)
        self.go(lambda: remote(self.grad.at[self.group(d, self.x), self.slab], self.zr.at[pl.ds((3 - d) * self.rows, self.rows)], self.zs.at[d - 1],
                               self.zw.at[3 - d], {"canvas": 2 * lax.rem(self.z + d, 4) + self.x}))

    def dests(self):
        sources = KEEP[self.name][2]
        if self.name[0] == "B":
            return [(0, 2 * self.k + int(self.name[1]))]
        return [(i, 2 * self.k + i if sources == 2 else i) for i in range(sources)]

    def finish(self):
        acc = self.sum_x(0).astype(F32)
        for i in (2, 0, 1):
            rows = pl.ds(i * self.rows, self.rows)
            pltpu.make_async_copy(self.zr.at[rows], self.zr.at[rows], self.zw.at[i]).wait()
            acc = acc + self.zr[rows].astype(F32)
        n, held, sources = KEEP[self.name]
        slab = self.wide + self.mid
        if self.name[0] == "B":
            self.stage[0] = acc.astype(BF)
        else:
            self.total[0:self.rows, 0:slab] = acc
            for i in range(sources):
                self.stage[i, 0:n] = self.total[n * i:n * i + n, 0:slab].astype(BF)
                self.stage[i, n:held] = jnp.zeros((held - n, slab), BF)
        slot = self.b if sources == 4 else self.y
        for i, dest in self.dests():
            @pl.when(self.b == dest)
            def _():
                self.fr[slot] = self.stage[i]

            @pl.when(self.b != dest)
            def _():
                remote(self.stage.at[i], self.fr.at[slot], self.fs.at[i], self.fw.at[slot], {"band": dest}).start()

    def sent(self):
        for i, dest in self.dests():
            @pl.when(self.b != dest)
            def _():
                remote(self.stage.at[i], self.fr.at[0], self.fs.at[i], self.fw.at[0], {"band": dest}).wait_send()

    def collect(self, out):
        n, held, sources = KEEP[self.name]
        for i in range(sources):
            src = i if sources == 4 else 2 * i + self.y

            @pl.when(self.b != src)
            def _():
                pltpu.make_async_copy(self.fr.at[i], self.fr.at[i], self.fw.at[i]).wait()
        w, l = self.wide, self.mid
        for half in range(sources // 2):
            lo, hi = self.fr[half].astype(F32)[:n], self.fr[half + sources // 2].astype(F32)[:n]
            dst = out.at[half] if sources == 4 else out
            dst[:, 0:w] = lo[:, :w]
            dst[:, w:w + l] = lo[:, w:] + hi[:, :l]
            dst[:, w + l:] = hi[:, l:]


def everyone():
    c, b, y, k = place()
    return [{"band": lax.rem(b + d, 4)} for d in (1, 2, 3)] + [{"canvas": lax.rem(c + d, 8)} for d in range(1, 8)]


def fill_part(grad, left, right, cols, lefts, rights):
    def step(i, _):
        r = pl.multiple_of(i * 384, 128)
        grad[pl.ds(r, 384), cols] = dot_tn(left[:, pl.ds(r + lefts, 384)], right[:, rights]).astype(BF)
        return 0

    lax.fori_loop(0, grad.shape[0] // 384, step, 0)


def mlp_back_kernel(cot, filled, gains, WI0, WI1, WB0, WB1, hres, hn, g, gp, df_in, gb0, gb1,
                    out, dh, da, gain, out_b, grad_i0, grad_i1,
                    grad_b0, grad_b1, du, gi, x_send, x_recv, f_send, f_recv, dn, ds_, dr_, xs, xr, as_, ar, ls, gs, *scratch):
    c, b, y, k = place()
    sib = {"band": b + 1 - 2 * k}
    df = da
    loads = [pltpu.make_async_copy(src, dst, ls.at[i])
             for i, (src, dst) in enumerate(((gb0, grad_b0), (gb1, grad_b1), (df_in, df), (gp, du), (hres, dh)))]
    for cp in loads:
        cp.start()
    greet([{"band": lax.rem(b + d, 4)} for d in (1, 2, 3)] + [{"canvas": c + 1 - 2 * lax.rem(c, 2)}] + [{"canvas": lax.rem(c + d, 8)} for d in (2, 4, 6)])
    pend = []
    rs = [Scatter("B0", grad_b0, None, scratch[:N_SCATTER], pend), Scatter("B1", grad_b1, None, scratch[N_SCATTER:], pend)]
    rs[1].fr, rs[1].fw = rs[0].fr, rs[0].fw

    def half(m, which):
        return pl.ds(pl.multiple_of(TOK * m + HALF * which, 16), HALF)

    for s in range(2):
        loads[s].wait()
        rs[s].send_y()
        rs[s].send_mid()
    for cp in loads[2:]:
        cp.wait()
    for m in range(2):
        def down_other(i, _):
            cols = pl.ds(pl.multiple_of(i * 384, 128), 384)
            f_send[m, :, cols] = (dot(g[half(m, 1 - k), 0:D], WB0[:, cols]) + dot(g[half(m, 1 - k), D:], WB1[:, cols])).astype(BF)
            return 0

        lax.fori_loop(0, 3, down_other, 0)
        loads.append(remote(f_send.at[m], f_recv.at[m], ds_.at[m], dr_.at[m], sib))
        loads[-1].start()

        def down(i, _):
            cols = pl.ds(pl.multiple_of(i * 384, 128), 384)
            dn[m, :, cols] = dot(g[half(m, k), 0:D], WB0[:, cols]) + dot(g[half(m, k), D:], WB1[:, cols])
            return 0

        lax.fori_loop(0, 3, down, 0)

    def back_act(m, s):
        def step(i, _):
            r = pl.multiple_of(i * 384, 128)
            cols = pl.ds(pl.multiple_of(r + D * s, 128), 384)
            rows = pl.ds(TOK * m, TOK)
            du[rows, cols] = (dot_nt(df[rows], (WB0, WB1)[s][pl.ds(r, 384)]) * du[rows, cols].astype(F32)).astype(BF)
            return 0

        lax.fori_loop(0, 3, step, 0)

    rs[0].side_x(1)
    back_act(0, 0)
    rs[0].side_x(3)
    rs[0].send_z(1)
    for m in range(2):
        v = f_recv.at[m]
        pltpu.make_async_copy(v, v, dr_.at[m]).wait()
        out[m] = ((dh[m] + (dn[m] + v[...].astype(F32))) * filled[m]).astype(BF)
    back_act(1, 0)
    rs[0].side_x(2)
    rs[0].send_z(3)
    back_act(0, 1)
    rs[0].side_x(0)
    rs[0].send_z(2)
    back_act(1, 1)
    rs[1].side_x(1)
    saves = []
    for s in range(2):
        def step(i, _):
            r = pl.multiple_of(i * 384, 128)
            gi[s, pl.ds(r, 384)] = dot_tn(hn[:, pl.ds(r, 384)], du[:, D * s:D * s + D]).astype(BF)
            return 0

        lax.fori_loop(0, 3, step, 0)
        cp = pltpu.make_async_copy(gi.at[s], (grad_i0, grad_i1)[s], gs.at[s])
        cp.start()
        saves.append(cp)
        if s == 0:
            rs[1].side_x(3)
            rs[1].send_z(1)
            rs[0].finish()
        else:
            rs[1].side_x(2)
            rs[1].send_z(3)

    for m in range(2):
        def hid(i, _):
            r = pl.multiple_of(i * 384, 128)
            rows = pl.ds(r, 384)
            v = dot_nt(du[half(m, 1 - k), 0:D], WI0[rows]) + dot_nt(du[half(m, 1 - k), D:], WI1[rows])
            x_send[m, :, rows] = v.astype(BF)
            return 0

        lax.fori_loop(0, 3, hid, 0)
        cp = remote(x_send.at[m], x_recv.at[m], xs.at[m], xr.at[m], sib)
        cp.start()
        loads.append(cp)

        def hid_own(i, _):
            r = pl.multiple_of(i * 384, 128)
            rows = pl.ds(r, 384)
            dn[m, :, rows] = dot_nt(du[half(m, k), 0:D], WI0[rows]) + dot_nt(du[half(m, k), D:], WI1[rows])
            return 0

        lax.fori_loop(0, 3, hid_own, 0)
        if m == 0:
            rs[1].side_x(0)
            rs[1].send_z(2)
    gain_two = jnp.zeros((1, D), F32)
    for m in range(2):
        pltpu.make_async_copy(x_recv.at[m], x_recv.at[m], xr.at[m]).wait()
        grad = dn[m] + x_recv[m].astype(F32)
        n, r = norm(dh[m])
        gain_two = gain_two + jnp.sum(grad * n, 0, keepdims=True)
        v = cot[m].astype(F32) * filled[m] + norm_back(n, r, grad * gains[1:2])
        dh[m] = v
        da[half(m, k)] = v.astype(BF)
        cp = remote(da.at[half(m, k)], da.at[half(m, k)], as_.at[m], ar.at[m], sib)
        cp.start()
        loads.append(cp)
    gain[...] = jnp.broadcast_to(gain_two, (8, D))
    for m in range(2):
        v = da.at[half(m, 1 - k)]
        pltpu.make_async_copy(v, v, ar.at[m]).wait()
    rs[1].finish()
    rs[0].collect(out_b)
    rs[0].sent()
    rs[1].sent()
    for cp in saves:
        cp.wait()
    for cp in loads[5:]:
        cp.wait_send()
    for make in pend:
        make().wait_send()


def mlp_back(*args):
    S = jax.ShapeDtypeStruct
    dma = pltpu.SemaphoreType.DMA
    V, anyspace = pl.BlockSpec(memory_space=pltpu.VMEM), pl.BlockSpec(memory_space=pl.ANY)
    return pl.pallas_call(
        mlp_back_kernel,
        out_shape=[S((2, HALF, D), BF), S((2, HALF, D), F32), S((2 * TOK, D), BF), S((8, D), F32), S((144, D), F32), S((D, D), BF), S((D, D), BF)],
        in_specs=[V] * 7 + [anyspace, V, V] + [anyspace] * 4, out_specs=[V] * 5 + [anyspace] * 2,
        scratch_shapes=[pltpu.VMEM((D, D), BF), pltpu.VMEM((D, D), BF), pltpu.VMEM((2 * TOK, FH), BF), pltpu.VMEM((2, D, D), BF),
                        pltpu.VMEM((2, HALF, D), BF), pltpu.VMEM((2, HALF, D), BF), pltpu.VMEM((2, HALF, D), BF), pltpu.VMEM((2, HALF, D), BF),
                        pltpu.VMEM((2, HALF, D), F32)]
        + [dma((2,))] * 6 + [dma((5,)), dma((2,))] + scatter_scratch("B0") + scatter_scratch("B1"),
        compiler_params=pltpu.CompilerParams(collective_id=2, has_side_effects=True, vmem_limit_bytes=127 * 2 ** 19),
        name="mlp_back")(*args)


def attn_back_kernel(WA, WO, ti, gains, lat, xn, q, kb, vb, lse, o, da, dh, mask, base, onehot, gain_two, gi0, gi1,
                     dlat, dt_all, gt, small, out_o, out_a, out_i0, out_i1,
                     grad_o, grad_a, grad_i0, grad_i1, do, dqkv, rim, rim_in, tsum, tsum_in, gt_send, gt_in, x_send, x_recv, dbias, sm_send, sm_in, total,
                     ks, kr, ts, tr, ps, pr, us, ur, vs, vr, ls, xs, xr, ss, sr, bs, br, *scratch):
    c, b, y, k = place()
    sib, ynb = {"band": b + 1 - 2 * k}, {"band": b + 2 - 4 * y}
    peers = [lax.rem(c + d, 8) for d in range(1, 8)]
    pend, waits = [], iter(range(20))

    def load(src, dst):
        cp = pltpu.make_async_copy(src, dst, ls.at[next(waits)])
        cp.start()
        return cp

    loads_i = [load(gi0, grad_i0), load(gi1, grad_i1)]
    load_dh = load(dh, dlat)
    greet(everyone())
    n = N_SCATTER
    rs_o = Scatter("O", grad_o, total, scratch[:n], pend)
    rs_a = Scatter("A", grad_a, total, scratch[n:2 * n], pend)
    rs_i = [Scatter("I0", grad_i0, total, scratch[2 * n:3 * n], pend), Scatter("I1", grad_i1, total, scratch[3 * n:], pend)]

    def go(make):
        make().start()
        pend.append(make)

    def arrive(view, sem):
        pltpu.make_async_copy(view, view, sem).wait()

    slots = pl.ds(pl.multiple_of(16 * c, 16), 16)
    for s in range(2):
        loads_i[s].wait()
        rs_i[s].send_y()
        rs_i[s].send_mid()

    def first(o_v, da_v, wo_v):
        parts = [load(o, o_v), load(da, da_v), load(WO, wo_v)]
        for cp in parts:
            cp.wait()
        for i, cols in enumerate(rs_o.parts()):
            grad_o[:, cols] = dot_tn(o_v[...], da_v[:, cols]).astype(BF)
            if i == 0:
                rs_o.send_y()
            if i == 1:
                rs_o.send_mid()
        for m in range(2):
            do[m] = dot_nt(da_v[pl.ds(TOK * m, TOK)], wo_v[...]).astype(BF)

    pl.run_scoped(first, pltpu.VMEM((2 * TOK, QC), BF), pltpu.VMEM((2 * TOK, D), BF), pltpu.VMEM((QC, D), BF))

    def second(q_v, kb_v, vb_v, dqf, dkf, dvf, toep, dsum):
        parts = [load(q, q_v), load(kb, kb_v), load(vb, vb_v)]
        dqf[...] = jnp.zeros_like(dqf)
        dkf[...] = jnp.zeros_like(dkf)
        dvf[...] = jnp.zeros_like(dvf)
        for cp in parts:
            cp.wait()

        def head(h, _):
            win, hm = head_window(h)
            toep[...] = toeplitz(base, h)
            dsum[...] = jnp.zeros_like(dsum)
            lane_h = lax.broadcasted_iota(jnp.int32, (1, 128), 1) == h

            def tile(t, _):
                m, j = t // 2, lax.rem(t, 2)
                rows = pl.ds(pl.multiple_of(HALF * j, 16), HALF)
                krows = pl.ds(pl.multiple_of(HALF * j, 16), KW)
                qm, dm = q_v[m, rows, win] * hm, do[m, rows, win] * hm
                kw = kb_v[m, krows, win]
                level = jnp.sum(jnp.where(lane_h, lse[m, rows], 0.0), -1, keepdims=True)
                p = jnp.exp(dot_nt(qm, kw) * SCALE + (toep[...] + mask[m, j]) - level)
                dp = dot_nt(dm, vb_v[m, krows, win])
                delta = jnp.sum(p * dp, -1, keepdims=True)
                ds = (p * (dp - delta)).astype(BF)
                dsum[...] += ds.astype(F32)
                dqf[m, rows, win] += dot(ds, kw * hm)
                dkf[m, krows, win] += dot_tn(ds, qm)
                dvf[m, krows, win] += dot_tn(p.astype(BF), dm)
                return 0

            lax.fori_loop(0, 4, tile, 0)
            strip = dsum[0:8]
            for r in range(8, HALF, 8):
                strip = strip + pltpu.roll(dsum[r:r + 8], KW - r, 1)
            line = strip[0:1]
            for r in range(1, 8):
                line = line + pltpu.roll(strip, KW - r, 1)[r:r + 1]
            dbias[pl.ds(h, 1)] = line
            return 0

        for i in range(4):
            lax.fori_loop(2 * i, 2 * i + 2, head, 0)
            if i == 0:
                for d in (1, 3, 2):
                    rs_i[0].side_x(d)
            elif i == 1:
                rs_i[0].side_x(0)
                for d in (1, 3, 2):
                    rs_i[0].send_z(d)
                rs_i[1].side_x(1)
            elif i == 2:
                for d in (3, 2, 0):
                    rs_i[1].side_x(d)
                rs_i[1].send_z(1)
        away = pl.ds(pl.multiple_of(624 * (1 - y), 16), 80)
        edge = pl.ds(pl.multiple_of(544 - 464 * y, 16), 80)
        for m in range(2):
            rim[m, 0] = (dkf[m, away] * SCALE).astype(BF)
            rim[m, 1] = dvf[m, away].astype(BF)
            go(lambda m=m: remote(rim.at[m], rim_in.at[m], ks.at[m], kr.at[m], ynb))
        for m in range(2):
            tok = pl.ds(TOK * m, TOK)
            dqkv[tok, 0:QC] = (dqf[m] * SCALE).astype(BF)
        for d in ORDER:
            rs_o.side_x(d)
        rs_i[1].send_z(3)
        rs_i[1].send_z(2)
        for m in range(2):
            arrive(rim_in.at[m], kr.at[m])
            tok = pl.ds(TOK * m, TOK)
            dkf[m, edge] += rim_in[m, 0].astype(F32) * (1.0 / SCALE)
            dvf[m, edge] += rim_in[m, 1].astype(F32)
            dqkv[tok, QC:2 * QC] = (dkf[m, 80:624] * SCALE).astype(BF)
            dqkv[tok, 2 * QC:] = dvf[m, 80:624].astype(BF)

    pl.run_scoped(second, pltpu.VMEM((2, TOK, QC), BF), pltpu.VMEM((2, KEYS, QC), BF), pltpu.VMEM((2, KEYS, QC), BF),
                  pltpu.VMEM((2, TOK, QC), F32), pltpu.VMEM((2, KEYS, QC), F32), pltpu.VMEM((2, KEYS, QC), F32),
                  pltpu.VMEM((HALF, KW), F32), pltpu.VMEM((HALF, KW), F32))

    def third(xn_v, wa_v, dn):
        loads = [load(xn, xn_v), load(WA, wa_v)]
        tq = dot_tn(onehot[0], dqkv[0:TOK, 0:QC]) + dot_tn(onehot[1], dqkv[TOK:, 0:QC])
        tv = dot_tn(onehot[0], dqkv[0:TOK, 2 * QC:]) + dot_tn(onehot[1], dqkv[TOK:, 2 * QC:])
        tsum[:, 0:QC] = tq[0:16].astype(BF)
        tsum[:, QC:] = tv[0:16].astype(BF)
        go(lambda: remote(tsum, tsum_in, ts.at[0], tr.at[0], ynb))
        loads[0].wait()
        for i, cols in enumerate(rs_a.parts()):
            fill_part(grad_a, xn_v, dqkv, cols, 0, cols)
            if i == 0:
                rs_a.send_y()
                arrive(tsum_in, tr.at[0])
                dt_all[k, slots] = (tsum[...].astype(F32) + tsum_in[...].astype(F32)).astype(BF)
                for n, p in enumerate(peers):
                    go(lambda n=n, p=p: remote(dt_all.at[k, slots], dt_all.at[k, slots], ps.at[n], pr.at[6 - n], {"canvas": p}))
            if i == 1:
                rs_a.send_mid()
        for d in (1, 3, 2):
            rs_o.send_z(d)
        rs_i[0].finish()
        loads[1].wait()
        for m in range(2):
            rows = pl.ds(pl.multiple_of(TOK * m + HALF * (1 - k), 16), HALF)
            rows_own = pl.ds(pl.multiple_of(TOK * m + HALF * k, 16), HALF)

            def back(n, _):
                cols = pl.ds(pl.multiple_of(n * 384, 128), 384)
                x_send[m, :, cols] = dot_nt(dqkv[rows], wa_v[cols]).astype(BF)
                return 0

            lax.fori_loop(0, 3, back, 0)
            go(lambda m=m: remote(x_send.at[m], x_recv.at[m], xs.at[m], xr.at[m], sib))

            def back_own(n, _):
                cols = pl.ds(pl.multiple_of(n * 384, 128), 384)
                dn[m, :, cols] = dot_nt(dqkv[rows_own], wa_v[cols])
                return 0

            lax.fori_loop(0, 3, back_own, 0)
        rs_i[1].finish()
        rs_a.side_x(1)
        for n in range(7):
            arrive(dt_all.at[k, pl.ds(pl.multiple_of(16 * lax.rem(c + n + 1, 8), 16), 16)], pr.at[n])
        go(lambda: remote(dt_all.at[k], dt_all.at[k], us.at[0], ur.at[0], sib))
        gt_send[...] = dot_nt(dt_all[k], ti[...])
        go(lambda: remote(gt_send, gt_in, us.at[1], ur.at[1], sib))
        rs_a.side_x(3)
        rs_a.send_z(1)
        load_dh.wait()
        gain_one = jnp.zeros((1, D), F32)
        for m in range(2):
            arrive(x_recv.at[m], xr.at[m])
            grad = dn[m] + x_recv[m].astype(F32)
            n, r = norm(lat[m].astype(F32))
            gain_one = gain_one + jnp.sum(grad * n, 0, keepdims=True)
            dlat[m] = dlat[m] + norm_back(n, r, grad * gains[0:1])
            if m == 0:
                rs_a.side_x(2)
                rs_a.send_z(3)
        first_row = lax.broadcasted_iota(jnp.int32, (8, 1), 0) == 0
        both = jnp.where(first_row, jnp.broadcast_to(gain_one, (8, D)), gain_two[...])
        for p in range(8):
            sm_send[p, 0:8] = dbias[...]
            sm_send[p, 8:16] = (pltpu.roll(both, D - 144 * p, 1) if p else both)[:, 0:KW]

    pl.run_scoped(third, pltpu.VMEM((2 * TOK, D), BF), pltpu.VMEM((D, 3 * QC), BF), pltpu.VMEM((2, HALF, D), F32))
    for n, p in enumerate(peers):
        go(lambda n=n, p=p: remote(sm_send.at[p], sm_in.at[6 - n], ss.at[n], sr.at[6 - n], {"canvas": p}))
    rs_o.finish()
    arrive(gt_in, ur.at[1])
    gt_in[...] = gt_in[...] + gt_send[...]
    for n, p in enumerate(peers):
        go(lambda n=n, p=p: remote(gt_in.at[pl.ds(pl.multiple_of(16 * p, 16), 16)], gt.at[c], vs.at[n], vr.at[6 - n], {"canvas": p}))
    gt[c] = gt_in[pl.ds(pl.multiple_of(16 * c, 16), 16)]
    rs_a.side_x(0)
    rs_a.send_z(2)
    acc = sm_send[c]
    for n in range(7):
        arrive(sm_in.at[n], sr.at[n])
        acc = acc + sm_in[n]
    small[b] = acc
    for i in range(3):
        go(lambda i=i: remote(small.at[b], small.at[b], bs.at[i], br.at[2 - i], {"band": lax.rem(b + i + 1, 4)}))
    rs_i[0].collect(out_i0)
    rs_i[1].collect(out_i1)
    rs_o.collect(out_o)
    for n in range(7):
        arrive(gt.at[lax.rem(c + n + 1, 8)], vr.at[n])
    arrive(dt_all.at[1 - k], ur.at[0])
    for i in range(3):
        arrive(small.at[lax.rem(b + i + 1, 4)], br.at[i])
    rs_a.finish()
    rs_a.collect(out_a)
    for rs in (rs_o, rs_a, *rs_i):
        rs.sent()
    for make in pend:
        make().wait_send()


def attn_back(*args):
    S = jax.ShapeDtypeStruct
    dma = pltpu.SemaphoreType.DMA
    V, anyspace = pl.BlockSpec(memory_space=pltpu.VMEM), pl.BlockSpec(memory_space=pl.ANY)
    return pl.pallas_call(
        attn_back_kernel,
        out_shape=[S((2, HALF, D), F32), S((2, 128, 2 * QC), BF), S((8, 16, 144), F32), S((4, 16, KW), F32),
                   S((36, D), F32), S((2, 36, 3 * QC), F32), S((2, 36, D), F32), S((2, 36, D), F32)],
        in_specs=[anyspace, anyspace, V, V, V] + [anyspace] * 4 + [V] + [anyspace] * 3 + [V] * 4 + [anyspace] * 2, out_specs=[V] * 8,
        scratch_shapes=[pltpu.VMEM((QC, D), BF), pltpu.VMEM((D, 3 * QC), BF), pltpu.VMEM((D, D), BF), pltpu.VMEM((D, D), BF), pltpu.VMEM((2, TOK, QC), BF),
                        pltpu.VMEM((2 * TOK, 3 * QC), BF),
                        pltpu.VMEM((2, 2, 80, QC), BF), pltpu.VMEM((2, 2, 80, QC), BF), pltpu.VMEM((16, 2 * QC), BF), pltpu.VMEM((16, 2 * QC), BF),
                        pltpu.VMEM((128, 144), F32), pltpu.VMEM((128, 144), F32),
                        pltpu.VMEM((2, HALF, D), BF), pltpu.VMEM((2, HALF, D), BF), pltpu.VMEM((8, KW), F32), pltpu.VMEM((8, 16, KW), F32), pltpu.VMEM((7, 16, KW), F32),
                        pltpu.VMEM((144, 1280), F32),
                        dma((2,)), dma((2,)), dma((1,)), dma((1,)), dma((7,)), dma((7,)), dma((2,)), dma((2,)), dma((7,)), dma((7,)), dma((20,)), dma((2,)), dma((2,)),
                        dma((7,)), dma((7,)), dma((3,)), dma((3,))]
        + scatter_scratch("O") + scatter_scratch("A") + scatter_scratch("I0") + scatter_scratch("I1"),
        compiler_params=pltpu.CompilerParams(collective_id=3, has_side_effects=True, vmem_limit_bytes=127 * 2 ** 19),
        name="attn_back")(*args)


def local_fast(*args):
    p = prologue(*args)
    c, b, y, k = place()
    cot = args[10].reshape(2, HALF, D)
    (xn, q, kb, vb, lse, o, hres, hn, g, gp, df, gb0, gb1, WA, WO, WI0, WI1, WB0, WB1, te_all, mask, onehot) = gather_forward(p["own"], p, cot)
    out, dh, da, gain_two, out_b, gi0, gi1 = mlp_back(cot, p["filled"], p["gains"], WI0, WI1, WB0, WB1, hres, hn.reshape(2 * TOK, D), g, gp, df, gb0, gb1)
    dlat, dt_all, gt, small, out_o, out_a, out_i0, out_i1 = attn_back(
        WA, WO, p["ti"], p["gains"], p["lat"], xn.reshape(2 * TOK, D), q, kb, vb, lse, o.reshape(2 * TOK, QC), da, dh,
        mask, p["base"], onehot, gain_two, gi0, gi1)
    shape = (2, 1, 8, 34, D)
    places = [80 + 34 * dr + dc for dr in range(-2, 3) for dc in range(-2, 3)]
    bias = small[0:2, 0:8] + small[2:4, 0:8]
    grad_bias = bias[:, :, jnp.array(places)].transpose(2, 1, 0).reshape(25, 16)
    mine = lax.dynamic_slice_in_dim(small[:, 8:10, 0:144].sum(0), 36 * b, 36, 1)
    grad_a = out_a.reshape(2, 36, 3, 8, 80)[..., :72].transpose(1, 2, 3, 0, 4).reshape(36, 3 * D)
    grad_i = jnp.stack([out_i0, out_i1]).reshape(2, 2, 36, 8, 144).transpose(2, 3, 1, 0, 4).reshape(36, 2 * FH)
    dt = dt_all.reshape(2, 128, 2, 8, 80)[..., :72].transpose(1, 2, 3, 0, 4).reshape(128, 2 * D)
    te_mine = lax.dynamic_slice_in_dim(te_all.reshape(128, 144), 36 * b, 36, 1)
    grad_time_in = dot_tn(te_mine, dt)
    grad_time = gt.transpose(1, 0, 2).reshape(16, D)[:10].reshape(2, 1, 5, D)
    return (out.reshape(shape), dlat.reshape(shape), grad_time, mine.T, grad_a, grad_time_in, grad_bias, out_o, grad_i, out_b)


def solution(mesh):
    return jax.shard_map(
        local_fast if mesh.shape["canvas"] == 8 and mesh.shape["band"] == 4 else local,
        mesh=mesh,
        in_specs=(
            P(None, "canvas", "band", None, None),
            P(None, "canvas", "band", None),
            P(None, "canvas", None, None),
            P(),
            P("canvas", None),
            P("canvas", None),
            P(),
            P("canvas", None),
            P("canvas", None),
            P("canvas", None),
            P(None, "canvas", "band", None, None),
        ),
        out_specs=(
            P(None, "canvas", "band", None, None),
            P(None, "canvas", "band", None, None),
            P(None, "canvas", None, None),
            P(("canvas", "band"), None),
            P(("canvas", "band"), None),
            P(("canvas", "band"), None),
            P(),
            P(("canvas", "band"), None),
            P(("canvas", "band"), None),
            P(("canvas", "band"), None),
        ),
        check_vma=False,
    )
```

```python
from functools import partial
import jax
import jax.numpy as jnp
from jax import lax
from jax.experimental import pallas as pl
from jax.experimental.pallas import tpu as pltpu

from jax.sharding import PartitionSpec as P

WIN = 5


EPSILON = 1e-05


def padded_2(shard, sides, width):
    for axis, dim in sides:
        devices, length = (lax.axis_size(axis), shard.shape[dim])
        up = [(i, (i + 1) % devices) for i in range(devices - 1)]
        down = [(j, i) for i, j in up]
        last = lax.slice_in_dim(shard, length - width, length, axis=dim)
        first = lax.slice_in_dim(shard, 0, width, axis=dim)
        before = lax.ppermute(last, axis, up)
        after = lax.ppermute(first, axis, down)
        shard = jnp.concatenate([before, shard, after], axis=dim)
    return shard


def shifted(shard, axis, by):
    devices = lax.axis_size(axis)
    pairs = [(i, i + by) for i in range(devices) if 0 <= i + by < devices]
    return lax.ppermute(shard, axis, pairs)


def shortened(shard):

    def short(part):
        return part.astype(jnp.bfloat16) if part.dtype == jnp.float32 else part

    return jax.tree.map(short, shard)


def normalize(value, gain):
    center = value - jnp.mean(value, -1, keepdims=True)
    scaled = lax.rsqrt(jnp.mean(center * center, -1, keepdims=True) + EPSILON)
    unit = center * scaled
    return (unit, scaled, unit * gain)


def normalize_back(unit, scaled, gain, grad_out):
    part = grad_out * gain
    return scaled * (
        part - jnp.mean(part, -1, keepdims=True) - unit * jnp.mean(part * unit, -1, keepdims=True)
    )


def rows_dot(left, right):
    return lax.dot_general(
        left, right, (((0,), (0,)), ((), ())), preferred_element_type=jnp.float32
    )


def back_dot(left, weight):
    return lax.dot_general(
        left, weight, (((1,), (1,)), ((), ())), preferred_element_type=jnp.float32
    )


def neighbour_stack(padded, band_rows, columns):
    pieces = [padded[:, i : i + band_rows, j : j + columns] for i in range(WIN) for j in range(WIN)]
    stacked = jnp.stack(pieces)
    return stacked.reshape((WIN * WIN, -1) + padded.shape[3:])


def spread_back(terms, canvases, band_rows, columns):
    reach = WIN // 2
    shaped = terms.reshape((WIN * WIN, canvases, band_rows, columns, terms.shape[-1]))
    summed = None
    for i in range(WIN):
        for j in range(WIN):
            placed = jnp.pad(
                shaped[i * WIN + j], ((0, 0), (i, 2 * reach - i), (j, 2 * reach - j), (0, 0))
            )
            summed = placed if summed is None else summed + placed
    return summed


def head_total(terms, head_sum):
    flat = terms.reshape(-1, terms.shape[-1])
    return jnp.dot(flat, head_sum, precision=lax.Precision.HIGHEST).reshape(
        terms.shape[:-1] + (head_sum.shape[1],)
    )


def head_widen(values, head_spread):
    flat = values.reshape(-1, values.shape[-1])
    return jnp.dot(flat, head_spread, preferred_element_type=jnp.bfloat16).reshape(
        values.shape[:-1] + (head_spread.shape[1],)
    )


def local(
    latents,
    segment_ids,
    time_embed,
    norm_gains,
    attn_in,
    time_in,
    rel_bias,
    out_proj,
    mlp_in,
    mlp_out,
    cotangent,
):
    micro_count, canvases, band_rows, columns, width = latents.shape
    slots = time_embed.shape[2]
    heads = rel_bias.shape[1]
    head_dim = width // heads
    reach = WIN // 2
    tokens = canvases * band_rows * columns
    score_scale = head_dim ** (-0.5)
    head_sum = (jnp.arange(width)[:, None] // head_dim == jnp.arange(heads)[None, :]).astype(
        jnp.float32
    )
    head_spread = head_sum.T.astype(jnp.bfloat16)
    owned = (attn_in, time_in, out_proj, mlp_in, mlp_out)
    seg_code = segment_ids + 2
    seg_rims = padded_2(seg_code, (("band", 2),), reach)
    seg_rims = jnp.pad(seg_rims, ((0, 0), (0, 0), (0, 0), (reach, reach)))
    band_share = 1.0 / lax.axis_size("band")
    outputs = []
    input_grads = []
    time_grads = []
    accum = None
    shards = None
    bias_accum = jnp.zeros(rel_bias.shape, jnp.float32)
    for batch_index in range(micro_count):
        full_weights = (
            lax.all_gather(owned[0], "canvas", axis=0, tiled=True),
            lax.all_gather(owned[1], "canvas", axis=0, tiled=True),
            lax.all_gather(owned[2], "canvas", axis=0, tiled=True),
            lax.all_gather(owned[3], "canvas", axis=0, tiled=True),
            lax.all_gather(owned[4], "canvas", axis=0, tiled=True),
        )
        w_attn, w_time, w_out, w_in, w_back = full_weights
        inputs = latents[batch_index].astype(jnp.float32).reshape(tokens, width)
        unit_one, scaled_one, normed_one = normalize(inputs, norm_gains[:, 0])
        normed = normed_one.astype(jnp.bfloat16)
        time_rows = time_embed[batch_index].reshape(canvases * slots, width)
        time_proj = jnp.dot(time_rows, w_time, preferred_element_type=jnp.float32).reshape(
            canvases, slots, 2 * width
        )
        seg_here = segment_ids[batch_index]
        member = (seg_here[..., None] == jnp.arange(slots)).astype(jnp.float32)
        token_time = jnp.einsum(
            "krcs,kse->krce", member, time_proj, precision=lax.Precision.HIGHEST
        ).reshape(tokens, 2 * width)
        qkv = jnp.dot(normed, w_attn, preferred_element_type=jnp.float32)
        query = (qkv[:, :width] + token_time[:, :width]).astype(jnp.bfloat16)
        keys = qkv[:, width : 2 * width].astype(jnp.bfloat16)
        values = (qkv[:, 2 * width :] + token_time[:, width:]).astype(jnp.bfloat16)
        paired = jnp.stack([keys, values]).reshape(2, canvases, band_rows, columns, width)
        paired = padded_2(paired, (("band", 2),), reach)
        paired = jnp.pad(paired, ((0, 0), (0, 0), (0, 0), (reach, reach), (0, 0)))
        key_win = neighbour_stack(paired[0], band_rows, columns)
        value_win = neighbour_stack(paired[1], band_rows, columns)
        seg_win = neighbour_stack(seg_rims[batch_index], band_rows, columns)
        allowed = (seg_win == seg_code[batch_index].reshape(1, tokens))[..., None]
        query_wide = query.astype(jnp.float32)
        raw = head_total(query_wide[None] * key_win.astype(jnp.float32), head_sum)
        logit_scores = raw * score_scale + rel_bias[:, None, :]
        masked = jnp.where(allowed, logit_scores, -1e30)
        peak = jnp.max(masked, 0)
        raised = jnp.where(allowed, jnp.exp(masked - peak), 0.0)
        probs_full = raised / jnp.sum(raised, 0)
        attention_probabilities = probs_full.astype(jnp.bfloat16)
        probs_wide = head_widen(attention_probabilities, head_spread)
        mixed_values = jnp.sum(probs_wide.astype(jnp.float32) * value_win.astype(jnp.float32), 0)
        attended = mixed_values.astype(jnp.bfloat16)
        branch = jnp.dot(attended, w_out, preferred_element_type=jnp.float32)
        resid = inputs + branch
        unit_two, scaled_two, normed_two = normalize(resid, norm_gains[:, 1])
        hidden_in = normed_two.astype(jnp.bfloat16)
        pre_act = jnp.dot(hidden_in, w_in, preferred_element_type=jnp.float32)
        activated = jax.nn.gelu(pre_act, approximate=False).astype(jnp.bfloat16)
        mlp_y = jnp.dot(activated, w_back, preferred_element_type=jnp.float32)
        filled = (seg_here >= 0).reshape(tokens, 1)
        outputs.append(
            jnp.where(filled, resid + mlp_y, 0.0)
            .astype(jnp.bfloat16)
            .reshape(canvases, band_rows, columns, width)
        )
        grad_y = cotangent[batch_index].reshape(tokens, width)
        grad_f = jnp.where(filled, grad_y, jnp.zeros_like(grad_y))
        grad_back = rows_dot(activated, grad_f)
        grad_act = back_dot(grad_f, w_back)
        gelu_out, gelu_pull = jax.vjp(partial(jax.nn.gelu, approximate=False), pre_act)
        grad_pre = gelu_pull(grad_act)[0].astype(jnp.bfloat16)
        grad_in = rows_dot(hidden_in, grad_pre)
        grad_hidden = back_dot(grad_pre, w_in)
        grad_resid = jnp.where(filled, grad_y.astype(jnp.float32), 0.0) + normalize_back(
            unit_two, scaled_two, norm_gains[:, 1], grad_hidden
        )
        gain_two = jnp.sum(grad_hidden * unit_two, 0)
        grad_branch = grad_resid.astype(jnp.bfloat16)
        grad_out = rows_dot(attended, grad_branch)
        grad_att = back_dot(grad_branch, w_out).astype(jnp.bfloat16)
        grad_att_wide = grad_att.astype(jnp.float32)
        grad_probs = head_total(grad_att_wide[None] * value_win.astype(jnp.float32), head_sum)
        centered = jnp.sum(probs_full * grad_probs, 0)
        grad_scores = (probs_full * (grad_probs - centered)).astype(jnp.bfloat16)
        bias_accum = bias_accum + jnp.sum(grad_scores.astype(jnp.float32), axis=1)
        scores_wide = head_widen(grad_scores, head_spread).astype(jnp.float32)
        grad_query = jnp.sum(scores_wide * key_win.astype(jnp.float32), 0) * score_scale
        key_summed = (
            spread_back(scores_wide * query_wide[None], canvases, band_rows, columns) * score_scale
        )
        value_summed = spread_back(
            probs_wide.astype(jnp.float32) * grad_att_wide[None], canvases, band_rows, columns
        )
        pair_grad = jnp.stack([key_summed, value_summed])[:, :, :, reach : reach + columns]
        upper_rim = pair_grad[:, :, :reach]
        lower_rim = pair_grad[:, :, band_rows + reach :]
        owned_rows = pair_grad[:, :, reach : reach + band_rows]
        from_below = shifted(upper_rim.astype(jnp.bfloat16), "band", -1).astype(upper_rim.dtype)
        from_above = shifted(lower_rim.astype(jnp.bfloat16), "band", 1).astype(lower_rim.dtype)
        owned_rows = owned_rows.at[:, :, band_rows - reach :].add(from_below)
        owned_rows = owned_rows.at[:, :, :reach].add(from_above)
        grad_keys = owned_rows[0].reshape(tokens, width).astype(jnp.bfloat16)
        grad_values = owned_rows[1].reshape(tokens, width).astype(jnp.bfloat16)
        grad_q_low = grad_query.astype(jnp.bfloat16)
        member_low = member.astype(jnp.bfloat16).reshape(canvases, band_rows * columns, slots)
        slot_query = jnp.einsum(
            "kns,knd->ksd",
            member_low,
            grad_q_low.reshape(canvases, band_rows * columns, width),
            preferred_element_type=jnp.float32,
        )
        slot_value = jnp.einsum(
            "kns,knd->ksd",
            member_low,
            grad_values.reshape(canvases, band_rows * columns, width),
            preferred_element_type=jnp.float32,
        )
        slot_part = jnp.concatenate([slot_query, slot_value], -1)
        slot_total = lax.psum(slot_part.astype(jnp.bfloat16), "band")
        slot_low = slot_total.reshape(canvases * slots, 2 * width)
        time_grads.append(back_dot(slot_low, w_time).reshape(canvases, slots, width))
        grad_time_in = rows_dot(time_rows, slot_low) * band_share
        grad_qkv = jnp.concatenate([grad_q_low, grad_keys, grad_values], -1)
        grad_attn = rows_dot(normed, grad_qkv)
        grad_normed = back_dot(grad_qkv, w_attn)
        grad_inputs = grad_resid + normalize_back(
            unit_one, scaled_one, norm_gains[:, 0], grad_normed
        )
        gain_one = jnp.sum(grad_normed * unit_one, 0)
        input_grads.append(grad_inputs.reshape(canvases, band_rows, columns, width))
        micro_grads = (
            grad_attn,
            grad_time_in,
            grad_out,
            grad_in,
            grad_back,
            jnp.stack([gain_one, gain_two], 1),
        )
        accum = micro_grads if accum is None else jax.tree.map(jnp.add, accum, micro_grads)
    wide_sums = jax.tree.map(
        lambda part: part.astype(jnp.float32),
        lax.psum_scatter(shortened(accum), "canvas", scatter_dimension=0, tiled=True),
    )
    shards = jax.tree.map(
        lambda part: part.astype(jnp.float32),
        lax.psum_scatter(shortened(wide_sums), "band", scatter_dimension=0, tiled=True),
    )
    bias_grad = lax.psum(bias_accum, ("canvas", "band"))
    return (
        jnp.stack(outputs),
        jnp.stack(input_grads),
        jnp.stack(time_grads),
        shards[5],
        shards[0],
        shards[1],
        bias_grad,
        shards[2],
        shards[3],
        shards[4],
    )


MESH = pl.DeviceIdType.MESH
BF, F32 = jnp.bfloat16, jnp.float32
EPS = 1e-5
TOK, HALF, D, QC, FH = 544, 272, 1152, 640, 2304
KEYS, KW, PADK = 784, 512, 80
SCALE = 72 ** -0.5
NEG = -1e30


def dot(a, b):
    return jnp.dot(a, b, preferred_element_type=F32)


def dot_nt(a, b):
    return lax.dot_general(a, b, (((1,), (1,)), ((), ())), preferred_element_type=F32)


def dot_tn(a, b):
    return lax.dot_general(a, b, (((0,), (0,)), ((), ())), preferred_element_type=F32)


def norm(v):
    center = v - jnp.mean(v, -1, keepdims=True)
    r = lax.rsqrt(jnp.mean(center * center, -1, keepdims=True) + EPS)
    return center * r, r


def norm_back(n, r, e):
    return r * (e - jnp.mean(e, -1, keepdims=True) - n * jnp.mean(e * n, -1, keepdims=True))


def place():
    c, b = lax.axis_index("canvas"), lax.axis_index("band")
    return c, b, b // 2, lax.rem(b, 2)


def greet(devs):
    bar = pltpu.get_barrier_semaphore()
    for dev in devs:
        pl.semaphore_signal(bar, 1, device_id=dev, device_id_type=MESH)
    pl.semaphore_wait(bar, len(devs))


def remote(src, dst, ss, rs, dev):
    return pltpu.make_async_remote_copy(src, dst, ss, rs, device_id=dev, device_id_type=MESH)


def head_window(h):
    ws = pl.multiple_of(jnp.minimum(80 * h // 128, 3) * 128, 128)
    lane = lax.broadcasted_iota(jnp.int32, (1, 256), 1) + ws - 80 * h
    hm = jnp.where((lane >= 0) & (lane < 80), 1.0, 0.0).astype(BF)
    return pl.ds(ws, 256), hm


def toeplitz(base, h):
    row = jnp.broadcast_to(base[pl.ds(h, 1)], (HALF, KW))
    return pltpu.roll(row, 0, 1, stride=1, stride_axis=0)


GSPEC = {"A": (144, 640, 640), "O": (80, 384, 384), "I0": (144, 384, 384), "I1": (144, 384, 384), "B0": (144, 384, 384), "B1": (144, 384, 384)}
GNAMES = list(GSPEC)


FIRST, STEP, SPARE = 4.0, 2.2, -4


class Gather:
    def __init__(self, own, full, s_sem, r_sem, y_sem, l_sem, pend):
        self.own, self.full, self.pend = dict(zip(GNAMES, own)), dict(zip(GNAMES, full)), pend
        self.s_sem, self.r_sem, self.y_sem, self.l_sem = s_sem, r_sem, y_sem, l_sem
        self.c, self.b, self.y, _ = place()
        self.z, self.x = self.c // 2, lax.rem(self.c, 2)
        z = self.z
        self.zp = [jnp.where(z == 0, t[0], jnp.where(z == 1, t[1], jnp.where(z == 2, t[2], t[3]))) for t in ((1, 0, 3, 2), (2, 2, 1, 1), (3, 3, 0, 0))]
        self.xdev, self.ydev = {"canvas": self.c + 1 - 2 * self.x}, {"band": self.b + 2 - 4 * self.y}
        self.count = dict.fromkeys(GNAMES, 0)

    def part(self, name, src, plane, side):
        rows, wide, mid = GSPEC[name]
        at = pl.ds(pl.multiple_of(src * rows, 16), rows)
        if plane:
            return at, pl.ds(pl.multiple_of(wide * side, 128), wide + mid)
        return at, pl.ds(pl.multiple_of((wide + mid) * side, 128), wide)

    def send(self, name, src, dev, plane, first=False, when=None):
        n = GNAMES.index(name)
        at, cols = self.part(name, src, plane, self.y)
        held = self.full[name].at[at, cols] if self.own[name] is None or not first else self.own[name].at[:, cols]
        cp = remote(held, self.full[name].at[at, cols],
                    self.s_sem.at[n, self.count[name]], (self.r_sem if plane else self.y_sem).at[n, src], dev)
        self.count[name] += 1
        if when is None:
            cp.start()
            self.pend.append(cp.wait_send)
        else:
            pl.when(when)(cp.start)
            self.pend.append(lambda: pl.when(when)(cp.wait_send))

    def own_sends(self, name):
        rows = GSPEC[name][0]
        for up in (1, -1):
            to = self.z + up
            self.send(name, self.c, {"canvas": jnp.clip(to, 0, 3) * 2 + self.x}, True, True, (to >= 0) & (to <= 3))
        self.send(name, self.c, self.xdev, True, True)
        if self.own[name] is not None:
            pltpu.make_async_copy(self.own[name], self.full[name].at[pl.ds(pl.multiple_of(self.c * rows, 16), rows)],
                                  self.l_sem.at[GNAMES.index(name)]).start()

    def wait(self, name, src, plane):
        at, cols = self.part(name, src, plane, self.y if plane else 1 - self.y)
        view = self.full[name].at[at, cols]
        pltpu.make_async_copy(view, view, (self.r_sem if plane else self.y_sem).at[GNAMES.index(name), src]).wait()

    def from_z(self, name, i):
        src = self.zp[i] * 2 + self.x
        self.wait(name, src, True)
        to = jnp.where(self.zp[i] < self.z, self.z + 1, self.z - 1)
        self.send(name, src, {"canvas": jnp.clip(to, 0, 3) * 2 + self.x}, True, False, (to >= 0) & (to <= 3))
        self.send(name, src, self.xdev, True)
        self.send(name, src, self.ydev, False)

    def from_x(self, name, i):
        src = (self.z if i == 0 else self.zp[i - 1]) * 2 + 1 - self.x
        self.wait(name, src, True)
        self.send(name, src, self.ydev, False)

    def complete(self, name):
        rows = GSPEC[name][0]
        for d in range(1, 8):
            self.wait(name, lax.rem(self.c + d, 8), False)
        if self.own[name] is not None:
            pltpu.make_async_copy(self.own[name], self.full[name].at[pl.ds(pl.multiple_of(self.c * rows, 16), rows)],
                                  self.l_sem.at[GNAMES.index(name)]).wait()

    def events(self, name):
        return [partial(self.from_z, name, 0), partial(self.from_x, name, 0), partial(self.from_z, name, 1), partial(self.from_x, name, 1),
                partial(self.from_z, name, 2), partial(self.from_x, name, 2), partial(self.from_x, name, 3)]


def gather_forward_kernel(attn_in, time_in, mlp_in, O, mlp_out, lat_in, cot_in, gains, te, seg_row, seg_col, base,
                          xn_o, q_o, kb_o, vb_o, lse_o, o_o, hres_o, hn_o, g_o, gp_o, df_o, gb0_o, gb1_o,
                          WA_o, WO_o, WI0_o, WI1_o, WB0_o, WB1_o, te_o, mask_o, onehot_o, ti,
                          WA, WO, WI0, WI1, WB0, WB1, xn, q, kb, vb, lse, o, hres, hn, g, gp, df, gb0, gb1, te_in, seg_in, col_in, onehot,
                          tp_send, tp_recv, tmix, mask, toep, of, x_send, x_recv, lat, cot,
                          s_sem, r_sem, y_sem, l_sem, es, er, gs, gr, cs, cr,
                          xs, xr, ts, tr, ks, kr, as_, ar, hs, hr, fs, fr, ls, outs):
    blocks = [(attn_in, 0), (attn_in, 1), (attn_in, 2), (time_in, 0), (time_in, 1)] + [(mlp_in, j) for j in range(4)]
    spots = [g.at[144 * (i // 2):144 * (i // 2) + 144, D * (i % 2):D * (i % 2) + D] for i in range(9)]
    loads = [pltpu.make_async_copy(lat_in, lat, ls.at[0]), pltpu.make_async_copy(cot_in, cot, ls.at[1])]
    loads += [pltpu.make_async_copy(src.at[:, D * j:D * j + D], spots[i], ls.at[2 + i]) for i, (src, j) in enumerate(blocks)]
    for cp in loads:
        cp.start()
    c, b, y, k = place()
    sib, ynb = {"band": b + 1 - 2 * k}, {"band": b + 2 - 4 * y}
    peers = [lax.rem(c + d, 8) for d in range(1, 8)]
    pend, saves = [], []

    def go(src, dst, ss, rs, dev):
        cp = remote(src, dst, ss, rs, dev)
        cp.start()
        pend.append(cp.wait_send)

    def arrive(view, sem):
        pltpu.make_async_copy(view, view, sem).wait()

    def save(src, dst):
        cp = pltpu.make_async_copy(src, dst, outs.at[len(saves)])
        cp.start()
        saves.append(cp)

    shares = [mlp_out.at[pl.ds(pl.multiple_of(288 * k + 144 * i, 16), 144)] for i in range(2)]
    gat = Gather((None, O, None, None, *shares), (WA, WO, WI0, WI1, WB0, WB1), s_sem, r_sem, y_sem, l_sem, pend)
    queue, ends = [], {}
    for name, nxt in (("A", "I0"), ("O", "I1"), ("I0", "B0"), ("I1", "B1"), ("B0", None), ("B1", None)):
        steps = gat.events(name)
        if nxt:
            steps.insert(1, partial(gat.own_sends, nxt))
        queue += steps
        ends[name] = len(queue)

    total, clock = len(queue), [0.0]

    def tick(us):
        clock[0] += us
        while queue and FIRST + STEP * (total - len(queue)) <= clock[0]:
            queue.pop(0)()

    def complete(name):
        left = total - ends[name]
        while len(queue) > max(left + SPARE, 0):
            queue.pop(0)()
        gat.complete(name)
        clock[0] = max(clock[0], FIRST + STEP * (total - left))

    greet([{"band": lax.rem(b + d, 4)} for d in (1, 2, 3)] + [{"canvas": p} for p in peers])
    for i, p in enumerate(peers):
        go(te.at[p], te_in.at[c], es.at[i], er.at[6 - i], {"canvas": p})
    te_in[c] = te[c]
    for i in range(3):
        go(seg_row, seg_in.at[b], gs.at[i], gr.at[2 - i], {"band": lax.rem(b + i + 1, 4)})
    seg_in[b] = seg_row[...]
    go(seg_col, col_in.at[k], cs.at[0], cr.at[0], sib)
    col_in[k] = seg_col[...]
    mine_rows = pl.ds(pl.multiple_of(144 * c, 16), 144)

    def pick_matrix(source, wide):
        gb0[:, 0:wide] = jnp.where(lax.broadcasted_iota(jnp.int32, (D, wide), 0) == source, 1.0, 0.0).astype(BF)

    lane = lax.broadcasted_iota(jnp.int32, (1, QC), 1).astype(F32)
    place_h = jnp.floor((lane + 0.5) * (1.0 / 80))
    inside = lane - 80 * place_h
    pick_matrix(jnp.where(inside < 71.5, 144 * place_h + inside + 72 * k.astype(F32), -1.0).astype(jnp.int32), QC)
    for i in range(3):
        loads[2 + i].wait()
        WA[mine_rows, QC * i:QC * i + QC] = dot(spots[i][...], gb0[:, 0:QC]).astype(BF)
    gat.own_sends("A")
    gat.own_sends("O")
    for i in range(2):
        loads[5 + i].wait()
        ti[:, QC * i:QC * i + QC] = dot(spots[3 + i][...], gb0[:, 0:QC]).astype(BF)

    def pick_hidden(s, W):
        for j in range(4):
            n = lax.broadcasted_iota(jnp.int32, (1, 384), 1).astype(F32) + 256 * j
            cc = jnp.floor((n + 0.5) * (1.0 / 144))
            fits = (cc > 2 * j - 0.5) & (cc < 2 * j + 1.5)
            pick_matrix(jnp.where(fits, 576 * (cc - 2 * j) + (n - 144 * cc) + 288 * k.astype(F32) + 144 * s, -1.0).astype(jnp.int32), 384)
            part = dot(spots[5 + j][...], gb0[:, 0:384]).astype(BF)
            if j:
                W[mine_rows, 256 * j:256 * j + 128] += part[:, 0:128]
                W[mine_rows, 256 * j + 128:256 * j + 384] = part[:, 128:]
            else:
                W[mine_rows, 0:384] = part

    loads[0].wait()
    mine = pl.ds(pl.multiple_of(HALF * k, 16), HALF)
    other = pl.ds(pl.multiple_of(HALF * (1 - k), 16), HALF)
    for m in range(2):
        n, _ = norm(lat[m].astype(F32))
        xn[m, mine] = (n * gains[0:1]).astype(BF)
        go(xn.at[m, mine], xn.at[m, mine], xs.at[m], xr.at[m], sib)
        if m == 0:
            for i in range(7):
                arrive(te_in.at[lax.rem(c + i + 1, 8)], er.at[i])
            for p in range(8):
                tp_send[16 * p:16 * p + 16] = dot(te_in[p], ti[...]).astype(BF)
            for i, p in enumerate(peers):
                go(tp_send.at[pl.ds(pl.multiple_of(16 * p, 16), 16)], tp_recv.at[6 - i], ts.at[i], tr.at[6 - i], {"canvas": p})
    save(te_in, te_o)
    for i in range(4):
        loads[7 + i].wait()
    pick_hidden(0, WI0)
    arrive(col_in.at[1 - k], cr.at[0])
    for i in range(3):
        arrive(seg_in.at[lax.rem(b + i + 1, 4)], gr.at[i])
    slot = lax.rem(lax.broadcasted_iota(jnp.int32, (1, 32), 1), 16)
    lane = lax.broadcasted_iota(jnp.int32, (1, KW), 1)

    def column(t):
        return t - 34 * jnp.floor((t + 0.5) * (1.0 / 34))

    colq = column(lax.broadcasted_iota(jnp.int32, (HALF, 1), 0).astype(F32))
    near = jnp.abs(colq - column(lax.broadcasted_iota(jnp.int32, (1, KW), 1).astype(F32) + 22)) < 2.5
    for j in range(2):
        at = 2 * y + j
        before, here, after = seg_in[jnp.maximum(at - 1, 0)], seg_in[at], seg_in[jnp.minimum(at + 1, 3)]
        before = pltpu.roll(jnp.where(at > 0, before, 0.0), KW - HALF, 1)
        after = pltpu.roll(jnp.where(at < 3, after, 0.0), HALF, 1)
        keys = jnp.where(lane < 80, before, jnp.where(lane < 352, here, jnp.where(lane < 432, after, 0.0)))
        for m in range(2):
            code = col_in[j, m, :, 0:1]
            mask[m, j] = jnp.where((code == keys[m:m + 1]) & near, 0.0, NEG).astype(BF)
            hit = (code.astype(jnp.int32) + (5 * m - 2) == slot) & (code >= 1.5)
            onehot[m, HALF * j:HALF * j + HALF] = jnp.where(hit, 1.0, 0.0).astype(BF)
    loads[1].wait()
    for m in range(2):
        filled = jnp.where(col_in[k, m, :, 0:1] >= 1.5, 1.0, 0.0)
        rows = pl.ds(pl.multiple_of(TOK * m + HALF * k, 16), HALF)
        df[rows] = (cot[m].astype(F32) * filled).astype(BF)
        go(df.at[rows], df.at[rows], fs.at[m], fr.at[m], sib)
    save(mask, mask_o)
    save(onehot, onehot_o)
    tick(13.0)
    for i in range(7):
        arrive(tp_recv.at[i], tr.at[i])
    tproj = tp_send[pl.ds(pl.multiple_of(16 * c, 16), 16)].astype(F32)
    for i in range(7):
        tproj = tproj + tp_recv[i].astype(F32)
    hi = tproj.astype(BF)
    tmix[0:16] = hi
    tmix[16:32] = (tproj - hi.astype(F32)).astype(BF)
    dead = pl.ds(pl.multiple_of(y * 624, 16), 80)
    for m in range(2):
        for ref in (kb, vb):
            ref[m, dead] = jnp.zeros((80, QC), BF)
            ref[m, 704:784] = jnp.zeros((80, QC), BF)
    of[...] = jnp.zeros_like(of)
    lse[...] = jnp.zeros_like(lse)
    pick_hidden(1, WI1)
    complete("A")
    save(WA, WA_o)

    edge = pl.ds(pl.multiple_of(544 - 464 * y, 16), 80)
    land = pl.ds(pl.multiple_of(624 * y, 16), 80)
    land_here = pl.ds(pl.multiple_of(624 * (1 - y), 16), 80)
    for m in range(2):
        arrive(xn.at[m, other], xr.at[m])
        x = xn[m]
        kb[m, 80:624] = dot(x, WA[:, QC:2 * QC]).astype(BF)
        tick(1.2)
        vb[m, 80:624] = (dot(x, WA[:, 2 * QC:]) + dot(onehot[m], tmix[:, QC:])).astype(BF)
        for i, ref in enumerate((kb, vb)):
            go(ref.at[m, edge], ref.at[m, land], ks.at[m, i], kr.at[m, i], ynb)
        q[m] = (dot(x, WA[:, :QC]) + dot(onehot[m], tmix[:, :QC])).astype(BF)
        tick(2.5)
    save(xn, xn_o)
    save(q, q_o)
    for m in range(2):
        for i, ref in enumerate((kb, vb)):
            arrive(ref.at[m, land_here], kr.at[m, i])
    save(kb, kb_o)
    save(vb, vb_o)

    def head(h, _):
        win, hm = head_window(h)
        toep[...] = toeplitz(base, h)
        lane_h = lax.broadcasted_iota(jnp.int32, (1, 128), 1) == h

        def tile(t, _):
            m, j = t // 2, lax.rem(t, 2)
            rows = pl.ds(pl.multiple_of(HALF * j, 16), HALF)
            krows = pl.ds(pl.multiple_of(HALF * j, 16), KW)
            s = dot_nt(q[m, rows, win] * hm, kb[m, krows, win])
            s = s * SCALE + (toep[...] + mask[m, j])
            peak = jnp.max(s, -1, keepdims=True)
            e = jnp.exp(s - peak)
            total = jnp.sum(e, -1, keepdims=True)
            p = (e * (1.0 / total)).astype(BF)
            of[m, rows, win] += dot(p, vb[m, krows, win] * hm)
            lse[m, rows] = jnp.where(lane_h, peak + jnp.log(total), lse[m, rows])
            return 0

        return lax.fori_loop(0, 4, tile, 0)

    for n in range(8):
        lax.fori_loop(n, n + 1, head, 0)
        tick(3.1)
    save(lse, lse_o)
    for m in range(2):
        o[m] = of[m].astype(BF)
    save(o, o_o)
    complete("O")
    save(WO, WO_o)

    for m in range(2):
        x_send[m] = dot(o[m, other], WO[...]).astype(BF)
        go(x_send.at[m], x_recv.at[m], as_.at[m], ar.at[m], sib)
    for m in range(2):
        hres[m] = lat[m].astype(F32) + dot(o[m, mine], WO[...])
    tick(4.0)
    for m in range(2):
        arrive(x_recv.at[m], ar.at[m])
        hv = hres[m] + x_recv[m].astype(F32)
        hres[m] = hv
        n, _ = norm(hv)
        hn[m, mine] = (n * gains[1:2]).astype(BF)
        go(hn.at[m, mine], hn.at[m, mine], hs.at[m], hr.at[m], sib)
        tick(2.5)
    save(hres, hres_o)
    for m in range(2):
        arrive(hn.at[m, other], hr.at[m])
    save(hn, hn_o)
    for s, W in enumerate((WI0, WI1)):
        complete("I0" if s == 0 else "I1")
        save(W, (WI0_o, WI1_o)[s])
        for m in range(2):
            def up(i, _):
                cols = pl.ds(pl.multiple_of(i * 384, 128), 384)
                put = pl.ds(pl.multiple_of(i * 384 + D * s, 128), 384)
                u = dot(hn[m], W[:, cols])
                phi = 0.5 + 0.5 * lax.erf(u * (0.5 ** 0.5))
                g[pl.ds(TOK * m, TOK), put] = (u * phi).astype(BF)
                gp[pl.ds(TOK * m, TOK), put] = (phi + u * (jnp.exp(-0.5 * u * u) * 0.3989422804014327)).astype(BF)
                return 0

            lax.fori_loop(0, 3, up, 0)
            tick(3.3)
    save(g, g_o)
    save(gp, gp_o)
    for m in range(2):
        rows = pl.ds(pl.multiple_of(TOK * m + HALF * (1 - k), 16), HALF)
        arrive(df.at[rows], fr.at[m])
    save(df, df_o)
    for s, grad in enumerate((gb0, gb1)):
        for i in range(3):
            cols = pl.ds(384 * i, 384)
            fill_part(grad, g, df, cols, D * s, cols)
            tick(1.3)
        save(grad, (gb0_o, gb1_o)[s])
    for s, W in enumerate((WB0, WB1)):
        complete("B0" if s == 0 else "B1")
        save(W, (WB0_o, WB1_o)[s])
    for cp in saves:
        cp.wait()
    for wait in pend:
        wait()


def gather_forward(p, cot):
    S = jax.ShapeDtypeStruct
    dma = pltpu.SemaphoreType.DMA
    V, anyspace = pl.BlockSpec(memory_space=pltpu.VMEM), pl.BlockSpec(memory_space=pl.ANY)
    weights = [(D, 3 * QC), (QC, D), (D, D), (D, D), (D, D), (D, D)]
    kept = [((2, TOK, D), BF), ((2, TOK, QC), BF), ((2, KEYS, QC), BF), ((2, KEYS, QC), BF), ((2, TOK, 128), F32), ((2, TOK, QC), BF),
            ((2, HALF, D), F32), ((2, TOK, D), BF), ((2 * TOK, FH), BF), ((2 * TOK, FH), BF), ((2 * TOK, D), BF), ((D, D), BF), ((D, D), BF)]
    return pl.pallas_call(
        gather_forward_kernel,
        out_shape=[S(s, t) for s, t in kept] + [S(s, BF) for s in weights]
        + [S((8, 16, 144), BF), S((2, 2, HALF, KW), BF), S((2, TOK, 32), BF), S((144, 2 * QC), BF)],
        in_specs=[anyspace] * 7 + [V] * 5, out_specs=[anyspace] * 22 + [V],
        scratch_shapes=[pltpu.VMEM(s, BF) for s in weights] + [pltpu.VMEM(s, t) for s, t in kept]
        + [pltpu.VMEM((8, 16, 144), BF), pltpu.VMEM((4, 8, KW), F32), pltpu.VMEM((2, 2, HALF, 128), F32), pltpu.VMEM((2, TOK, 32), BF),
           pltpu.VMEM((128, 2 * QC), BF), pltpu.VMEM((7, 16, 2 * QC), BF), pltpu.VMEM((32, 2 * QC), BF), pltpu.VMEM((2, 2, HALF, KW), BF),
           pltpu.VMEM((HALF, KW), F32), pltpu.VMEM((2, TOK, QC), F32), pltpu.VMEM((2, HALF, D), BF), pltpu.VMEM((2, HALF, D), BF),
           pltpu.VMEM((2, HALF, D), BF), pltpu.VMEM((2, HALF, D), BF),
           dma((6, 16)), dma((6, 8)), dma((6, 8)), dma((6,)), dma((7,)), dma((7,)), dma((3,)), dma((3,)), dma((1,)), dma((1,)),
           dma((2,)), dma((2,)), dma((7,)), dma((7,)), dma((2, 2)), dma((2, 2)), dma((2,)), dma((2,)), dma((2,)), dma((2,)), dma((2,)), dma((2,)), dma((11,)), dma((22,))],
        compiler_params=pltpu.CompilerParams(collective_id=1, has_side_effects=True, vmem_limit_bytes=127 * 2 ** 19),
        name="gather_forward")(*p["raw"], p["lat"], cot, p["gains"], p["te"], p["seg_row"], p["seg_col"], p["base"])


def prologue(latents, segment_ids, time_embed, norm_gains, attn_in, time_in, rel_bias, out_proj, mlp_in, mlp_out, cotangent):
    c, b, y, k = place()

    def pick(v, axis):
        return lax.dynamic_index_in_dim(v, k, axis, keepdims=False)

    raw = (attn_in, time_in, mlp_in, jnp.pad(pick(out_proj.reshape(2, 72, D), 0), ((0, 8), (0, 0))), mlp_out)
    code = (segment_ids.reshape(2, HALF) + 2).astype(F32)
    seg_row = jnp.pad(code, ((0, 6), (80, KW - 80 - HALF)))
    seg_col = jnp.broadcast_to(code[..., None], (2, HALF, 128))
    te = jnp.pad(time_embed.reshape(10, D), ((0, 6), (0, 0))).reshape(16, 8, 144).transpose(1, 0, 2)
    bias = pick(rel_bias.reshape(25, 8, 2), 2)
    base = jnp.full((8, KW), NEG, F32)
    places = [80 + 34 * dr + dc for dr in range(-2, 3) for dc in range(-2, 3)]
    base = base.at[:, jnp.array(places)].set(bias.T)
    filled = (segment_ids.reshape(2, HALF, 1) >= 0).astype(F32)
    return dict(raw=raw, te=te, seg_row=seg_row, seg_col=seg_col, base=base, filled=filled, lat=latents.reshape(2, HALF, D), gains=norm_gains.T)


RSPEC = {"A": (144, 640, 640), "O": (80, 384, 384), "I0": (144, 384, 384), "I1": (144, 384, 384), "B0": (144, 384, 384), "B1": (144, 384, 384)}
KEEP = {"A": (36, 48, 4), "I0": (36, 48, 4), "I1": (36, 48, 4), "O": (36, 48, 2), "B0": (144, 144, 2), "B1": (144, 144, 2)}
ORDER = (1, 3, 2, 0)


def scatter_scratch(name):
    rows, wide, mid = RSPEC[name]
    slab = wide + mid
    dma = pltpu.SemaphoreType.DMA
    _, held, sources = KEEP[name]
    sends = {"A": 4, "I": 4, "O": 2, "B": 1}[name[0]]
    return [pltpu.VMEM((8 * rows, wide), BF), pltpu.VMEM((4 * rows, slab), BF), pltpu.VMEM((3 * rows, slab), BF),
            pltpu.VMEM((sends, held, slab), BF), pltpu.VMEM((sources, held, slab), BF),
            dma((4,)), dma((4,)), dma((8,)), dma((8,)), dma((3,)), dma((3,)), dma((4,)), dma((4,))]


N_SCATTER = 13


class Scatter:
    def __init__(self, name, grad, total, scratch, pend):
        self.name, self.grad, self.total, self.pend = name, grad, total, pend
        (self.yr, self.xr, self.zr, self.stage, self.fr, self.ys, self.yw, self.xs, self.xw, self.zs, self.zw, self.fs, self.fw) = scratch
        self.rows, self.wide, self.mid = RSPEC[name]
        self.c, self.b, self.y, self.k = place()
        self.z, self.x = self.c // 2, lax.rem(self.c, 2)
        y, w, l = self.y, self.wide, self.mid
        self.slab = pl.ds(pl.multiple_of(w * y, 128), w + l)
        self.mids = pl.ds(w, l)
        self.side = pl.ds(pl.multiple_of((w + l) * y, 128), w)
        self.away = pl.ds(pl.multiple_of((w + l) * (1 - y), 128), w)
        self.slab_mid = pl.ds(pl.multiple_of(w * (1 - y), 128), l)
        self.slab_side = pl.ds(pl.multiple_of(l * y, 128), w)
        self.xdev, self.ydev = {"canvas": self.c + 1 - 2 * self.x}, {"band": self.b + 2 - 4 * self.y}

    def at(self, group):
        return pl.ds(pl.multiple_of(group * self.rows, 16), self.rows)

    def pair(self, d):
        return pl.ds(pl.multiple_of(lax.rem(self.z + d, 4) * (2 * self.rows), 16), 2 * self.rows)

    def go(self, make):
        make().start()
        self.pend.append(make)

    def parts(self):
        return self.away, self.mids, self.side

    def group(self, d, x):
        return self.at(2 * lax.rem(self.z + d, 4) + x)

    def send_y(self):
        for d in ORDER:
            self.go(lambda d=d: remote(self.grad.at[self.pair(d), self.away], self.yr.at[self.pair(d)], self.ys.at[d], self.yw.at[d], self.ydev))

    def send_mid(self):
        for d in ORDER:
            self.go(lambda d=d: remote(self.grad.at[self.group(d, 1 - self.x), self.mids], self.xr.at[pl.ds(self.rows * d, self.rows), self.slab_mid],
                                       self.xs.at[d], self.xw.at[d], self.xdev))

    def side_x(self, d):
        rows2 = self.pair(d)
        pltpu.make_async_copy(self.yr.at[rows2], self.yr.at[rows2], self.yw.at[d]).wait()
        self.grad[rows2, self.side] += self.yr[rows2]
        self.go(lambda: remote(self.grad.at[self.group(d, 1 - self.x), self.side], self.xr.at[pl.ds(self.rows * d, self.rows), self.slab_side],
                               self.xs.at[4 + d], self.xw.at[4 + d], self.xdev))

    def sum_x(self, d):
        rows = pl.ds(self.rows * d, self.rows)
        for view, sem in ((self.xr.at[rows, self.slab_mid], d), (self.xr.at[rows, self.slab_side], 4 + d)):
            pltpu.make_async_copy(view, view, self.xw.at[sem]).wait()
        return self.grad[self.group(d, self.x), self.slab] + self.xr[rows]

    def send_z(self, d):
        self.grad[self.group(d, self.x), self.slab] = self.sum_x(d)
        self.go(lambda: remote(self.grad.at[self.group(d, self.x), self.slab], self.zr.at[pl.ds((3 - d) * self.rows, self.rows)], self.zs.at[d - 1],
                               self.zw.at[3 - d], {"canvas": 2 * lax.rem(self.z + d, 4) + self.x}))

    def dests(self):
        sources = KEEP[self.name][2]
        if self.name[0] == "B":
            return [(0, 2 * self.k + int(self.name[1]))]
        return [(i, 2 * self.k + i if sources == 2 else i) for i in range(sources)]

    def finish(self):
        acc = self.sum_x(0).astype(F32)
        for i in (2, 0, 1):
            rows = pl.ds(i * self.rows, self.rows)
            pltpu.make_async_copy(self.zr.at[rows], self.zr.at[rows], self.zw.at[i]).wait()
            acc = acc + self.zr[rows].astype(F32)
        n, held, sources = KEEP[self.name]
        slab = self.wide + self.mid
        if self.name[0] == "B":
            self.stage[0] = acc.astype(BF)
        else:
            self.total[0:self.rows, 0:slab] = acc
            for i in range(sources):
                self.stage[i, 0:n] = self.total[n * i:n * i + n, 0:slab].astype(BF)
                self.stage[i, n:held] = jnp.zeros((held - n, slab), BF)
        slot = self.b if sources == 4 else self.y
        for i, dest in self.dests():
            @pl.when(self.b == dest)
            def _():
                self.fr[slot] = self.stage[i]

            @pl.when(self.b != dest)
            def _():
                remote(self.stage.at[i], self.fr.at[slot], self.fs.at[i], self.fw.at[slot], {"band": dest}).start()

    def sent(self):
        for i, dest in self.dests():
            @pl.when(self.b != dest)
            def _():
                remote(self.stage.at[i], self.fr.at[0], self.fs.at[i], self.fw.at[0], {"band": dest}).wait_send()

    def collect(self, out):
        n, held, sources = KEEP[self.name]
        for i in range(sources):
            src = i if sources == 4 else 2 * i + self.y

            @pl.when(self.b != src)
            def _():
                pltpu.make_async_copy(self.fr.at[i], self.fr.at[i], self.fw.at[i]).wait()
        w, l = self.wide, self.mid
        for half in range(sources // 2):
            lo, hi = self.fr[half].astype(F32)[:n], self.fr[half + sources // 2].astype(F32)[:n]
            dst = out.at[half] if sources == 4 else out
            dst[:, 0:w] = lo[:, :w]
            dst[:, w:w + l] = lo[:, w:] + hi[:, :l]
            dst[:, w + l:] = hi[:, l:]


def everyone():
    c, b, y, k = place()
    return [{"band": lax.rem(b + d, 4)} for d in (1, 2, 3)] + [{"canvas": lax.rem(c + d, 8)} for d in range(1, 8)]


def fill_part(grad, left, right, cols, lefts, rights):
    def step(i, _):
        r = pl.multiple_of(i * 384, 128)
        grad[pl.ds(r, 384), cols] = dot_tn(left[:, pl.ds(r + lefts, 384)], right[:, rights]).astype(BF)
        return 0

    lax.fori_loop(0, grad.shape[0] // 384, step, 0)


def mlp_back_kernel(cot, filled, gains, WI0, WI1, WB0, WB1, hres, hn, g, gp, df_in, gb0, gb1,
                    out, dh, da, gain, out_b, grad_i0, grad_i1,
                    grad_b0, grad_b1, du, gi, x_send, x_recv, f_send, f_recv, dn, ds_, dr_, xs, xr, as_, ar, ls, gs, *scratch):
    c, b, y, k = place()
    sib = {"band": b + 1 - 2 * k}
    df = da
    loads = [pltpu.make_async_copy(src, dst, ls.at[i])
             for i, (src, dst) in enumerate(((gb0, grad_b0), (gb1, grad_b1), (df_in, df), (gp, du), (hres, dh)))]
    for cp in loads:
        cp.start()
    greet([{"band": lax.rem(b + d, 4)} for d in (1, 2, 3)] + [{"canvas": c + 1 - 2 * lax.rem(c, 2)}] + [{"canvas": lax.rem(c + d, 8)} for d in (2, 4, 6)])
    pend = []
    rs = [Scatter("B0", grad_b0, None, scratch[:N_SCATTER], pend), Scatter("B1", grad_b1, None, scratch[N_SCATTER:], pend)]
    rs[1].fr, rs[1].fw = rs[0].fr, rs[0].fw

    def half(m, which):
        return pl.ds(pl.multiple_of(TOK * m + HALF * which, 16), HALF)

    for s in range(2):
        loads[s].wait()
        rs[s].send_y()
        if s == 0:
            rs[s].send_mid()
    for cp in loads[2:]:
        cp.wait()
    for m in range(2):
        def down_other(i, _):
            cols = pl.ds(pl.multiple_of(i * 384, 128), 384)
            f_send[m, :, cols] = (dot(g[half(m, 1 - k), 0:D], WB0[:, cols]) + dot(g[half(m, 1 - k), D:], WB1[:, cols])).astype(BF)
            return 0

        lax.fori_loop(0, 3, down_other, 0)
        loads.append(remote(f_send.at[m], f_recv.at[m], ds_.at[m], dr_.at[m], sib))
        loads[-1].start()

        def down(i, _):
            cols = pl.ds(pl.multiple_of(i * 384, 128), 384)
            dn[m, :, cols] = dot(g[half(m, k), 0:D], WB0[:, cols]) + dot(g[half(m, k), D:], WB1[:, cols])
            return 0

        lax.fori_loop(0, 3, down, 0)

    def back_act(m, s):
        def step(i, _):
            r = pl.multiple_of(i * 384, 128)
            cols = pl.ds(pl.multiple_of(r + D * s, 128), 384)
            rows = pl.ds(TOK * m, TOK)
            du[rows, cols] = (dot_nt(df[rows], (WB0, WB1)[s][pl.ds(r, 384)]) * du[rows, cols].astype(F32)).astype(BF)
            return 0

        lax.fori_loop(0, 3, step, 0)

    rs[0].side_x(1)
    back_act(0, 0)
    rs[0].side_x(3)
    rs[0].send_z(1)
    for m in range(2):
        v = f_recv.at[m]
        pltpu.make_async_copy(v, v, dr_.at[m]).wait()
        out[m] = ((dh[m] + (dn[m] + v[...].astype(F32))) * filled[m]).astype(BF)
    back_act(1, 0)
    rs[0].side_x(2)
    rs[0].send_z(3)
    back_act(0, 1)
    rs[0].side_x(0)
    rs[1].send_mid()
    rs[0].send_z(2)
    back_act(1, 1)
    rs[1].side_x(1)
    saves = []
    for s in range(2):
        def step(i, _):
            r = pl.multiple_of(i * 384, 128)
            gi[s, pl.ds(r, 384)] = dot_tn(hn[:, pl.ds(r, 384)], du[:, D * s:D * s + D]).astype(BF)
            return 0

        lax.fori_loop(0, 3, step, 0)
        cp = pltpu.make_async_copy(gi.at[s], (grad_i0, grad_i1)[s], gs.at[s])
        cp.start()
        saves.append(cp)
        if s == 0:
            rs[1].side_x(3)
            rs[1].send_z(1)
            rs[0].finish()
        else:
            rs[1].side_x(2)
            rs[1].send_z(3)

    for m in range(2):
        def hid(i, _):
            r = pl.multiple_of(i * 384, 128)
            rows = pl.ds(r, 384)
            v = dot_nt(du[half(m, 1 - k), 0:D], WI0[rows]) + dot_nt(du[half(m, 1 - k), D:], WI1[rows])
            x_send[m, :, rows] = v.astype(BF)
            return 0

        lax.fori_loop(0, 3, hid, 0)
        cp = remote(x_send.at[m], x_recv.at[m], xs.at[m], xr.at[m], sib)
        cp.start()
        loads.append(cp)

        def hid_own(i, _):
            r = pl.multiple_of(i * 384, 128)
            rows = pl.ds(r, 384)
            dn[m, :, rows] = dot_nt(du[half(m, k), 0:D], WI0[rows]) + dot_nt(du[half(m, k), D:], WI1[rows])
            return 0

        lax.fori_loop(0, 3, hid_own, 0)
        if m == 0:
            rs[1].side_x(0)
            rs[1].send_z(2)
    gain_two = jnp.zeros((1, D), F32)
    for m in range(2):
        pltpu.make_async_copy(x_recv.at[m], x_recv.at[m], xr.at[m]).wait()
        grad = dn[m] + x_recv[m].astype(F32)
        n, r = norm(dh[m])
        gain_two = gain_two + jnp.sum(grad * n, 0, keepdims=True)
        v = cot[m].astype(F32) * filled[m] + norm_back(n, r, grad * gains[1:2])
        dh[m] = v
        da[half(m, k)] = v.astype(BF)
        cp = remote(da.at[half(m, k)], da.at[half(m, k)], as_.at[m], ar.at[m], sib)
        cp.start()
        loads.append(cp)
    gain[...] = jnp.broadcast_to(gain_two, (8, D))
    for m in range(2):
        v = da.at[half(m, 1 - k)]
        pltpu.make_async_copy(v, v, ar.at[m]).wait()
    rs[1].finish()
    rs[0].collect(out_b)
    rs[0].sent()
    rs[1].sent()
    for cp in saves:
        cp.wait()
    for cp in loads[5:]:
        cp.wait_send()
    for make in pend:
        make().wait_send()


def mlp_back(*args):
    S = jax.ShapeDtypeStruct
    dma = pltpu.SemaphoreType.DMA
    V, anyspace = pl.BlockSpec(memory_space=pltpu.VMEM), pl.BlockSpec(memory_space=pl.ANY)
    return pl.pallas_call(
        mlp_back_kernel,
        out_shape=[S((2, HALF, D), BF), S((2, HALF, D), F32), S((2 * TOK, D), BF), S((8, D), F32), S((144, D), F32), S((D, D), BF), S((D, D), BF)],
        in_specs=[V] * 7 + [anyspace, V, V] + [anyspace] * 4, out_specs=[V] * 5 + [anyspace] * 2,
        scratch_shapes=[pltpu.VMEM((D, D), BF), pltpu.VMEM((D, D), BF), pltpu.VMEM((2 * TOK, FH), BF), pltpu.VMEM((2, D, D), BF),
                        pltpu.VMEM((2, HALF, D), BF), pltpu.VMEM((2, HALF, D), BF), pltpu.VMEM((2, HALF, D), BF), pltpu.VMEM((2, HALF, D), BF),
                        pltpu.VMEM((2, HALF, D), F32)]
        + [dma((2,))] * 6 + [dma((5,)), dma((2,))] + scatter_scratch("B0") + scatter_scratch("B1"),
        compiler_params=pltpu.CompilerParams(collective_id=2, has_side_effects=True, vmem_limit_bytes=127 * 2 ** 19),
        name="mlp_back")(*args)


def attn_back_kernel(WA, WO, ti, gains, lat, xn, q, kb, vb, lse, o, da, dh, mask, base, onehot, gain_two, gi0, gi1,
                     dlat, dt_all, gt, small, out_o, out_a, out_i0, out_i1,
                     grad_o, grad_a, grad_i0, grad_i1, do, dqkv, rim, rim_in, tsum, tsum_in, gt_send, gt_in, x_send, x_recv, dbias, sm_send, sm_in, total,
                     ks, kr, ts, tr, ps, pr, us, ur, vs, vr, ls, xs, xr, ss, sr, bs, br, *scratch):
    c, b, y, k = place()
    sib, ynb = {"band": b + 1 - 2 * k}, {"band": b + 2 - 4 * y}
    peers = [lax.rem(c + d, 8) for d in range(1, 8)]
    pend, waits = [], iter(range(20))

    def load(src, dst):
        cp = pltpu.make_async_copy(src, dst, ls.at[next(waits)])
        cp.start()
        return cp

    loads_i = [load(gi0, grad_i0), load(gi1, grad_i1)]
    load_dh = load(dh, dlat)
    greet(everyone())
    n = N_SCATTER
    rs_o = Scatter("O", grad_o, total, scratch[:n], pend)
    rs_a = Scatter("A", grad_a, total, scratch[n:2 * n], pend)
    rs_i = [Scatter("I0", grad_i0, total, scratch[2 * n:3 * n], pend), Scatter("I1", grad_i1, total, scratch[3 * n:], pend)]

    def go(make):
        make().start()
        pend.append(make)

    def arrive(view, sem):
        pltpu.make_async_copy(view, view, sem).wait()

    slots = pl.ds(pl.multiple_of(16 * c, 16), 16)
    for s in range(2):
        loads_i[s].wait()
        rs_i[s].send_y()
        rs_i[s].send_mid()

    def first(o_v, da_v, wo_v):
        parts = [load(o, o_v), load(da, da_v), load(WO, wo_v)]
        for cp in parts:
            cp.wait()
        for i, cols in enumerate(rs_o.parts()):
            grad_o[:, cols] = dot_tn(o_v[...], da_v[:, cols]).astype(BF)
            if i == 0:
                rs_o.send_y()
            if i == 1:
                rs_o.send_mid()
        for m in range(2):
            do[m] = dot_nt(da_v[pl.ds(TOK * m, TOK)], wo_v[...]).astype(BF)

    pl.run_scoped(first, pltpu.VMEM((2 * TOK, QC), BF), pltpu.VMEM((2 * TOK, D), BF), pltpu.VMEM((QC, D), BF))

    def second(q_v, kb_v, vb_v, dqf, dkf, dvf, toep, dsum):
        parts = [load(q, q_v), load(kb, kb_v), load(vb, vb_v)]
        dqf[...] = jnp.zeros_like(dqf)
        dkf[...] = jnp.zeros_like(dkf)
        dvf[...] = jnp.zeros_like(dvf)
        for cp in parts:
            cp.wait()

        def head(h, _):
            win, hm = head_window(h)
            toep[...] = toeplitz(base, h)
            dsum[...] = jnp.zeros_like(dsum)
            lane_h = lax.broadcasted_iota(jnp.int32, (1, 128), 1) == h

            def tile(t, _):
                m, j = t // 2, lax.rem(t, 2)
                rows = pl.ds(pl.multiple_of(HALF * j, 16), HALF)
                krows = pl.ds(pl.multiple_of(HALF * j, 16), KW)
                qm, dm = q_v[m, rows, win] * hm, do[m, rows, win] * hm
                kw = kb_v[m, krows, win]
                level = jnp.sum(jnp.where(lane_h, lse[m, rows], 0.0), -1, keepdims=True)
                p = jnp.exp(dot_nt(qm, kw) * SCALE + (toep[...] + mask[m, j]) - level)
                dp = dot_nt(dm, vb_v[m, krows, win])
                delta = jnp.sum(p * dp, -1, keepdims=True)
                ds = (p * (dp - delta)).astype(BF)
                dsum[...] += ds.astype(F32)
                dqf[m, rows, win] += dot(ds, kw * hm)
                dkf[m, krows, win] += dot_tn(ds, qm)
                dvf[m, krows, win] += dot_tn(p.astype(BF), dm)
                return 0

            lax.fori_loop(0, 4, tile, 0)
            strip = dsum[0:8]
            for r in range(8, HALF, 8):
                strip = strip + pltpu.roll(dsum[r:r + 8], KW - r, 1)
            line = strip[0:1]
            for r in range(1, 8):
                line = line + pltpu.roll(strip, KW - r, 1)[r:r + 1]
            dbias[pl.ds(h, 1)] = line
            return 0

        for i in range(4):
            lax.fori_loop(2 * i, 2 * i + 2, head, 0)
            if i == 0:
                for d in (1, 3, 2):
                    rs_i[0].side_x(d)
            elif i == 1:
                rs_i[0].side_x(0)
                for d in (1, 3, 2):
                    rs_i[0].send_z(d)
                rs_i[1].side_x(1)
            elif i == 2:
                for d in (3, 2, 0):
                    rs_i[1].side_x(d)
                rs_i[1].send_z(1)
        away = pl.ds(pl.multiple_of(624 * (1 - y), 16), 80)
        edge = pl.ds(pl.multiple_of(544 - 464 * y, 16), 80)
        for m in range(2):
            rim[m, 0] = (dkf[m, away] * SCALE).astype(BF)
            rim[m, 1] = dvf[m, away].astype(BF)
            go(lambda m=m: remote(rim.at[m], rim_in.at[m], ks.at[m], kr.at[m], ynb))
        for m in range(2):
            tok = pl.ds(TOK * m, TOK)
            dqkv[tok, 0:QC] = (dqf[m] * SCALE).astype(BF)
        for d in ORDER:
            rs_o.side_x(d)
        rs_i[1].send_z(3)
        rs_i[1].send_z(2)
        for m in range(2):
            arrive(rim_in.at[m], kr.at[m])
            tok = pl.ds(TOK * m, TOK)
            dkf[m, edge] += rim_in[m, 0].astype(F32) * (1.0 / SCALE)
            dvf[m, edge] += rim_in[m, 1].astype(F32)
            dqkv[tok, QC:2 * QC] = (dkf[m, 80:624] * SCALE).astype(BF)
            dqkv[tok, 2 * QC:] = dvf[m, 80:624].astype(BF)

    pl.run_scoped(second, pltpu.VMEM((2, TOK, QC), BF), pltpu.VMEM((2, KEYS, QC), BF), pltpu.VMEM((2, KEYS, QC), BF),
                  pltpu.VMEM((2, TOK, QC), F32), pltpu.VMEM((2, KEYS, QC), F32), pltpu.VMEM((2, KEYS, QC), F32),
                  pltpu.VMEM((HALF, KW), F32), pltpu.VMEM((HALF, KW), F32))

    def third(xn_v, wa_v, dn):
        loads = [load(xn, xn_v), load(WA, wa_v)]
        tq = dot_tn(onehot[0], dqkv[0:TOK, 0:QC]) + dot_tn(onehot[1], dqkv[TOK:, 0:QC])
        tv = dot_tn(onehot[0], dqkv[0:TOK, 2 * QC:]) + dot_tn(onehot[1], dqkv[TOK:, 2 * QC:])
        tsum[:, 0:QC] = tq[0:16].astype(BF)
        tsum[:, QC:] = tv[0:16].astype(BF)
        go(lambda: remote(tsum, tsum_in, ts.at[0], tr.at[0], ynb))
        loads[0].wait()
        for i, cols in enumerate(rs_a.parts()):
            fill_part(grad_a, xn_v, dqkv, cols, 0, cols)
            if i == 0:
                rs_a.send_y()
                arrive(tsum_in, tr.at[0])
                dt_all[k, slots] = (tsum[...].astype(F32) + tsum_in[...].astype(F32)).astype(BF)
                for n, p in enumerate(peers):
                    go(lambda n=n, p=p: remote(dt_all.at[k, slots], dt_all.at[k, slots], ps.at[n], pr.at[6 - n], {"canvas": p}))
            if i == 1:
                rs_a.send_mid()
        for d in (1, 3, 2):
            rs_o.send_z(d)
        rs_i[0].finish()
        loads[1].wait()
        for m in range(2):
            rows = pl.ds(pl.multiple_of(TOK * m + HALF * (1 - k), 16), HALF)
            rows_own = pl.ds(pl.multiple_of(TOK * m + HALF * k, 16), HALF)

            def back(n, _):
                cols = pl.ds(pl.multiple_of(n * 384, 128), 384)
                x_send[m, :, cols] = dot_nt(dqkv[rows], wa_v[cols]).astype(BF)
                return 0

            lax.fori_loop(0, 3, back, 0)
            go(lambda m=m: remote(x_send.at[m], x_recv.at[m], xs.at[m], xr.at[m], sib))

            def back_own(n, _):
                cols = pl.ds(pl.multiple_of(n * 384, 128), 384)
                dn[m, :, cols] = dot_nt(dqkv[rows_own], wa_v[cols])
                return 0

            lax.fori_loop(0, 3, back_own, 0)
        rs_i[1].finish()
        rs_a.side_x(1)
        for n in range(7):
            arrive(dt_all.at[k, pl.ds(pl.multiple_of(16 * lax.rem(c + n + 1, 8), 16), 16)], pr.at[n])
        go(lambda: remote(dt_all.at[k], dt_all.at[k], us.at[0], ur.at[0], sib))
        gt_send[...] = dot_nt(dt_all[k], ti[...])
        go(lambda: remote(gt_send, gt_in, us.at[1], ur.at[1], sib))
        rs_a.side_x(3)
        rs_a.send_z(1)
        load_dh.wait()
        gain_one = jnp.zeros((1, D), F32)
        for m in range(2):
            arrive(x_recv.at[m], xr.at[m])
            grad = dn[m] + x_recv[m].astype(F32)
            n, r = norm(lat[m].astype(F32))
            gain_one = gain_one + jnp.sum(grad * n, 0, keepdims=True)
            dlat[m] = dlat[m] + norm_back(n, r, grad * gains[0:1])
            if m == 0:
                rs_a.side_x(2)
                rs_a.send_z(3)
        first_row = lax.broadcasted_iota(jnp.int32, (8, 1), 0) == 0
        both = jnp.where(first_row, jnp.broadcast_to(gain_one, (8, D)), gain_two[...])
        for p in range(8):
            sm_send[p, 0:8] = dbias[...]
            sm_send[p, 8:16] = (pltpu.roll(both, D - 144 * p, 1) if p else both)[:, 0:KW]

    pl.run_scoped(third, pltpu.VMEM((2 * TOK, D), BF), pltpu.VMEM((D, 3 * QC), BF), pltpu.VMEM((2, HALF, D), F32))
    for n, p in enumerate(peers):
        go(lambda n=n, p=p: remote(sm_send.at[p], sm_in.at[6 - n], ss.at[n], sr.at[6 - n], {"canvas": p}))
    rs_o.finish()
    arrive(gt_in, ur.at[1])
    gt_in[...] = gt_in[...] + gt_send[...]
    for n, p in enumerate(peers):
        go(lambda n=n, p=p: remote(gt_in.at[pl.ds(pl.multiple_of(16 * p, 16), 16)], gt.at[c], vs.at[n], vr.at[6 - n], {"canvas": p}))
    gt[c] = gt_in[pl.ds(pl.multiple_of(16 * c, 16), 16)]
    rs_a.side_x(0)
    rs_a.send_z(2)
    acc = sm_send[c]
    for n in range(7):
        arrive(sm_in.at[n], sr.at[n])
        acc = acc + sm_in[n]
    small[b] = acc
    for i in range(3):
        go(lambda i=i: remote(small.at[b], small.at[b], bs.at[i], br.at[2 - i], {"band": lax.rem(b + i + 1, 4)}))
    rs_i[0].collect(out_i0)
    rs_i[1].collect(out_i1)
    rs_o.collect(out_o)
    for n in range(7):
        arrive(gt.at[lax.rem(c + n + 1, 8)], vr.at[n])
    arrive(dt_all.at[1 - k], ur.at[0])
    for i in range(3):
        arrive(small.at[lax.rem(b + i + 1, 4)], br.at[i])
    rs_a.finish()
    rs_a.collect(out_a)
    for rs in (rs_o, rs_a, *rs_i):
        rs.sent()
    for make in pend:
        make().wait_send()


def attn_back(*args):
    S = jax.ShapeDtypeStruct
    dma = pltpu.SemaphoreType.DMA
    V, anyspace = pl.BlockSpec(memory_space=pltpu.VMEM), pl.BlockSpec(memory_space=pl.ANY)
    return pl.pallas_call(
        attn_back_kernel,
        out_shape=[S((2, HALF, D), F32), S((2, 128, 2 * QC), BF), S((8, 16, 144), F32), S((4, 16, KW), F32),
                   S((36, D), F32), S((2, 36, 3 * QC), F32), S((2, 36, D), F32), S((2, 36, D), F32)],
        in_specs=[anyspace, anyspace, V, V, V] + [anyspace] * 4 + [V] + [anyspace] * 3 + [V] * 4 + [anyspace] * 2, out_specs=[V] * 8,
        scratch_shapes=[pltpu.VMEM((QC, D), BF), pltpu.VMEM((D, 3 * QC), BF), pltpu.VMEM((D, D), BF), pltpu.VMEM((D, D), BF), pltpu.VMEM((2, TOK, QC), BF),
                        pltpu.VMEM((2 * TOK, 3 * QC), BF),
                        pltpu.VMEM((2, 2, 80, QC), BF), pltpu.VMEM((2, 2, 80, QC), BF), pltpu.VMEM((16, 2 * QC), BF), pltpu.VMEM((16, 2 * QC), BF),
                        pltpu.VMEM((128, 144), F32), pltpu.VMEM((128, 144), F32),
                        pltpu.VMEM((2, HALF, D), BF), pltpu.VMEM((2, HALF, D), BF), pltpu.VMEM((8, KW), F32), pltpu.VMEM((8, 16, KW), F32), pltpu.VMEM((7, 16, KW), F32),
                        pltpu.VMEM((144, 1280), F32),
                        dma((2,)), dma((2,)), dma((1,)), dma((1,)), dma((7,)), dma((7,)), dma((2,)), dma((2,)), dma((7,)), dma((7,)), dma((20,)), dma((2,)), dma((2,)),
                        dma((7,)), dma((7,)), dma((3,)), dma((3,))]
        + scatter_scratch("O") + scatter_scratch("A") + scatter_scratch("I0") + scatter_scratch("I1"),
        compiler_params=pltpu.CompilerParams(collective_id=3, has_side_effects=True, vmem_limit_bytes=127 * 2 ** 19),
        name="attn_back")(*args)


def local_fast(*args):
    p = prologue(*args)
    c, b, y, k = place()
    cot = args[10].reshape(2, HALF, D)
    (xn, q, kb, vb, lse, o, hres, hn, g, gp, df, gb0, gb1, WA, WO, WI0, WI1, WB0, WB1, te_all, mask, onehot, ti) = gather_forward(p, cot)
    out, dh, da, gain_two, out_b, gi0, gi1 = mlp_back(cot, p["filled"], p["gains"], WI0, WI1, WB0, WB1, hres, hn.reshape(2 * TOK, D), g, gp, df, gb0, gb1)
    dlat, dt_all, gt, small, out_o, out_a, out_i0, out_i1 = attn_back(
        WA, WO, ti, p["gains"], p["lat"], xn.reshape(2 * TOK, D), q, kb, vb, lse, o.reshape(2 * TOK, QC), da, dh,
        mask, p["base"], onehot, gain_two, gi0, gi1)
    shape = (2, 1, 8, 34, D)
    places = [80 + 34 * dr + dc for dr in range(-2, 3) for dc in range(-2, 3)]
    bias = small[0:2, 0:8] + small[2:4, 0:8]
    grad_bias = bias[:, :, jnp.array(places)].transpose(2, 1, 0).reshape(25, 16)
    mine = lax.dynamic_slice_in_dim(small[:, 8:10, 0:144].sum(0), 36 * b, 36, 1)
    grad_a = out_a.reshape(2, 36, 3, 8, 80)[..., :72].transpose(1, 2, 3, 0, 4).reshape(36, 3 * D)
    grad_i = jnp.stack([out_i0, out_i1]).reshape(2, 2, 36, 8, 144).transpose(2, 3, 1, 0, 4).reshape(36, 2 * FH)
    dt = dt_all.reshape(2, 128, 2, 8, 80)[..., :72].transpose(1, 2, 3, 0, 4).reshape(128, 2 * D)
    te_mine = lax.dynamic_slice_in_dim(te_all.reshape(128, 144), 36 * b, 36, 1)
    grad_time_in = dot_tn(te_mine, dt)
    grad_time = gt.transpose(1, 0, 2).reshape(16, D)[:10].reshape(2, 1, 5, D)
    return (out.reshape(shape), dlat.reshape(shape), grad_time, mine.T, grad_a, grad_time_in, grad_bias, out_o, grad_i, out_b)


def solution(mesh):
    return jax.shard_map(
        local_fast if mesh.shape["canvas"] == 8 and mesh.shape["band"] == 4 else local,
        mesh=mesh,
        in_specs=(
            P(None, "canvas", "band", None, None),
            P(None, "canvas", "band", None),
            P(None, "canvas", None, None),
            P(),
            P("canvas", None),
            P("canvas", None),
            P(),
            P("canvas", None),
            P("canvas", None),
            P("canvas", None),
            P(None, "canvas", "band", None, None),
        ),
        out_specs=(
            P(None, "canvas", "band", None, None),
            P(None, "canvas", "band", None, None),
            P(None, "canvas", None, None),
            P(("canvas", "band"), None),
            P(("canvas", "band"), None),
            P(("canvas", "band"), None),
            P(),
            P(("canvas", "band"), None),
            P(("canvas", "band"), None),
            P(("canvas", "band"), None),
        ),
        check_vma=False,
    )
```

```python
from functools import partial
import jax
import jax.numpy as jnp
from jax import lax
from jax.experimental import pallas as pl
from jax.experimental.pallas import tpu as pltpu

from jax.sharding import PartitionSpec as P

WIN = 5


EPSILON = 1e-05


def padded_2(shard, sides, width):
    for axis, dim in sides:
        devices, length = (lax.axis_size(axis), shard.shape[dim])
        up = [(i, (i + 1) % devices) for i in range(devices - 1)]
        down = [(j, i) for i, j in up]
        last = lax.slice_in_dim(shard, length - width, length, axis=dim)
        first = lax.slice_in_dim(shard, 0, width, axis=dim)
        before = lax.ppermute(last, axis, up)
        after = lax.ppermute(first, axis, down)
        shard = jnp.concatenate([before, shard, after], axis=dim)
    return shard


def shifted(shard, axis, by):
    devices = lax.axis_size(axis)
    pairs = [(i, i + by) for i in range(devices) if 0 <= i + by < devices]
    return lax.ppermute(shard, axis, pairs)


def shortened(shard):

    def short(part):
        return part.astype(jnp.bfloat16) if part.dtype == jnp.float32 else part

    return jax.tree.map(short, shard)


def normalize(value, gain):
    center = value - jnp.mean(value, -1, keepdims=True)
    scaled = lax.rsqrt(jnp.mean(center * center, -1, keepdims=True) + EPSILON)
    unit = center * scaled
    return (unit, scaled, unit * gain)


def normalize_back(unit, scaled, gain, grad_out):
    part = grad_out * gain
    return scaled * (
        part - jnp.mean(part, -1, keepdims=True) - unit * jnp.mean(part * unit, -1, keepdims=True)
    )


def rows_dot(left, right):
    return lax.dot_general(
        left, right, (((0,), (0,)), ((), ())), preferred_element_type=jnp.float32
    )


def back_dot(left, weight):
    return lax.dot_general(
        left, weight, (((1,), (1,)), ((), ())), preferred_element_type=jnp.float32
    )


def neighbour_stack(padded, band_rows, columns):
    pieces = [padded[:, i : i + band_rows, j : j + columns] for i in range(WIN) for j in range(WIN)]
    stacked = jnp.stack(pieces)
    return stacked.reshape((WIN * WIN, -1) + padded.shape[3:])


def spread_back(terms, canvases, band_rows, columns):
    reach = WIN // 2
    shaped = terms.reshape((WIN * WIN, canvases, band_rows, columns, terms.shape[-1]))
    summed = None
    for i in range(WIN):
        for j in range(WIN):
            placed = jnp.pad(
                shaped[i * WIN + j], ((0, 0), (i, 2 * reach - i), (j, 2 * reach - j), (0, 0))
            )
            summed = placed if summed is None else summed + placed
    return summed


def head_total(terms, head_sum):
    flat = terms.reshape(-1, terms.shape[-1])
    return jnp.dot(flat, head_sum, precision=lax.Precision.HIGHEST).reshape(
        terms.shape[:-1] + (head_sum.shape[1],)
    )


def head_widen(values, head_spread):
    flat = values.reshape(-1, values.shape[-1])
    return jnp.dot(flat, head_spread, preferred_element_type=jnp.bfloat16).reshape(
        values.shape[:-1] + (head_spread.shape[1],)
    )


def local(
    latents,
    segment_ids,
    time_embed,
    norm_gains,
    attn_in,
    time_in,
    rel_bias,
    out_proj,
    mlp_in,
    mlp_out,
    cotangent,
):
    micro_count, canvases, band_rows, columns, width = latents.shape
    slots = time_embed.shape[2]
    heads = rel_bias.shape[1]
    head_dim = width // heads
    reach = WIN // 2
    tokens = canvases * band_rows * columns
    score_scale = head_dim ** (-0.5)
    head_sum = (jnp.arange(width)[:, None] // head_dim == jnp.arange(heads)[None, :]).astype(
        jnp.float32
    )
    head_spread = head_sum.T.astype(jnp.bfloat16)
    owned = (attn_in, time_in, out_proj, mlp_in, mlp_out)
    seg_code = segment_ids + 2
    seg_rims = padded_2(seg_code, (("band", 2),), reach)
    seg_rims = jnp.pad(seg_rims, ((0, 0), (0, 0), (0, 0), (reach, reach)))
    band_share = 1.0 / lax.axis_size("band")
    outputs = []
    input_grads = []
    time_grads = []
    accum = None
    shards = None
    bias_accum = jnp.zeros(rel_bias.shape, jnp.float32)
    for batch_index in range(micro_count):
        full_weights = (
            lax.all_gather(owned[0], "canvas", axis=0, tiled=True),
            lax.all_gather(owned[1], "canvas", axis=0, tiled=True),
            lax.all_gather(owned[2], "canvas", axis=0, tiled=True),
            lax.all_gather(owned[3], "canvas", axis=0, tiled=True),
            lax.all_gather(owned[4], "canvas", axis=0, tiled=True),
        )
        w_attn, w_time, w_out, w_in, w_back = full_weights
        inputs = latents[batch_index].astype(jnp.float32).reshape(tokens, width)
        unit_one, scaled_one, normed_one = normalize(inputs, norm_gains[:, 0])
        normed = normed_one.astype(jnp.bfloat16)
        time_rows = time_embed[batch_index].reshape(canvases * slots, width)
        time_proj = jnp.dot(time_rows, w_time, preferred_element_type=jnp.float32).reshape(
            canvases, slots, 2 * width
        )
        seg_here = segment_ids[batch_index]
        member = (seg_here[..., None] == jnp.arange(slots)).astype(jnp.float32)
        token_time = jnp.einsum(
            "krcs,kse->krce", member, time_proj, precision=lax.Precision.HIGHEST
        ).reshape(tokens, 2 * width)
        qkv = jnp.dot(normed, w_attn, preferred_element_type=jnp.float32)
        query = (qkv[:, :width] + token_time[:, :width]).astype(jnp.bfloat16)
        keys = qkv[:, width : 2 * width].astype(jnp.bfloat16)
        values = (qkv[:, 2 * width :] + token_time[:, width:]).astype(jnp.bfloat16)
        paired = jnp.stack([keys, values]).reshape(2, canvases, band_rows, columns, width)
        paired = padded_2(paired, (("band", 2),), reach)
        paired = jnp.pad(paired, ((0, 0), (0, 0), (0, 0), (reach, reach), (0, 0)))
        key_win = neighbour_stack(paired[0], band_rows, columns)
        value_win = neighbour_stack(paired[1], band_rows, columns)
        seg_win = neighbour_stack(seg_rims[batch_index], band_rows, columns)
        allowed = (seg_win == seg_code[batch_index].reshape(1, tokens))[..., None]
        query_wide = query.astype(jnp.float32)
        raw = head_total(query_wide[None] * key_win.astype(jnp.float32), head_sum)
        logit_scores = raw * score_scale + rel_bias[:, None, :]
        masked = jnp.where(allowed, logit_scores, -1e30)
        peak = jnp.max(masked, 0)
        raised = jnp.where(allowed, jnp.exp(masked - peak), 0.0)
        probs_full = raised / jnp.sum(raised, 0)
        attention_probabilities = probs_full.astype(jnp.bfloat16)
        probs_wide = head_widen(attention_probabilities, head_spread)
        mixed_values = jnp.sum(probs_wide.astype(jnp.float32) * value_win.astype(jnp.float32), 0)
        attended = mixed_values.astype(jnp.bfloat16)
        branch = jnp.dot(attended, w_out, preferred_element_type=jnp.float32)
        resid = inputs + branch
        unit_two, scaled_two, normed_two = normalize(resid, norm_gains[:, 1])
        hidden_in = normed_two.astype(jnp.bfloat16)
        pre_act = jnp.dot(hidden_in, w_in, preferred_element_type=jnp.float32)
        activated = jax.nn.gelu(pre_act, approximate=False).astype(jnp.bfloat16)
        mlp_y = jnp.dot(activated, w_back, preferred_element_type=jnp.float32)
        filled = (seg_here >= 0).reshape(tokens, 1)
        outputs.append(
            jnp.where(filled, resid + mlp_y, 0.0)
            .astype(jnp.bfloat16)
            .reshape(canvases, band_rows, columns, width)
        )
        grad_y = cotangent[batch_index].reshape(tokens, width)
        grad_f = jnp.where(filled, grad_y, jnp.zeros_like(grad_y))
        grad_back = rows_dot(activated, grad_f)
        grad_act = back_dot(grad_f, w_back)
        gelu_out, gelu_pull = jax.vjp(partial(jax.nn.gelu, approximate=False), pre_act)
        grad_pre = gelu_pull(grad_act)[0].astype(jnp.bfloat16)
        grad_in = rows_dot(hidden_in, grad_pre)
        grad_hidden = back_dot(grad_pre, w_in)
        grad_resid = jnp.where(filled, grad_y.astype(jnp.float32), 0.0) + normalize_back(
            unit_two, scaled_two, norm_gains[:, 1], grad_hidden
        )
        gain_two = jnp.sum(grad_hidden * unit_two, 0)
        grad_branch = grad_resid.astype(jnp.bfloat16)
        grad_out = rows_dot(attended, grad_branch)
        grad_att = back_dot(grad_branch, w_out).astype(jnp.bfloat16)
        grad_att_wide = grad_att.astype(jnp.float32)
        grad_probs = head_total(grad_att_wide[None] * value_win.astype(jnp.float32), head_sum)
        centered = jnp.sum(probs_full * grad_probs, 0)
        grad_scores = (probs_full * (grad_probs - centered)).astype(jnp.bfloat16)
        bias_accum = bias_accum + jnp.sum(grad_scores.astype(jnp.float32), axis=1)
        scores_wide = head_widen(grad_scores, head_spread).astype(jnp.float32)
        grad_query = jnp.sum(scores_wide * key_win.astype(jnp.float32), 0) * score_scale
        key_summed = (
            spread_back(scores_wide * query_wide[None], canvases, band_rows, columns) * score_scale
        )
        value_summed = spread_back(
            probs_wide.astype(jnp.float32) * grad_att_wide[None], canvases, band_rows, columns
        )
        pair_grad = jnp.stack([key_summed, value_summed])[:, :, :, reach : reach + columns]
        upper_rim = pair_grad[:, :, :reach]
        lower_rim = pair_grad[:, :, band_rows + reach :]
        owned_rows = pair_grad[:, :, reach : reach + band_rows]
        from_below = shifted(upper_rim.astype(jnp.bfloat16), "band", -1).astype(upper_rim.dtype)
        from_above = shifted(lower_rim.astype(jnp.bfloat16), "band", 1).astype(lower_rim.dtype)
        owned_rows = owned_rows.at[:, :, band_rows - reach :].add(from_below)
        owned_rows = owned_rows.at[:, :, :reach].add(from_above)
        grad_keys = owned_rows[0].reshape(tokens, width).astype(jnp.bfloat16)
        grad_values = owned_rows[1].reshape(tokens, width).astype(jnp.bfloat16)
        grad_q_low = grad_query.astype(jnp.bfloat16)
        member_low = member.astype(jnp.bfloat16).reshape(canvases, band_rows * columns, slots)
        slot_query = jnp.einsum(
            "kns,knd->ksd",
            member_low,
            grad_q_low.reshape(canvases, band_rows * columns, width),
            preferred_element_type=jnp.float32,
        )
        slot_value = jnp.einsum(
            "kns,knd->ksd",
            member_low,
            grad_values.reshape(canvases, band_rows * columns, width),
            preferred_element_type=jnp.float32,
        )
        slot_part = jnp.concatenate([slot_query, slot_value], -1)
        slot_total = lax.psum(slot_part.astype(jnp.bfloat16), "band")
        slot_low = slot_total.reshape(canvases * slots, 2 * width)
        time_grads.append(back_dot(slot_low, w_time).reshape(canvases, slots, width))
        grad_time_in = rows_dot(time_rows, slot_low) * band_share
        grad_qkv = jnp.concatenate([grad_q_low, grad_keys, grad_values], -1)
        grad_attn = rows_dot(normed, grad_qkv)
        grad_normed = back_dot(grad_qkv, w_attn)
        grad_inputs = grad_resid + normalize_back(
            unit_one, scaled_one, norm_gains[:, 0], grad_normed
        )
        gain_one = jnp.sum(grad_normed * unit_one, 0)
        input_grads.append(grad_inputs.reshape(canvases, band_rows, columns, width))
        micro_grads = (
            grad_attn,
            grad_time_in,
            grad_out,
            grad_in,
            grad_back,
            jnp.stack([gain_one, gain_two], 1),
        )
        accum = micro_grads if accum is None else jax.tree.map(jnp.add, accum, micro_grads)
    wide_sums = jax.tree.map(
        lambda part: part.astype(jnp.float32),
        lax.psum_scatter(shortened(accum), "canvas", scatter_dimension=0, tiled=True),
    )
    shards = jax.tree.map(
        lambda part: part.astype(jnp.float32),
        lax.psum_scatter(shortened(wide_sums), "band", scatter_dimension=0, tiled=True),
    )
    bias_grad = lax.psum(bias_accum, ("canvas", "band"))
    return (
        jnp.stack(outputs),
        jnp.stack(input_grads),
        jnp.stack(time_grads),
        shards[5],
        shards[0],
        shards[1],
        bias_grad,
        shards[2],
        shards[3],
        shards[4],
    )


MESH = pl.DeviceIdType.MESH
BF, F32 = jnp.bfloat16, jnp.float32
EPS = 1e-5
TOK, HALF, D, QC, FH = 544, 272, 1152, 640, 2304
KEYS, KW, PADK = 784, 512, 80
SCALE = 72 ** -0.5
NEG = -1e30


def dot(a, b):
    return jnp.dot(a, b, preferred_element_type=F32)


def dot_nt(a, b):
    return lax.dot_general(a, b, (((1,), (1,)), ((), ())), preferred_element_type=F32)


def dot_tn(a, b):
    return lax.dot_general(a, b, (((0,), (0,)), ((), ())), preferred_element_type=F32)


def norm(v):
    center = v - jnp.mean(v, -1, keepdims=True)
    r = lax.rsqrt(jnp.mean(center * center, -1, keepdims=True) + EPS)
    return center * r, r


def norm_back(n, r, e):
    return r * (e - jnp.mean(e, -1, keepdims=True) - n * jnp.mean(e * n, -1, keepdims=True))


def place():
    c, b = lax.axis_index("canvas"), lax.axis_index("band")
    return c, b, b // 2, lax.rem(b, 2)


def greet(devs):
    bar = pltpu.get_barrier_semaphore()
    for dev in devs:
        pl.semaphore_signal(bar, 1, device_id=dev, device_id_type=MESH)
    pl.semaphore_wait(bar, len(devs))


def remote(src, dst, ss, rs, dev):
    return pltpu.make_async_remote_copy(src, dst, ss, rs, device_id=dev, device_id_type=MESH)


def head_window(h):
    ws = pl.multiple_of(jnp.minimum(80 * h // 128, 3) * 128, 128)
    lane = lax.broadcasted_iota(jnp.int32, (1, 256), 1) + ws - 80 * h
    hm = jnp.where((lane >= 0) & (lane < 80), 1.0, 0.0).astype(BF)
    return pl.ds(ws, 256), hm


def toeplitz(base, h):
    row = jnp.broadcast_to(base[pl.ds(h, 1)], (HALF, KW))
    return pltpu.roll(row, 0, 1, stride=1, stride_axis=0)


GSPEC = {"A": (144, 640, 640), "O": (80, 384, 384), "I0": (144, 384, 384), "I1": (144, 384, 384), "B0": (144, 384, 384), "B1": (144, 384, 384)}
GNAMES = list(GSPEC)


FIRST, STEP, SPARE = 4.0, 1.7, -2


class Gather:
    def __init__(self, own, full, s_sem, r_sem, y_sem, l_sem, pend):
        self.own, self.full, self.pend = dict(zip(GNAMES, own)), dict(zip(GNAMES, full)), pend
        self.s_sem, self.r_sem, self.y_sem, self.l_sem = s_sem, r_sem, y_sem, l_sem
        self.c, self.b, self.y, _ = place()
        self.z, self.x = self.c // 2, lax.rem(self.c, 2)
        z = self.z
        self.zp = [jnp.where(z == 0, t[0], jnp.where(z == 1, t[1], jnp.where(z == 2, t[2], t[3]))) for t in ((1, 0, 3, 2), (2, 2, 1, 1), (3, 3, 0, 0))]
        self.xdev, self.ydev = {"canvas": self.c + 1 - 2 * self.x}, {"band": self.b + 2 - 4 * self.y}
        self.count = dict.fromkeys(GNAMES, 0)

    def part(self, name, src, plane, side):
        rows, wide, mid = GSPEC[name]
        at = pl.ds(pl.multiple_of(src * rows, 16), rows)
        if plane:
            return at, pl.ds(pl.multiple_of(wide * side, 128), wide + mid)
        return at, pl.ds(pl.multiple_of((wide + mid) * side, 128), wide)

    def send(self, name, src, dev, plane, first=False, when=None):
        n = GNAMES.index(name)
        at, cols = self.part(name, src, plane, self.y)
        held = self.full[name].at[at, cols] if self.own[name] is None or not first else self.own[name].at[:, cols]
        cp = remote(held, self.full[name].at[at, cols],
                    self.s_sem.at[n, self.count[name]], (self.r_sem if plane else self.y_sem).at[n, src], dev)
        self.count[name] += 1
        if when is None:
            cp.start()
            self.pend.append(cp.wait_send)
        else:
            pl.when(when)(cp.start)
            self.pend.append(lambda: pl.when(when)(cp.wait_send))

    def own_sends(self, name):
        rows = GSPEC[name][0]
        for up in (1, -1):
            to = self.z + up
            self.send(name, self.c, {"canvas": jnp.clip(to, 0, 3) * 2 + self.x}, True, True, (to >= 0) & (to <= 3))
        self.send(name, self.c, self.xdev, True, True)
        if self.own[name] is not None:
            pltpu.make_async_copy(self.own[name], self.full[name].at[pl.ds(pl.multiple_of(self.c * rows, 16), rows)],
                                  self.l_sem.at[GNAMES.index(name)]).start()

    def wait(self, name, src, plane):
        at, cols = self.part(name, src, plane, self.y if plane else 1 - self.y)
        view = self.full[name].at[at, cols]
        pltpu.make_async_copy(view, view, (self.r_sem if plane else self.y_sem).at[GNAMES.index(name), src]).wait()

    def from_z(self, name, i):
        src = self.zp[i] * 2 + self.x
        self.wait(name, src, True)
        to = jnp.where(self.zp[i] < self.z, self.z + 1, self.z - 1)
        self.send(name, src, {"canvas": jnp.clip(to, 0, 3) * 2 + self.x}, True, False, (to >= 0) & (to <= 3))
        self.send(name, src, self.xdev, True)
        self.send(name, src, self.ydev, False)

    def from_x(self, name, i):
        src = (self.z if i == 0 else self.zp[i - 1]) * 2 + 1 - self.x
        self.wait(name, src, True)
        self.send(name, src, self.ydev, False)

    def complete(self, name):
        rows = GSPEC[name][0]
        for d in range(1, 8):
            self.wait(name, lax.rem(self.c + d, 8), False)
        if self.own[name] is not None:
            pltpu.make_async_copy(self.own[name], self.full[name].at[pl.ds(pl.multiple_of(self.c * rows, 16), rows)],
                                  self.l_sem.at[GNAMES.index(name)]).wait()

    def events(self, name):
        return [partial(self.from_z, name, 0), partial(self.from_x, name, 0), partial(self.from_z, name, 1), partial(self.from_x, name, 1),
                partial(self.from_z, name, 2), partial(self.from_x, name, 2), partial(self.from_x, name, 3)]


def gather_forward_kernel(attn_in, time_in, mlp_in, O, mlp_out, lat_in, cot_in, gains, te, seg_row, seg_col, base,
                          xn_o, q_o, kb_o, vb_o, lse_o, o_o, hres_o, hn_o, g_o, gp_o, df_o, gb0_o, gb1_o,
                          WA_o, WO_o, WI0_o, WI1_o, WB0_o, WB1_o, te_o, mask_o, onehot_o, ti,
                          WA, WO, WI0, WI1, WB0, WB1, xn, q, kb, vb, lse, o, hres, hn, g, gp, df, gb0, gb1, te_in, seg_in, col_in, onehot,
                          tp_send, tp_recv, tmix, mask, toep, of, x_send, x_recv, lat, cot,
                          s_sem, r_sem, y_sem, l_sem, es, er, gs, gr, cs, cr,
                          xs, xr, ts, tr, ks, kr, as_, ar, hs, hr, fs, fr, ls, outs):
    blocks = [(attn_in, 0), (attn_in, 1), (attn_in, 2), (time_in, 0), (time_in, 1)] + [(mlp_in, j) for j in range(4)]
    spots = [g.at[144 * (i // 2):144 * (i // 2) + 144, D * (i % 2):D * (i % 2) + D] for i in range(9)]
    loads = [pltpu.make_async_copy(lat_in, lat, ls.at[0]), pltpu.make_async_copy(cot_in, cot, ls.at[1])]
    loads += [pltpu.make_async_copy(src.at[:, D * j:D * j + D], spots[i], ls.at[2 + i]) for i, (src, j) in enumerate(blocks)]
    for cp in loads:
        cp.start()
    c, b, y, k = place()
    sib, ynb = {"band": b + 1 - 2 * k}, {"band": b + 2 - 4 * y}
    peers = [lax.rem(c + d, 8) for d in range(1, 8)]
    pend, saves = [], []

    def go(src, dst, ss, rs, dev):
        cp = remote(src, dst, ss, rs, dev)
        cp.start()
        pend.append(cp.wait_send)

    def arrive(view, sem):
        pltpu.make_async_copy(view, view, sem).wait()

    def save(src, dst):
        cp = pltpu.make_async_copy(src, dst, outs.at[len(saves)])
        cp.start()
        saves.append(cp)

    shares = [mlp_out.at[pl.ds(pl.multiple_of(288 * k + 144 * i, 16), 144)] for i in range(2)]
    gat = Gather((None, O, None, None, *shares), (WA, WO, WI0, WI1, WB0, WB1), s_sem, r_sem, y_sem, l_sem, pend)
    queue, ends = [], {}
    for name, nxt in (("A", "I0"), ("O", "I1"), ("I0", "B0"), ("I1", "B1"), ("B0", None), ("B1", None)):
        steps = gat.events(name)
        if nxt:
            steps.insert(1, partial(gat.own_sends, nxt))
        queue += steps
        ends[name] = len(queue)

    total, clock = len(queue), [0.0]

    def tick(us):
        clock[0] += us
        while queue and FIRST + STEP * (total - len(queue)) <= clock[0]:
            queue.pop(0)()

    def complete(name):
        left = total - ends[name]
        while len(queue) > max(left + SPARE, 0):
            queue.pop(0)()
        gat.complete(name)
        clock[0] = max(clock[0], FIRST + STEP * (total - left))

    greet([{"band": lax.rem(b + d, 4)} for d in (1, 2, 3)] + [{"canvas": p} for p in peers])
    for i, p in enumerate(peers):
        go(te.at[p], te_in.at[c], es.at[i], er.at[6 - i], {"canvas": p})
    te_in[c] = te[c]
    for i in range(3):
        go(seg_row, seg_in.at[b], gs.at[i], gr.at[2 - i], {"band": lax.rem(b + i + 1, 4)})
    seg_in[b] = seg_row[...]
    go(seg_col, col_in.at[k], cs.at[0], cr.at[0], sib)
    col_in[k] = seg_col[...]
    mine_rows = pl.ds(pl.multiple_of(144 * c, 16), 144)

    def pick_matrix(source, wide):
        gb0[:, 0:wide] = jnp.where(lax.broadcasted_iota(jnp.int32, (D, wide), 0) == source, 1.0, 0.0).astype(BF)

    lane = lax.broadcasted_iota(jnp.int32, (1, QC), 1).astype(F32)
    place_h = jnp.floor((lane + 0.5) * (1.0 / 80))
    inside = lane - 80 * place_h
    pick_matrix(jnp.where(inside < 71.5, 144 * place_h + inside + 72 * k.astype(F32), -1.0).astype(jnp.int32), QC)
    for i in range(3):
        loads[2 + i].wait()
        WA[mine_rows, QC * i:QC * i + QC] = dot(spots[i][...], gb0[:, 0:QC]).astype(BF)
    gat.own_sends("A")
    gat.own_sends("O")
    for i in range(2):
        loads[5 + i].wait()
        ti[:, QC * i:QC * i + QC] = dot(spots[3 + i][...], gb0[:, 0:QC]).astype(BF)

    def pick_hidden(s, W):
        for j in range(4):
            n = lax.broadcasted_iota(jnp.int32, (1, 384), 1).astype(F32) + 256 * j
            cc = jnp.floor((n + 0.5) * (1.0 / 144))
            fits = (cc > 2 * j - 0.5) & (cc < 2 * j + 1.5)
            pick_matrix(jnp.where(fits, 576 * (cc - 2 * j) + (n - 144 * cc) + 288 * k.astype(F32) + 144 * s, -1.0).astype(jnp.int32), 384)
            part = dot(spots[5 + j][...], gb0[:, 0:384]).astype(BF)
            if j:
                W[mine_rows, 256 * j:256 * j + 128] += part[:, 0:128]
                W[mine_rows, 256 * j + 128:256 * j + 384] = part[:, 128:]
            else:
                W[mine_rows, 0:384] = part

    loads[0].wait()
    mine = pl.ds(pl.multiple_of(HALF * k, 16), HALF)
    other = pl.ds(pl.multiple_of(HALF * (1 - k), 16), HALF)
    for m in range(2):
        n, _ = norm(lat[m].astype(F32))
        xn[m, mine] = (n * gains[0:1]).astype(BF)
        go(xn.at[m, mine], xn.at[m, mine], xs.at[m], xr.at[m], sib)
        if m == 0:
            for i in range(7):
                arrive(te_in.at[lax.rem(c + i + 1, 8)], er.at[i])
            for p in range(8):
                tp_send[16 * p:16 * p + 16] = dot(te_in[p], ti[...]).astype(BF)
            for i, p in enumerate(peers):
                go(tp_send.at[pl.ds(pl.multiple_of(16 * p, 16), 16)], tp_recv.at[6 - i], ts.at[i], tr.at[6 - i], {"canvas": p})
    save(te_in, te_o)
    for i in range(4):
        loads[7 + i].wait()
    pick_hidden(0, WI0)
    arrive(col_in.at[1 - k], cr.at[0])
    for i in range(3):
        arrive(seg_in.at[lax.rem(b + i + 1, 4)], gr.at[i])
    slot = lax.rem(lax.broadcasted_iota(jnp.int32, (1, 32), 1), 16)
    lane = lax.broadcasted_iota(jnp.int32, (1, KW), 1)

    def column(t):
        return t - 34 * jnp.floor((t + 0.5) * (1.0 / 34))

    colq = column(lax.broadcasted_iota(jnp.int32, (HALF, 1), 0).astype(F32))
    near = jnp.abs(colq - column(lax.broadcasted_iota(jnp.int32, (1, KW), 1).astype(F32) + 22)) < 2.5
    for j in range(2):
        at = 2 * y + j
        before, here, after = seg_in[jnp.maximum(at - 1, 0)], seg_in[at], seg_in[jnp.minimum(at + 1, 3)]
        before = pltpu.roll(jnp.where(at > 0, before, 0.0), KW - HALF, 1)
        after = pltpu.roll(jnp.where(at < 3, after, 0.0), HALF, 1)
        keys = jnp.where(lane < 80, before, jnp.where(lane < 352, here, jnp.where(lane < 432, after, 0.0)))
        for m in range(2):
            code = col_in[j, m, :, 0:1]
            mask[m, j] = jnp.where((code == keys[m:m + 1]) & near, 0.0, NEG).astype(BF)
            hit = (code.astype(jnp.int32) + (5 * m - 2) == slot) & (code >= 1.5)
            onehot[m, HALF * j:HALF * j + HALF] = jnp.where(hit, 1.0, 0.0).astype(BF)
    loads[1].wait()
    for m in range(2):
        filled = jnp.where(col_in[k, m, :, 0:1] >= 1.5, 1.0, 0.0)
        rows = pl.ds(pl.multiple_of(TOK * m + HALF * k, 16), HALF)
        df[rows] = (cot[m].astype(F32) * filled).astype(BF)
        go(df.at[rows], df.at[rows], fs.at[m], fr.at[m], sib)
    save(mask, mask_o)
    save(onehot, onehot_o)
    tick(13.0)
    for i in range(7):
        arrive(tp_recv.at[i], tr.at[i])
    tproj = tp_send[pl.ds(pl.multiple_of(16 * c, 16), 16)].astype(F32)
    for i in range(7):
        tproj = tproj + tp_recv[i].astype(F32)
    hi = tproj.astype(BF)
    tmix[0:16] = hi
    tmix[16:32] = (tproj - hi.astype(F32)).astype(BF)
    dead = pl.ds(pl.multiple_of(y * 624, 16), 80)
    for m in range(2):
        for ref in (kb, vb):
            ref[m, dead] = jnp.zeros((80, QC), BF)
            ref[m, 704:784] = jnp.zeros((80, QC), BF)
    of[...] = jnp.zeros_like(of)
    lse[...] = jnp.zeros_like(lse)
    pick_hidden(1, WI1)
    complete("A")
    save(WA, WA_o)

    edge = pl.ds(pl.multiple_of(544 - 464 * y, 16), 80)
    land = pl.ds(pl.multiple_of(624 * y, 16), 80)
    land_here = pl.ds(pl.multiple_of(624 * (1 - y), 16), 80)
    for m in range(2):
        arrive(xn.at[m, other], xr.at[m])
        x = xn[m]
        kb[m, 80:624] = dot(x, WA[:, QC:2 * QC]).astype(BF)
        tick(1.2)
        vb[m, 80:624] = (dot(x, WA[:, 2 * QC:]) + dot(onehot[m], tmix[:, QC:])).astype(BF)
        for i, ref in enumerate((kb, vb)):
            go(ref.at[m, edge], ref.at[m, land], ks.at[m, i], kr.at[m, i], ynb)
        q[m] = (dot(x, WA[:, :QC]) + dot(onehot[m], tmix[:, :QC])).astype(BF)
        tick(2.5)
    save(xn, xn_o)
    save(q, q_o)
    for m in range(2):
        for i, ref in enumerate((kb, vb)):
            arrive(ref.at[m, land_here], kr.at[m, i])
    save(kb, kb_o)
    save(vb, vb_o)

    def head(h, _):
        win, hm = head_window(h)
        toep[...] = toeplitz(base, h)
        lane_h = lax.broadcasted_iota(jnp.int32, (1, 128), 1) == h

        def tile(t, _):
            m, j = t // 2, lax.rem(t, 2)
            rows = pl.ds(pl.multiple_of(HALF * j, 16), HALF)
            krows = pl.ds(pl.multiple_of(HALF * j, 16), KW)
            s = dot_nt(q[m, rows, win] * hm, kb[m, krows, win])
            s = s * SCALE + (toep[...] + mask[m, j])
            peak = jnp.max(s, -1, keepdims=True)
            e = jnp.exp(s - peak)
            total = jnp.sum(e, -1, keepdims=True)
            p = (e * (1.0 / total)).astype(BF)
            of[m, rows, win] += dot(p, vb[m, krows, win] * hm)
            lse[m, rows] = jnp.where(lane_h, peak + jnp.log(total), lse[m, rows])
            return 0

        return lax.fori_loop(0, 4, tile, 0)

    for n in range(8):
        lax.fori_loop(n, n + 1, head, 0)
        tick(3.1)
    save(lse, lse_o)
    for m in range(2):
        o[m] = of[m].astype(BF)
    save(o, o_o)
    complete("O")
    save(WO, WO_o)

    for m in range(2):
        x_send[m] = dot(o[m, other], WO[...]).astype(BF)
        go(x_send.at[m], x_recv.at[m], as_.at[m], ar.at[m], sib)
    for m in range(2):
        hres[m] = lat[m].astype(F32) + dot(o[m, mine], WO[...])
    tick(4.0)
    for m in range(2):
        arrive(x_recv.at[m], ar.at[m])
        hv = hres[m] + x_recv[m].astype(F32)
        hres[m] = hv
        n, _ = norm(hv)
        hn[m, mine] = (n * gains[1:2]).astype(BF)
        go(hn.at[m, mine], hn.at[m, mine], hs.at[m], hr.at[m], sib)
        tick(2.5)
    save(hres, hres_o)
    for m in range(2):
        arrive(hn.at[m, other], hr.at[m])
    save(hn, hn_o)
    for s, W in enumerate((WI0, WI1)):
        complete("I0" if s == 0 else "I1")
        save(W, (WI0_o, WI1_o)[s])
        for m in range(2):
            def up(i, _):
                cols = pl.ds(pl.multiple_of(i * 384, 128), 384)
                put = pl.ds(pl.multiple_of(i * 384 + D * s, 128), 384)
                u = dot(hn[m], W[:, cols])
                phi = 0.5 + 0.5 * lax.erf(u * (0.5 ** 0.5))
                g[pl.ds(TOK * m, TOK), put] = (u * phi).astype(BF)
                gp[pl.ds(TOK * m, TOK), put] = (phi + u * (jnp.exp(-0.5 * u * u) * 0.3989422804014327)).astype(BF)
                return 0

            lax.fori_loop(0, 3, up, 0)
            tick(3.3)
    save(g, g_o)
    save(gp, gp_o)
    for m in range(2):
        rows = pl.ds(pl.multiple_of(TOK * m + HALF * (1 - k), 16), HALF)
        arrive(df.at[rows], fr.at[m])
    save(df, df_o)
    for s, grad in enumerate((gb0, gb1)):
        for i in range(3):
            cols = pl.ds(384 * i, 384)
            fill_part(grad, g, df, cols, D * s, cols)
            tick(1.3)
        save(grad, (gb0_o, gb1_o)[s])
    for s, W in enumerate((WB0, WB1)):
        complete("B0" if s == 0 else "B1")
        save(W, (WB0_o, WB1_o)[s])
    for cp in saves:
        cp.wait()
    for wait in pend:
        wait()


def gather_forward(p, cot):
    S = jax.ShapeDtypeStruct
    dma = pltpu.SemaphoreType.DMA
    V, anyspace = pl.BlockSpec(memory_space=pltpu.VMEM), pl.BlockSpec(memory_space=pl.ANY)
    weights = [(D, 3 * QC), (QC, D), (D, D), (D, D), (D, D), (D, D)]
    kept = [((2, TOK, D), BF), ((2, TOK, QC), BF), ((2, KEYS, QC), BF), ((2, KEYS, QC), BF), ((2, TOK, 128), F32), ((2, TOK, QC), BF),
            ((2, HALF, D), F32), ((2, TOK, D), BF), ((2 * TOK, FH), BF), ((2 * TOK, FH), BF), ((2 * TOK, D), BF), ((D, D), BF), ((D, D), BF)]
    return pl.pallas_call(
        gather_forward_kernel,
        out_shape=[S(s, t) for s, t in kept] + [S(s, BF) for s in weights]
        + [S((8, 16, 144), BF), S((2, 2, HALF, KW), BF), S((2, TOK, 32), BF), S((144, 2 * QC), BF)],
        in_specs=[anyspace] * 7 + [V] * 5, out_specs=[anyspace] * 22 + [V],
        scratch_shapes=[pltpu.VMEM(s, BF) for s in weights] + [pltpu.VMEM(s, t) for s, t in kept]
        + [pltpu.VMEM((8, 16, 144), BF), pltpu.VMEM((4, 8, KW), F32), pltpu.VMEM((2, 2, HALF, 128), F32), pltpu.VMEM((2, TOK, 32), BF),
           pltpu.VMEM((128, 2 * QC), BF), pltpu.VMEM((7, 16, 2 * QC), BF), pltpu.VMEM((32, 2 * QC), BF), pltpu.VMEM((2, 2, HALF, KW), BF),
           pltpu.VMEM((HALF, KW), F32), pltpu.VMEM((2, TOK, QC), F32), pltpu.VMEM((2, HALF, D), BF), pltpu.VMEM((2, HALF, D), BF),
           pltpu.VMEM((2, HALF, D), BF), pltpu.VMEM((2, HALF, D), BF),
           dma((6, 16)), dma((6, 8)), dma((6, 8)), dma((6,)), dma((7,)), dma((7,)), dma((3,)), dma((3,)), dma((1,)), dma((1,)),
           dma((2,)), dma((2,)), dma((7,)), dma((7,)), dma((2, 2)), dma((2, 2)), dma((2,)), dma((2,)), dma((2,)), dma((2,)), dma((2,)), dma((2,)), dma((11,)), dma((22,))],
        compiler_params=pltpu.CompilerParams(collective_id=1, has_side_effects=True, vmem_limit_bytes=127 * 2 ** 19),
        name="gather_forward")(*p["raw"], p["lat"], cot, p["gains"], p["te"], p["seg_row"], p["seg_col"], p["base"])


def prologue(latents, segment_ids, time_embed, norm_gains, attn_in, time_in, rel_bias, out_proj, mlp_in, mlp_out, cotangent):
    c, b, y, k = place()

    def pick(v, axis):
        return lax.dynamic_index_in_dim(v, k, axis, keepdims=False)

    raw = (attn_in, time_in, mlp_in, jnp.pad(pick(out_proj.reshape(2, 72, D), 0), ((0, 8), (0, 0))), mlp_out)
    code = (segment_ids.reshape(2, HALF) + 2).astype(F32)
    seg_row = jnp.pad(code, ((0, 6), (80, KW - 80 - HALF)))
    seg_col = jnp.broadcast_to(code[..., None], (2, HALF, 128))
    te = jnp.pad(time_embed.reshape(10, D), ((0, 6), (0, 0))).reshape(16, 8, 144).transpose(1, 0, 2)
    bias = pick(rel_bias.reshape(25, 8, 2), 2)
    base = jnp.full((8, KW), NEG, F32)
    places = [80 + 34 * dr + dc for dr in range(-2, 3) for dc in range(-2, 3)]
    base = base.at[:, jnp.array(places)].set(bias.T)
    filled = (segment_ids.reshape(2, HALF, 1) >= 0).astype(F32)
    return dict(raw=raw, te=te, seg_row=seg_row, seg_col=seg_col, base=base, filled=filled, lat=latents.reshape(2, HALF, D), gains=norm_gains.T)


RSPEC = {"A": (144, 640, 640), "O": (80, 384, 384), "I0": (144, 384, 384), "I1": (144, 384, 384), "B0": (144, 384, 384), "B1": (144, 384, 384)}
KEEP = {"A": (36, 48, 4), "I0": (36, 48, 4), "I1": (36, 48, 4), "O": (36, 48, 2), "B0": (144, 144, 2), "B1": (144, 144, 2)}
ORDER = (1, 3, 2, 0)


def scatter_scratch(name):
    rows, wide, mid = RSPEC[name]
    slab = wide + mid
    dma = pltpu.SemaphoreType.DMA
    _, held, sources = KEEP[name]
    sends = {"A": 4, "I": 4, "O": 2, "B": 1}[name[0]]
    return [pltpu.VMEM((8 * rows, wide), BF), pltpu.VMEM((4 * rows, slab), BF), pltpu.VMEM((3 * rows, slab), BF),
            pltpu.VMEM((sends, held, slab), BF), pltpu.VMEM((sources, held, slab), BF),
            dma((4,)), dma((4,)), dma((8,)), dma((8,)), dma((3,)), dma((3,)), dma((4,)), dma((4,))]


N_SCATTER = 13


class Scatter:
    def __init__(self, name, grad, total, scratch, pend):
        self.name, self.grad, self.total, self.pend = name, grad, total, pend
        (self.yr, self.xr, self.zr, self.stage, self.fr, self.ys, self.yw, self.xs, self.xw, self.zs, self.zw, self.fs, self.fw) = scratch
        self.rows, self.wide, self.mid = RSPEC[name]
        self.c, self.b, self.y, self.k = place()
        self.z, self.x = self.c // 2, lax.rem(self.c, 2)
        y, w, l = self.y, self.wide, self.mid
        self.slab = pl.ds(pl.multiple_of(w * y, 128), w + l)
        self.mids = pl.ds(w, l)
        self.side = pl.ds(pl.multiple_of((w + l) * y, 128), w)
        self.away = pl.ds(pl.multiple_of((w + l) * (1 - y), 128), w)
        self.slab_mid = pl.ds(pl.multiple_of(w * (1 - y), 128), l)
        self.slab_side = pl.ds(pl.multiple_of(l * y, 128), w)
        self.xdev, self.ydev = {"canvas": self.c + 1 - 2 * self.x}, {"band": self.b + 2 - 4 * self.y}

    def at(self, group):
        return pl.ds(pl.multiple_of(group * self.rows, 16), self.rows)

    def pair(self, d):
        return pl.ds(pl.multiple_of(lax.rem(self.z + d, 4) * (2 * self.rows), 16), 2 * self.rows)

    def go(self, make):
        make().start()
        self.pend.append(make)

    def parts(self):
        return self.away, self.mids, self.side

    def group(self, d, x):
        return self.at(2 * lax.rem(self.z + d, 4) + x)

    def send_y(self):
        for d in ORDER:
            self.go(lambda d=d: remote(self.grad.at[self.pair(d), self.away], self.yr.at[self.pair(d)], self.ys.at[d], self.yw.at[d], self.ydev))

    def send_mid(self):
        for d in ORDER:
            self.go(lambda d=d: remote(self.grad.at[self.group(d, 1 - self.x), self.mids], self.xr.at[pl.ds(self.rows * d, self.rows), self.slab_mid],
                                       self.xs.at[d], self.xw.at[d], self.xdev))

    def side_x(self, d):
        rows2 = self.pair(d)
        pltpu.make_async_copy(self.yr.at[rows2], self.yr.at[rows2], self.yw.at[d]).wait()
        self.grad[rows2, self.side] += self.yr[rows2]
        self.go(lambda: remote(self.grad.at[self.group(d, 1 - self.x), self.side], self.xr.at[pl.ds(self.rows * d, self.rows), self.slab_side],
                               self.xs.at[4 + d], self.xw.at[4 + d], self.xdev))

    def sum_x(self, d):
        rows = pl.ds(self.rows * d, self.rows)
        for view, sem in ((self.xr.at[rows, self.slab_mid], d), (self.xr.at[rows, self.slab_side], 4 + d)):
            pltpu.make_async_copy(view, view, self.xw.at[sem]).wait()
        return self.grad[self.group(d, self.x), self.slab] + self.xr[rows]

    def send_z(self, d):
        self.grad[self.group(d, self.x), self.slab] = self.sum_x(d)
        self.go(lambda: remote(self.grad.at[self.group(d, self.x), self.slab], self.zr.at[pl.ds((3 - d) * self.rows, self.rows)], self.zs.at[d - 1],
                               self.zw.at[3 - d], {"canvas": 2 * lax.rem(self.z + d, 4) + self.x}))

    def dests(self):
        sources = KEEP[self.name][2]
        if self.name[0] == "B":
            return [(0, 2 * self.k + int(self.name[1]))]
        return [(i, 2 * self.k + i if sources == 2 else i) for i in range(sources)]

    def finish(self):
        acc = self.sum_x(0).astype(F32)
        for i in (2, 0, 1):
            rows = pl.ds(i * self.rows, self.rows)
            pltpu.make_async_copy(self.zr.at[rows], self.zr.at[rows], self.zw.at[i]).wait()
            acc = acc + self.zr[rows].astype(F32)
        n, held, sources = KEEP[self.name]
        slab = self.wide + self.mid
        if self.name[0] == "B":
            self.stage[0] = acc.astype(BF)
        else:
            self.total[0:self.rows, 0:slab] = acc
            for i in range(sources):
                self.stage[i, 0:n] = self.total[n * i:n * i + n, 0:slab].astype(BF)
                self.stage[i, n:held] = jnp.zeros((held - n, slab), BF)
        slot = self.b if sources == 4 else self.y
        for i, dest in self.dests():
            @pl.when(self.b == dest)
            def _():
                self.fr[slot] = self.stage[i]

            @pl.when(self.b != dest)
            def _():
                remote(self.stage.at[i], self.fr.at[slot], self.fs.at[i], self.fw.at[slot], {"band": dest}).start()

    def sent(self):
        for i, dest in self.dests():
            @pl.when(self.b != dest)
            def _():
                remote(self.stage.at[i], self.fr.at[0], self.fs.at[i], self.fw.at[0], {"band": dest}).wait_send()

    def collect(self, out):
        n, held, sources = KEEP[self.name]
        for i in range(sources):
            src = i if sources == 4 else 2 * i + self.y

            @pl.when(self.b != src)
            def _():
                pltpu.make_async_copy(self.fr.at[i], self.fr.at[i], self.fw.at[i]).wait()
        w, l = self.wide, self.mid
        for half in range(sources // 2):
            lo, hi = self.fr[half].astype(F32)[:n], self.fr[half + sources // 2].astype(F32)[:n]
            dst = out.at[half] if sources == 4 else out
            dst[:, 0:w] = lo[:, :w]
            dst[:, w:w + l] = lo[:, w:] + hi[:, :l]
            dst[:, w + l:] = hi[:, l:]


def everyone():
    c, b, y, k = place()
    return [{"band": lax.rem(b + d, 4)} for d in (1, 2, 3)] + [{"canvas": lax.rem(c + d, 8)} for d in range(1, 8)]


def fill_part(grad, left, right, cols, lefts, rights):
    def step(i, _):
        r = pl.multiple_of(i * 384, 128)
        grad[pl.ds(r, 384), cols] = dot_tn(left[:, pl.ds(r + lefts, 384)], right[:, rights]).astype(BF)
        return 0

    lax.fori_loop(0, grad.shape[0] // 384, step, 0)


def mlp_back_kernel(cot_in, filled, gains, WI0_in, WI1_in, WB0_in, WB1_in, hres, hn_in, g_in, gp, df_in, gb0, gb1,
                    out, dh, da, gain, out_b, grad_i0, grad_i1,
                    grad_b0, grad_b1, cot, WI0, WI1, WB0, WB1, hn, g, du, gi, x_send, x_recv, f_send, f_recv, dn, ds_, dr_, xs, xr, as_, ar, ls, gs, *scratch):
    c, b, y, k = place()
    sib = {"band": b + 1 - 2 * k}
    df = da
    loads = [pltpu.make_async_copy(src, dst, ls.at[i])
             for i, (src, dst) in enumerate(((gb0, grad_b0), (gb1, grad_b1), (WB0_in, WB0), (WB1_in, WB1), (g_in, g), (df_in, df), (gp, du), (hres, dh), (cot_in, cot), (hn_in, hn),
                                            (WI0_in, WI0), (WI1_in, WI1)))]
    for cp in loads:
        cp.start()
    greet([{"band": lax.rem(b + d, 4)} for d in (1, 2, 3)] + [{"canvas": c + 1 - 2 * lax.rem(c, 2)}] + [{"canvas": lax.rem(c + d, 8)} for d in (2, 4, 6)])
    pend = []
    rs = [Scatter("B0", grad_b0, None, scratch[:N_SCATTER], pend), Scatter("B1", grad_b1, None, scratch[N_SCATTER:], pend)]
    rs[1].fr, rs[1].fw = rs[0].fr, rs[0].fw

    def half(m, which):
        return pl.ds(pl.multiple_of(TOK * m + HALF * which, 16), HALF)

    for s in range(2):
        loads[s].wait()
        rs[s].send_y()
        if s == 0:
            rs[s].send_mid()
    for cp in loads[2:5]:
        cp.wait()
    for m in range(2):
        def down_other(i, _):
            cols = pl.ds(pl.multiple_of(i * 384, 128), 384)
            f_send[m, :, cols] = (dot(g[half(m, 1 - k), 0:D], WB0[:, cols]) + dot(g[half(m, 1 - k), D:], WB1[:, cols])).astype(BF)
            return 0

        lax.fori_loop(0, 3, down_other, 0)
        loads.append(remote(f_send.at[m], f_recv.at[m], ds_.at[m], dr_.at[m], sib))
        loads[-1].start()

        def down(i, _):
            cols = pl.ds(pl.multiple_of(i * 384, 128), 384)
            dn[m, :, cols] = dot(g[half(m, k), 0:D], WB0[:, cols]) + dot(g[half(m, k), D:], WB1[:, cols])
            return 0

        lax.fori_loop(0, 3, down, 0)

    def back_act(m, s):
        def step(i, _):
            r = pl.multiple_of(i * 384, 128)
            cols = pl.ds(pl.multiple_of(r + D * s, 128), 384)
            rows = pl.ds(TOK * m, TOK)
            du[rows, cols] = (dot_nt(df[rows], (WB0, WB1)[s][pl.ds(r, 384)]) * du[rows, cols].astype(F32)).astype(BF)
            return 0

        lax.fori_loop(0, 3, step, 0)

    rs[0].side_x(1)
    for cp in loads[5:12]:
        cp.wait()
    back_act(0, 0)
    rs[0].side_x(3)
    rs[0].send_z(1)
    for m in range(2):
        v = f_recv.at[m]
        pltpu.make_async_copy(v, v, dr_.at[m]).wait()
        out[m] = ((dh[m] + (dn[m] + v[...].astype(F32))) * filled[m]).astype(BF)
    back_act(1, 0)
    rs[0].side_x(2)
    rs[0].send_z(3)
    back_act(0, 1)
    rs[0].side_x(0)
    rs[1].send_mid()
    rs[0].send_z(2)
    back_act(1, 1)
    rs[1].side_x(1)
    saves = []
    for s in range(2):
        def step(i, _):
            r = pl.multiple_of(i * 384, 128)
            gi[s, pl.ds(r, 384)] = dot_tn(hn[:, pl.ds(r, 384)], du[:, D * s:D * s + D]).astype(BF)
            return 0

        lax.fori_loop(0, 3, step, 0)
        cp = pltpu.make_async_copy(gi.at[s], (grad_i0, grad_i1)[s], gs.at[s])
        cp.start()
        saves.append(cp)
        if s == 0:
            rs[1].side_x(3)
            rs[1].send_z(1)
            rs[0].finish()
        else:
            rs[1].side_x(2)
            rs[1].send_z(3)

    for m in range(2):
        def hid(i, _):
            r = pl.multiple_of(i * 384, 128)
            rows = pl.ds(r, 384)
            v = dot_nt(du[half(m, 1 - k), 0:D], WI0[rows]) + dot_nt(du[half(m, 1 - k), D:], WI1[rows])
            x_send[m, :, rows] = v.astype(BF)
            return 0

        lax.fori_loop(0, 3, hid, 0)
        cp = remote(x_send.at[m], x_recv.at[m], xs.at[m], xr.at[m], sib)
        cp.start()
        loads.append(cp)

        def hid_own(i, _):
            r = pl.multiple_of(i * 384, 128)
            rows = pl.ds(r, 384)
            dn[m, :, rows] = dot_nt(du[half(m, k), 0:D], WI0[rows]) + dot_nt(du[half(m, k), D:], WI1[rows])
            return 0

        lax.fori_loop(0, 3, hid_own, 0)
        if m == 0:
            rs[1].side_x(0)
            rs[1].send_z(2)
    gain_two = jnp.zeros((1, D), F32)
    for m in range(2):
        pltpu.make_async_copy(x_recv.at[m], x_recv.at[m], xr.at[m]).wait()
        grad = dn[m] + x_recv[m].astype(F32)
        n, r = norm(dh[m])
        gain_two = gain_two + jnp.sum(grad * n, 0, keepdims=True)
        v = cot[m].astype(F32) * filled[m] + norm_back(n, r, grad * gains[1:2])
        dh[m] = v
        da[half(m, k)] = v.astype(BF)
        cp = remote(da.at[half(m, k)], da.at[half(m, k)], as_.at[m], ar.at[m], sib)
        cp.start()
        loads.append(cp)
    gain[...] = jnp.broadcast_to(gain_two, (8, D))
    for m in range(2):
        v = da.at[half(m, 1 - k)]
        pltpu.make_async_copy(v, v, ar.at[m]).wait()
    rs[1].finish()
    rs[0].collect(out_b)
    rs[0].sent()
    rs[1].sent()
    for cp in saves:
        cp.wait()
    for cp in loads[12:]:
        cp.wait_send()
    for make in pend:
        make().wait_send()


def mlp_back(*args):
    S = jax.ShapeDtypeStruct
    dma = pltpu.SemaphoreType.DMA
    V, anyspace = pl.BlockSpec(memory_space=pltpu.VMEM), pl.BlockSpec(memory_space=pl.ANY)
    return pl.pallas_call(
        mlp_back_kernel,
        out_shape=[S((2, HALF, D), BF), S((2, HALF, D), F32), S((2 * TOK, D), BF), S((8, D), F32), S((144, D), F32), S((D, D), BF), S((D, D), BF)],
        in_specs=[anyspace, V, V] + [anyspace] * 11, out_specs=[V] * 5 + [anyspace] * 2,
        scratch_shapes=[pltpu.VMEM((D, D), BF), pltpu.VMEM((D, D), BF), pltpu.VMEM((2, HALF, D), BF)] + [pltpu.VMEM((D, D), BF)] * 4
        + [pltpu.VMEM((2 * TOK, D), BF), pltpu.VMEM((2 * TOK, FH), BF), pltpu.VMEM((2 * TOK, FH), BF), pltpu.VMEM((2, D, D), BF),
                        pltpu.VMEM((2, HALF, D), BF), pltpu.VMEM((2, HALF, D), BF), pltpu.VMEM((2, HALF, D), BF), pltpu.VMEM((2, HALF, D), BF),
                        pltpu.VMEM((2, HALF, D), F32)]
        + [dma((2,))] * 6 + [dma((12,)), dma((2,))] + scatter_scratch("B0") + scatter_scratch("B1"),
        compiler_params=pltpu.CompilerParams(collective_id=2, has_side_effects=True, vmem_limit_bytes=127 * 2 ** 19),
        name="mlp_back")(*args)


def attn_back_kernel(WA, WO, ti, gains, lat, xn, q, kb, vb, lse, o, da, dh, mask, base, onehot, gain_two, gi0, gi1,
                     dlat, dt_all, gt, small, out_o, out_a, out_i0, out_i1,
                     q_v, kb_v, vb_v, grad_o, grad_a, grad_i0, grad_i1, do, dqkv, rim, rim_in, tsum, tsum_in, gt_send, gt_in, x_send, x_recv, dbias, sm_send, sm_in, total,
                     ks, kr, ts, tr, ps, pr, us, ur, vs, vr, ls, xs, xr, ss, sr, bs, br, *scratch):
    c, b, y, k = place()
    sib, ynb = {"band": b + 1 - 2 * k}, {"band": b + 2 - 4 * y}
    peers = [lax.rem(c + d, 8) for d in range(1, 8)]
    pend, waits = [], iter(range(20))

    def load(src, dst):
        cp = pltpu.make_async_copy(src, dst, ls.at[next(waits)])
        cp.start()
        return cp

    loads_i = [load(gi0, grad_i0), load(gi1, grad_i1)]
    load_dh = load(dh, dlat)
    load_q = [load(q, q_v), load(kb, kb_v), load(vb, vb_v)]
    greet(everyone())
    n = N_SCATTER
    rs_o = Scatter("O", grad_o, total, scratch[:n], pend)
    rs_a = Scatter("A", grad_a, total, scratch[n:2 * n], pend)
    rs_i = [Scatter("I0", grad_i0, total, scratch[2 * n:3 * n], pend), Scatter("I1", grad_i1, total, scratch[3 * n:], pend)]

    def go(make):
        make().start()
        pend.append(make)

    def arrive(view, sem):
        pltpu.make_async_copy(view, view, sem).wait()

    slots = pl.ds(pl.multiple_of(16 * c, 16), 16)
    for s in range(2):
        loads_i[s].wait()
        rs_i[s].send_y()
        rs_i[s].send_mid()

    def first(o_v, da_v, wo_v):
        parts = [load(o, o_v), load(da, da_v), load(WO, wo_v)]
        for cp in parts:
            cp.wait()
        for i, cols in enumerate(rs_o.parts()):
            grad_o[:, cols] = dot_tn(o_v[...], da_v[:, cols]).astype(BF)
            if i == 0:
                rs_o.send_y()
            if i == 1:
                rs_o.send_mid()
        for m in range(2):
            do[m] = dot_nt(da_v[pl.ds(TOK * m, TOK)], wo_v[...]).astype(BF)

    pl.run_scoped(first, pltpu.VMEM((2 * TOK, QC), BF), pltpu.VMEM((2 * TOK, D), BF), pltpu.VMEM((QC, D), BF))

    def second(dqf, dkf, dvf, toep, dsum):
        dqf[...] = jnp.zeros_like(dqf)
        dkf[...] = jnp.zeros_like(dkf)
        dvf[...] = jnp.zeros_like(dvf)
        for cp in load_q:
            cp.wait()

        def head(h, _):
            win, hm = head_window(h)
            toep[...] = toeplitz(base, h)
            dsum[...] = jnp.zeros_like(dsum)
            lane_h = lax.broadcasted_iota(jnp.int32, (1, 128), 1) == h

            def tile(t, _):
                m, j = t // 2, lax.rem(t, 2)
                rows = pl.ds(pl.multiple_of(HALF * j, 16), HALF)
                krows = pl.ds(pl.multiple_of(HALF * j, 16), KW)
                qm, dm = q_v[m, rows, win] * hm, do[m, rows, win] * hm
                kw = kb_v[m, krows, win]
                level = jnp.sum(jnp.where(lane_h, lse[m, rows], 0.0), -1, keepdims=True)
                p = jnp.exp(dot_nt(qm, kw) * SCALE + (toep[...] + mask[m, j]) - level)
                dp = dot_nt(dm, vb_v[m, krows, win])
                delta = jnp.sum(p * dp, -1, keepdims=True)
                ds = (p * (dp - delta)).astype(BF)
                dsum[...] += ds.astype(F32)
                dqf[m, rows, win] += dot(ds, kw * hm)
                dkf[m, krows, win] += dot_tn(ds, qm)
                dvf[m, krows, win] += dot_tn(p.astype(BF), dm)
                return 0

            lax.fori_loop(0, 4, tile, 0)
            strip = dsum[0:8]
            for r in range(8, HALF, 8):
                strip = strip + pltpu.roll(dsum[r:r + 8], KW - r, 1)
            line = strip[0:1]
            for r in range(1, 8):
                line = line + pltpu.roll(strip, KW - r, 1)[r:r + 1]
            dbias[pl.ds(h, 1)] = line
            return 0

        for i in range(4):
            lax.fori_loop(2 * i, 2 * i + 2, head, 0)
            if i == 0:
                for d in (1, 3, 2):
                    rs_i[0].side_x(d)
            elif i == 1:
                rs_i[0].side_x(0)
                for d in (1, 3, 2):
                    rs_i[0].send_z(d)
                rs_i[1].side_x(1)
            elif i == 2:
                for d in (3, 2, 0):
                    rs_i[1].side_x(d)
                rs_i[1].send_z(1)
        away = pl.ds(pl.multiple_of(624 * (1 - y), 16), 80)
        edge = pl.ds(pl.multiple_of(544 - 464 * y, 16), 80)
        for m in range(2):
            rim[m, 0] = (dkf[m, away] * SCALE).astype(BF)
            rim[m, 1] = dvf[m, away].astype(BF)
            go(lambda m=m: remote(rim.at[m], rim_in.at[m], ks.at[m], kr.at[m], ynb))
        for m in range(2):
            tok = pl.ds(TOK * m, TOK)
            dqkv[tok, 0:QC] = (dqf[m] * SCALE).astype(BF)
        for d in ORDER:
            rs_o.side_x(d)
        rs_i[1].send_z(3)
        rs_i[1].send_z(2)
        for m in range(2):
            arrive(rim_in.at[m], kr.at[m])
            tok = pl.ds(TOK * m, TOK)
            dkf[m, edge] += rim_in[m, 0].astype(F32) * (1.0 / SCALE)
            dvf[m, edge] += rim_in[m, 1].astype(F32)
            dqkv[tok, QC:2 * QC] = (dkf[m, 80:624] * SCALE).astype(BF)
            dqkv[tok, 2 * QC:] = dvf[m, 80:624].astype(BF)

    pl.run_scoped(second, pltpu.VMEM((2, TOK, QC), F32), pltpu.VMEM((2, KEYS, QC), F32), pltpu.VMEM((2, KEYS, QC), F32),
                  pltpu.VMEM((HALF, KW), F32), pltpu.VMEM((HALF, KW), F32))

    def third(xn_v, wa_v, dn):
        loads = [load(xn, xn_v), load(WA, wa_v)]
        tq = dot_tn(onehot[0], dqkv[0:TOK, 0:QC]) + dot_tn(onehot[1], dqkv[TOK:, 0:QC])
        tv = dot_tn(onehot[0], dqkv[0:TOK, 2 * QC:]) + dot_tn(onehot[1], dqkv[TOK:, 2 * QC:])
        tsum[:, 0:QC] = tq[0:16].astype(BF)
        tsum[:, QC:] = tv[0:16].astype(BF)
        go(lambda: remote(tsum, tsum_in, ts.at[0], tr.at[0], ynb))
        loads[0].wait()
        for i, cols in enumerate(rs_a.parts()):
            fill_part(grad_a, xn_v, dqkv, cols, 0, cols)
            if i == 0:
                rs_a.send_y()
                arrive(tsum_in, tr.at[0])
                dt_all[k, slots] = (tsum[...].astype(F32) + tsum_in[...].astype(F32)).astype(BF)
                for n, p in enumerate(peers):
                    go(lambda n=n, p=p: remote(dt_all.at[k, slots], dt_all.at[k, slots], ps.at[n], pr.at[6 - n], {"canvas": p}))
            if i == 1:
                rs_a.send_mid()
        for d in (1, 3, 2):
            rs_o.send_z(d)
        rs_i[0].finish()
        loads[1].wait()
        for m in range(2):
            rows = pl.ds(pl.multiple_of(TOK * m + HALF * (1 - k), 16), HALF)
            rows_own = pl.ds(pl.multiple_of(TOK * m + HALF * k, 16), HALF)

            def back(n, _):
                cols = pl.ds(pl.multiple_of(n * 384, 128), 384)
                x_send[m, :, cols] = dot_nt(dqkv[rows], wa_v[cols]).astype(BF)
                return 0

            lax.fori_loop(0, 3, back, 0)
            go(lambda m=m: remote(x_send.at[m], x_recv.at[m], xs.at[m], xr.at[m], sib))

            def back_own(n, _):
                cols = pl.ds(pl.multiple_of(n * 384, 128), 384)
                dn[m, :, cols] = dot_nt(dqkv[rows_own], wa_v[cols])
                return 0

            lax.fori_loop(0, 3, back_own, 0)
        rs_i[1].finish()
        rs_a.side_x(1)
        for n in range(7):
            arrive(dt_all.at[k, pl.ds(pl.multiple_of(16 * lax.rem(c + n + 1, 8), 16), 16)], pr.at[n])
        go(lambda: remote(dt_all.at[k], dt_all.at[k], us.at[0], ur.at[0], sib))
        gt_send[...] = dot_nt(dt_all[k], ti[...])
        go(lambda: remote(gt_send, gt_in, us.at[1], ur.at[1], sib))
        rs_a.side_x(3)
        rs_a.send_z(1)
        load_dh.wait()
        gain_one = jnp.zeros((1, D), F32)
        for m in range(2):
            arrive(x_recv.at[m], xr.at[m])
            grad = dn[m] + x_recv[m].astype(F32)
            n, r = norm(lat[m].astype(F32))
            gain_one = gain_one + jnp.sum(grad * n, 0, keepdims=True)
            dlat[m] = dlat[m] + norm_back(n, r, grad * gains[0:1])
            if m == 0:
                rs_a.side_x(2)
                rs_a.send_z(3)
        first_row = lax.broadcasted_iota(jnp.int32, (8, 1), 0) == 0
        both = jnp.where(first_row, jnp.broadcast_to(gain_one, (8, D)), gain_two[...])
        for p in range(8):
            sm_send[p, 0:8] = dbias[...]
            sm_send[p, 8:16] = (pltpu.roll(both, D - 144 * p, 1) if p else both)[:, 0:KW]

    pl.run_scoped(third, pltpu.VMEM((2 * TOK, D), BF), pltpu.VMEM((D, 3 * QC), BF), pltpu.VMEM((2, HALF, D), F32))
    for n, p in enumerate(peers):
        go(lambda n=n, p=p: remote(sm_send.at[p], sm_in.at[6 - n], ss.at[n], sr.at[6 - n], {"canvas": p}))
    rs_o.finish()
    arrive(gt_in, ur.at[1])
    gt_in[...] = gt_in[...] + gt_send[...]
    for n, p in enumerate(peers):
        go(lambda n=n, p=p: remote(gt_in.at[pl.ds(pl.multiple_of(16 * p, 16), 16)], gt.at[c], vs.at[n], vr.at[6 - n], {"canvas": p}))
    gt[c] = gt_in[pl.ds(pl.multiple_of(16 * c, 16), 16)]
    rs_a.side_x(0)
    rs_a.send_z(2)
    acc = sm_send[c]
    for n in range(7):
        arrive(sm_in.at[n], sr.at[n])
        acc = acc + sm_in[n]
    small[b] = acc
    for i in range(3):
        go(lambda i=i: remote(small.at[b], small.at[b], bs.at[i], br.at[2 - i], {"band": lax.rem(b + i + 1, 4)}))
    rs_i[0].collect(out_i0)
    rs_i[1].collect(out_i1)
    rs_o.collect(out_o)
    for n in range(7):
        arrive(gt.at[lax.rem(c + n + 1, 8)], vr.at[n])
    arrive(dt_all.at[1 - k], ur.at[0])
    for i in range(3):
        arrive(small.at[lax.rem(b + i + 1, 4)], br.at[i])
    rs_a.finish()
    rs_a.collect(out_a)
    for rs in (rs_o, rs_a, *rs_i):
        rs.sent()
    for make in pend:
        make().wait_send()


def attn_back(*args):
    S = jax.ShapeDtypeStruct
    dma = pltpu.SemaphoreType.DMA
    V, anyspace = pl.BlockSpec(memory_space=pltpu.VMEM), pl.BlockSpec(memory_space=pl.ANY)
    return pl.pallas_call(
        attn_back_kernel,
        out_shape=[S((2, HALF, D), F32), S((2, 128, 2 * QC), BF), S((8, 16, 144), F32), S((4, 16, KW), F32),
                   S((36, D), F32), S((2, 36, 3 * QC), F32), S((2, 36, D), F32), S((2, 36, D), F32)],
        in_specs=[anyspace, anyspace, V, V, V] + [anyspace] * 4 + [V] + [anyspace] * 3 + [V] * 4 + [anyspace] * 2, out_specs=[V] * 8,
        scratch_shapes=[pltpu.VMEM((2, TOK, QC), BF), pltpu.VMEM((2, KEYS, QC), BF), pltpu.VMEM((2, KEYS, QC), BF),
                        pltpu.VMEM((QC, D), BF), pltpu.VMEM((D, 3 * QC), BF), pltpu.VMEM((D, D), BF), pltpu.VMEM((D, D), BF), pltpu.VMEM((2, TOK, QC), BF),
                        pltpu.VMEM((2 * TOK, 3 * QC), BF),
                        pltpu.VMEM((2, 2, 80, QC), BF), pltpu.VMEM((2, 2, 80, QC), BF), pltpu.VMEM((16, 2 * QC), BF), pltpu.VMEM((16, 2 * QC), BF),
                        pltpu.VMEM((128, 144), F32), pltpu.VMEM((128, 144), F32),
                        pltpu.VMEM((2, HALF, D), BF), pltpu.VMEM((2, HALF, D), BF), pltpu.VMEM((8, KW), F32), pltpu.VMEM((8, 16, KW), F32), pltpu.VMEM((7, 16, KW), F32),
                        pltpu.VMEM((144, 1280), F32),
                        dma((2,)), dma((2,)), dma((1,)), dma((1,)), dma((7,)), dma((7,)), dma((2,)), dma((2,)), dma((7,)), dma((7,)), dma((20,)), dma((2,)), dma((2,)),
                        dma((7,)), dma((7,)), dma((3,)), dma((3,))]
        + scatter_scratch("O") + scatter_scratch("A") + scatter_scratch("I0") + scatter_scratch("I1"),
        compiler_params=pltpu.CompilerParams(collective_id=3, has_side_effects=True, vmem_limit_bytes=127 * 2 ** 19),
        name="attn_back")(*args)


def local_fast(*args):
    p = prologue(*args)
    c, b, y, k = place()
    cot = args[10].reshape(2, HALF, D)
    (xn, q, kb, vb, lse, o, hres, hn, g, gp, df, gb0, gb1, WA, WO, WI0, WI1, WB0, WB1, te_all, mask, onehot, ti) = gather_forward(p, cot)
    out, dh, da, gain_two, out_b, gi0, gi1 = mlp_back(cot, p["filled"], p["gains"], WI0, WI1, WB0, WB1, hres, hn.reshape(2 * TOK, D), g, gp, df, gb0, gb1)
    dlat, dt_all, gt, small, out_o, out_a, out_i0, out_i1 = attn_back(
        WA, WO, ti, p["gains"], p["lat"], xn.reshape(2 * TOK, D), q, kb, vb, lse, o.reshape(2 * TOK, QC), da, dh,
        mask, p["base"], onehot, gain_two, gi0, gi1)
    shape = (2, 1, 8, 34, D)
    places = [80 + 34 * dr + dc for dr in range(-2, 3) for dc in range(-2, 3)]
    bias = small[0:2, 0:8] + small[2:4, 0:8]
    grad_bias = bias[:, :, jnp.array(places)].transpose(2, 1, 0).reshape(25, 16)
    mine = lax.dynamic_slice_in_dim(small[:, 8:10, 0:144].sum(0), 36 * b, 36, 1)
    grad_a = out_a.reshape(2, 36, 3, 8, 80)[..., :72].transpose(1, 2, 3, 0, 4).reshape(36, 3 * D)
    grad_i = jnp.stack([out_i0, out_i1]).reshape(2, 2, 36, 8, 144).transpose(2, 3, 1, 0, 4).reshape(36, 2 * FH)
    dt = dt_all.reshape(2, 128, 2, 8, 80)[..., :72].transpose(1, 2, 3, 0, 4).reshape(128, 2 * D)
    te_mine = lax.dynamic_slice_in_dim(te_all.reshape(128, 144), 36 * b, 36, 1)
    grad_time_in = dot_tn(te_mine, dt)
    grad_time = gt.transpose(1, 0, 2).reshape(16, D)[:10].reshape(2, 1, 5, D)
    return (out.reshape(shape), dlat.reshape(shape), grad_time, mine.T, grad_a, grad_time_in, grad_bias, out_o, grad_i, out_b)


def solution(mesh):
    return jax.shard_map(
        local_fast if mesh.shape["canvas"] == 8 and mesh.shape["band"] == 4 else local,
        mesh=mesh,
        in_specs=(
            P(None, "canvas", "band", None, None),
            P(None, "canvas", "band", None),
            P(None, "canvas", None, None),
            P(),
            P("canvas", None),
            P("canvas", None),
            P(),
            P("canvas", None),
            P("canvas", None),
            P("canvas", None),
            P(None, "canvas", "band", None, None),
        ),
        out_specs=(
            P(None, "canvas", "band", None, None),
            P(None, "canvas", "band", None, None),
            P(None, "canvas", None, None),
            P(("canvas", "band"), None),
            P(("canvas", "band"), None),
            P(("canvas", "band"), None),
            P(),
            P(("canvas", "band"), None),
            P(("canvas", "band"), None),
            P(("canvas", "band"), None),
        ),
        check_vma=False,
    )
```

```python
from functools import partial
import jax
import jax.numpy as jnp
from jax import lax
from jax.experimental import pallas as pl
from jax.experimental.pallas import tpu as pltpu

from jax.sharding import PartitionSpec as P

WIN = 5


EPSILON = 1e-05


def padded_2(shard, sides, width):
    for axis, dim in sides:
        devices, length = (lax.axis_size(axis), shard.shape[dim])
        up = [(i, (i + 1) % devices) for i in range(devices - 1)]
        down = [(j, i) for i, j in up]
        last = lax.slice_in_dim(shard, length - width, length, axis=dim)
        first = lax.slice_in_dim(shard, 0, width, axis=dim)
        before = lax.ppermute(last, axis, up)
        after = lax.ppermute(first, axis, down)
        shard = jnp.concatenate([before, shard, after], axis=dim)
    return shard


def shifted(shard, axis, by):
    devices = lax.axis_size(axis)
    pairs = [(i, i + by) for i in range(devices) if 0 <= i + by < devices]
    return lax.ppermute(shard, axis, pairs)


def shortened(shard):

    def short(part):
        return part.astype(jnp.bfloat16) if part.dtype == jnp.float32 else part

    return jax.tree.map(short, shard)


def normalize(value, gain):
    center = value - jnp.mean(value, -1, keepdims=True)
    scaled = lax.rsqrt(jnp.mean(center * center, -1, keepdims=True) + EPSILON)
    unit = center * scaled
    return (unit, scaled, unit * gain)


def normalize_back(unit, scaled, gain, grad_out):
    part = grad_out * gain
    return scaled * (
        part - jnp.mean(part, -1, keepdims=True) - unit * jnp.mean(part * unit, -1, keepdims=True)
    )


def rows_dot(left, right):
    return lax.dot_general(
        left, right, (((0,), (0,)), ((), ())), preferred_element_type=jnp.float32
    )


def back_dot(left, weight):
    return lax.dot_general(
        left, weight, (((1,), (1,)), ((), ())), preferred_element_type=jnp.float32
    )


def neighbour_stack(padded, band_rows, columns):
    pieces = [padded[:, i : i + band_rows, j : j + columns] for i in range(WIN) for j in range(WIN)]
    stacked = jnp.stack(pieces)
    return stacked.reshape((WIN * WIN, -1) + padded.shape[3:])


def spread_back(terms, canvases, band_rows, columns):
    reach = WIN // 2
    shaped = terms.reshape((WIN * WIN, canvases, band_rows, columns, terms.shape[-1]))
    summed = None
    for i in range(WIN):
        for j in range(WIN):
            placed = jnp.pad(
                shaped[i * WIN + j], ((0, 0), (i, 2 * reach - i), (j, 2 * reach - j), (0, 0))
            )
            summed = placed if summed is None else summed + placed
    return summed


def head_total(terms, head_sum):
    flat = terms.reshape(-1, terms.shape[-1])
    return jnp.dot(flat, head_sum, precision=lax.Precision.HIGHEST).reshape(
        terms.shape[:-1] + (head_sum.shape[1],)
    )


def head_widen(values, head_spread):
    flat = values.reshape(-1, values.shape[-1])
    return jnp.dot(flat, head_spread, preferred_element_type=jnp.bfloat16).reshape(
        values.shape[:-1] + (head_spread.shape[1],)
    )


def local(
    latents,
    segment_ids,
    time_embed,
    norm_gains,
    attn_in,
    time_in,
    rel_bias,
    out_proj,
    mlp_in,
    mlp_out,
    cotangent,
):
    micro_count, canvases, band_rows, columns, width = latents.shape
    slots = time_embed.shape[2]
    heads = rel_bias.shape[1]
    head_dim = width // heads
    reach = WIN // 2
    tokens = canvases * band_rows * columns
    score_scale = head_dim ** (-0.5)
    head_sum = (jnp.arange(width)[:, None] // head_dim == jnp.arange(heads)[None, :]).astype(
        jnp.float32
    )
    head_spread = head_sum.T.astype(jnp.bfloat16)
    owned = (attn_in, time_in, out_proj, mlp_in, mlp_out)
    seg_code = segment_ids + 2
    seg_rims = padded_2(seg_code, (("band", 2),), reach)
    seg_rims = jnp.pad(seg_rims, ((0, 0), (0, 0), (0, 0), (reach, reach)))
    band_share = 1.0 / lax.axis_size("band")
    outputs = []
    input_grads = []
    time_grads = []
    accum = None
    shards = None
    bias_accum = jnp.zeros(rel_bias.shape, jnp.float32)
    for batch_index in range(micro_count):
        full_weights = (
            lax.all_gather(owned[0], "canvas", axis=0, tiled=True),
            lax.all_gather(owned[1], "canvas", axis=0, tiled=True),
            lax.all_gather(owned[2], "canvas", axis=0, tiled=True),
            lax.all_gather(owned[3], "canvas", axis=0, tiled=True),
            lax.all_gather(owned[4], "canvas", axis=0, tiled=True),
        )
        w_attn, w_time, w_out, w_in, w_back = full_weights
        inputs = latents[batch_index].astype(jnp.float32).reshape(tokens, width)
        unit_one, scaled_one, normed_one = normalize(inputs, norm_gains[:, 0])
        normed = normed_one.astype(jnp.bfloat16)
        time_rows = time_embed[batch_index].reshape(canvases * slots, width)
        time_proj = jnp.dot(time_rows, w_time, preferred_element_type=jnp.float32).reshape(
            canvases, slots, 2 * width
        )
        seg_here = segment_ids[batch_index]
        member = (seg_here[..., None] == jnp.arange(slots)).astype(jnp.float32)
        token_time = jnp.einsum(
            "krcs,kse->krce", member, time_proj, precision=lax.Precision.HIGHEST
        ).reshape(tokens, 2 * width)
        qkv = jnp.dot(normed, w_attn, preferred_element_type=jnp.float32)
        query = (qkv[:, :width] + token_time[:, :width]).astype(jnp.bfloat16)
        keys = qkv[:, width : 2 * width].astype(jnp.bfloat16)
        values = (qkv[:, 2 * width :] + token_time[:, width:]).astype(jnp.bfloat16)
        paired = jnp.stack([keys, values]).reshape(2, canvases, band_rows, columns, width)
        paired = padded_2(paired, (("band", 2),), reach)
        paired = jnp.pad(paired, ((0, 0), (0, 0), (0, 0), (reach, reach), (0, 0)))
        key_win = neighbour_stack(paired[0], band_rows, columns)
        value_win = neighbour_stack(paired[1], band_rows, columns)
        seg_win = neighbour_stack(seg_rims[batch_index], band_rows, columns)
        allowed = (seg_win == seg_code[batch_index].reshape(1, tokens))[..., None]
        query_wide = query.astype(jnp.float32)
        raw = head_total(query_wide[None] * key_win.astype(jnp.float32), head_sum)
        logit_scores = raw * score_scale + rel_bias[:, None, :]
        masked = jnp.where(allowed, logit_scores, -1e30)
        peak = jnp.max(masked, 0)
        raised = jnp.where(allowed, jnp.exp(masked - peak), 0.0)
        probs_full = raised / jnp.sum(raised, 0)
        attention_probabilities = probs_full.astype(jnp.bfloat16)
        probs_wide = head_widen(attention_probabilities, head_spread)
        mixed_values = jnp.sum(probs_wide.astype(jnp.float32) * value_win.astype(jnp.float32), 0)
        attended = mixed_values.astype(jnp.bfloat16)
        branch = jnp.dot(attended, w_out, preferred_element_type=jnp.float32)
        resid = inputs + branch
        unit_two, scaled_two, normed_two = normalize(resid, norm_gains[:, 1])
        hidden_in = normed_two.astype(jnp.bfloat16)
        pre_act = jnp.dot(hidden_in, w_in, preferred_element_type=jnp.float32)
        activated = jax.nn.gelu(pre_act, approximate=False).astype(jnp.bfloat16)
        mlp_y = jnp.dot(activated, w_back, preferred_element_type=jnp.float32)
        filled = (seg_here >= 0).reshape(tokens, 1)
        outputs.append(
            jnp.where(filled, resid + mlp_y, 0.0)
            .astype(jnp.bfloat16)
            .reshape(canvases, band_rows, columns, width)
        )
        grad_y = cotangent[batch_index].reshape(tokens, width)
        grad_f = jnp.where(filled, grad_y, jnp.zeros_like(grad_y))
        grad_back = rows_dot(activated, grad_f)
        grad_act = back_dot(grad_f, w_back)
        gelu_out, gelu_pull = jax.vjp(partial(jax.nn.gelu, approximate=False), pre_act)
        grad_pre = gelu_pull(grad_act)[0].astype(jnp.bfloat16)
        grad_in = rows_dot(hidden_in, grad_pre)
        grad_hidden = back_dot(grad_pre, w_in)
        grad_resid = jnp.where(filled, grad_y.astype(jnp.float32), 0.0) + normalize_back(
            unit_two, scaled_two, norm_gains[:, 1], grad_hidden
        )
        gain_two = jnp.sum(grad_hidden * unit_two, 0)
        grad_branch = grad_resid.astype(jnp.bfloat16)
        grad_out = rows_dot(attended, grad_branch)
        grad_att = back_dot(grad_branch, w_out).astype(jnp.bfloat16)
        grad_att_wide = grad_att.astype(jnp.float32)
        grad_probs = head_total(grad_att_wide[None] * value_win.astype(jnp.float32), head_sum)
        centered = jnp.sum(probs_full * grad_probs, 0)
        grad_scores = (probs_full * (grad_probs - centered)).astype(jnp.bfloat16)
        bias_accum = bias_accum + jnp.sum(grad_scores.astype(jnp.float32), axis=1)
        scores_wide = head_widen(grad_scores, head_spread).astype(jnp.float32)
        grad_query = jnp.sum(scores_wide * key_win.astype(jnp.float32), 0) * score_scale
        key_summed = (
            spread_back(scores_wide * query_wide[None], canvases, band_rows, columns) * score_scale
        )
        value_summed = spread_back(
            probs_wide.astype(jnp.float32) * grad_att_wide[None], canvases, band_rows, columns
        )
        pair_grad = jnp.stack([key_summed, value_summed])[:, :, :, reach : reach + columns]
        upper_rim = pair_grad[:, :, :reach]
        lower_rim = pair_grad[:, :, band_rows + reach :]
        owned_rows = pair_grad[:, :, reach : reach + band_rows]
        from_below = shifted(upper_rim.astype(jnp.bfloat16), "band", -1).astype(upper_rim.dtype)
        from_above = shifted(lower_rim.astype(jnp.bfloat16), "band", 1).astype(lower_rim.dtype)
        owned_rows = owned_rows.at[:, :, band_rows - reach :].add(from_below)
        owned_rows = owned_rows.at[:, :, :reach].add(from_above)
        grad_keys = owned_rows[0].reshape(tokens, width).astype(jnp.bfloat16)
        grad_values = owned_rows[1].reshape(tokens, width).astype(jnp.bfloat16)
        grad_q_low = grad_query.astype(jnp.bfloat16)
        member_low = member.astype(jnp.bfloat16).reshape(canvases, band_rows * columns, slots)
        slot_query = jnp.einsum(
            "kns,knd->ksd",
            member_low,
            grad_q_low.reshape(canvases, band_rows * columns, width),
            preferred_element_type=jnp.float32,
        )
        slot_value = jnp.einsum(
            "kns,knd->ksd",
            member_low,
            grad_values.reshape(canvases, band_rows * columns, width),
            preferred_element_type=jnp.float32,
        )
        slot_part = jnp.concatenate([slot_query, slot_value], -1)
        slot_total = lax.psum(slot_part.astype(jnp.bfloat16), "band")
        slot_low = slot_total.reshape(canvases * slots, 2 * width)
        time_grads.append(back_dot(slot_low, w_time).reshape(canvases, slots, width))
        grad_time_in = rows_dot(time_rows, slot_low) * band_share
        grad_qkv = jnp.concatenate([grad_q_low, grad_keys, grad_values], -1)
        grad_attn = rows_dot(normed, grad_qkv)
        grad_normed = back_dot(grad_qkv, w_attn)
        grad_inputs = grad_resid + normalize_back(
            unit_one, scaled_one, norm_gains[:, 0], grad_normed
        )
        gain_one = jnp.sum(grad_normed * unit_one, 0)
        input_grads.append(grad_inputs.reshape(canvases, band_rows, columns, width))
        micro_grads = (
            grad_attn,
            grad_time_in,
            grad_out,
            grad_in,
            grad_back,
            jnp.stack([gain_one, gain_two], 1),
        )
        accum = micro_grads if accum is None else jax.tree.map(jnp.add, accum, micro_grads)
    wide_sums = jax.tree.map(
        lambda part: part.astype(jnp.float32),
        lax.psum_scatter(shortened(accum), "canvas", scatter_dimension=0, tiled=True),
    )
    shards = jax.tree.map(
        lambda part: part.astype(jnp.float32),
        lax.psum_scatter(shortened(wide_sums), "band", scatter_dimension=0, tiled=True),
    )
    bias_grad = lax.psum(bias_accum, ("canvas", "band"))
    return (
        jnp.stack(outputs),
        jnp.stack(input_grads),
        jnp.stack(time_grads),
        shards[5],
        shards[0],
        shards[1],
        bias_grad,
        shards[2],
        shards[3],
        shards[4],
    )


MESH = pl.DeviceIdType.MESH
BF, F32 = jnp.bfloat16, jnp.float32
EPS = 1e-5
TOK, HALF, D, QC, FH = 544, 272, 1152, 640, 2304
KEYS, KW, PADK = 784, 512, 80
SCALE = 72 ** -0.5
NEG = -1e30


def dot(a, b):
    return jnp.dot(a, b, preferred_element_type=F32)


def dot_nt(a, b):
    return lax.dot_general(a, b, (((1,), (1,)), ((), ())), preferred_element_type=F32)


def dot_tn(a, b):
    return lax.dot_general(a, b, (((0,), (0,)), ((), ())), preferred_element_type=F32)


def norm(v):
    center = v - jnp.mean(v, -1, keepdims=True)
    r = lax.rsqrt(jnp.mean(center * center, -1, keepdims=True) + EPS)
    return center * r, r


def norm_back(n, r, e):
    return r * (e - jnp.mean(e, -1, keepdims=True) - n * jnp.mean(e * n, -1, keepdims=True))


def place():
    c, b = lax.axis_index("canvas"), lax.axis_index("band")
    return c, b, b // 2, lax.rem(b, 2)


def greet(devs):
    bar = pltpu.get_barrier_semaphore()
    for dev in devs:
        pl.semaphore_signal(bar, 1, device_id=dev, device_id_type=MESH)
    pl.semaphore_wait(bar, len(devs))


def remote(src, dst, ss, rs, dev):
    return pltpu.make_async_remote_copy(src, dst, ss, rs, device_id=dev, device_id_type=MESH)


def head_window(h):
    ws = pl.multiple_of(jnp.minimum(80 * h // 128, 3) * 128, 128)
    lane = lax.broadcasted_iota(jnp.int32, (1, 256), 1) + ws - 80 * h
    hm = jnp.where((lane >= 0) & (lane < 80), 1.0, 0.0).astype(BF)
    return pl.ds(ws, 256), hm


def toeplitz(base, h):
    row = jnp.broadcast_to(base[pl.ds(h, 1)], (HALF, KW))
    return pltpu.roll(row, 0, 1, stride=1, stride_axis=0)


GSPEC = {"A": (144, 640, 640), "O": (80, 384, 384), "I0": (144, 384, 384), "I1": (144, 384, 384), "B0": (144, 384, 384), "B1": (144, 384, 384)}
GNAMES = list(GSPEC)


FIRST, STEP, SPARE = 4.0, 1.7, -2


class Gather:
    def __init__(self, own, full, s_sem, r_sem, y_sem, l_sem, pend):
        self.own, self.full, self.pend = dict(zip(GNAMES, own)), dict(zip(GNAMES, full)), pend
        self.s_sem, self.r_sem, self.y_sem, self.l_sem = s_sem, r_sem, y_sem, l_sem
        self.c, self.b, self.y, _ = place()
        self.z, self.x = self.c // 2, lax.rem(self.c, 2)
        z = self.z
        self.zp = [jnp.where(z == 0, t[0], jnp.where(z == 1, t[1], jnp.where(z == 2, t[2], t[3]))) for t in ((1, 0, 3, 2), (2, 2, 1, 1), (3, 3, 0, 0))]
        self.xdev, self.ydev = {"canvas": self.c + 1 - 2 * self.x}, {"band": self.b + 2 - 4 * self.y}
        self.count = dict.fromkeys(GNAMES, 0)

    def part(self, name, src, plane, side):
        rows, wide, mid = GSPEC[name]
        at = pl.ds(pl.multiple_of(src * rows, 16), rows)
        if plane:
            return at, pl.ds(pl.multiple_of(wide * side, 128), wide + mid)
        return at, pl.ds(pl.multiple_of((wide + mid) * side, 128), wide)

    def send(self, name, src, dev, plane, first=False, when=None):
        n = GNAMES.index(name)
        at, cols = self.part(name, src, plane, self.y)
        held = self.full[name].at[at, cols] if self.own[name] is None or not first else self.own[name].at[:, cols]
        cp = remote(held, self.full[name].at[at, cols],
                    self.s_sem.at[n, self.count[name]], (self.r_sem if plane else self.y_sem).at[n, src], dev)
        self.count[name] += 1
        if when is None:
            cp.start()
            self.pend.append(cp.wait_send)
        else:
            pl.when(when)(cp.start)
            self.pend.append(lambda: pl.when(when)(cp.wait_send))

    def own_sends(self, name):
        rows = GSPEC[name][0]
        for up in (1, -1):
            to = self.z + up
            self.send(name, self.c, {"canvas": jnp.clip(to, 0, 3) * 2 + self.x}, True, True, (to >= 0) & (to <= 3))
        self.send(name, self.c, self.xdev, True, True)
        if self.own[name] is not None:
            pltpu.make_async_copy(self.own[name], self.full[name].at[pl.ds(pl.multiple_of(self.c * rows, 16), rows)],
                                  self.l_sem.at[GNAMES.index(name)]).start()

    def wait(self, name, src, plane):
        at, cols = self.part(name, src, plane, self.y if plane else 1 - self.y)
        view = self.full[name].at[at, cols]
        pltpu.make_async_copy(view, view, (self.r_sem if plane else self.y_sem).at[GNAMES.index(name), src]).wait()

    def from_z(self, name, i):
        src = self.zp[i] * 2 + self.x
        self.wait(name, src, True)
        to = jnp.where(self.zp[i] < self.z, self.z + 1, self.z - 1)
        self.send(name, src, {"canvas": jnp.clip(to, 0, 3) * 2 + self.x}, True, False, (to >= 0) & (to <= 3))
        self.send(name, src, self.xdev, True)
        self.send(name, src, self.ydev, False)

    def from_x(self, name, i):
        src = (self.z if i == 0 else self.zp[i - 1]) * 2 + 1 - self.x
        self.wait(name, src, True)
        self.send(name, src, self.ydev, False)

    def complete(self, name):
        rows = GSPEC[name][0]
        for d in range(1, 8):
            self.wait(name, lax.rem(self.c + d, 8), False)
        if self.own[name] is not None:
            pltpu.make_async_copy(self.own[name], self.full[name].at[pl.ds(pl.multiple_of(self.c * rows, 16), rows)],
                                  self.l_sem.at[GNAMES.index(name)]).wait()

    def events(self, name):
        return [partial(self.from_z, name, 0), partial(self.from_x, name, 0), partial(self.from_z, name, 1), partial(self.from_x, name, 1),
                partial(self.from_z, name, 2), partial(self.from_x, name, 2), partial(self.from_x, name, 3)]


def gather_forward_kernel(attn_in, time_in, mlp_in, O, mlp_out, lat_in, cot_in, gains, te, seg_row, seg_col, base,
                          xn_o, q_o, kb_o, vb_o, lse_o, o_o, hres_o, hn_o, g_o, gp_o, df_o, gb0_o, gb1_o,
                          WA_o, WO_o, WI0_o, WI1_o, WB0_o, WB1_o, te_o, mask_o, onehot_o, ti,
                          WA, WO, WI0, WI1, WB0, WB1, xn, q, kb, vb, lse, o, hres, hn, g, gp, df, gb0, gb1, te_in, seg_in, col_in, onehot,
                          tp_send, tp_recv, tmix, mask, toep, of, x_send, x_recv, lat, cot,
                          s_sem, r_sem, y_sem, l_sem, es, er, gs, gr, cs, cr,
                          xs, xr, ts, tr, ks, kr, as_, ar, hs, hr, fs, fr, ls, outs):
    blocks = [(attn_in, 0), (attn_in, 1), (attn_in, 2), (time_in, 0), (time_in, 1)] + [(mlp_in, j) for j in range(4)]
    spots = [g.at[144 * (i // 2):144 * (i // 2) + 144, D * (i % 2):D * (i % 2) + D] for i in range(9)]
    loads = [pltpu.make_async_copy(lat_in, lat, ls.at[0]), pltpu.make_async_copy(cot_in, cot, ls.at[1])]
    loads += [pltpu.make_async_copy(src.at[:, D * j:D * j + D], spots[i], ls.at[2 + i]) for i, (src, j) in enumerate(blocks)]
    for cp in loads:
        cp.start()
    c, b, y, k = place()
    sib, ynb = {"band": b + 1 - 2 * k}, {"band": b + 2 - 4 * y}
    peers = [lax.rem(c + d, 8) for d in range(1, 8)]
    pend, saves = [], []

    def go(src, dst, ss, rs, dev):
        cp = remote(src, dst, ss, rs, dev)
        cp.start()
        pend.append(cp.wait_send)

    def arrive(view, sem):
        pltpu.make_async_copy(view, view, sem).wait()

    def save(src, dst):
        cp = pltpu.make_async_copy(src, dst, outs.at[len(saves)])
        cp.start()
        saves.append(cp)

    shares = [mlp_out.at[pl.ds(pl.multiple_of(288 * k + 144 * i, 16), 144)] for i in range(2)]
    gat = Gather((None, O, None, None, *shares), (WA, WO, WI0, WI1, WB0, WB1), s_sem, r_sem, y_sem, l_sem, pend)
    queue, ends = [], {}
    for name, nxt in (("A", "I0"), ("O", "I1"), ("I0", "B0"), ("I1", "B1"), ("B0", None), ("B1", None)):
        steps = gat.events(name)
        if nxt:
            steps.insert(1, partial(gat.own_sends, nxt))
        queue += steps
        ends[name] = len(queue)

    total, clock = len(queue), [0.0]

    def tick(us):
        clock[0] += us
        while queue and FIRST + STEP * (total - len(queue)) <= clock[0]:
            queue.pop(0)()

    def complete(name):
        left = total - ends[name]
        while len(queue) > max(left + SPARE, 0):
            queue.pop(0)()
        gat.complete(name)
        clock[0] = max(clock[0], FIRST + STEP * (total - left))

    greet([{"band": lax.rem(b + d, 4)} for d in (1, 2, 3)] + [{"canvas": p} for p in peers])
    for i, p in enumerate(peers):
        go(te.at[p], te_in.at[c], es.at[i], er.at[6 - i], {"canvas": p})
    te_in[c] = te[c]
    for i in range(3):
        go(seg_row, seg_in.at[b], gs.at[i], gr.at[2 - i], {"band": lax.rem(b + i + 1, 4)})
    seg_in[b] = seg_row[...]
    go(seg_col, col_in.at[k], cs.at[0], cr.at[0], sib)
    col_in[k] = seg_col[...]
    mine_rows = pl.ds(pl.multiple_of(144 * c, 16), 144)

    def pick_matrix(source, wide):
        gb0[:, 0:wide] = jnp.where(lax.broadcasted_iota(jnp.int32, (D, wide), 0) == source, 1.0, 0.0).astype(BF)

    lane = lax.broadcasted_iota(jnp.int32, (1, QC), 1).astype(F32)
    place_h = jnp.floor((lane + 0.5) * (1.0 / 80))
    inside = lane - 80 * place_h
    pick_matrix(jnp.where(inside < 71.5, 144 * place_h + inside + 72 * k.astype(F32), -1.0).astype(jnp.int32), QC)
    for i in range(3):
        loads[2 + i].wait()
        WA[mine_rows, QC * i:QC * i + QC] = dot(spots[i][...], gb0[:, 0:QC]).astype(BF)
    gat.own_sends("A")
    gat.own_sends("O")
    for i in range(2):
        loads[5 + i].wait()
        ti[:, QC * i:QC * i + QC] = dot(spots[3 + i][...], gb0[:, 0:QC]).astype(BF)

    def pick_hidden(s, W):
        for j in range(4):
            n = lax.broadcasted_iota(jnp.int32, (1, 384), 1).astype(F32) + 256 * j
            cc = jnp.floor((n + 0.5) * (1.0 / 144))
            fits = (cc > 2 * j - 0.5) & (cc < 2 * j + 1.5)
            pick_matrix(jnp.where(fits, 576 * (cc - 2 * j) + (n - 144 * cc) + 288 * k.astype(F32) + 144 * s, -1.0).astype(jnp.int32), 384)
            part = dot(spots[5 + j][...], gb0[:, 0:384]).astype(BF)
            if j:
                W[mine_rows, 256 * j:256 * j + 128] += part[:, 0:128]
                W[mine_rows, 256 * j + 128:256 * j + 384] = part[:, 128:]
            else:
                W[mine_rows, 0:384] = part

    loads[0].wait()
    mine = pl.ds(pl.multiple_of(HALF * k, 16), HALF)
    other = pl.ds(pl.multiple_of(HALF * (1 - k), 16), HALF)
    for m in range(2):
        n, _ = norm(lat[m].astype(F32))
        xn[m, mine] = (n * gains[0:1]).astype(BF)
        go(xn.at[m, mine], xn.at[m, mine], xs.at[m], xr.at[m], sib)
        if m == 0:
            for i in range(7):
                arrive(te_in.at[lax.rem(c + i + 1, 8)], er.at[i])
            for p in range(8):
                tp_send[16 * p:16 * p + 16] = dot(te_in[p], ti[...]).astype(BF)
            for i, p in enumerate(peers):
                go(tp_send.at[pl.ds(pl.multiple_of(16 * p, 16), 16)], tp_recv.at[6 - i], ts.at[i], tr.at[6 - i], {"canvas": p})
    save(te_in, te_o)
    for i in range(4):
        loads[7 + i].wait()
    pick_hidden(0, WI0)
    arrive(col_in.at[1 - k], cr.at[0])
    for i in range(3):
        arrive(seg_in.at[lax.rem(b + i + 1, 4)], gr.at[i])
    slot = lax.rem(lax.broadcasted_iota(jnp.int32, (1, 32), 1), 16)
    lane = lax.broadcasted_iota(jnp.int32, (1, KW), 1)

    def column(t):
        return t - 34 * jnp.floor((t + 0.5) * (1.0 / 34))

    colq = column(lax.broadcasted_iota(jnp.int32, (HALF, 1), 0).astype(F32))
    near = jnp.abs(colq - column(lax.broadcasted_iota(jnp.int32, (1, KW), 1).astype(F32) + 22)) < 2.5
    for j in range(2):
        at = 2 * y + j
        before, here, after = seg_in[jnp.maximum(at - 1, 0)], seg_in[at], seg_in[jnp.minimum(at + 1, 3)]
        before = pltpu.roll(jnp.where(at > 0, before, 0.0), KW - HALF, 1)
        after = pltpu.roll(jnp.where(at < 3, after, 0.0), HALF, 1)
        keys = jnp.where(lane < 80, before, jnp.where(lane < 352, here, jnp.where(lane < 432, after, 0.0)))
        for m in range(2):
            code = col_in[j, m, :, 0:1]
            mask[m, j] = jnp.where((code == keys[m:m + 1]) & near, 0.0, NEG).astype(BF)
            hit = (code.astype(jnp.int32) + (5 * m - 2) == slot) & (code >= 1.5)
            onehot[m, HALF * j:HALF * j + HALF] = jnp.where(hit, 1.0, 0.0).astype(BF)
    loads[1].wait()
    for m in range(2):
        filled = jnp.where(col_in[k, m, :, 0:1] >= 1.5, 1.0, 0.0)
        rows = pl.ds(pl.multiple_of(TOK * m + HALF * k, 16), HALF)
        df[rows] = (cot[m].astype(F32) * filled).astype(BF)
        go(df.at[rows], df.at[rows], fs.at[m], fr.at[m], sib)
    save(mask, mask_o)
    save(onehot, onehot_o)
    tick(13.0)
    for i in range(7):
        arrive(tp_recv.at[i], tr.at[i])
    tproj = tp_send[pl.ds(pl.multiple_of(16 * c, 16), 16)].astype(F32)
    for i in range(7):
        tproj = tproj + tp_recv[i].astype(F32)
    hi = tproj.astype(BF)
    tmix[0:16] = hi
    tmix[16:32] = (tproj - hi.astype(F32)).astype(BF)
    dead = pl.ds(pl.multiple_of(y * 624, 16), 80)
    for m in range(2):
        for ref in (kb, vb):
            ref[m, dead] = jnp.zeros((80, QC), BF)
            ref[m, 704:784] = jnp.zeros((80, QC), BF)
    of[...] = jnp.zeros_like(of)
    lse[...] = jnp.zeros_like(lse)
    pick_hidden(1, WI1)
    complete("A")
    save(WA, WA_o)

    edge = pl.ds(pl.multiple_of(544 - 464 * y, 16), 80)
    land = pl.ds(pl.multiple_of(624 * y, 16), 80)
    land_here = pl.ds(pl.multiple_of(624 * (1 - y), 16), 80)
    for m in range(2):
        arrive(xn.at[m, other], xr.at[m])
        x = xn[m]
        kb[m, 80:624] = dot(x, WA[:, QC:2 * QC]).astype(BF)
        tick(1.2)
        vb[m, 80:624] = (dot(x, WA[:, 2 * QC:]) + dot(onehot[m], tmix[:, QC:])).astype(BF)
        for i, ref in enumerate((kb, vb)):
            go(ref.at[m, edge], ref.at[m, land], ks.at[m, i], kr.at[m, i], ynb)
        q[m] = (dot(x, WA[:, :QC]) + dot(onehot[m], tmix[:, :QC])).astype(BF)
        tick(2.5)
    save(xn, xn_o)
    save(q, q_o)
    for m in range(2):
        for i, ref in enumerate((kb, vb)):
            arrive(ref.at[m, land_here], kr.at[m, i])
    save(kb, kb_o)
    save(vb, vb_o)

    def head(h, _):
        win, hm = head_window(h)
        toep[...] = toeplitz(base, h)
        lane_h = lax.broadcasted_iota(jnp.int32, (1, 128), 1) == h

        def tile(t, _):
            m, j = t // 2, lax.rem(t, 2)
            rows = pl.ds(pl.multiple_of(HALF * j, 16), HALF)
            krows = pl.ds(pl.multiple_of(HALF * j, 16), KW)
            s = dot_nt(q[m, rows, win] * hm, kb[m, krows, win])
            s = s * SCALE + (toep[...] + mask[m, j])
            peak = jnp.max(s, -1, keepdims=True)
            e = jnp.exp(s - peak)
            total = jnp.sum(e, -1, keepdims=True)
            p = (e * (1.0 / total)).astype(BF)
            of[m, rows, win] += dot(p, vb[m, krows, win] * hm)
            lse[m, rows] = jnp.where(lane_h, peak + jnp.log(total), lse[m, rows])
            return 0

        return lax.fori_loop(0, 4, tile, 0)

    for n in range(8):
        lax.fori_loop(n, n + 1, head, 0)
        tick(3.1)
    save(lse, lse_o)
    for m in range(2):
        o[m] = of[m].astype(BF)
    save(o, o_o)
    complete("O")
    save(WO, WO_o)

    for m in range(2):
        x_send[m] = dot(o[m, other], WO[...]).astype(BF)
        go(x_send.at[m], x_recv.at[m], as_.at[m], ar.at[m], sib)
    for m in range(2):
        hres[m] = lat[m].astype(F32) + dot(o[m, mine], WO[...])
    tick(4.0)
    for m in range(2):
        arrive(x_recv.at[m], ar.at[m])
        hv = hres[m] + x_recv[m].astype(F32)
        hres[m] = hv
        n, _ = norm(hv)
        hn[m, mine] = (n * gains[1:2]).astype(BF)
        go(hn.at[m, mine], hn.at[m, mine], hs.at[m], hr.at[m], sib)
        tick(2.5)
    save(hres, hres_o)
    for m in range(2):
        arrive(hn.at[m, other], hr.at[m])
    save(hn, hn_o)
    for s, W in enumerate((WI0, WI1)):
        complete("I0" if s == 0 else "I1")
        save(W, (WI0_o, WI1_o)[s])
        for m in range(2):
            def up(i, _):
                cols = pl.ds(pl.multiple_of(i * 384, 128), 384)
                put = pl.ds(pl.multiple_of(i * 384 + D * s, 128), 384)
                u = dot(hn[m], W[:, cols])
                phi = 0.5 + 0.5 * lax.erf(u * (0.5 ** 0.5))
                g[pl.ds(TOK * m, TOK), put] = (u * phi).astype(BF)
                gp[pl.ds(TOK * m, TOK), put] = (phi + u * (jnp.exp(-0.5 * u * u) * 0.3989422804014327)).astype(BF)
                return 0

            lax.fori_loop(0, 3, up, 0)
            tick(3.3)
    save(g, g_o)
    save(gp, gp_o)
    for m in range(2):
        rows = pl.ds(pl.multiple_of(TOK * m + HALF * (1 - k), 16), HALF)
        arrive(df.at[rows], fr.at[m])
    save(df, df_o)
    for s, grad in enumerate((gb0, gb1)):
        for i in range(3):
            cols = pl.ds(384 * i, 384)
            fill_part(grad, g, df, cols, D * s, cols)
            tick(1.3)
        save(grad, (gb0_o, gb1_o)[s])
    for s, W in enumerate((WB0, WB1)):
        complete("B0" if s == 0 else "B1")
        save(W, (WB0_o, WB1_o)[s])
    for cp in saves:
        cp.wait()
    for wait in pend:
        wait()


def gather_forward(p, cot):
    S = jax.ShapeDtypeStruct
    dma = pltpu.SemaphoreType.DMA
    V, anyspace = pl.BlockSpec(memory_space=pltpu.VMEM), pl.BlockSpec(memory_space=pl.ANY)
    weights = [(D, 3 * QC), (QC, D), (D, D), (D, D), (D, D), (D, D)]
    kept = [((2, TOK, D), BF), ((2, TOK, QC), BF), ((2, KEYS, QC), BF), ((2, KEYS, QC), BF), ((2, TOK, 128), F32), ((2, TOK, QC), BF),
            ((2, HALF, D), F32), ((2, TOK, D), BF), ((2 * TOK, FH), BF), ((2 * TOK, FH), BF), ((2 * TOK, D), BF), ((D, D), BF), ((D, D), BF)]
    return pl.pallas_call(
        gather_forward_kernel,
        out_shape=[S(s, t) for s, t in kept] + [S(s, BF) for s in weights]
        + [S((8, 16, 144), BF), S((2, 2, HALF, KW), BF), S((2, TOK, 32), BF), S((144, 2 * QC), BF)],
        in_specs=[anyspace] * 7 + [V] * 5, out_specs=[anyspace] * 22 + [V],
        scratch_shapes=[pltpu.VMEM(s, BF) for s in weights] + [pltpu.VMEM(s, t) for s, t in kept]
        + [pltpu.VMEM((8, 16, 144), BF), pltpu.VMEM((4, 8, KW), F32), pltpu.VMEM((2, 2, HALF, 128), F32), pltpu.VMEM((2, TOK, 32), BF),
           pltpu.VMEM((128, 2 * QC), BF), pltpu.VMEM((7, 16, 2 * QC), BF), pltpu.VMEM((32, 2 * QC), BF), pltpu.VMEM((2, 2, HALF, KW), BF),
           pltpu.VMEM((HALF, KW), F32), pltpu.VMEM((2, TOK, QC), F32), pltpu.VMEM((2, HALF, D), BF), pltpu.VMEM((2, HALF, D), BF),
           pltpu.VMEM((2, HALF, D), BF), pltpu.VMEM((2, HALF, D), BF),
           dma((6, 16)), dma((6, 8)), dma((6, 8)), dma((6,)), dma((7,)), dma((7,)), dma((3,)), dma((3,)), dma((1,)), dma((1,)),
           dma((2,)), dma((2,)), dma((7,)), dma((7,)), dma((2, 2)), dma((2, 2)), dma((2,)), dma((2,)), dma((2,)), dma((2,)), dma((2,)), dma((2,)), dma((11,)), dma((22,))],
        compiler_params=pltpu.CompilerParams(collective_id=1, has_side_effects=True, vmem_limit_bytes=127 * 2 ** 19),
        name="gather_forward")(*p["raw"], p["lat"], cot, p["gains"], p["te"], p["seg_row"], p["seg_col"], p["base"])


def prologue(latents, segment_ids, time_embed, norm_gains, attn_in, time_in, rel_bias, out_proj, mlp_in, mlp_out, cotangent):
    c, b, y, k = place()

    def pick(v, axis):
        return lax.dynamic_index_in_dim(v, k, axis, keepdims=False)

    raw = (attn_in, time_in, mlp_in, jnp.pad(pick(out_proj.reshape(2, 72, D), 0), ((0, 8), (0, 0))), mlp_out)
    code = (segment_ids.reshape(2, HALF) + 2).astype(F32)
    seg_row = jnp.pad(code, ((0, 6), (80, KW - 80 - HALF)))
    seg_col = jnp.broadcast_to(code[..., None], (2, HALF, 128))
    te = jnp.pad(time_embed.reshape(10, D), ((0, 6), (0, 0))).reshape(16, 8, 144).transpose(1, 0, 2)
    bias = pick(rel_bias.reshape(25, 8, 2), 2)
    base = jnp.full((8, KW), NEG, F32)
    places = [80 + 34 * dr + dc for dr in range(-2, 3) for dc in range(-2, 3)]
    base = base.at[:, jnp.array(places)].set(bias.T)
    filled = (segment_ids.reshape(2, HALF, 1) >= 0).astype(F32)
    return dict(raw=raw, te=te, seg_row=seg_row, seg_col=seg_col, base=base, filled=filled, lat=latents.reshape(2, HALF, D), gains=norm_gains.T)


RSPEC = {"A": (144, 640, 640), "O": (80, 384, 384), "I0": (144, 384, 384), "I1": (144, 384, 384), "B0": (144, 384, 384), "B1": (144, 384, 384)}
KEEP = {"A": (36, 48, 4), "I0": (36, 48, 4), "I1": (36, 48, 4), "O": (36, 48, 2), "B0": (144, 144, 2), "B1": (144, 144, 2)}
ORDER = (1, 3, 2, 0)


def scatter_scratch(name):
    rows, wide, mid = RSPEC[name]
    slab = wide + mid
    dma = pltpu.SemaphoreType.DMA
    _, held, sources = KEEP[name]
    sends = {"A": 4, "I": 4, "O": 2, "B": 1}[name[0]]
    return [pltpu.VMEM((8 * rows, wide), BF), pltpu.VMEM((4 * rows, slab), BF), pltpu.VMEM((3 * rows, slab), BF),
            pltpu.VMEM((sends, held, slab), BF), pltpu.VMEM((sources, held, slab), BF),
            dma((4,)), dma((4,)), dma((8,)), dma((8,)), dma((3,)), dma((3,)), dma((4,)), dma((4,))]


N_SCATTER = 13


class Scatter:
    def __init__(self, name, grad, total, scratch, pend):
        self.name, self.grad, self.total, self.pend = name, grad, total, pend
        (self.yr, self.xr, self.zr, self.stage, self.fr, self.ys, self.yw, self.xs, self.xw, self.zs, self.zw, self.fs, self.fw) = scratch
        self.rows, self.wide, self.mid = RSPEC[name]
        self.c, self.b, self.y, self.k = place()
        self.z, self.x = self.c // 2, lax.rem(self.c, 2)
        y, w, l = self.y, self.wide, self.mid
        self.slab = pl.ds(pl.multiple_of(w * y, 128), w + l)
        self.mids = pl.ds(w, l)
        self.side = pl.ds(pl.multiple_of((w + l) * y, 128), w)
        self.away = pl.ds(pl.multiple_of((w + l) * (1 - y), 128), w)
        self.slab_mid = pl.ds(pl.multiple_of(w * (1 - y), 128), l)
        self.slab_side = pl.ds(pl.multiple_of(l * y, 128), w)
        self.xdev, self.ydev = {"canvas": self.c + 1 - 2 * self.x}, {"band": self.b + 2 - 4 * self.y}

    def at(self, group):
        return pl.ds(pl.multiple_of(group * self.rows, 16), self.rows)

    def pair(self, d):
        return pl.ds(pl.multiple_of(lax.rem(self.z + d, 4) * (2 * self.rows), 16), 2 * self.rows)

    def go(self, make):
        make().start()
        self.pend.append(make)

    def parts(self):
        return self.away, self.mids, self.side

    def group(self, d, x):
        return self.at(2 * lax.rem(self.z + d, 4) + x)

    def send_y(self):
        for d in ORDER:
            self.go(lambda d=d: remote(self.grad.at[self.pair(d), self.away], self.yr.at[self.pair(d)], self.ys.at[d], self.yw.at[d], self.ydev))

    def send_mid(self):
        for d in ORDER:
            self.go(lambda d=d: remote(self.grad.at[self.group(d, 1 - self.x), self.mids], self.xr.at[pl.ds(self.rows * d, self.rows), self.slab_mid],
                                       self.xs.at[d], self.xw.at[d], self.xdev))

    def side_x(self, d):
        rows2 = self.pair(d)
        pltpu.make_async_copy(self.yr.at[rows2], self.yr.at[rows2], self.yw.at[d]).wait()
        self.grad[rows2, self.side] += self.yr[rows2]
        self.go(lambda: remote(self.grad.at[self.group(d, 1 - self.x), self.side], self.xr.at[pl.ds(self.rows * d, self.rows), self.slab_side],
                               self.xs.at[4 + d], self.xw.at[4 + d], self.xdev))

    def sum_x(self, d):
        rows = pl.ds(self.rows * d, self.rows)
        for view, sem in ((self.xr.at[rows, self.slab_mid], d), (self.xr.at[rows, self.slab_side], 4 + d)):
            pltpu.make_async_copy(view, view, self.xw.at[sem]).wait()
        return self.grad[self.group(d, self.x), self.slab] + self.xr[rows]

    def send_z(self, d):
        self.grad[self.group(d, self.x), self.slab] = self.sum_x(d)
        self.go(lambda: remote(self.grad.at[self.group(d, self.x), self.slab], self.zr.at[pl.ds((3 - d) * self.rows, self.rows)], self.zs.at[d - 1],
                               self.zw.at[3 - d], {"canvas": 2 * lax.rem(self.z + d, 4) + self.x}))

    def dests(self):
        sources = KEEP[self.name][2]
        if self.name[0] == "B":
            return [(0, 2 * self.k + int(self.name[1]))]
        return [(i, 2 * self.k + i if sources == 2 else i) for i in range(sources)]

    def finish(self):
        acc = self.sum_x(0).astype(F32)
        for i in (2, 0, 1):
            rows = pl.ds(i * self.rows, self.rows)
            pltpu.make_async_copy(self.zr.at[rows], self.zr.at[rows], self.zw.at[i]).wait()
            acc = acc + self.zr[rows].astype(F32)
        n, held, sources = KEEP[self.name]
        slab = self.wide + self.mid
        if self.name[0] == "B":
            self.stage[0] = acc.astype(BF)
        else:
            self.total[0:self.rows, 0:slab] = acc
            for i in range(sources):
                self.stage[i, 0:n] = self.total[n * i:n * i + n, 0:slab].astype(BF)
                self.stage[i, n:held] = jnp.zeros((held - n, slab), BF)
        slot = self.b if sources == 4 else self.y
        for i, dest in self.dests():
            @pl.when(self.b == dest)
            def _():
                self.fr[slot] = self.stage[i]

            @pl.when(self.b != dest)
            def _():
                remote(self.stage.at[i], self.fr.at[slot], self.fs.at[i], self.fw.at[slot], {"band": dest}).start()

    def sent(self):
        for i, dest in self.dests():
            @pl.when(self.b != dest)
            def _():
                remote(self.stage.at[i], self.fr.at[0], self.fs.at[i], self.fw.at[0], {"band": dest}).wait_send()

    def collect(self, out):
        n, held, sources = KEEP[self.name]
        for i in range(sources):
            src = i if sources == 4 else 2 * i + self.y

            @pl.when(self.b != src)
            def _():
                pltpu.make_async_copy(self.fr.at[i], self.fr.at[i], self.fw.at[i]).wait()
        w, l = self.wide, self.mid
        for half in range(sources // 2):
            lo, hi = self.fr[half].astype(F32)[:n], self.fr[half + sources // 2].astype(F32)[:n]
            dst = out.at[half] if sources == 4 else out
            dst[:, 0:w] = lo[:, :w]
            dst[:, w:w + l] = lo[:, w:] + hi[:, :l]
            dst[:, w + l:] = hi[:, l:]


def everyone():
    c, b, y, k = place()
    return [{"band": lax.rem(b + d, 4)} for d in (1, 2, 3)] + [{"canvas": lax.rem(c + d, 8)} for d in range(1, 8)]


def fill_part(grad, left, right, cols, lefts, rights):
    def step(i, _):
        r = pl.multiple_of(i * 384, 128)
        grad[pl.ds(r, 384), cols] = dot_tn(left[:, pl.ds(r + lefts, 384)], right[:, rights]).astype(BF)
        return 0

    lax.fori_loop(0, grad.shape[0] // 384, step, 0)


def mlp_back_kernel(cot_in, filled, gains, WI0_in, WI1_in, WB0_in, WB1_in, hres, hn_in, g_in, gp, df_in, gb0, gb1,
                    out, dh, da, gain, out_b, grad_i0, grad_i1,
                    grad_b0, grad_b1, cot, WI0, WI1, WB0, WB1, hn, g, du, gi, x_send, x_recv, f_send, f_recv, dn, ds_, dr_, xs, xr, as_, ar, ls, gs, *scratch):
    c, b, y, k = place()
    sib = {"band": b + 1 - 2 * k}
    df = da
    loads = [pltpu.make_async_copy(src, dst, ls.at[i])
             for i, (src, dst) in enumerate(((gb0, grad_b0), (gb1, grad_b1), (WB0_in, WB0), (WB1_in, WB1), (g_in, g), (df_in, df), (gp, du), (hres, dh), (cot_in, cot), (hn_in, hn),
                                            (WI0_in, WI0), (WI1_in, WI1)))]
    for cp in loads:
        cp.start()
    greet([{"band": lax.rem(b + d, 4)} for d in (1, 2, 3)] + [{"canvas": c + 1 - 2 * lax.rem(c, 2)}] + [{"canvas": lax.rem(c + d, 8)} for d in (2, 4, 6)])
    pend = []
    rs = [Scatter("B0", grad_b0, None, scratch[:N_SCATTER], pend), Scatter("B1", grad_b1, None, scratch[N_SCATTER:], pend)]
    rs[1].fr, rs[1].fw = rs[0].fr, rs[0].fw

    def half(m, which):
        return pl.ds(pl.multiple_of(TOK * m + HALF * which, 16), HALF)

    for s in range(2):
        loads[s].wait()
        rs[s].send_y()
        if s == 0:
            rs[s].send_mid()
    for cp in loads[2:5]:
        cp.wait()
    for m in range(2):
        def down_other(i, _):
            cols = pl.ds(pl.multiple_of(i * 384, 128), 384)
            f_send[m, :, cols] = (dot(g[half(m, 1 - k), 0:D], WB0[:, cols]) + dot(g[half(m, 1 - k), D:], WB1[:, cols])).astype(BF)
            return 0

        lax.fori_loop(0, 3, down_other, 0)
        loads.append(remote(f_send.at[m], f_recv.at[m], ds_.at[m], dr_.at[m], sib))
        loads[-1].start()

        def down(i, _):
            cols = pl.ds(pl.multiple_of(i * 384, 128), 384)
            dn[m, :, cols] = dot(g[half(m, k), 0:D], WB0[:, cols]) + dot(g[half(m, k), D:], WB1[:, cols])
            return 0

        lax.fori_loop(0, 3, down, 0)

    def back_act(m, s):
        def step(i, _):
            r = pl.multiple_of(i * 384, 128)
            cols = pl.ds(pl.multiple_of(r + D * s, 128), 384)
            rows = pl.ds(TOK * m, TOK)
            du[rows, cols] = (dot_nt(df[rows], (WB0, WB1)[s][pl.ds(r, 384)]) * du[rows, cols].astype(F32)).astype(BF)
            return 0

        lax.fori_loop(0, 3, step, 0)

    rs[0].side_x(1)
    for cp in loads[5:12]:
        cp.wait()
    back_act(0, 0)
    rs[0].side_x(3)
    rs[0].send_z(1)
    for m in range(2):
        v = f_recv.at[m]
        pltpu.make_async_copy(v, v, dr_.at[m]).wait()
        out[m] = ((dh[m] + (dn[m] + v[...].astype(F32))) * filled[m]).astype(BF)
    back_act(1, 0)
    rs[0].side_x(2)
    rs[0].send_z(3)
    back_act(0, 1)
    rs[0].side_x(0)
    rs[1].send_mid()
    rs[0].send_z(2)
    back_act(1, 1)
    rs[1].side_x(1)
    saves = []
    for s in range(2):
        def step(i, _):
            r = pl.multiple_of(i * 384, 128)
            gi[s, pl.ds(r, 384)] = dot_tn(hn[:, pl.ds(r, 384)], du[:, D * s:D * s + D]).astype(BF)
            return 0

        lax.fori_loop(0, 3, step, 0)
        cp = pltpu.make_async_copy(gi.at[s], (grad_i0, grad_i1)[s], gs.at[s])
        cp.start()
        saves.append(cp)
        if s == 0:
            rs[1].side_x(3)
            rs[1].send_z(1)
            rs[0].finish()
        else:
            rs[1].side_x(2)
            rs[1].send_z(3)

    for m in range(2):
        def hid(i, _):
            r = pl.multiple_of(i * 384, 128)
            rows = pl.ds(r, 384)
            v = dot_nt(du[half(m, 1 - k), 0:D], WI0[rows]) + dot_nt(du[half(m, 1 - k), D:], WI1[rows])
            x_send[m, :, rows] = v.astype(BF)
            return 0

        lax.fori_loop(0, 3, hid, 0)
        cp = remote(x_send.at[m], x_recv.at[m], xs.at[m], xr.at[m], sib)
        cp.start()
        loads.append(cp)

        def hid_own(i, _):
            r = pl.multiple_of(i * 384, 128)
            rows = pl.ds(r, 384)
            dn[m, :, rows] = dot_nt(du[half(m, k), 0:D], WI0[rows]) + dot_nt(du[half(m, k), D:], WI1[rows])
            return 0

        lax.fori_loop(0, 3, hid_own, 0)
        if m == 0:
            rs[1].side_x(0)
            rs[1].send_z(2)
    gain_two = jnp.zeros((1, D), F32)
    for m in range(2):
        pltpu.make_async_copy(x_recv.at[m], x_recv.at[m], xr.at[m]).wait()
        grad = dn[m] + x_recv[m].astype(F32)
        n, r = norm(dh[m])
        gain_two = gain_two + jnp.sum(grad * n, 0, keepdims=True)
        v = cot[m].astype(F32) * filled[m] + norm_back(n, r, grad * gains[1:2])
        dh[m] = v
        da[half(m, k)] = v.astype(BF)
        cp = remote(da.at[half(m, k)], da.at[half(m, k)], as_.at[m], ar.at[m], sib)
        cp.start()
        loads.append(cp)
    gain[...] = jnp.broadcast_to(gain_two, (8, D))
    for m in range(2):
        v = da.at[half(m, 1 - k)]
        pltpu.make_async_copy(v, v, ar.at[m]).wait()
    rs[1].finish()
    rs[0].collect(out_b)
    rs[0].sent()
    rs[1].sent()
    for cp in saves:
        cp.wait()
    for cp in loads[12:]:
        cp.wait_send()
    for make in pend:
        make().wait_send()


def mlp_back(*args):
    S = jax.ShapeDtypeStruct
    dma = pltpu.SemaphoreType.DMA
    V, anyspace = pl.BlockSpec(memory_space=pltpu.VMEM), pl.BlockSpec(memory_space=pl.ANY)
    return pl.pallas_call(
        mlp_back_kernel,
        out_shape=[S((2, HALF, D), BF), S((2, HALF, D), F32), S((2 * TOK, D), BF), S((8, D), F32), S((144, D), F32), S((D, D), BF), S((D, D), BF)],
        in_specs=[anyspace, V, V] + [anyspace] * 11, out_specs=[V] * 5 + [anyspace] * 2,
        scratch_shapes=[pltpu.VMEM((D, D), BF), pltpu.VMEM((D, D), BF), pltpu.VMEM((2, HALF, D), BF)] + [pltpu.VMEM((D, D), BF)] * 4
        + [pltpu.VMEM((2 * TOK, D), BF), pltpu.VMEM((2 * TOK, FH), BF), pltpu.VMEM((2 * TOK, FH), BF), pltpu.VMEM((2, D, D), BF),
                        pltpu.VMEM((2, HALF, D), BF), pltpu.VMEM((2, HALF, D), BF), pltpu.VMEM((2, HALF, D), BF), pltpu.VMEM((2, HALF, D), BF),
                        pltpu.VMEM((2, HALF, D), F32)]
        + [dma((2,))] * 6 + [dma((12,)), dma((2,))] + scatter_scratch("B0") + scatter_scratch("B1"),
        compiler_params=pltpu.CompilerParams(collective_id=2, has_side_effects=True, vmem_limit_bytes=127 * 2 ** 19),
        name="mlp_back")(*args)


def attn_back_kernel(WA, WO, ti, gains, lat, xn, q, kb, vb, lse, o, da, dh, mask, base, onehot, gain_two, te, gi0, gi1,
                     dlat, gt, small, out_o, out_a, out_i, out_t,
                     dt_all,
                     q_v, kb_v, vb_v, grad_o, grad_a, grad_i0, grad_i1, do, dqkv, rim, rim_in, tsum, tsum_in, gt_send, gt_in, x_send, x_recv, dbias, sm_send, sm_in, total,
                     ks, kr, ts, tr, ps, pr, us, ur, vs, vr, ls, xs, xr, ss, sr, bs, br, *scratch):
    c, b, y, k = place()
    sib, ynb = {"band": b + 1 - 2 * k}, {"band": b + 2 - 4 * y}
    peers = [lax.rem(c + d, 8) for d in range(1, 8)]
    pend, waits = [], iter(range(20))

    def load(src, dst):
        cp = pltpu.make_async_copy(src, dst, ls.at[next(waits)])
        cp.start()
        return cp

    loads_i = [load(gi0, grad_i0), load(gi1, grad_i1)]
    load_dh = load(dh, dlat)
    load_q = [load(q, q_v), load(kb, kb_v), load(vb, vb_v)]
    greet(everyone())
    n = N_SCATTER
    rs_o = Scatter("O", grad_o, total, scratch[:n], pend)
    rs_a = Scatter("A", grad_a, total, scratch[n:2 * n], pend)
    rs_i = [Scatter("I0", grad_i0, total, scratch[2 * n:3 * n], pend), Scatter("I1", grad_i1, total, scratch[3 * n:], pend)]

    def go(make):
        make().start()
        pend.append(make)

    def arrive(view, sem):
        pltpu.make_async_copy(view, view, sem).wait()

    slots = pl.ds(pl.multiple_of(16 * c, 16), 16)
    for s in range(2):
        loads_i[s].wait()
        rs_i[s].send_y()
        rs_i[s].send_mid()

    def first(o_v, da_v, wo_v):
        parts = [load(o, o_v), load(da, da_v), load(WO, wo_v)]
        for cp in parts:
            cp.wait()
        for i, cols in enumerate(rs_o.parts()):
            grad_o[:, cols] = dot_tn(o_v[...], da_v[:, cols]).astype(BF)
            if i == 0:
                rs_o.send_y()
            if i == 1:
                rs_o.send_mid()
        for m in range(2):
            do[m] = dot_nt(da_v[pl.ds(TOK * m, TOK)], wo_v[...]).astype(BF)

    pl.run_scoped(first, pltpu.VMEM((2 * TOK, QC), BF), pltpu.VMEM((2 * TOK, D), BF), pltpu.VMEM((QC, D), BF))

    def second(dqf, dkf, dvf, toep, dsum):
        dqf[...] = jnp.zeros_like(dqf)
        dkf[...] = jnp.zeros_like(dkf)
        dvf[...] = jnp.zeros_like(dvf)
        for cp in load_q:
            cp.wait()

        def head(h, _):
            win, hm = head_window(h)
            toep[...] = toeplitz(base, h)
            dsum[...] = jnp.zeros_like(dsum)
            lane_h = lax.broadcasted_iota(jnp.int32, (1, 128), 1) == h

            def tile(t, _):
                m, j = t // 2, lax.rem(t, 2)
                rows = pl.ds(pl.multiple_of(HALF * j, 16), HALF)
                krows = pl.ds(pl.multiple_of(HALF * j, 16), KW)
                qm, dm = q_v[m, rows, win] * hm, do[m, rows, win] * hm
                kw = kb_v[m, krows, win]
                level = jnp.sum(jnp.where(lane_h, lse[m, rows], 0.0), -1, keepdims=True)
                p = jnp.exp(dot_nt(qm, kw) * SCALE + (toep[...] + mask[m, j]) - level)
                dp = dot_nt(dm, vb_v[m, krows, win])
                delta = jnp.sum(p * dp, -1, keepdims=True)
                ds = (p * (dp - delta)).astype(BF)
                dsum[...] += ds.astype(F32)
                dqf[m, rows, win] += dot(ds, kw * hm)
                dkf[m, krows, win] += dot_tn(ds, qm)
                dvf[m, krows, win] += dot_tn(p.astype(BF), dm)
                return 0

            lax.fori_loop(0, 4, tile, 0)
            strip = dsum[0:8]
            for r in range(8, HALF, 8):
                strip = strip + pltpu.roll(dsum[r:r + 8], KW - r, 1)
            line = strip[0:1]
            for r in range(1, 8):
                line = line + pltpu.roll(strip, KW - r, 1)[r:r + 1]
            dbias[pl.ds(h, 1)] = line
            return 0

        for i in range(4):
            lax.fori_loop(2 * i, 2 * i + 2, head, 0)
            if i == 0:
                for d in (1, 3, 2):
                    rs_i[0].side_x(d)
            elif i == 1:
                rs_i[0].side_x(0)
                for d in (1, 3, 2):
                    rs_i[0].send_z(d)
                rs_i[1].side_x(1)
            elif i == 2:
                for d in (3, 2, 0):
                    rs_i[1].side_x(d)
                rs_i[1].send_z(1)
        away = pl.ds(pl.multiple_of(624 * (1 - y), 16), 80)
        edge = pl.ds(pl.multiple_of(544 - 464 * y, 16), 80)
        for m in range(2):
            rim[m, 0] = (dkf[m, away] * SCALE).astype(BF)
            rim[m, 1] = dvf[m, away].astype(BF)
            go(lambda m=m: remote(rim.at[m], rim_in.at[m], ks.at[m], kr.at[m], ynb))
        for m in range(2):
            tok = pl.ds(TOK * m, TOK)
            dqkv[tok, 0:QC] = (dqf[m] * SCALE).astype(BF)
        for d in ORDER:
            rs_o.side_x(d)
        rs_i[1].send_z(3)
        rs_i[1].send_z(2)
        for m in range(2):
            arrive(rim_in.at[m], kr.at[m])
            tok = pl.ds(TOK * m, TOK)
            dkf[m, edge] += rim_in[m, 0].astype(F32) * (1.0 / SCALE)
            dvf[m, edge] += rim_in[m, 1].astype(F32)
            dqkv[tok, QC:2 * QC] = (dkf[m, 80:624] * SCALE).astype(BF)
            dqkv[tok, 2 * QC:] = dvf[m, 80:624].astype(BF)

    pl.run_scoped(second, pltpu.VMEM((2, TOK, QC), F32), pltpu.VMEM((2, KEYS, QC), F32), pltpu.VMEM((2, KEYS, QC), F32),
                  pltpu.VMEM((HALF, KW), F32), pltpu.VMEM((HALF, KW), F32))

    def third(xn_v, wa_v, dn):
        loads = [load(xn, xn_v), load(WA, wa_v)]
        tq = dot_tn(onehot[0], dqkv[0:TOK, 0:QC]) + dot_tn(onehot[1], dqkv[TOK:, 0:QC])
        tv = dot_tn(onehot[0], dqkv[0:TOK, 2 * QC:]) + dot_tn(onehot[1], dqkv[TOK:, 2 * QC:])
        tsum[:, 0:QC] = tq[0:16].astype(BF)
        tsum[:, QC:] = tv[0:16].astype(BF)
        go(lambda: remote(tsum, tsum_in, ts.at[0], tr.at[0], ynb))
        loads[0].wait()
        for i, cols in enumerate(rs_a.parts()):
            fill_part(grad_a, xn_v, dqkv, cols, 0, cols)
            if i == 0:
                rs_a.send_y()
                arrive(tsum_in, tr.at[0])
                dt_all[k, slots] = (tsum[...].astype(F32) + tsum_in[...].astype(F32)).astype(BF)
                for n, p in enumerate(peers):
                    go(lambda n=n, p=p: remote(dt_all.at[k, slots], dt_all.at[k, slots], ps.at[n], pr.at[6 - n], {"canvas": p}))
            if i == 1:
                rs_a.send_mid()
        for d in (1, 3, 2):
            rs_o.send_z(d)
        rs_i[0].finish()
        loads[1].wait()
        for m in range(2):
            rows = pl.ds(pl.multiple_of(TOK * m + HALF * (1 - k), 16), HALF)
            rows_own = pl.ds(pl.multiple_of(TOK * m + HALF * k, 16), HALF)

            def back(n, _):
                cols = pl.ds(pl.multiple_of(n * 384, 128), 384)
                x_send[m, :, cols] = dot_nt(dqkv[rows], wa_v[cols]).astype(BF)
                return 0

            lax.fori_loop(0, 3, back, 0)
            go(lambda m=m: remote(x_send.at[m], x_recv.at[m], xs.at[m], xr.at[m], sib))

            def back_own(n, _):
                cols = pl.ds(pl.multiple_of(n * 384, 128), 384)
                dn[m, :, cols] = dot_nt(dqkv[rows_own], wa_v[cols])
                return 0

            lax.fori_loop(0, 3, back_own, 0)
        rs_i[1].finish()
        rs_a.side_x(1)
        for n in range(7):
            arrive(dt_all.at[k, pl.ds(pl.multiple_of(16 * lax.rem(c + n + 1, 8), 16), 16)], pr.at[n])
        go(lambda: remote(dt_all.at[k], dt_all.at[k], us.at[0], ur.at[0], sib))
        gt_send[...] = dot_nt(dt_all[k], ti[...])
        go(lambda: remote(gt_send, gt_in, us.at[1], ur.at[1], sib))
        rs_a.side_x(3)
        rs_a.send_z(1)
        load_dh.wait()
        gain_one = jnp.zeros((1, D), F32)
        for m in range(2):
            arrive(x_recv.at[m], xr.at[m])
            grad = dn[m] + x_recv[m].astype(F32)
            n, r = norm(lat[m].astype(F32))
            gain_one = gain_one + jnp.sum(grad * n, 0, keepdims=True)
            dlat[m] = dlat[m] + norm_back(n, r, grad * gains[0:1])
            if m == 0:
                rs_a.side_x(2)
                rs_a.send_z(3)
        first_row = lax.broadcasted_iota(jnp.int32, (8, 1), 0) == 0
        both = jnp.where(first_row, jnp.broadcast_to(gain_one, (8, D)), gain_two[...])
        for p in range(8):
            sm_send[p, 0:8] = dbias[...]
            sm_send[p, 8:16] = (pltpu.roll(both, D - 144 * p, 1) if p else both)[:, 0:KW]

    pl.run_scoped(third, pltpu.VMEM((2 * TOK, D), BF), pltpu.VMEM((D, 3 * QC), BF), pltpu.VMEM((2, HALF, D), F32))
    for n, p in enumerate(peers):
        go(lambda n=n, p=p: remote(sm_send.at[p], sm_in.at[6 - n], ss.at[n], sr.at[6 - n], {"canvas": p}))
    rs_o.finish()
    arrive(gt_in, ur.at[1])
    gt_in[...] = gt_in[...] + gt_send[...]
    for n, p in enumerate(peers):
        go(lambda n=n, p=p: remote(gt_in.at[pl.ds(pl.multiple_of(16 * p, 16), 16)], gt.at[c], vs.at[n], vr.at[6 - n], {"canvas": p}))
    gt[c] = gt_in[pl.ds(pl.multiple_of(16 * c, 16), 16)]
    rs_a.side_x(0)
    rs_a.send_z(2)
    acc = sm_send[c]
    for n in range(7):
        arrive(sm_in.at[n], sr.at[n])
        acc = acc + sm_in[n]
    small[b] = acc
    for i in range(3):
        go(lambda i=i: remote(small.at[b], small.at[b], bs.at[i], br.at[2 - i], {"band": lax.rem(b + i + 1, 4)}))
    def last(buf_a, buf_i, buf_t):
        for s in range(2):
            rs_i[s].collect(buf_i.at[s])
            for half in range(2):
                for n in range(8):
                    at = 576 * n + 288 * half + 144 * s
                    out_i[:, at:at + 144] = buf_i[s, half, :, 144 * n:144 * n + 144]
        rs_o.collect(out_o)
        for n in range(7):
            arrive(gt.at[lax.rem(c + n + 1, 8)], vr.at[n])
        arrive(dt_all.at[1 - k], ur.at[0])
        slots_all = te[...].reshape(128, 144)
        for half in range(2):
            total[...] = dot_tn(slots_all, dt_all[half])
            for i in range(4):
                @pl.when(b == i)
                def _():
                    buf_t[...] = total[36 * i:36 * i + 36]

            for t in range(2):
                for i in range(8):
                    at = D * t + 144 * i + 72 * half
                    out_t[:, at:at + 72] = buf_t[:, QC * t + 80 * i:QC * t + 80 * i + 72]
        for i in range(3):
            arrive(small.at[lax.rem(b + i + 1, 4)], br.at[i])
        rs_a.finish()
        rs_a.collect(buf_a)
        for half in range(2):
            for t in range(3):
                for i in range(8):
                    at = D * t + 144 * i + 72 * half
                    out_a[:, at:at + 72] = buf_a[half, :, QC * t + 80 * i:QC * t + 80 * i + 72]

    pl.run_scoped(last, pltpu.VMEM((2, 36, 3 * QC), F32), pltpu.VMEM((2, 2, 36, D), F32), pltpu.VMEM((36, 2 * QC), F32))
    for rs in (rs_o, rs_a, *rs_i):
        rs.sent()
    for make in pend:
        make().wait_send()


def attn_back(*args):
    S = jax.ShapeDtypeStruct
    dma = pltpu.SemaphoreType.DMA
    V, anyspace = pl.BlockSpec(memory_space=pltpu.VMEM), pl.BlockSpec(memory_space=pl.ANY)
    return pl.pallas_call(
        attn_back_kernel,
        out_shape=[S((2, HALF, D), F32), S((8, 16, 144), F32), S((4, 16, KW), F32), S((36, D), F32), S((36, 3 * D), F32), S((36, 2 * FH), F32), S((36, 2 * D), F32)],
        in_specs=[anyspace, anyspace, V, V, V] + [anyspace] * 4 + [V] + [anyspace] * 3 + [V] * 5 + [anyspace] * 2, out_specs=[V] * 7,
        scratch_shapes=[pltpu.VMEM((2, 128, 2 * QC), BF),
                        pltpu.VMEM((2, TOK, QC), BF), pltpu.VMEM((2, KEYS, QC), BF), pltpu.VMEM((2, KEYS, QC), BF),
                        pltpu.VMEM((QC, D), BF), pltpu.VMEM((D, 3 * QC), BF), pltpu.VMEM((D, D), BF), pltpu.VMEM((D, D), BF), pltpu.VMEM((2, TOK, QC), BF),
                        pltpu.VMEM((2 * TOK, 3 * QC), BF),
                        pltpu.VMEM((2, 2, 80, QC), BF), pltpu.VMEM((2, 2, 80, QC), BF), pltpu.VMEM((16, 2 * QC), BF), pltpu.VMEM((16, 2 * QC), BF),
                        pltpu.VMEM((128, 144), F32), pltpu.VMEM((128, 144), F32),
                        pltpu.VMEM((2, HALF, D), BF), pltpu.VMEM((2, HALF, D), BF), pltpu.VMEM((8, KW), F32), pltpu.VMEM((8, 16, KW), F32), pltpu.VMEM((7, 16, KW), F32),
                        pltpu.VMEM((144, 1280), F32),
                        dma((2,)), dma((2,)), dma((1,)), dma((1,)), dma((7,)), dma((7,)), dma((2,)), dma((2,)), dma((7,)), dma((7,)), dma((20,)), dma((2,)), dma((2,)),
                        dma((7,)), dma((7,)), dma((3,)), dma((3,))]
        + scatter_scratch("O") + scatter_scratch("A") + scatter_scratch("I0") + scatter_scratch("I1"),
        compiler_params=pltpu.CompilerParams(collective_id=3, has_side_effects=True, vmem_limit_bytes=127 * 2 ** 19),
        name="attn_back")(*args)


def local_fast(*args):
    p = prologue(*args)
    c, b, y, k = place()
    cot = args[10].reshape(2, HALF, D)
    (xn, q, kb, vb, lse, o, hres, hn, g, gp, df, gb0, gb1, WA, WO, WI0, WI1, WB0, WB1, te_all, mask, onehot, ti) = gather_forward(p, cot)
    out, dh, da, gain_two, out_b, gi0, gi1 = mlp_back(cot, p["filled"], p["gains"], WI0, WI1, WB0, WB1, hres, hn.reshape(2 * TOK, D), g, gp, df, gb0, gb1)
    dlat, gt, small, grad_out, grad_a, grad_i, grad_time_in = attn_back(
        WA, WO, ti, p["gains"], p["lat"], xn.reshape(2 * TOK, D), q, kb, vb, lse, o.reshape(2 * TOK, QC), da, dh,
        mask, p["base"], onehot, gain_two, te_all, gi0, gi1)
    shape = (2, 1, 8, 34, D)
    places = [80 + 34 * dr + dc for dr in range(-2, 3) for dc in range(-2, 3)]
    bias = small[0:2, 0:8] + small[2:4, 0:8]
    grad_bias = bias[:, :, jnp.array(places)].transpose(2, 1, 0).reshape(25, 16)
    mine = lax.dynamic_slice_in_dim(small[:, 8:10, 0:144].sum(0), 36 * b, 36, 1)
    grad_time = gt.transpose(1, 0, 2).reshape(16, D)[:10].reshape(2, 1, 5, D)
    return (out.reshape(shape), dlat.reshape(shape), grad_time, mine.T, grad_a, grad_time_in, grad_bias, grad_out, grad_i, out_b)


def solution(mesh):
    return jax.shard_map(
        local_fast if mesh.shape["canvas"] == 8 and mesh.shape["band"] == 4 else local,
        mesh=mesh,
        in_specs=(
            P(None, "canvas", "band", None, None),
            P(None, "canvas", "band", None),
            P(None, "canvas", None, None),
            P(),
            P("canvas", None),
            P("canvas", None),
            P(),
            P("canvas", None),
            P("canvas", None),
            P("canvas", None),
            P(None, "canvas", "band", None, None),
        ),
        out_specs=(
            P(None, "canvas", "band", None, None),
            P(None, "canvas", "band", None, None),
            P(None, "canvas", None, None),
            P(("canvas", "band"), None),
            P(("canvas", "band"), None),
            P(("canvas", "band"), None),
            P(),
            P(("canvas", "band"), None),
            P(("canvas", "band"), None),
            P(("canvas", "band"), None),
        ),
        check_vma=False,
    )
```

```python
from functools import partial
import jax
import jax.numpy as jnp
from jax import lax
from jax.experimental import pallas as pl
from jax.experimental.pallas import tpu as pltpu

from jax.sharding import PartitionSpec as P

WIN = 5


EPSILON = 1e-05


def padded_2(shard, sides, width):
    for axis, dim in sides:
        devices, length = (lax.axis_size(axis), shard.shape[dim])
        up = [(i, (i + 1) % devices) for i in range(devices - 1)]
        down = [(j, i) for i, j in up]
        last = lax.slice_in_dim(shard, length - width, length, axis=dim)
        first = lax.slice_in_dim(shard, 0, width, axis=dim)
        before = lax.ppermute(last, axis, up)
        after = lax.ppermute(first, axis, down)
        shard = jnp.concatenate([before, shard, after], axis=dim)
    return shard


def shifted(shard, axis, by):
    devices = lax.axis_size(axis)
    pairs = [(i, i + by) for i in range(devices) if 0 <= i + by < devices]
    return lax.ppermute(shard, axis, pairs)


def shortened(shard):

    def short(part):
        return part.astype(jnp.bfloat16) if part.dtype == jnp.float32 else part

    return jax.tree.map(short, shard)


def normalize(value, gain):
    center = value - jnp.mean(value, -1, keepdims=True)
    scaled = lax.rsqrt(jnp.mean(center * center, -1, keepdims=True) + EPSILON)
    unit = center * scaled
    return (unit, scaled, unit * gain)


def normalize_back(unit, scaled, gain, grad_out):
    part = grad_out * gain
    return scaled * (
        part - jnp.mean(part, -1, keepdims=True) - unit * jnp.mean(part * unit, -1, keepdims=True)
    )


def rows_dot(left, right):
    return lax.dot_general(
        left, right, (((0,), (0,)), ((), ())), preferred_element_type=jnp.float32
    )


def back_dot(left, weight):
    return lax.dot_general(
        left, weight, (((1,), (1,)), ((), ())), preferred_element_type=jnp.float32
    )


def neighbour_stack(padded, band_rows, columns):
    pieces = [padded[:, i : i + band_rows, j : j + columns] for i in range(WIN) for j in range(WIN)]
    stacked = jnp.stack(pieces)
    return stacked.reshape((WIN * WIN, -1) + padded.shape[3:])


def spread_back(terms, canvases, band_rows, columns):
    reach = WIN // 2
    shaped = terms.reshape((WIN * WIN, canvases, band_rows, columns, terms.shape[-1]))
    summed = None
    for i in range(WIN):
        for j in range(WIN):
            placed = jnp.pad(
                shaped[i * WIN + j], ((0, 0), (i, 2 * reach - i), (j, 2 * reach - j), (0, 0))
            )
            summed = placed if summed is None else summed + placed
    return summed


def head_total(terms, head_sum):
    flat = terms.reshape(-1, terms.shape[-1])
    return jnp.dot(flat, head_sum, precision=lax.Precision.HIGHEST).reshape(
        terms.shape[:-1] + (head_sum.shape[1],)
    )


def head_widen(values, head_spread):
    flat = values.reshape(-1, values.shape[-1])
    return jnp.dot(flat, head_spread, preferred_element_type=jnp.bfloat16).reshape(
        values.shape[:-1] + (head_spread.shape[1],)
    )


def local(
    latents,
    segment_ids,
    time_embed,
    norm_gains,
    attn_in,
    time_in,
    rel_bias,
    out_proj,
    mlp_in,
    mlp_out,
    cotangent,
):
    micro_count, canvases, band_rows, columns, width = latents.shape
    slots = time_embed.shape[2]
    heads = rel_bias.shape[1]
    head_dim = width // heads
    reach = WIN // 2
    tokens = canvases * band_rows * columns
    score_scale = head_dim ** (-0.5)
    head_sum = (jnp.arange(width)[:, None] // head_dim == jnp.arange(heads)[None, :]).astype(
        jnp.float32
    )
    head_spread = head_sum.T.astype(jnp.bfloat16)
    owned = (attn_in, time_in, out_proj, mlp_in, mlp_out)
    seg_code = segment_ids + 2
    seg_rims = padded_2(seg_code, (("band", 2),), reach)
    seg_rims = jnp.pad(seg_rims, ((0, 0), (0, 0), (0, 0), (reach, reach)))
    band_share = 1.0 / lax.axis_size("band")
    outputs = []
    input_grads = []
    time_grads = []
    accum = None
    shards = None
    bias_accum = jnp.zeros(rel_bias.shape, jnp.float32)
    for batch_index in range(micro_count):
        full_weights = (
            lax.all_gather(owned[0], "canvas", axis=0, tiled=True),
            lax.all_gather(owned[1], "canvas", axis=0, tiled=True),
            lax.all_gather(owned[2], "canvas", axis=0, tiled=True),
            lax.all_gather(owned[3], "canvas", axis=0, tiled=True),
            lax.all_gather(owned[4], "canvas", axis=0, tiled=True),
        )
        w_attn, w_time, w_out, w_in, w_back = full_weights
        inputs = latents[batch_index].astype(jnp.float32).reshape(tokens, width)
        unit_one, scaled_one, normed_one = normalize(inputs, norm_gains[:, 0])
        normed = normed_one.astype(jnp.bfloat16)
        time_rows = time_embed[batch_index].reshape(canvases * slots, width)
        time_proj = jnp.dot(time_rows, w_time, preferred_element_type=jnp.float32).reshape(
            canvases, slots, 2 * width
        )
        seg_here = segment_ids[batch_index]
        member = (seg_here[..., None] == jnp.arange(slots)).astype(jnp.float32)
        token_time = jnp.einsum(
            "krcs,kse->krce", member, time_proj, precision=lax.Precision.HIGHEST
        ).reshape(tokens, 2 * width)
        qkv = jnp.dot(normed, w_attn, preferred_element_type=jnp.float32)
        query = (qkv[:, :width] + token_time[:, :width]).astype(jnp.bfloat16)
        keys = qkv[:, width : 2 * width].astype(jnp.bfloat16)
        values = (qkv[:, 2 * width :] + token_time[:, width:]).astype(jnp.bfloat16)
        paired = jnp.stack([keys, values]).reshape(2, canvases, band_rows, columns, width)
        paired = padded_2(paired, (("band", 2),), reach)
        paired = jnp.pad(paired, ((0, 0), (0, 0), (0, 0), (reach, reach), (0, 0)))
        key_win = neighbour_stack(paired[0], band_rows, columns)
        value_win = neighbour_stack(paired[1], band_rows, columns)
        seg_win = neighbour_stack(seg_rims[batch_index], band_rows, columns)
        allowed = (seg_win == seg_code[batch_index].reshape(1, tokens))[..., None]
        query_wide = query.astype(jnp.float32)
        raw = head_total(query_wide[None] * key_win.astype(jnp.float32), head_sum)
        logit_scores = raw * score_scale + rel_bias[:, None, :]
        masked = jnp.where(allowed, logit_scores, -1e30)
        peak = jnp.max(masked, 0)
        raised = jnp.where(allowed, jnp.exp(masked - peak), 0.0)
        probs_full = raised / jnp.sum(raised, 0)
        attention_probabilities = probs_full.astype(jnp.bfloat16)
        probs_wide = head_widen(attention_probabilities, head_spread)
        mixed_values = jnp.sum(probs_wide.astype(jnp.float32) * value_win.astype(jnp.float32), 0)
        attended = mixed_values.astype(jnp.bfloat16)
        branch = jnp.dot(attended, w_out, preferred_element_type=jnp.float32)
        resid = inputs + branch
        unit_two, scaled_two, normed_two = normalize(resid, norm_gains[:, 1])
        hidden_in = normed_two.astype(jnp.bfloat16)
        pre_act = jnp.dot(hidden_in, w_in, preferred_element_type=jnp.float32)
        activated = jax.nn.gelu(pre_act, approximate=False).astype(jnp.bfloat16)
        mlp_y = jnp.dot(activated, w_back, preferred_element_type=jnp.float32)
        filled = (seg_here >= 0).reshape(tokens, 1)
        outputs.append(
            jnp.where(filled, resid + mlp_y, 0.0)
            .astype(jnp.bfloat16)
            .reshape(canvases, band_rows, columns, width)
        )
        grad_y = cotangent[batch_index].reshape(tokens, width)
        grad_f = jnp.where(filled, grad_y, jnp.zeros_like(grad_y))
        grad_back = rows_dot(activated, grad_f)
        grad_act = back_dot(grad_f, w_back)
        gelu_out, gelu_pull = jax.vjp(partial(jax.nn.gelu, approximate=False), pre_act)
        grad_pre = gelu_pull(grad_act)[0].astype(jnp.bfloat16)
        grad_in = rows_dot(hidden_in, grad_pre)
        grad_hidden = back_dot(grad_pre, w_in)
        grad_resid = jnp.where(filled, grad_y.astype(jnp.float32), 0.0) + normalize_back(
            unit_two, scaled_two, norm_gains[:, 1], grad_hidden
        )
        gain_two = jnp.sum(grad_hidden * unit_two, 0)
        grad_branch = grad_resid.astype(jnp.bfloat16)
        grad_out = rows_dot(attended, grad_branch)
        grad_att = back_dot(grad_branch, w_out).astype(jnp.bfloat16)
        grad_att_wide = grad_att.astype(jnp.float32)
        grad_probs = head_total(grad_att_wide[None] * value_win.astype(jnp.float32), head_sum)
        centered = jnp.sum(probs_full * grad_probs, 0)
        grad_scores = (probs_full * (grad_probs - centered)).astype(jnp.bfloat16)
        bias_accum = bias_accum + jnp.sum(grad_scores.astype(jnp.float32), axis=1)
        scores_wide = head_widen(grad_scores, head_spread).astype(jnp.float32)
        grad_query = jnp.sum(scores_wide * key_win.astype(jnp.float32), 0) * score_scale
        key_summed = (
            spread_back(scores_wide * query_wide[None], canvases, band_rows, columns) * score_scale
        )
        value_summed = spread_back(
            probs_wide.astype(jnp.float32) * grad_att_wide[None], canvases, band_rows, columns
        )
        pair_grad = jnp.stack([key_summed, value_summed])[:, :, :, reach : reach + columns]
        upper_rim = pair_grad[:, :, :reach]
        lower_rim = pair_grad[:, :, band_rows + reach :]
        owned_rows = pair_grad[:, :, reach : reach + band_rows]
        from_below = shifted(upper_rim.astype(jnp.bfloat16), "band", -1).astype(upper_rim.dtype)
        from_above = shifted(lower_rim.astype(jnp.bfloat16), "band", 1).astype(lower_rim.dtype)
        owned_rows = owned_rows.at[:, :, band_rows - reach :].add(from_below)
        owned_rows = owned_rows.at[:, :, :reach].add(from_above)
        grad_keys = owned_rows[0].reshape(tokens, width).astype(jnp.bfloat16)
        grad_values = owned_rows[1].reshape(tokens, width).astype(jnp.bfloat16)
        grad_q_low = grad_query.astype(jnp.bfloat16)
        member_low = member.astype(jnp.bfloat16).reshape(canvases, band_rows * columns, slots)
        slot_query = jnp.einsum(
            "kns,knd->ksd",
            member_low,
            grad_q_low.reshape(canvases, band_rows * columns, width),
            preferred_element_type=jnp.float32,
        )
        slot_value = jnp.einsum(
            "kns,knd->ksd",
            member_low,
            grad_values.reshape(canvases, band_rows * columns, width),
            preferred_element_type=jnp.float32,
        )
        slot_part = jnp.concatenate([slot_query, slot_value], -1)
        slot_total = lax.psum(slot_part.astype(jnp.bfloat16), "band")
        slot_low = slot_total.reshape(canvases * slots, 2 * width)
        time_grads.append(back_dot(slot_low, w_time).reshape(canvases, slots, width))
        grad_time_in = rows_dot(time_rows, slot_low) * band_share
        grad_qkv = jnp.concatenate([grad_q_low, grad_keys, grad_values], -1)
        grad_attn = rows_dot(normed, grad_qkv)
        grad_normed = back_dot(grad_qkv, w_attn)
        grad_inputs = grad_resid + normalize_back(
            unit_one, scaled_one, norm_gains[:, 0], grad_normed
        )
        gain_one = jnp.sum(grad_normed * unit_one, 0)
        input_grads.append(grad_inputs.reshape(canvases, band_rows, columns, width))
        micro_grads = (
            grad_attn,
            grad_time_in,
            grad_out,
            grad_in,
            grad_back,
            jnp.stack([gain_one, gain_two], 1),
        )
        accum = micro_grads if accum is None else jax.tree.map(jnp.add, accum, micro_grads)
    wide_sums = jax.tree.map(
        lambda part: part.astype(jnp.float32),
        lax.psum_scatter(shortened(accum), "canvas", scatter_dimension=0, tiled=True),
    )
    shards = jax.tree.map(
        lambda part: part.astype(jnp.float32),
        lax.psum_scatter(shortened(wide_sums), "band", scatter_dimension=0, tiled=True),
    )
    bias_grad = lax.psum(bias_accum, ("canvas", "band"))
    return (
        jnp.stack(outputs),
        jnp.stack(input_grads),
        jnp.stack(time_grads),
        shards[5],
        shards[0],
        shards[1],
        bias_grad,
        shards[2],
        shards[3],
        shards[4],
    )


MESH = pl.DeviceIdType.MESH
BF, F32 = jnp.bfloat16, jnp.float32
EPS = 1e-5
TOK, HALF, D, QC, FH = 544, 272, 1152, 640, 2304
KEYS, KW, PADK = 784, 512, 80
SCALE = 72 ** -0.5
NEG = -1e30


def dot(a, b):
    return jnp.dot(a, b, preferred_element_type=F32)


def dot_nt(a, b):
    return lax.dot_general(a, b, (((1,), (1,)), ((), ())), preferred_element_type=F32)


def dot_tn(a, b):
    return lax.dot_general(a, b, (((0,), (0,)), ((), ())), preferred_element_type=F32)


def norm(v):
    center = v - jnp.mean(v, -1, keepdims=True)
    r = lax.rsqrt(jnp.mean(center * center, -1, keepdims=True) + EPS)
    return center * r, r


def norm_back(n, r, e):
    return r * (e - jnp.mean(e, -1, keepdims=True) - n * jnp.mean(e * n, -1, keepdims=True))


def place():
    c, b = lax.axis_index("canvas"), lax.axis_index("band")
    return c, b, b // 2, lax.rem(b, 2)


def greet(devs):
    bar = pltpu.get_barrier_semaphore()
    for dev in devs:
        pl.semaphore_signal(bar, 1, device_id=dev, device_id_type=MESH)
    pl.semaphore_wait(bar, len(devs))


def remote(src, dst, ss, rs, dev):
    return pltpu.make_async_remote_copy(src, dst, ss, rs, device_id=dev, device_id_type=MESH)


def head_window(h):
    ws = pl.multiple_of(jnp.minimum(80 * h // 128, 3) * 128, 128)
    lane = lax.broadcasted_iota(jnp.int32, (1, 256), 1) + ws - 80 * h
    hm = jnp.where((lane >= 0) & (lane < 80), 1.0, 0.0).astype(BF)
    return pl.ds(ws, 256), hm


def toeplitz(base, h):
    row = jnp.broadcast_to(base[pl.ds(h, 1)], (HALF, KW))
    return pltpu.roll(row, 0, 1, stride=1, stride_axis=0)


GSPEC = {"A": (144, 640, 640), "O": (80, 384, 384), "I0": (144, 384, 384), "I1": (144, 384, 384), "B0": (144, 384, 384), "B1": (144, 384, 384)}
GNAMES = list(GSPEC)


FIRST, STEP, SPARE = 4.0, 1.7, -2


class Gather:
    def __init__(self, own, full, s_sem, r_sem, y_sem, l_sem, pend):
        self.own, self.full, self.pend = dict(zip(GNAMES, own)), dict(zip(GNAMES, full)), pend
        self.s_sem, self.r_sem, self.y_sem, self.l_sem = s_sem, r_sem, y_sem, l_sem
        self.c, self.b, self.y, _ = place()
        self.z, self.x = self.c // 2, lax.rem(self.c, 2)
        z = self.z
        self.zp = [jnp.where(z == 0, t[0], jnp.where(z == 1, t[1], jnp.where(z == 2, t[2], t[3]))) for t in ((1, 0, 3, 2), (2, 2, 1, 1), (3, 3, 0, 0))]
        self.xdev, self.ydev = {"canvas": self.c + 1 - 2 * self.x}, {"band": self.b + 2 - 4 * self.y}
        self.count = dict.fromkeys(GNAMES, 0)

    def part(self, name, src, plane, side):
        rows, wide, mid = GSPEC[name]
        at = pl.ds(pl.multiple_of(src * rows, 16), rows)
        if plane:
            return at, pl.ds(pl.multiple_of(wide * side, 128), wide + mid)
        return at, pl.ds(pl.multiple_of((wide + mid) * side, 128), wide)

    def send(self, name, src, dev, plane, first=False, when=None):
        n = GNAMES.index(name)
        at, cols = self.part(name, src, plane, self.y)
        held = self.full[name].at[at, cols] if self.own[name] is None or not first else self.own[name].at[:, cols]
        cp = remote(held, self.full[name].at[at, cols],
                    self.s_sem.at[n, self.count[name]], (self.r_sem if plane else self.y_sem).at[n, src], dev)
        self.count[name] += 1
        if when is None:
            cp.start()
            self.pend.append(cp.wait_send)
        else:
            pl.when(when)(cp.start)
            self.pend.append(lambda: pl.when(when)(cp.wait_send))

    def own_sends(self, name):
        rows = GSPEC[name][0]
        for up in (1, -1):
            to = self.z + up
            self.send(name, self.c, {"canvas": jnp.clip(to, 0, 3) * 2 + self.x}, True, True, (to >= 0) & (to <= 3))
        self.send(name, self.c, self.xdev, True, True)
        if self.own[name] is not None:
            pltpu.make_async_copy(self.own[name], self.full[name].at[pl.ds(pl.multiple_of(self.c * rows, 16), rows)],
                                  self.l_sem.at[GNAMES.index(name)]).start()

    def wait(self, name, src, plane):
        at, cols = self.part(name, src, plane, self.y if plane else 1 - self.y)
        view = self.full[name].at[at, cols]
        pltpu.make_async_copy(view, view, (self.r_sem if plane else self.y_sem).at[GNAMES.index(name), src]).wait()

    def from_z(self, name, i):
        src = self.zp[i] * 2 + self.x
        self.wait(name, src, True)
        to = jnp.where(self.zp[i] < self.z, self.z + 1, self.z - 1)
        self.send(name, src, {"canvas": jnp.clip(to, 0, 3) * 2 + self.x}, True, False, (to >= 0) & (to <= 3))
        self.send(name, src, self.xdev, True)
        self.send(name, src, self.ydev, False)

    def from_x(self, name, i):
        src = (self.z if i == 0 else self.zp[i - 1]) * 2 + 1 - self.x
        self.wait(name, src, True)
        self.send(name, src, self.ydev, False)

    def complete(self, name):
        rows = GSPEC[name][0]
        for d in range(1, 8):
            self.wait(name, lax.rem(self.c + d, 8), False)
        if self.own[name] is not None:
            pltpu.make_async_copy(self.own[name], self.full[name].at[pl.ds(pl.multiple_of(self.c * rows, 16), rows)],
                                  self.l_sem.at[GNAMES.index(name)]).wait()

    def events(self, name):
        return [partial(self.from_z, name, 0), partial(self.from_x, name, 0), partial(self.from_z, name, 1), partial(self.from_x, name, 1),
                partial(self.from_z, name, 2), partial(self.from_x, name, 2), partial(self.from_x, name, 3)]


def gather_forward_kernel(attn_in, time_in, mlp_in, O, mlp_out, lat_in, cot_in, gains, te, seg_row, seg_col, base,
                          xn_o, q_o, kb_o, vb_o, lse_o, o_o, hres_o, hn_o, g_o, gp_o, df_o, gb0_o, gb1_o,
                          WA_o, WO_o, WI0_o, WI1_o, WB0_o, WB1_o, te_o, mask_o, onehot_o, ti,
                          WA, WO, WI0, WI1, WB0, WB1, xn, q, kb, vb, lse, o, hres, hn, g, gp, df, gb0, gb1, te_in, seg_in, col_in, onehot,
                          tp_send, tp_recv, tmix, mask, toep, of, x_send, x_recv, lat, cot,
                          s_sem, r_sem, y_sem, l_sem, es, er, gs, gr, cs, cr,
                          xs, xr, ts, tr, ks, kr, as_, ar, hs, hr, fs, fr, ls, outs):
    blocks = [(attn_in, 0), (attn_in, 1), (attn_in, 2), (time_in, 0), (time_in, 1)] + [(mlp_in, j) for j in range(4)]
    spots = [g.at[144 * (i // 2):144 * (i // 2) + 144, D * (i % 2):D * (i % 2) + D] for i in range(9)]
    loads = [pltpu.make_async_copy(lat_in, lat, ls.at[0]), pltpu.make_async_copy(cot_in, cot, ls.at[1])]
    loads += [pltpu.make_async_copy(src.at[:, D * j:D * j + D], spots[i], ls.at[2 + i]) for i, (src, j) in enumerate(blocks)]
    for cp in loads:
        cp.start()
    c, b, y, k = place()
    sib, ynb = {"band": b + 1 - 2 * k}, {"band": b + 2 - 4 * y}
    peers = [lax.rem(c + d, 8) for d in range(1, 8)]
    pend, saves = [], []

    def go(src, dst, ss, rs, dev):
        cp = remote(src, dst, ss, rs, dev)
        cp.start()
        pend.append(cp.wait_send)

    def arrive(view, sem):
        pltpu.make_async_copy(view, view, sem).wait()

    def save(src, dst):
        cp = pltpu.make_async_copy(src, dst, outs.at[len(saves)])
        cp.start()
        saves.append(cp)

    shares = [mlp_out.at[pl.ds(pl.multiple_of(288 * k + 144 * i, 16), 144)] for i in range(2)]
    gat = Gather((None, O, None, None, *shares), (WA, WO, WI0, WI1, WB0, WB1), s_sem, r_sem, y_sem, l_sem, pend)
    queue, ends = [], {}
    for name, nxt in (("A", "I0"), ("O", "I1"), ("I0", "B0"), ("I1", "B1"), ("B0", None), ("B1", None)):
        steps = gat.events(name)
        if nxt:
            steps.insert(1, partial(gat.own_sends, nxt))
        queue += steps
        ends[name] = len(queue)

    total, clock = len(queue), [0.0]

    def tick(us):
        clock[0] += us
        while queue and FIRST + STEP * (total - len(queue)) <= clock[0]:
            queue.pop(0)()

    def complete(name):
        left = total - ends[name]
        while len(queue) > max(left + SPARE, 0):
            queue.pop(0)()
        gat.complete(name)
        clock[0] = max(clock[0], FIRST + STEP * (total - left))

    greet([{"band": lax.rem(b + d, 4)} for d in (1, 2, 3)] + [{"canvas": p} for p in peers])
    for i, p in enumerate(peers):
        go(te.at[p], te_in.at[c], es.at[i], er.at[6 - i], {"canvas": p})
    te_in[c] = te[c]
    for i in range(3):
        go(seg_row, seg_in.at[b], gs.at[i], gr.at[2 - i], {"band": lax.rem(b + i + 1, 4)})
    seg_in[b] = seg_row[...]
    go(seg_col, col_in.at[k], cs.at[0], cr.at[0], sib)
    col_in[k] = seg_col[...]
    mine_rows = pl.ds(pl.multiple_of(144 * c, 16), 144)

    def pick_matrix(source, wide):
        gb0[:, 0:wide] = jnp.where(lax.broadcasted_iota(jnp.int32, (D, wide), 0) == source, 1.0, 0.0).astype(BF)

    lane = lax.broadcasted_iota(jnp.int32, (1, QC), 1).astype(F32)
    place_h = jnp.floor((lane + 0.5) * (1.0 / 80))
    inside = lane - 80 * place_h
    pick_matrix(jnp.where(inside < 71.5, 144 * place_h + inside + 72 * k.astype(F32), -1.0).astype(jnp.int32), QC)
    for i in range(3):
        loads[2 + i].wait()
        WA[mine_rows, QC * i:QC * i + QC] = dot(spots[i][...], gb0[:, 0:QC]).astype(BF)
    gat.own_sends("A")
    gat.own_sends("O")
    for i in range(2):
        loads[5 + i].wait()
        ti[:, QC * i:QC * i + QC] = dot(spots[3 + i][...], gb0[:, 0:QC]).astype(BF)

    def pick_hidden(s, W):
        for j in range(4):
            n = lax.broadcasted_iota(jnp.int32, (1, 384), 1).astype(F32) + 256 * j
            cc = jnp.floor((n + 0.5) * (1.0 / 144))
            fits = (cc > 2 * j - 0.5) & (cc < 2 * j + 1.5)
            pick_matrix(jnp.where(fits, 576 * (cc - 2 * j) + (n - 144 * cc) + 288 * k.astype(F32) + 144 * s, -1.0).astype(jnp.int32), 384)
            part = dot(spots[5 + j][...], gb0[:, 0:384]).astype(BF)
            if j:
                W[mine_rows, 256 * j:256 * j + 128] += part[:, 0:128]
                W[mine_rows, 256 * j + 128:256 * j + 384] = part[:, 128:]
            else:
                W[mine_rows, 0:384] = part

    loads[0].wait()
    mine = pl.ds(pl.multiple_of(HALF * k, 16), HALF)
    other = pl.ds(pl.multiple_of(HALF * (1 - k), 16), HALF)
    for m in range(2):
        n, _ = norm(lat[m].astype(F32))
        xn[m, mine] = (n * gains[0:1]).astype(BF)
        go(xn.at[m, mine], xn.at[m, mine], xs.at[m], xr.at[m], sib)
        if m == 0:
            for i in range(7):
                arrive(te_in.at[lax.rem(c + i + 1, 8)], er.at[i])
            for p in range(8):
                tp_send[16 * p:16 * p + 16] = dot(te_in[p], ti[...]).astype(BF)
            for i, p in enumerate(peers):
                go(tp_send.at[pl.ds(pl.multiple_of(16 * p, 16), 16)], tp_recv.at[6 - i], ts.at[i], tr.at[6 - i], {"canvas": p})
    save(te_in, te_o)
    for i in range(4):
        loads[7 + i].wait()
    pick_hidden(0, WI0)
    arrive(col_in.at[1 - k], cr.at[0])
    for i in range(3):
        arrive(seg_in.at[lax.rem(b + i + 1, 4)], gr.at[i])
    slot = lax.rem(lax.broadcasted_iota(jnp.int32, (1, 32), 1), 16)
    lane = lax.broadcasted_iota(jnp.int32, (1, KW), 1)

    def column(t):
        return t - 34 * jnp.floor((t + 0.5) * (1.0 / 34))

    colq = column(lax.broadcasted_iota(jnp.int32, (HALF, 1), 0).astype(F32))
    near = jnp.abs(colq - column(lax.broadcasted_iota(jnp.int32, (1, KW), 1).astype(F32) + 22)) < 2.5
    for j in range(2):
        at = 2 * y + j
        before, here, after = seg_in[jnp.maximum(at - 1, 0)], seg_in[at], seg_in[jnp.minimum(at + 1, 3)]
        before = pltpu.roll(jnp.where(at > 0, before, 0.0), KW - HALF, 1)
        after = pltpu.roll(jnp.where(at < 3, after, 0.0), HALF, 1)
        keys = jnp.where(lane < 80, before, jnp.where(lane < 352, here, jnp.where(lane < 432, after, 0.0)))
        for m in range(2):
            code = col_in[j, m, :, 0:1]
            mask[m, j] = jnp.where((code == keys[m:m + 1]) & near, 0.0, NEG).astype(BF)
            hit = (code.astype(jnp.int32) + (5 * m - 2) == slot) & (code >= 1.5)
            onehot[m, HALF * j:HALF * j + HALF] = jnp.where(hit, 1.0, 0.0).astype(BF)
    loads[1].wait()
    for m in range(2):
        filled = jnp.where(col_in[k, m, :, 0:1] >= 1.5, 1.0, 0.0)
        rows = pl.ds(pl.multiple_of(TOK * m + HALF * k, 16), HALF)
        df[rows] = (cot[m].astype(F32) * filled).astype(BF)
        go(df.at[rows], df.at[rows], fs.at[m], fr.at[m], sib)
    save(mask, mask_o)
    save(onehot, onehot_o)
    tick(13.0)
    for i in range(7):
        arrive(tp_recv.at[i], tr.at[i])
    tproj = tp_send[pl.ds(pl.multiple_of(16 * c, 16), 16)].astype(F32)
    for i in range(7):
        tproj = tproj + tp_recv[i].astype(F32)
    hi = tproj.astype(BF)
    tmix[0:16] = hi
    tmix[16:32] = (tproj - hi.astype(F32)).astype(BF)
    dead = pl.ds(pl.multiple_of(y * 624, 16), 80)
    for m in range(2):
        for ref in (kb, vb):
            ref[m, dead] = jnp.zeros((80, QC), BF)
            ref[m, 704:784] = jnp.zeros((80, QC), BF)
    of[...] = jnp.zeros_like(of)
    lse[...] = jnp.zeros_like(lse)
    pick_hidden(1, WI1)
    complete("A")
    save(WA, WA_o)

    edge = pl.ds(pl.multiple_of(544 - 464 * y, 16), 80)
    land = pl.ds(pl.multiple_of(624 * y, 16), 80)
    land_here = pl.ds(pl.multiple_of(624 * (1 - y), 16), 80)
    for m in range(2):
        arrive(xn.at[m, other], xr.at[m])
        x = xn[m]
        kb[m, 80:624] = dot(x, WA[:, QC:2 * QC]).astype(BF)
        tick(1.2)
        vb[m, 80:624] = (dot(x, WA[:, 2 * QC:]) + dot(onehot[m], tmix[:, QC:])).astype(BF)
        for i, ref in enumerate((kb, vb)):
            go(ref.at[m, edge], ref.at[m, land], ks.at[m, i], kr.at[m, i], ynb)
        q[m] = (dot(x, WA[:, :QC]) + dot(onehot[m], tmix[:, :QC])).astype(BF)
        tick(2.5)
    save(xn, xn_o)
    save(q, q_o)
    for m in range(2):
        for i, ref in enumerate((kb, vb)):
            arrive(ref.at[m, land_here], kr.at[m, i])
    save(kb, kb_o)
    save(vb, vb_o)

    def head(h, _):
        win, hm = head_window(h)
        toep[...] = toeplitz(base, h)
        lane_h = lax.broadcasted_iota(jnp.int32, (1, 128), 1) == h

        def tile(t, _):
            m, j = t // 2, lax.rem(t, 2)
            rows = pl.ds(pl.multiple_of(HALF * j, 16), HALF)
            krows = pl.ds(pl.multiple_of(HALF * j, 16), KW)
            s = dot_nt(q[m, rows, win] * hm, kb[m, krows, win])
            s = s * SCALE + (toep[...] + mask[m, j])
            peak = jnp.max(s, -1, keepdims=True)
            e = jnp.exp(s - peak)
            total = jnp.sum(e, -1, keepdims=True)
            p = (e * (1.0 / total)).astype(BF)
            of[m, rows, win] += dot(p, vb[m, krows, win] * hm)
            lse[m, rows] = jnp.where(lane_h, peak + jnp.log(total), lse[m, rows])
            return 0

        return lax.fori_loop(0, 4, tile, 0)

    for n in range(8):
        lax.fori_loop(n, n + 1, head, 0)
        tick(3.1)
    save(lse, lse_o)
    for m in range(2):
        o[m] = of[m].astype(BF)
    save(o, o_o)
    complete("O")
    save(WO, WO_o)

    for m in range(2):
        x_send[m] = dot(o[m, other], WO[...]).astype(BF)
        go(x_send.at[m], x_recv.at[m], as_.at[m], ar.at[m], sib)
    for m in range(2):
        hres[m] = lat[m].astype(F32) + dot(o[m, mine], WO[...])
    tick(4.0)
    for m in range(2):
        arrive(x_recv.at[m], ar.at[m])
        hv = hres[m] + x_recv[m].astype(F32)
        hres[m] = hv
        n, _ = norm(hv)
        hn[m, mine] = (n * gains[1:2]).astype(BF)
        go(hn.at[m, mine], hn.at[m, mine], hs.at[m], hr.at[m], sib)
        tick(2.5)
    save(hres, hres_o)
    for m in range(2):
        arrive(hn.at[m, other], hr.at[m])
    save(hn, hn_o)
    for s, W in enumerate((WI0, WI1)):
        complete("I0" if s == 0 else "I1")
        save(W, (WI0_o, WI1_o)[s])
        for m in range(2):
            def up(i, _):
                cols = pl.ds(pl.multiple_of(i * 384, 128), 384)
                put = pl.ds(pl.multiple_of(i * 384 + D * s, 128), 384)
                u = dot(hn[m], W[:, cols])
                phi = 0.5 + 0.5 * lax.erf(u * (0.5 ** 0.5))
                g[pl.ds(TOK * m, TOK), put] = (u * phi).astype(BF)
                gp[pl.ds(TOK * m, TOK), put] = (phi + u * (jnp.exp(-0.5 * u * u) * 0.3989422804014327)).astype(BF)
                return 0

            lax.fori_loop(0, 3, up, 0)
            tick(3.3)
    save(g, g_o)
    save(gp, gp_o)
    for m in range(2):
        rows = pl.ds(pl.multiple_of(TOK * m + HALF * (1 - k), 16), HALF)
        arrive(df.at[rows], fr.at[m])
    save(df, df_o)
    for s, grad in enumerate((gb0, gb1)):
        for i in range(3):
            cols = pl.ds(384 * i, 384)
            fill_part(grad, g, df, cols, D * s, cols)
            tick(1.3)
        save(grad, (gb0_o, gb1_o)[s])
    for s, W in enumerate((WB0, WB1)):
        complete("B0" if s == 0 else "B1")
        save(W, (WB0_o, WB1_o)[s])
    for cp in saves:
        cp.wait()
    for wait in pend:
        wait()


def gather_forward(p, cot):
    S = jax.ShapeDtypeStruct
    dma = pltpu.SemaphoreType.DMA
    V, anyspace = pl.BlockSpec(memory_space=pltpu.VMEM), pl.BlockSpec(memory_space=pl.ANY)
    weights = [(D, 3 * QC), (QC, D), (D, D), (D, D), (D, D), (D, D)]
    kept = [((2, TOK, D), BF), ((2, TOK, QC), BF), ((2, KEYS, QC), BF), ((2, KEYS, QC), BF), ((2, TOK, 128), F32), ((2, TOK, QC), BF),
            ((2, HALF, D), F32), ((2, TOK, D), BF), ((2 * TOK, FH), BF), ((2 * TOK, FH), BF), ((2 * TOK, D), BF), ((D, D), BF), ((D, D), BF)]
    return pl.pallas_call(
        gather_forward_kernel,
        out_shape=[S(s, t) for s, t in kept] + [S(s, BF) for s in weights]
        + [S((8, 16, 144), BF), S((2, 2, HALF, KW), BF), S((2, TOK, 32), BF), S((144, 2 * QC), BF)],
        in_specs=[anyspace] * 7 + [V] * 5, out_specs=[anyspace] * 22 + [V],
        scratch_shapes=[pltpu.VMEM(s, BF) for s in weights] + [pltpu.VMEM(s, t) for s, t in kept]
        + [pltpu.VMEM((8, 16, 144), BF), pltpu.VMEM((4, 8, KW), F32), pltpu.VMEM((2, 2, HALF, 128), F32), pltpu.VMEM((2, TOK, 32), BF),
           pltpu.VMEM((128, 2 * QC), BF), pltpu.VMEM((7, 16, 2 * QC), BF), pltpu.VMEM((32, 2 * QC), BF), pltpu.VMEM((2, 2, HALF, KW), BF),
           pltpu.VMEM((HALF, KW), F32), pltpu.VMEM((2, TOK, QC), F32), pltpu.VMEM((2, HALF, D), BF), pltpu.VMEM((2, HALF, D), BF),
           pltpu.VMEM((2, HALF, D), BF), pltpu.VMEM((2, HALF, D), BF),
           dma((6, 16)), dma((6, 8)), dma((6, 8)), dma((6,)), dma((7,)), dma((7,)), dma((3,)), dma((3,)), dma((1,)), dma((1,)),
           dma((2,)), dma((2,)), dma((7,)), dma((7,)), dma((2, 2)), dma((2, 2)), dma((2,)), dma((2,)), dma((2,)), dma((2,)), dma((2,)), dma((2,)), dma((11,)), dma((22,))],
        compiler_params=pltpu.CompilerParams(collective_id=1, has_side_effects=True, vmem_limit_bytes=127 * 2 ** 19),
        name="gather_forward")(*p["raw"], p["lat"], cot, p["gains"], p["te"], p["seg_row"], p["seg_col"], p["base"])


def prologue(latents, segment_ids, time_embed, norm_gains, attn_in, time_in, rel_bias, out_proj, mlp_in, mlp_out, cotangent):
    c, b, y, k = place()

    def pick(v, axis):
        return lax.dynamic_index_in_dim(v, k, axis, keepdims=False)

    raw = (attn_in, time_in, mlp_in, jnp.pad(pick(out_proj.reshape(2, 72, D), 0), ((0, 8), (0, 0))), mlp_out)
    code = (segment_ids.reshape(2, HALF) + 2).astype(F32)
    seg_row = jnp.pad(code, ((0, 6), (80, KW - 80 - HALF)))
    seg_col = jnp.broadcast_to(code[..., None], (2, HALF, 128))
    te = jnp.pad(time_embed.reshape(10, D), ((0, 6), (0, 0))).reshape(16, 8, 144).transpose(1, 0, 2)
    bias = pick(rel_bias.reshape(25, 8, 2), 2)
    base = jnp.full((8, KW), NEG, F32)
    places = [80 + 34 * dr + dc for dr in range(-2, 3) for dc in range(-2, 3)]
    base = base.at[:, jnp.array(places)].set(bias.T)
    filled = (segment_ids.reshape(2, HALF, 1) >= 0).astype(F32)
    return dict(raw=raw, te=te, seg_row=seg_row, seg_col=seg_col, base=base, filled=filled, lat=latents.reshape(2, HALF, D), gains=norm_gains.T)


RSPEC = {"A": (144, 640, 640), "O": (80, 384, 384), "I0": (144, 384, 384), "I1": (144, 384, 384), "B0": (144, 384, 384), "B1": (144, 384, 384)}
KEEP = {"A": (36, 48, 4), "I0": (36, 48, 4), "I1": (36, 48, 4), "O": (36, 48, 2), "B0": (144, 144, 2), "B1": (144, 144, 2)}
ORDER = (1, 3, 2, 0)


def scatter_scratch(name):
    rows, wide, mid = RSPEC[name]
    slab = wide + mid
    dma = pltpu.SemaphoreType.DMA
    _, held, sources = KEEP[name]
    sends = {"A": 4, "I": 4, "O": 2, "B": 1}[name[0]]
    return [pltpu.VMEM((8 * rows, wide), BF), pltpu.VMEM((4 * rows, slab), BF), pltpu.VMEM((3 * rows, slab), BF),
            pltpu.VMEM((sends, held, slab), BF), pltpu.VMEM((sources, held, slab), BF),
            dma((4,)), dma((4,)), dma((8,)), dma((8,)), dma((3,)), dma((3,)), dma((4,)), dma((4,))]


N_SCATTER = 13


class Scatter:
    def __init__(self, name, grad, total, scratch, pend):
        self.name, self.grad, self.total, self.pend = name, grad, total, pend
        (self.yr, self.xr, self.zr, self.stage, self.fr, self.ys, self.yw, self.xs, self.xw, self.zs, self.zw, self.fs, self.fw) = scratch
        self.rows, self.wide, self.mid = RSPEC[name]
        self.c, self.b, self.y, self.k = place()
        self.z, self.x = self.c // 2, lax.rem(self.c, 2)
        y, w, l = self.y, self.wide, self.mid
        self.slab = pl.ds(pl.multiple_of(w * y, 128), w + l)
        self.mids = pl.ds(w, l)
        self.side = pl.ds(pl.multiple_of((w + l) * y, 128), w)
        self.away = pl.ds(pl.multiple_of((w + l) * (1 - y), 128), w)
        self.slab_mid = pl.ds(pl.multiple_of(w * (1 - y), 128), l)
        self.slab_side = pl.ds(pl.multiple_of(l * y, 128), w)
        self.xdev, self.ydev = {"canvas": self.c + 1 - 2 * self.x}, {"band": self.b + 2 - 4 * self.y}

    def at(self, group):
        return pl.ds(pl.multiple_of(group * self.rows, 16), self.rows)

    def pair(self, d):
        return pl.ds(pl.multiple_of(lax.rem(self.z + d, 4) * (2 * self.rows), 16), 2 * self.rows)

    def go(self, make):
        make().start()
        self.pend.append(make)

    def parts(self):
        return self.away, self.mids, self.side

    def group(self, d, x):
        return self.at(2 * lax.rem(self.z + d, 4) + x)

    def send_y(self):
        for d in ORDER:
            self.go(lambda d=d: remote(self.grad.at[self.pair(d), self.away], self.yr.at[self.pair(d)], self.ys.at[d], self.yw.at[d], self.ydev))

    def send_mid(self, steps=ORDER):
        for d in steps:
            self.go(lambda d=d: remote(self.grad.at[self.group(d, 1 - self.x), self.mids], self.xr.at[pl.ds(self.rows * d, self.rows), self.slab_mid],
                                       self.xs.at[d], self.xw.at[d], self.xdev))

    def side_x(self, d):
        rows2 = self.pair(d)
        pltpu.make_async_copy(self.yr.at[rows2], self.yr.at[rows2], self.yw.at[d]).wait()
        self.grad[rows2, self.side] += self.yr[rows2]
        self.go(lambda: remote(self.grad.at[self.group(d, 1 - self.x), self.side], self.xr.at[pl.ds(self.rows * d, self.rows), self.slab_side],
                               self.xs.at[4 + d], self.xw.at[4 + d], self.xdev))

    def sum_x(self, d):
        rows = pl.ds(self.rows * d, self.rows)
        for view, sem in ((self.xr.at[rows, self.slab_mid], d), (self.xr.at[rows, self.slab_side], 4 + d)):
            pltpu.make_async_copy(view, view, self.xw.at[sem]).wait()
        return self.grad[self.group(d, self.x), self.slab] + self.xr[rows]

    def send_z(self, d):
        self.grad[self.group(d, self.x), self.slab] = self.sum_x(d)
        self.go(lambda: remote(self.grad.at[self.group(d, self.x), self.slab], self.zr.at[pl.ds((3 - d) * self.rows, self.rows)], self.zs.at[d - 1],
                               self.zw.at[3 - d], {"canvas": 2 * lax.rem(self.z + d, 4) + self.x}))

    def dests(self):
        sources = KEEP[self.name][2]
        if self.name[0] == "B":
            return [(0, 2 * self.k + int(self.name[1]))]
        return [(i, 2 * self.k + i if sources == 2 else i) for i in range(sources)]

    def finish(self):
        acc = self.sum_x(0).astype(F32)
        for i in (2, 0, 1):
            rows = pl.ds(i * self.rows, self.rows)
            pltpu.make_async_copy(self.zr.at[rows], self.zr.at[rows], self.zw.at[i]).wait()
            acc = acc + self.zr[rows].astype(F32)
        n, held, sources = KEEP[self.name]
        slab = self.wide + self.mid
        if self.name[0] == "B":
            self.stage[0] = acc.astype(BF)
        else:
            self.total[0:self.rows, 0:slab] = acc
            for i in range(sources):
                self.stage[i, 0:n] = self.total[n * i:n * i + n, 0:slab].astype(BF)
                self.stage[i, n:held] = jnp.zeros((held - n, slab), BF)
        slot = self.b if sources == 4 else self.y
        for i, dest in self.dests():
            @pl.when(self.b == dest)
            def _():
                self.fr[slot] = self.stage[i]

            @pl.when(self.b != dest)
            def _():
                remote(self.stage.at[i], self.fr.at[slot], self.fs.at[i], self.fw.at[slot], {"band": dest}).start()

    def sent(self):
        for i, dest in self.dests():
            @pl.when(self.b != dest)
            def _():
                remote(self.stage.at[i], self.fr.at[0], self.fs.at[i], self.fw.at[0], {"band": dest}).wait_send()

    def collect(self, out):
        n, held, sources = KEEP[self.name]
        for i in range(sources):
            src = i if sources == 4 else 2 * i + self.y

            @pl.when(self.b != src)
            def _():
                pltpu.make_async_copy(self.fr.at[i], self.fr.at[i], self.fw.at[i]).wait()
        w, l = self.wide, self.mid
        for half in range(sources // 2):
            lo, hi = self.fr[half].astype(F32)[:n], self.fr[half + sources // 2].astype(F32)[:n]
            dst = out.at[half] if sources == 4 else out
            dst[:, 0:w] = lo[:, :w]
            dst[:, w:w + l] = lo[:, w:] + hi[:, :l]
            dst[:, w + l:] = hi[:, l:]


def everyone():
    c, b, y, k = place()
    return [{"band": lax.rem(b + d, 4)} for d in (1, 2, 3)] + [{"canvas": lax.rem(c + d, 8)} for d in range(1, 8)]


def fill_part(grad, left, right, cols, lefts, rights):
    def step(i, _):
        r = pl.multiple_of(i * 384, 128)
        grad[pl.ds(r, 384), cols] = dot_tn(left[:, pl.ds(r + lefts, 384)], right[:, rights]).astype(BF)
        return 0

    lax.fori_loop(0, grad.shape[0] // 384, step, 0)


def mlp_back_kernel(cot_in, filled, gains, WI0_in, WI1_in, WB0_in, WB1_in, hres, hn_in, g_in, gp, df_in, gb0, gb1,
                    out, dh, da, gain, out_b, grad_i0, grad_i1,
                    grad_b0, grad_b1, cot, WI0, WI1, WB0, WB1, hn, g, du, gi, x_send, x_recv, f_send, f_recv, dn, ds_, dr_, xs, xr, as_, ar, ls, gs, *scratch):
    c, b, y, k = place()
    sib = {"band": b + 1 - 2 * k}
    df = da
    loads = [pltpu.make_async_copy(src, dst, ls.at[i])
             for i, (src, dst) in enumerate(((gb0, grad_b0), (gb1, grad_b1), (WB0_in, WB0), (WB1_in, WB1), (g_in, g), (df_in, df), (gp, du), (hres, dh), (cot_in, cot), (hn_in, hn),
                                            (WI0_in, WI0), (WI1_in, WI1)))]
    for cp in loads:
        cp.start()
    greet([{"band": lax.rem(b + d, 4)} for d in (1, 2, 3)] + [{"canvas": c + 1 - 2 * lax.rem(c, 2)}] + [{"canvas": lax.rem(c + d, 8)} for d in (2, 4, 6)])
    pend = []
    rs = [Scatter("B0", grad_b0, None, scratch[:N_SCATTER], pend), Scatter("B1", grad_b1, None, scratch[N_SCATTER:], pend)]
    rs[1].fr, rs[1].fw = rs[0].fr, rs[0].fw

    def half(m, which):
        return pl.ds(pl.multiple_of(TOK * m + HALF * which, 16), HALF)

    for s in range(2):
        loads[s].wait()
        rs[s].send_y()
        if s == 0:
            rs[s].send_mid()
    for cp in loads[2:5]:
        cp.wait()
    for m in range(2):
        def down_other(i, _):
            cols = pl.ds(pl.multiple_of(i * 384, 128), 384)
            f_send[m, :, cols] = (dot(g[half(m, 1 - k), 0:D], WB0[:, cols]) + dot(g[half(m, 1 - k), D:], WB1[:, cols])).astype(BF)
            return 0

        lax.fori_loop(0, 3, down_other, 0)
        loads.append(remote(f_send.at[m], f_recv.at[m], ds_.at[m], dr_.at[m], sib))
        loads[-1].start()

        def down(i, _):
            cols = pl.ds(pl.multiple_of(i * 384, 128), 384)
            dn[m, :, cols] = dot(g[half(m, k), 0:D], WB0[:, cols]) + dot(g[half(m, k), D:], WB1[:, cols])
            return 0

        lax.fori_loop(0, 3, down, 0)

    def back_act(m, s):
        def step(i, _):
            r = pl.multiple_of(i * 384, 128)
            cols = pl.ds(pl.multiple_of(r + D * s, 128), 384)
            rows = pl.ds(TOK * m, TOK)
            du[rows, cols] = (dot_nt(df[rows], (WB0, WB1)[s][pl.ds(r, 384)]) * du[rows, cols].astype(F32)).astype(BF)
            return 0

        lax.fori_loop(0, 3, step, 0)

    rs[0].side_x(1)
    for cp in loads[5:12]:
        cp.wait()
    back_act(0, 0)
    rs[0].side_x(3)
    rs[0].send_z(1)
    for m in range(2):
        v = f_recv.at[m]
        pltpu.make_async_copy(v, v, dr_.at[m]).wait()
        out[m] = ((dh[m] + (dn[m] + v[...].astype(F32))) * filled[m]).astype(BF)
    back_act(1, 0)
    rs[0].side_x(2)
    rs[0].send_z(3)
    back_act(0, 1)
    rs[0].side_x(0)
    rs[1].send_mid()
    rs[0].send_z(2)
    back_act(1, 1)
    rs[1].side_x(1)
    saves = []
    for s in range(2):
        def step(i, _):
            r = pl.multiple_of(i * 384, 128)
            gi[s, pl.ds(r, 384)] = dot_tn(hn[:, pl.ds(r, 384)], du[:, D * s:D * s + D]).astype(BF)
            return 0

        lax.fori_loop(0, 3, step, 0)
        cp = pltpu.make_async_copy(gi.at[s], (grad_i0, grad_i1)[s], gs.at[s])
        cp.start()
        saves.append(cp)
        if s == 0:
            rs[1].side_x(3)
            rs[1].send_z(1)
            rs[0].finish()
        else:
            rs[1].side_x(2)
            rs[1].send_z(3)

    for m in range(2):
        def hid(i, _):
            r = pl.multiple_of(i * 384, 128)
            rows = pl.ds(r, 384)
            v = dot_nt(du[half(m, 1 - k), 0:D], WI0[rows]) + dot_nt(du[half(m, 1 - k), D:], WI1[rows])
            x_send[m, :, rows] = v.astype(BF)
            return 0

        lax.fori_loop(0, 3, hid, 0)
        cp = remote(x_send.at[m], x_recv.at[m], xs.at[m], xr.at[m], sib)
        cp.start()
        loads.append(cp)

        def hid_own(i, _):
            r = pl.multiple_of(i * 384, 128)
            rows = pl.ds(r, 384)
            dn[m, :, rows] = dot_nt(du[half(m, k), 0:D], WI0[rows]) + dot_nt(du[half(m, k), D:], WI1[rows])
            return 0

        lax.fori_loop(0, 3, hid_own, 0)
        if m == 0:
            rs[1].side_x(0)
            rs[1].send_z(2)
    gain_two = jnp.zeros((1, D), F32)
    for m in range(2):
        pltpu.make_async_copy(x_recv.at[m], x_recv.at[m], xr.at[m]).wait()
        grad = dn[m] + x_recv[m].astype(F32)
        n, r = norm(dh[m])
        gain_two = gain_two + jnp.sum(grad * n, 0, keepdims=True)
        v = cot[m].astype(F32) * filled[m] + norm_back(n, r, grad * gains[1:2])
        dh[m] = v
        da[half(m, k)] = v.astype(BF)
        cp = remote(da.at[half(m, k)], da.at[half(m, k)], as_.at[m], ar.at[m], sib)
        cp.start()
        loads.append(cp)
    gain[...] = jnp.broadcast_to(gain_two, (8, D))
    for m in range(2):
        v = da.at[half(m, 1 - k)]
        pltpu.make_async_copy(v, v, ar.at[m]).wait()
    rs[1].finish()
    rs[0].collect(out_b)
    rs[0].sent()
    rs[1].sent()
    for cp in saves:
        cp.wait()
    for cp in loads[12:]:
        cp.wait_send()
    for make in pend:
        make().wait_send()


def mlp_back(*args):
    S = jax.ShapeDtypeStruct
    dma = pltpu.SemaphoreType.DMA
    V, anyspace = pl.BlockSpec(memory_space=pltpu.VMEM), pl.BlockSpec(memory_space=pl.ANY)
    return pl.pallas_call(
        mlp_back_kernel,
        out_shape=[S((2, HALF, D), BF), S((2, HALF, D), F32), S((2 * TOK, D), BF), S((8, D), F32), S((144, D), F32), S((D, D), BF), S((D, D), BF)],
        in_specs=[anyspace, V, V] + [anyspace] * 11, out_specs=[V] * 5 + [anyspace] * 2,
        scratch_shapes=[pltpu.VMEM((D, D), BF), pltpu.VMEM((D, D), BF), pltpu.VMEM((2, HALF, D), BF)] + [pltpu.VMEM((D, D), BF)] * 4
        + [pltpu.VMEM((2 * TOK, D), BF), pltpu.VMEM((2 * TOK, FH), BF), pltpu.VMEM((2 * TOK, FH), BF), pltpu.VMEM((2, D, D), BF),
                        pltpu.VMEM((2, HALF, D), BF), pltpu.VMEM((2, HALF, D), BF), pltpu.VMEM((2, HALF, D), BF), pltpu.VMEM((2, HALF, D), BF),
                        pltpu.VMEM((2, HALF, D), F32)]
        + [dma((2,))] * 6 + [dma((12,)), dma((2,))] + scatter_scratch("B0") + scatter_scratch("B1"),
        compiler_params=pltpu.CompilerParams(collective_id=2, has_side_effects=True, vmem_limit_bytes=127 * 2 ** 19),
        name="mlp_back")(*args)


def attn_back_kernel(WA, WO, ti, gains, lat, xn, q, kb, vb, lse, o, da, dh, mask, base, onehot, gain_two, te, gi0, gi1,
                     dlat, gt, small, out_o, out_a, out_i, out_t,
                     dt_all,
                     q_v, kb_v, vb_v, grad_o, grad_a, grad_i0, grad_i1, do, dqkv, rim, rim_in, tsum, tsum_in, gt_send, gt_in, x_send, x_recv, dbias, sm_send, sm_in, total,
                     ks, kr, ts, tr, ps, pr, us, ur, vs, vr, ls, xs, xr, ss, sr, bs, br, *scratch):
    c, b, y, k = place()
    sib, ynb = {"band": b + 1 - 2 * k}, {"band": b + 2 - 4 * y}
    peers = [lax.rem(c + d, 8) for d in range(1, 8)]
    pend, waits = [], iter(range(20))

    def load(src, dst):
        cp = pltpu.make_async_copy(src, dst, ls.at[next(waits)])
        cp.start()
        return cp

    loads_i = [load(gi0, grad_i0), load(gi1, grad_i1)]
    load_dh = load(dh, dlat)
    load_q = [load(q, q_v), load(kb, kb_v), load(vb, vb_v)]
    greet(everyone())
    n = N_SCATTER
    rs_o = Scatter("O", grad_o, total, scratch[:n], pend)
    rs_a = Scatter("A", grad_a, total, scratch[n:2 * n], pend)
    rs_i = [Scatter("I0", grad_i0, total, scratch[2 * n:3 * n], pend), Scatter("I1", grad_i1, total, scratch[3 * n:], pend)]

    def go(make):
        make().start()
        pend.append(make)

    def arrive(view, sem):
        pltpu.make_async_copy(view, view, sem).wait()

    slots = pl.ds(pl.multiple_of(16 * c, 16), 16)
    for s in range(2):
        loads_i[s].wait()
        rs_i[s].send_y()
        rs_i[s].send_mid()

    def first(o_v, da_v, wo_v):
        parts = [load(o, o_v), load(da, da_v), load(WO, wo_v)]
        for cp in parts:
            cp.wait()
        for i, cols in enumerate(rs_o.parts()):
            grad_o[:, cols] = dot_tn(o_v[...], da_v[:, cols]).astype(BF)
            if i == 0:
                rs_o.send_y()
            if i == 1:
                rs_o.send_mid()
        for m in range(2):
            do[m] = dot_nt(da_v[pl.ds(TOK * m, TOK)], wo_v[...]).astype(BF)

    pl.run_scoped(first, pltpu.VMEM((2 * TOK, QC), BF), pltpu.VMEM((2 * TOK, D), BF), pltpu.VMEM((QC, D), BF))

    def second(dqf, dkf, dvf, toep, dsum):
        dqf[...] = jnp.zeros_like(dqf)
        dkf[...] = jnp.zeros_like(dkf)
        dvf[...] = jnp.zeros_like(dvf)
        for cp in load_q:
            cp.wait()

        def head(h, _):
            win, hm = head_window(h)
            toep[...] = toeplitz(base, h)
            dsum[...] = jnp.zeros_like(dsum)
            lane_h = lax.broadcasted_iota(jnp.int32, (1, 128), 1) == h

            def tile(t, _):
                m, j = t // 2, lax.rem(t, 2)
                rows = pl.ds(pl.multiple_of(HALF * j, 16), HALF)
                krows = pl.ds(pl.multiple_of(HALF * j, 16), KW)
                qm, dm = q_v[m, rows, win] * hm, do[m, rows, win] * hm
                kw = kb_v[m, krows, win]
                level = jnp.sum(jnp.where(lane_h, lse[m, rows], 0.0), -1, keepdims=True)
                p = jnp.exp(dot_nt(qm, kw) * SCALE + (toep[...] + mask[m, j]) - level)
                dp = dot_nt(dm, vb_v[m, krows, win])
                delta = jnp.sum(p * dp, -1, keepdims=True)
                ds = (p * (dp - delta)).astype(BF)
                dsum[...] += ds.astype(F32)
                dqf[m, rows, win] += dot(ds, kw * hm)
                dkf[m, krows, win] += dot_tn(ds, qm)
                dvf[m, krows, win] += dot_tn(p.astype(BF), dm)
                return 0

            lax.fori_loop(0, 4, tile, 0)
            strip = dsum[0:8]
            for r in range(8, HALF, 8):
                strip = strip + pltpu.roll(dsum[r:r + 8], KW - r, 1)
            line = strip[0:1]
            for r in range(1, 8):
                line = line + pltpu.roll(strip, KW - r, 1)[r:r + 1]
            dbias[pl.ds(h, 1)] = line
            return 0

        for i in range(4):
            lax.fori_loop(2 * i, 2 * i + 2, head, 0)
            if i == 0:
                for d in (1, 3, 2):
                    rs_i[0].side_x(d)
            elif i == 1:
                rs_i[0].side_x(0)
                for d in (1, 3, 2):
                    rs_i[0].send_z(d)
                rs_i[1].side_x(1)
            elif i == 2:
                for d in (3, 2, 0):
                    rs_i[1].side_x(d)
                rs_i[1].send_z(1)
        away = pl.ds(pl.multiple_of(624 * (1 - y), 16), 80)
        edge = pl.ds(pl.multiple_of(544 - 464 * y, 16), 80)
        for m in range(2):
            rim[m, 0] = (dkf[m, away] * SCALE).astype(BF)
            rim[m, 1] = dvf[m, away].astype(BF)
            go(lambda m=m: remote(rim.at[m], rim_in.at[m], ks.at[m], kr.at[m], ynb))
        for m in range(2):
            tok = pl.ds(TOK * m, TOK)
            dqkv[tok, 0:QC] = (dqf[m] * SCALE).astype(BF)
        for d in ORDER:
            rs_o.side_x(d)
        rs_i[1].send_z(3)
        rs_i[1].send_z(2)
        for m in range(2):
            arrive(rim_in.at[m], kr.at[m])
            tok = pl.ds(TOK * m, TOK)
            dkf[m, edge] += rim_in[m, 0].astype(F32) * (1.0 / SCALE)
            dvf[m, edge] += rim_in[m, 1].astype(F32)
            dqkv[tok, QC:2 * QC] = (dkf[m, 80:624] * SCALE).astype(BF)
            dqkv[tok, 2 * QC:] = dvf[m, 80:624].astype(BF)

    pl.run_scoped(second, pltpu.VMEM((2, TOK, QC), F32), pltpu.VMEM((2, KEYS, QC), F32), pltpu.VMEM((2, KEYS, QC), F32),
                  pltpu.VMEM((HALF, KW), F32), pltpu.VMEM((HALF, KW), F32))

    def third(xn_v, wa_v, dn):
        loads = [load(xn, xn_v), load(WA, wa_v)]
        tq = dot_tn(onehot[0], dqkv[0:TOK, 0:QC]) + dot_tn(onehot[1], dqkv[TOK:, 0:QC])
        tv = dot_tn(onehot[0], dqkv[0:TOK, 2 * QC:]) + dot_tn(onehot[1], dqkv[TOK:, 2 * QC:])
        tsum[:, 0:QC] = tq[0:16].astype(BF)
        tsum[:, QC:] = tv[0:16].astype(BF)
        go(lambda: remote(tsum, tsum_in, ts.at[0], tr.at[0], ynb))
        loads[0].wait()
        for i, cols in enumerate(rs_a.parts()):
            fill_part(grad_a, xn_v, dqkv, cols, 0, cols)
            if i == 0:
                rs_a.send_y()
                arrive(tsum_in, tr.at[0])
                dt_all[k, slots] = (tsum[...].astype(F32) + tsum_in[...].astype(F32)).astype(BF)
                for n, p in enumerate(peers):
                    go(lambda n=n, p=p: remote(dt_all.at[k, slots], dt_all.at[k, slots], ps.at[n], pr.at[6 - n], {"canvas": p}))
            if i == 1:
                rs_a.send_mid((1, 3))
        for d in (1, 3, 2):
            rs_o.send_z(d)
        rs_i[0].finish()
        loads[1].wait()
        for m in range(2):
            rows = pl.ds(pl.multiple_of(TOK * m + HALF * (1 - k), 16), HALF)
            rows_own = pl.ds(pl.multiple_of(TOK * m + HALF * k, 16), HALF)

            def back(n, _):
                cols = pl.ds(pl.multiple_of(n * 384, 128), 384)
                x_send[m, :, cols] = dot_nt(dqkv[rows], wa_v[cols]).astype(BF)
                return 0

            lax.fori_loop(0, 3, back, 0)
            go(lambda m=m: remote(x_send.at[m], x_recv.at[m], xs.at[m], xr.at[m], sib))

            def back_own(n, _):
                cols = pl.ds(pl.multiple_of(n * 384, 128), 384)
                dn[m, :, cols] = dot_nt(dqkv[rows_own], wa_v[cols])
                return 0

            lax.fori_loop(0, 3, back_own, 0)
        rs_i[1].finish()
        rs_a.side_x(1)
        rs_a.send_mid((2,))
        for n in range(7):
            arrive(dt_all.at[k, pl.ds(pl.multiple_of(16 * lax.rem(c + n + 1, 8), 16), 16)], pr.at[n])
        go(lambda: remote(dt_all.at[k], dt_all.at[k], us.at[0], ur.at[0], sib))
        gt_send[...] = dot_nt(dt_all[k], ti[...])
        go(lambda: remote(gt_send, gt_in, us.at[1], ur.at[1], sib))
        rs_a.side_x(3)
        rs_a.send_mid((0,))
        rs_a.send_z(1)
        load_dh.wait()
        gain_one = jnp.zeros((1, D), F32)
        for m in range(2):
            arrive(x_recv.at[m], xr.at[m])
            grad = dn[m] + x_recv[m].astype(F32)
            n, r = norm(lat[m].astype(F32))
            gain_one = gain_one + jnp.sum(grad * n, 0, keepdims=True)
            dlat[m] = dlat[m] + norm_back(n, r, grad * gains[0:1])
            if m == 0:
                rs_a.side_x(2)
                rs_a.send_z(3)
        first_row = lax.broadcasted_iota(jnp.int32, (8, 1), 0) == 0
        both = jnp.where(first_row, jnp.broadcast_to(gain_one, (8, D)), gain_two[...])
        for p in range(8):
            sm_send[p, 0:8] = dbias[...]
            sm_send[p, 8:16] = (pltpu.roll(both, D - 144 * p, 1) if p else both)[:, 0:KW]

    pl.run_scoped(third, pltpu.VMEM((2 * TOK, D), BF), pltpu.VMEM((D, 3 * QC), BF), pltpu.VMEM((2, HALF, D), F32))
    for n, p in enumerate(peers):
        go(lambda n=n, p=p: remote(sm_send.at[p], sm_in.at[6 - n], ss.at[n], sr.at[6 - n], {"canvas": p}))
    rs_o.finish()
    arrive(gt_in, ur.at[1])
    gt_in[...] = gt_in[...] + gt_send[...]
    for n, p in enumerate(peers):
        go(lambda n=n, p=p: remote(gt_in.at[pl.ds(pl.multiple_of(16 * p, 16), 16)], gt.at[c], vs.at[n], vr.at[6 - n], {"canvas": p}))
    gt[c] = gt_in[pl.ds(pl.multiple_of(16 * c, 16), 16)]
    rs_a.side_x(0)
    rs_a.send_z(2)
    acc = sm_send[c]
    for n in range(7):
        arrive(sm_in.at[n], sr.at[n])
        acc = acc + sm_in[n]
    small[b] = acc
    for i in range(3):
        go(lambda i=i: remote(small.at[b], small.at[b], bs.at[i], br.at[2 - i], {"band": lax.rem(b + i + 1, 4)}))
    def last(buf_a, buf_i, buf_t):
        for s in range(2):
            rs_i[s].collect(buf_i.at[s])
            for half in range(2):
                for n in range(8):
                    at = 576 * n + 288 * half + 144 * s
                    out_i[:, at:at + 144] = buf_i[s, half, :, 144 * n:144 * n + 144]
        rs_o.collect(out_o)
        for n in range(7):
            arrive(gt.at[lax.rem(c + n + 1, 8)], vr.at[n])
        arrive(dt_all.at[1 - k], ur.at[0])
        slots_all = te[...].reshape(128, 144)
        for half in range(2):
            total[...] = dot_tn(slots_all, dt_all[half])
            for i in range(4):
                @pl.when(b == i)
                def _():
                    buf_t[...] = total[36 * i:36 * i + 36]

            for t in range(2):
                for i in range(8):
                    at = D * t + 144 * i + 72 * half
                    out_t[:, at:at + 72] = buf_t[:, QC * t + 80 * i:QC * t + 80 * i + 72]
        for i in range(3):
            arrive(small.at[lax.rem(b + i + 1, 4)], br.at[i])
        rs_a.finish()
        rs_a.collect(buf_a)
        for half in range(2):
            for t in range(3):
                for i in range(8):
                    at = D * t + 144 * i + 72 * half
                    out_a[:, at:at + 72] = buf_a[half, :, QC * t + 80 * i:QC * t + 80 * i + 72]

    pl.run_scoped(last, pltpu.VMEM((2, 36, 3 * QC), F32), pltpu.VMEM((2, 2, 36, D), F32), pltpu.VMEM((36, 2 * QC), F32))
    for rs in (rs_o, rs_a, *rs_i):
        rs.sent()
    for make in pend:
        make().wait_send()


def attn_back(*args):
    S = jax.ShapeDtypeStruct
    dma = pltpu.SemaphoreType.DMA
    V, anyspace = pl.BlockSpec(memory_space=pltpu.VMEM), pl.BlockSpec(memory_space=pl.ANY)
    return pl.pallas_call(
        attn_back_kernel,
        out_shape=[S((2, HALF, D), F32), S((8, 16, 144), F32), S((4, 16, KW), F32), S((36, D), F32), S((36, 3 * D), F32), S((36, 2 * FH), F32), S((36, 2 * D), F32)],
        in_specs=[anyspace, anyspace, V, V, V] + [anyspace] * 4 + [V] + [anyspace] * 3 + [V] * 5 + [anyspace] * 2, out_specs=[V] * 7,
        scratch_shapes=[pltpu.VMEM((2, 128, 2 * QC), BF),
                        pltpu.VMEM((2, TOK, QC), BF), pltpu.VMEM((2, KEYS, QC), BF), pltpu.VMEM((2, KEYS, QC), BF),
                        pltpu.VMEM((QC, D), BF), pltpu.VMEM((D, 3 * QC), BF), pltpu.VMEM((D, D), BF), pltpu.VMEM((D, D), BF), pltpu.VMEM((2, TOK, QC), BF),
                        pltpu.VMEM((2 * TOK, 3 * QC), BF),
                        pltpu.VMEM((2, 2, 80, QC), BF), pltpu.VMEM((2, 2, 80, QC), BF), pltpu.VMEM((16, 2 * QC), BF), pltpu.VMEM((16, 2 * QC), BF),
                        pltpu.VMEM((128, 144), F32), pltpu.VMEM((128, 144), F32),
                        pltpu.VMEM((2, HALF, D), BF), pltpu.VMEM((2, HALF, D), BF), pltpu.VMEM((8, KW), F32), pltpu.VMEM((8, 16, KW), F32), pltpu.VMEM((7, 16, KW), F32),
                        pltpu.VMEM((144, 1280), F32),
                        dma((2,)), dma((2,)), dma((1,)), dma((1,)), dma((7,)), dma((7,)), dma((2,)), dma((2,)), dma((7,)), dma((7,)), dma((20,)), dma((2,)), dma((2,)),
                        dma((7,)), dma((7,)), dma((3,)), dma((3,))]
        + scatter_scratch("O") + scatter_scratch("A") + scatter_scratch("I0") + scatter_scratch("I1"),
        compiler_params=pltpu.CompilerParams(collective_id=3, has_side_effects=True, vmem_limit_bytes=127 * 2 ** 19),
        name="attn_back")(*args)


def local_fast(*args):
    p = prologue(*args)
    c, b, y, k = place()
    cot = args[10].reshape(2, HALF, D)
    (xn, q, kb, vb, lse, o, hres, hn, g, gp, df, gb0, gb1, WA, WO, WI0, WI1, WB0, WB1, te_all, mask, onehot, ti) = gather_forward(p, cot)
    out, dh, da, gain_two, out_b, gi0, gi1 = mlp_back(cot, p["filled"], p["gains"], WI0, WI1, WB0, WB1, hres, hn.reshape(2 * TOK, D), g, gp, df, gb0, gb1)
    dlat, gt, small, grad_out, grad_a, grad_i, grad_time_in = attn_back(
        WA, WO, ti, p["gains"], p["lat"], xn.reshape(2 * TOK, D), q, kb, vb, lse, o.reshape(2 * TOK, QC), da, dh,
        mask, p["base"], onehot, gain_two, te_all, gi0, gi1)
    shape = (2, 1, 8, 34, D)
    places = [80 + 34 * dr + dc for dr in range(-2, 3) for dc in range(-2, 3)]
    bias = small[0:2, 0:8] + small[2:4, 0:8]
    grad_bias = bias[:, :, jnp.array(places)].transpose(2, 1, 0).reshape(25, 16)
    mine = lax.dynamic_slice_in_dim(small[:, 8:10, 0:144].sum(0), 36 * b, 36, 1)
    grad_time = gt.transpose(1, 0, 2).reshape(16, D)[:10].reshape(2, 1, 5, D)
    return (out.reshape(shape), dlat.reshape(shape), grad_time, mine.T, grad_a, grad_time_in, grad_bias, grad_out, grad_i, out_b)


def solution(mesh):
    return jax.shard_map(
        local_fast if mesh.shape["canvas"] == 8 and mesh.shape["band"] == 4 else local,
        mesh=mesh,
        in_specs=(
            P(None, "canvas", "band", None, None),
            P(None, "canvas", "band", None),
            P(None, "canvas", None, None),
            P(),
            P("canvas", None),
            P("canvas", None),
            P(),
            P("canvas", None),
            P("canvas", None),
            P("canvas", None),
            P(None, "canvas", "band", None, None),
        ),
        out_specs=(
            P(None, "canvas", "band", None, None),
            P(None, "canvas", "band", None, None),
            P(None, "canvas", None, None),
            P(("canvas", "band"), None),
            P(("canvas", "band"), None),
            P(("canvas", "band"), None),
            P(),
            P(("canvas", "band"), None),
            P(("canvas", "band"), None),
            P(("canvas", "band"), None),
        ),
        check_vma=False,
    )
```

```python
from functools import partial
import jax
import jax.numpy as jnp
from jax import lax
from jax.experimental import pallas as pl
from jax.experimental.pallas import tpu as pltpu

from jax.sharding import PartitionSpec as P

WIN = 5


EPSILON = 1e-05


def padded_2(shard, sides, width):
    for axis, dim in sides:
        devices, length = (lax.axis_size(axis), shard.shape[dim])
        up = [(i, (i + 1) % devices) for i in range(devices - 1)]
        down = [(j, i) for i, j in up]
        last = lax.slice_in_dim(shard, length - width, length, axis=dim)
        first = lax.slice_in_dim(shard, 0, width, axis=dim)
        before = lax.ppermute(last, axis, up)
        after = lax.ppermute(first, axis, down)
        shard = jnp.concatenate([before, shard, after], axis=dim)
    return shard


def shifted(shard, axis, by):
    devices = lax.axis_size(axis)
    pairs = [(i, i + by) for i in range(devices) if 0 <= i + by < devices]
    return lax.ppermute(shard, axis, pairs)


def shortened(shard):

    def short(part):
        return part.astype(jnp.bfloat16) if part.dtype == jnp.float32 else part

    return jax.tree.map(short, shard)


def normalize(value, gain):
    center = value - jnp.mean(value, -1, keepdims=True)
    scaled = lax.rsqrt(jnp.mean(center * center, -1, keepdims=True) + EPSILON)
    unit = center * scaled
    return (unit, scaled, unit * gain)


def normalize_back(unit, scaled, gain, grad_out):
    part = grad_out * gain
    return scaled * (
        part - jnp.mean(part, -1, keepdims=True) - unit * jnp.mean(part * unit, -1, keepdims=True)
    )


def rows_dot(left, right):
    return lax.dot_general(
        left, right, (((0,), (0,)), ((), ())), preferred_element_type=jnp.float32
    )


def back_dot(left, weight):
    return lax.dot_general(
        left, weight, (((1,), (1,)), ((), ())), preferred_element_type=jnp.float32
    )


def neighbour_stack(padded, band_rows, columns):
    pieces = [padded[:, i : i + band_rows, j : j + columns] for i in range(WIN) for j in range(WIN)]
    stacked = jnp.stack(pieces)
    return stacked.reshape((WIN * WIN, -1) + padded.shape[3:])


def spread_back(terms, canvases, band_rows, columns):
    reach = WIN // 2
    shaped = terms.reshape((WIN * WIN, canvases, band_rows, columns, terms.shape[-1]))
    summed = None
    for i in range(WIN):
        for j in range(WIN):
            placed = jnp.pad(
                shaped[i * WIN + j], ((0, 0), (i, 2 * reach - i), (j, 2 * reach - j), (0, 0))
            )
            summed = placed if summed is None else summed + placed
    return summed


def head_total(terms, head_sum):
    flat = terms.reshape(-1, terms.shape[-1])
    return jnp.dot(flat, head_sum, precision=lax.Precision.HIGHEST).reshape(
        terms.shape[:-1] + (head_sum.shape[1],)
    )


def head_widen(values, head_spread):
    flat = values.reshape(-1, values.shape[-1])
    return jnp.dot(flat, head_spread, preferred_element_type=jnp.bfloat16).reshape(
        values.shape[:-1] + (head_spread.shape[1],)
    )


def local(
    latents,
    segment_ids,
    time_embed,
    norm_gains,
    attn_in,
    time_in,
    rel_bias,
    out_proj,
    mlp_in,
    mlp_out,
    cotangent,
):
    micro_count, canvases, band_rows, columns, width = latents.shape
    slots = time_embed.shape[2]
    heads = rel_bias.shape[1]
    head_dim = width // heads
    reach = WIN // 2
    tokens = canvases * band_rows * columns
    score_scale = head_dim ** (-0.5)
    head_sum = (jnp.arange(width)[:, None] // head_dim == jnp.arange(heads)[None, :]).astype(
        jnp.float32
    )
    head_spread = head_sum.T.astype(jnp.bfloat16)
    owned = (attn_in, time_in, out_proj, mlp_in, mlp_out)
    seg_code = segment_ids + 2
    seg_rims = padded_2(seg_code, (("band", 2),), reach)
    seg_rims = jnp.pad(seg_rims, ((0, 0), (0, 0), (0, 0), (reach, reach)))
    band_share = 1.0 / lax.axis_size("band")
    outputs = []
    input_grads = []
    time_grads = []
    accum = None
    shards = None
    bias_accum = jnp.zeros(rel_bias.shape, jnp.float32)
    for batch_index in range(micro_count):
        full_weights = (
            lax.all_gather(owned[0], "canvas", axis=0, tiled=True),
            lax.all_gather(owned[1], "canvas", axis=0, tiled=True),
            lax.all_gather(owned[2], "canvas", axis=0, tiled=True),
            lax.all_gather(owned[3], "canvas", axis=0, tiled=True),
            lax.all_gather(owned[4], "canvas", axis=0, tiled=True),
        )
        w_attn, w_time, w_out, w_in, w_back = full_weights
        inputs = latents[batch_index].astype(jnp.float32).reshape(tokens, width)
        unit_one, scaled_one, normed_one = normalize(inputs, norm_gains[:, 0])
        normed = normed_one.astype(jnp.bfloat16)
        time_rows = time_embed[batch_index].reshape(canvases * slots, width)
        time_proj = jnp.dot(time_rows, w_time, preferred_element_type=jnp.float32).reshape(
            canvases, slots, 2 * width
        )
        seg_here = segment_ids[batch_index]
        member = (seg_here[..., None] == jnp.arange(slots)).astype(jnp.float32)
        token_time = jnp.einsum(
            "krcs,kse->krce", member, time_proj, precision=lax.Precision.HIGHEST
        ).reshape(tokens, 2 * width)
        qkv = jnp.dot(normed, w_attn, preferred_element_type=jnp.float32)
        query = (qkv[:, :width] + token_time[:, :width]).astype(jnp.bfloat16)
        keys = qkv[:, width : 2 * width].astype(jnp.bfloat16)
        values = (qkv[:, 2 * width :] + token_time[:, width:]).astype(jnp.bfloat16)
        paired = jnp.stack([keys, values]).reshape(2, canvases, band_rows, columns, width)
        paired = padded_2(paired, (("band", 2),), reach)
        paired = jnp.pad(paired, ((0, 0), (0, 0), (0, 0), (reach, reach), (0, 0)))
        key_win = neighbour_stack(paired[0], band_rows, columns)
        value_win = neighbour_stack(paired[1], band_rows, columns)
        seg_win = neighbour_stack(seg_rims[batch_index], band_rows, columns)
        allowed = (seg_win == seg_code[batch_index].reshape(1, tokens))[..., None]
        query_wide = query.astype(jnp.float32)
        raw = head_total(query_wide[None] * key_win.astype(jnp.float32), head_sum)
        logit_scores = raw * score_scale + rel_bias[:, None, :]
        masked = jnp.where(allowed, logit_scores, -1e30)
        peak = jnp.max(masked, 0)
        raised = jnp.where(allowed, jnp.exp(masked - peak), 0.0)
        probs_full = raised / jnp.sum(raised, 0)
        attention_probabilities = probs_full.astype(jnp.bfloat16)
        probs_wide = head_widen(attention_probabilities, head_spread)
        mixed_values = jnp.sum(probs_wide.astype(jnp.float32) * value_win.astype(jnp.float32), 0)
        attended = mixed_values.astype(jnp.bfloat16)
        branch = jnp.dot(attended, w_out, preferred_element_type=jnp.float32)
        resid = inputs + branch
        unit_two, scaled_two, normed_two = normalize(resid, norm_gains[:, 1])
        hidden_in = normed_two.astype(jnp.bfloat16)
        pre_act = jnp.dot(hidden_in, w_in, preferred_element_type=jnp.float32)
        activated = jax.nn.gelu(pre_act, approximate=False).astype(jnp.bfloat16)
        mlp_y = jnp.dot(activated, w_back, preferred_element_type=jnp.float32)
        filled = (seg_here >= 0).reshape(tokens, 1)
        outputs.append(
            jnp.where(filled, resid + mlp_y, 0.0)
            .astype(jnp.bfloat16)
            .reshape(canvases, band_rows, columns, width)
        )
        grad_y = cotangent[batch_index].reshape(tokens, width)
        grad_f = jnp.where(filled, grad_y, jnp.zeros_like(grad_y))
        grad_back = rows_dot(activated, grad_f)
        grad_act = back_dot(grad_f, w_back)
        gelu_out, gelu_pull = jax.vjp(partial(jax.nn.gelu, approximate=False), pre_act)
        grad_pre = gelu_pull(grad_act)[0].astype(jnp.bfloat16)
        grad_in = rows_dot(hidden_in, grad_pre)
        grad_hidden = back_dot(grad_pre, w_in)
        grad_resid = jnp.where(filled, grad_y.astype(jnp.float32), 0.0) + normalize_back(
            unit_two, scaled_two, norm_gains[:, 1], grad_hidden
        )
        gain_two = jnp.sum(grad_hidden * unit_two, 0)
        grad_branch = grad_resid.astype(jnp.bfloat16)
        grad_out = rows_dot(attended, grad_branch)
        grad_att = back_dot(grad_branch, w_out).astype(jnp.bfloat16)
        grad_att_wide = grad_att.astype(jnp.float32)
        grad_probs = head_total(grad_att_wide[None] * value_win.astype(jnp.float32), head_sum)
        centered = jnp.sum(probs_full * grad_probs, 0)
        grad_scores = (probs_full * (grad_probs - centered)).astype(jnp.bfloat16)
        bias_accum = bias_accum + jnp.sum(grad_scores.astype(jnp.float32), axis=1)
        scores_wide = head_widen(grad_scores, head_spread).astype(jnp.float32)
        grad_query = jnp.sum(scores_wide * key_win.astype(jnp.float32), 0) * score_scale
        key_summed = (
            spread_back(scores_wide * query_wide[None], canvases, band_rows, columns) * score_scale
        )
        value_summed = spread_back(
            probs_wide.astype(jnp.float32) * grad_att_wide[None], canvases, band_rows, columns
        )
        pair_grad = jnp.stack([key_summed, value_summed])[:, :, :, reach : reach + columns]
        upper_rim = pair_grad[:, :, :reach]
        lower_rim = pair_grad[:, :, band_rows + reach :]
        owned_rows = pair_grad[:, :, reach : reach + band_rows]
        from_below = shifted(upper_rim.astype(jnp.bfloat16), "band", -1).astype(upper_rim.dtype)
        from_above = shifted(lower_rim.astype(jnp.bfloat16), "band", 1).astype(lower_rim.dtype)
        owned_rows = owned_rows.at[:, :, band_rows - reach :].add(from_below)
        owned_rows = owned_rows.at[:, :, :reach].add(from_above)
        grad_keys = owned_rows[0].reshape(tokens, width).astype(jnp.bfloat16)
        grad_values = owned_rows[1].reshape(tokens, width).astype(jnp.bfloat16)
        grad_q_low = grad_query.astype(jnp.bfloat16)
        member_low = member.astype(jnp.bfloat16).reshape(canvases, band_rows * columns, slots)
        slot_query = jnp.einsum(
            "kns,knd->ksd",
            member_low,
            grad_q_low.reshape(canvases, band_rows * columns, width),
            preferred_element_type=jnp.float32,
        )
        slot_value = jnp.einsum(
            "kns,knd->ksd",
            member_low,
            grad_values.reshape(canvases, band_rows * columns, width),
            preferred_element_type=jnp.float32,
        )
        slot_part = jnp.concatenate([slot_query, slot_value], -1)
        slot_total = lax.psum(slot_part.astype(jnp.bfloat16), "band")
        slot_low = slot_total.reshape(canvases * slots, 2 * width)
        time_grads.append(back_dot(slot_low, w_time).reshape(canvases, slots, width))
        grad_time_in = rows_dot(time_rows, slot_low) * band_share
        grad_qkv = jnp.concatenate([grad_q_low, grad_keys, grad_values], -1)
        grad_attn = rows_dot(normed, grad_qkv)
        grad_normed = back_dot(grad_qkv, w_attn)
        grad_inputs = grad_resid + normalize_back(
            unit_one, scaled_one, norm_gains[:, 0], grad_normed
        )
        gain_one = jnp.sum(grad_normed * unit_one, 0)
        input_grads.append(grad_inputs.reshape(canvases, band_rows, columns, width))
        micro_grads = (
            grad_attn,
            grad_time_in,
            grad_out,
            grad_in,
            grad_back,
            jnp.stack([gain_one, gain_two], 1),
        )
        accum = micro_grads if accum is None else jax.tree.map(jnp.add, accum, micro_grads)
    wide_sums = jax.tree.map(
        lambda part: part.astype(jnp.float32),
        lax.psum_scatter(shortened(accum), "canvas", scatter_dimension=0, tiled=True),
    )
    shards = jax.tree.map(
        lambda part: part.astype(jnp.float32),
        lax.psum_scatter(shortened(wide_sums), "band", scatter_dimension=0, tiled=True),
    )
    bias_grad = lax.psum(bias_accum, ("canvas", "band"))
    return (
        jnp.stack(outputs),
        jnp.stack(input_grads),
        jnp.stack(time_grads),
        shards[5],
        shards[0],
        shards[1],
        bias_grad,
        shards[2],
        shards[3],
        shards[4],
    )


MESH = pl.DeviceIdType.MESH
BF, F32 = jnp.bfloat16, jnp.float32
EPS = 1e-5
TOK, HALF, D, QC, FH = 544, 272, 1152, 640, 2304
KEYS, KW, PADK = 784, 512, 80
SCALE = 72 ** -0.5
NEG = -1e30


def dot(a, b):
    return jnp.dot(a, b, preferred_element_type=F32)


def dot_nt(a, b):
    return lax.dot_general(a, b, (((1,), (1,)), ((), ())), preferred_element_type=F32)


def dot_tn(a, b):
    return lax.dot_general(a, b, (((0,), (0,)), ((), ())), preferred_element_type=F32)


def norm(v):
    center = v - jnp.mean(v, -1, keepdims=True)
    r = lax.rsqrt(jnp.mean(center * center, -1, keepdims=True) + EPS)
    return center * r, r


def norm_back(n, r, e):
    return r * (e - jnp.mean(e, -1, keepdims=True) - n * jnp.mean(e * n, -1, keepdims=True))


def place():
    c, b = lax.axis_index("canvas"), lax.axis_index("band")
    return c, b, b // 2, lax.rem(b, 2)


def greet(devs):
    bar = pltpu.get_barrier_semaphore()
    for dev in devs:
        pl.semaphore_signal(bar, 1, device_id=dev, device_id_type=MESH)
    pl.semaphore_wait(bar, len(devs))


def remote(src, dst, ss, rs, dev):
    return pltpu.make_async_remote_copy(src, dst, ss, rs, device_id=dev, device_id_type=MESH)


def head_window(h):
    ws = pl.multiple_of(jnp.minimum(80 * h // 128, 3) * 128, 128)
    lane = lax.broadcasted_iota(jnp.int32, (1, 256), 1) + ws - 80 * h
    hm = jnp.where((lane >= 0) & (lane < 80), 1.0, 0.0).astype(BF)
    return pl.ds(ws, 256), hm


def toeplitz(base, h):
    row = jnp.broadcast_to(base[pl.ds(h, 1)], (HALF, KW))
    return pltpu.roll(row, 0, 1, stride=1, stride_axis=0)


GSPEC = {"A": (144, 640, 640), "O": (80, 384, 384), "I0": (144, 384, 384), "I1": (144, 384, 384), "B0": (144, 384, 384), "B1": (144, 384, 384)}
GNAMES = list(GSPEC)


FIRST, STEP, SPARE = 4.0, 1.7, -2


class Gather:
    def __init__(self, own, full, s_sem, r_sem, y_sem, l_sem, pend):
        self.own, self.full, self.pend = dict(zip(GNAMES, own)), dict(zip(GNAMES, full)), pend
        self.s_sem, self.r_sem, self.y_sem, self.l_sem = s_sem, r_sem, y_sem, l_sem
        self.c, self.b, self.y, _ = place()
        self.z, self.x = self.c // 2, lax.rem(self.c, 2)
        z = self.z
        self.zp = [jnp.where(z == 0, t[0], jnp.where(z == 1, t[1], jnp.where(z == 2, t[2], t[3]))) for t in ((1, 0, 3, 2), (2, 2, 1, 1), (3, 3, 0, 0))]
        self.xdev, self.ydev = {"canvas": self.c + 1 - 2 * self.x}, {"band": self.b + 2 - 4 * self.y}
        self.count = dict.fromkeys(GNAMES, 0)

    def part(self, name, src, plane, side):
        rows, wide, mid = GSPEC[name]
        at = pl.ds(pl.multiple_of(src * rows, 16), rows)
        if plane:
            return at, pl.ds(pl.multiple_of(wide * side, 128), wide + mid)
        return at, pl.ds(pl.multiple_of((wide + mid) * side, 128), wide)

    def send(self, name, src, dev, plane, first=False, when=None):
        n = GNAMES.index(name)
        at, cols = self.part(name, src, plane, self.y)
        held = self.full[name].at[at, cols] if self.own[name] is None or not first else self.own[name].at[:, cols]
        cp = remote(held, self.full[name].at[at, cols],
                    self.s_sem.at[n, self.count[name]], (self.r_sem if plane else self.y_sem).at[n, src], dev)
        self.count[name] += 1
        if when is None:
            cp.start()
            self.pend.append(cp.wait_send)
        else:
            pl.when(when)(cp.start)
            self.pend.append(lambda: pl.when(when)(cp.wait_send))

    def own_sends(self, name):
        rows = GSPEC[name][0]
        for up in (1, -1):
            to = self.z + up
            self.send(name, self.c, {"canvas": jnp.clip(to, 0, 3) * 2 + self.x}, True, True, (to >= 0) & (to <= 3))
        self.send(name, self.c, self.xdev, True, True)
        if self.own[name] is not None:
            pltpu.make_async_copy(self.own[name], self.full[name].at[pl.ds(pl.multiple_of(self.c * rows, 16), rows)],
                                  self.l_sem.at[GNAMES.index(name)]).start()

    def wait(self, name, src, plane):
        at, cols = self.part(name, src, plane, self.y if plane else 1 - self.y)
        view = self.full[name].at[at, cols]
        pltpu.make_async_copy(view, view, (self.r_sem if plane else self.y_sem).at[GNAMES.index(name), src]).wait()

    def from_z(self, name, i):
        src = self.zp[i] * 2 + self.x
        self.wait(name, src, True)
        to = jnp.where(self.zp[i] < self.z, self.z + 1, self.z - 1)
        self.send(name, src, {"canvas": jnp.clip(to, 0, 3) * 2 + self.x}, True, False, (to >= 0) & (to <= 3))
        self.send(name, src, self.xdev, True)
        self.send(name, src, self.ydev, False)

    def from_x(self, name, i):
        src = (self.z if i == 0 else self.zp[i - 1]) * 2 + 1 - self.x
        self.wait(name, src, True)
        self.send(name, src, self.ydev, False)

    def complete(self, name):
        rows = GSPEC[name][0]
        for d in range(1, 8):
            self.wait(name, lax.rem(self.c + d, 8), False)
        if self.own[name] is not None:
            pltpu.make_async_copy(self.own[name], self.full[name].at[pl.ds(pl.multiple_of(self.c * rows, 16), rows)],
                                  self.l_sem.at[GNAMES.index(name)]).wait()

    def events(self, name):
        return [partial(self.from_z, name, 0), partial(self.from_x, name, 0), partial(self.from_z, name, 1), partial(self.from_x, name, 1),
                partial(self.from_z, name, 2), partial(self.from_x, name, 2), partial(self.from_x, name, 3)]


def gather_forward_kernel(attn_in, time_in, mlp_in, O, mlp_out, lat_in, cot_in, gains, te, seg_row, seg_col, base,
                          xn_o, q_o, kb_o, vb_o, lse_o, o_o, hres_o, hn_o, g_o, gp_o, df_o, gb0_o, gb1_o,
                          WA_o, WO_o, WI0_o, WI1_o, WB0_o, WB1_o, te_o, mask_o, onehot_o, ti,
                          WA, WO, WI0, WI1, WB0, WB1, xn, q, kb, vb, lse, o, hres, hn, g, gp, df, gb0, gb1, te_in, seg_in, col_in, onehot,
                          tp_send, tp_recv, tmix, mask, toep, of, x_send, x_recv, lat, cot,
                          s_sem, r_sem, y_sem, l_sem, es, er, gs, gr, cs, cr,
                          xs, xr, ts, tr, ks, kr, as_, ar, hs, hr, fs, fr, ls, outs):
    blocks = [(attn_in, 0), (attn_in, 1), (attn_in, 2), (time_in, 0), (time_in, 1)] + [(mlp_in, j) for j in range(4)]
    spots = [g.at[144 * (i // 2):144 * (i // 2) + 144, D * (i % 2):D * (i % 2) + D] for i in range(9)]
    loads = [pltpu.make_async_copy(lat_in, lat, ls.at[0]), pltpu.make_async_copy(cot_in, cot, ls.at[1])]
    loads += [pltpu.make_async_copy(src.at[:, D * j:D * j + D], spots[i], ls.at[2 + i]) for i, (src, j) in enumerate(blocks)]
    for cp in loads:
        cp.start()
    c, b, y, k = place()
    sib, ynb = {"band": b + 1 - 2 * k}, {"band": b + 2 - 4 * y}
    peers = [lax.rem(c + d, 8) for d in range(1, 8)]
    pend, saves = [], []

    def go(src, dst, ss, rs, dev):
        cp = remote(src, dst, ss, rs, dev)
        cp.start()
        pend.append(cp.wait_send)

    def arrive(view, sem):
        pltpu.make_async_copy(view, view, sem).wait()

    def save(src, dst):
        cp = pltpu.make_async_copy(src, dst, outs.at[len(saves)])
        cp.start()
        saves.append(cp)

    shares = [mlp_out.at[pl.ds(pl.multiple_of(288 * k + 144 * i, 16), 144)] for i in range(2)]
    gat = Gather((None, O, None, None, *shares), (WA, WO, WI0, WI1, WB0, WB1), s_sem, r_sem, y_sem, l_sem, pend)
    queue, ends = [], {}
    for name, nxt in (("A", "I0"), ("O", "I1"), ("I0", "B0"), ("I1", "B1"), ("B0", None), ("B1", None)):
        steps = gat.events(name)
        if nxt:
            steps.insert(1, partial(gat.own_sends, nxt))
        queue += steps
        ends[name] = len(queue)

    total, clock = len(queue), [0.0]

    def tick(us):
        clock[0] += us
        while queue and FIRST + STEP * (total - len(queue)) <= clock[0]:
            queue.pop(0)()

    def complete(name):
        left = total - ends[name]
        while len(queue) > max(left + SPARE, 0):
            queue.pop(0)()
        gat.complete(name)
        clock[0] = max(clock[0], FIRST + STEP * (total - left))

    greet([{"band": lax.rem(b + d, 4)} for d in (1, 2, 3)] + [{"canvas": p} for p in peers])
    for i, p in enumerate(peers):
        go(te.at[p], te_in.at[c], es.at[i], er.at[6 - i], {"canvas": p})
    te_in[c] = te[c]
    for i in range(3):
        go(seg_row, seg_in.at[b], gs.at[i], gr.at[2 - i], {"band": lax.rem(b + i + 1, 4)})
    seg_in[b] = seg_row[...]
    go(seg_col, col_in.at[k], cs.at[0], cr.at[0], sib)
    col_in[k] = seg_col[...]
    mine_rows = pl.ds(pl.multiple_of(144 * c, 16), 144)

    def pick_matrix(source, wide):
        gb0[:, 0:wide] = jnp.where(lax.broadcasted_iota(jnp.int32, (D, wide), 0) == source, 1.0, 0.0).astype(BF)

    lane = lax.broadcasted_iota(jnp.int32, (1, QC), 1).astype(F32)
    place_h = jnp.floor((lane + 0.5) * (1.0 / 80))
    inside = lane - 80 * place_h
    pick_matrix(jnp.where(inside < 71.5, 144 * place_h + inside + 72 * k.astype(F32), -1.0).astype(jnp.int32), QC)
    for i in range(3):
        loads[2 + i].wait()
        WA[mine_rows, QC * i:QC * i + QC] = dot(spots[i][...], gb0[:, 0:QC]).astype(BF)
    gat.own_sends("A")
    gat.own_sends("O")
    for i in range(2):
        loads[5 + i].wait()
        ti[:, QC * i:QC * i + QC] = dot(spots[3 + i][...], gb0[:, 0:QC]).astype(BF)

    def pick_hidden(s, W):
        for j in range(4):
            n = lax.broadcasted_iota(jnp.int32, (1, 384), 1).astype(F32) + 256 * j
            cc = jnp.floor((n + 0.5) * (1.0 / 144))
            fits = (cc > 2 * j - 0.5) & (cc < 2 * j + 1.5)
            pick_matrix(jnp.where(fits, 576 * (cc - 2 * j) + (n - 144 * cc) + 288 * k.astype(F32) + 144 * s, -1.0).astype(jnp.int32), 384)
            part = dot(spots[5 + j][...], gb0[:, 0:384]).astype(BF)
            if j:
                W[mine_rows, 256 * j:256 * j + 128] += part[:, 0:128]
                W[mine_rows, 256 * j + 128:256 * j + 384] = part[:, 128:]
            else:
                W[mine_rows, 0:384] = part

    loads[0].wait()
    mine = pl.ds(pl.multiple_of(HALF * k, 16), HALF)
    other = pl.ds(pl.multiple_of(HALF * (1 - k), 16), HALF)
    for m in range(2):
        n, _ = norm(lat[m].astype(F32))
        xn[m, mine] = (n * gains[0:1]).astype(BF)
        go(xn.at[m, mine], xn.at[m, mine], xs.at[m], xr.at[m], sib)
        if m == 0:
            for i in range(7):
                arrive(te_in.at[lax.rem(c + i + 1, 8)], er.at[i])
            for p in range(8):
                tp_send[16 * p:16 * p + 16] = dot(te_in[p], ti[...]).astype(BF)
            for i, p in enumerate(peers):
                go(tp_send.at[pl.ds(pl.multiple_of(16 * p, 16), 16)], tp_recv.at[6 - i], ts.at[i], tr.at[6 - i], {"canvas": p})
    save(te_in, te_o)
    for i in range(4):
        loads[7 + i].wait()
    pick_hidden(0, WI0)
    arrive(col_in.at[1 - k], cr.at[0])
    for i in range(3):
        arrive(seg_in.at[lax.rem(b + i + 1, 4)], gr.at[i])
    slot = lax.rem(lax.broadcasted_iota(jnp.int32, (1, 32), 1), 16)
    lane = lax.broadcasted_iota(jnp.int32, (1, KW), 1)

    def column(t):
        return t - 34 * jnp.floor((t + 0.5) * (1.0 / 34))

    colq = column(lax.broadcasted_iota(jnp.int32, (HALF, 1), 0).astype(F32))
    near = jnp.abs(colq - column(lax.broadcasted_iota(jnp.int32, (1, KW), 1).astype(F32) + 22)) < 2.5
    for j in range(2):
        at = 2 * y + j
        before, here, after = seg_in[jnp.maximum(at - 1, 0)], seg_in[at], seg_in[jnp.minimum(at + 1, 3)]
        before = pltpu.roll(jnp.where(at > 0, before, 0.0), KW - HALF, 1)
        after = pltpu.roll(jnp.where(at < 3, after, 0.0), HALF, 1)
        keys = jnp.where(lane < 80, before, jnp.where(lane < 352, here, jnp.where(lane < 432, after, 0.0)))
        for m in range(2):
            code = col_in[j, m, :, 0:1]
            mask[m, j] = jnp.where((code == keys[m:m + 1]) & near, 0.0, NEG).astype(BF)
            hit = (code.astype(jnp.int32) + (5 * m - 2) == slot) & (code >= 1.5)
            onehot[m, HALF * j:HALF * j + HALF] = jnp.where(hit, 1.0, 0.0).astype(BF)
    loads[1].wait()
    for m in range(2):
        filled = jnp.where(col_in[k, m, :, 0:1] >= 1.5, 1.0, 0.0)
        rows = pl.ds(pl.multiple_of(TOK * m + HALF * k, 16), HALF)
        df[rows] = (cot[m].astype(F32) * filled).astype(BF)
        go(df.at[rows], df.at[rows], fs.at[m], fr.at[m], sib)
    save(mask, mask_o)
    save(onehot, onehot_o)
    tick(13.0)
    for i in range(7):
        arrive(tp_recv.at[i], tr.at[i])
    tproj = tp_send[pl.ds(pl.multiple_of(16 * c, 16), 16)].astype(F32)
    for i in range(7):
        tproj = tproj + tp_recv[i].astype(F32)
    hi = tproj.astype(BF)
    tmix[0:16] = hi
    tmix[16:32] = (tproj - hi.astype(F32)).astype(BF)
    dead = pl.ds(pl.multiple_of(y * 624, 16), 80)
    for m in range(2):
        for ref in (kb, vb):
            ref[m, dead] = jnp.zeros((80, QC), BF)
            ref[m, 704:784] = jnp.zeros((80, QC), BF)
    of[...] = jnp.zeros_like(of)
    lse[...] = jnp.zeros_like(lse)
    pick_hidden(1, WI1)
    complete("A")
    save(WA, WA_o)

    edge = pl.ds(pl.multiple_of(544 - 464 * y, 16), 80)
    land = pl.ds(pl.multiple_of(624 * y, 16), 80)
    land_here = pl.ds(pl.multiple_of(624 * (1 - y), 16), 80)
    for m in range(2):
        arrive(xn.at[m, other], xr.at[m])
        x = xn[m]
        kb[m, 80:624] = dot(x, WA[:, QC:2 * QC]).astype(BF)
        tick(1.2)
        vb[m, 80:624] = (dot(x, WA[:, 2 * QC:]) + dot(onehot[m], tmix[:, QC:])).astype(BF)
        for i, ref in enumerate((kb, vb)):
            go(ref.at[m, edge], ref.at[m, land], ks.at[m, i], kr.at[m, i], ynb)
        q[m] = (dot(x, WA[:, :QC]) + dot(onehot[m], tmix[:, :QC])).astype(BF)
        tick(2.5)
    save(xn, xn_o)
    save(q, q_o)
    for m in range(2):
        for i, ref in enumerate((kb, vb)):
            arrive(ref.at[m, land_here], kr.at[m, i])
    save(kb, kb_o)
    save(vb, vb_o)

    def head(h, _):
        win, hm = head_window(h)
        toep[...] = toeplitz(base, h)
        lane_h = lax.broadcasted_iota(jnp.int32, (1, 128), 1) == h

        def tile(t, _):
            m, j = t // 2, lax.rem(t, 2)
            rows = pl.ds(pl.multiple_of(HALF * j, 16), HALF)
            krows = pl.ds(pl.multiple_of(HALF * j, 16), KW)
            s = dot_nt(q[m, rows, win] * hm, kb[m, krows, win])
            s = s * SCALE + (toep[...] + mask[m, j])
            peak = jnp.max(s, -1, keepdims=True)
            e = jnp.exp(s - peak)
            total = jnp.sum(e, -1, keepdims=True)
            p = (e * (1.0 / total)).astype(BF)
            of[m, rows, win] += dot(p, vb[m, krows, win] * hm)
            lse[m, rows] = jnp.where(lane_h, peak + jnp.log(total), lse[m, rows])
            return 0

        return lax.fori_loop(0, 4, tile, 0)

    for n in range(8):
        lax.fori_loop(n, n + 1, head, 0)
        tick(3.1)
    save(lse, lse_o)
    for m in range(2):
        o[m] = of[m].astype(BF)
    save(o, o_o)
    complete("O")
    save(WO, WO_o)

    for m in range(2):
        x_send[m] = dot(o[m, other], WO[...]).astype(BF)
        go(x_send.at[m], x_recv.at[m], as_.at[m], ar.at[m], sib)
    for m in range(2):
        hres[m] = lat[m].astype(F32) + dot(o[m, mine], WO[...])
    tick(4.0)
    for m in range(2):
        arrive(x_recv.at[m], ar.at[m])
        hv = hres[m] + x_recv[m].astype(F32)
        hres[m] = hv
        n, _ = norm(hv)
        hn[m, mine] = (n * gains[1:2]).astype(BF)
        go(hn.at[m, mine], hn.at[m, mine], hs.at[m], hr.at[m], sib)
        tick(2.5)
    save(hres, hres_o)
    for m in range(2):
        arrive(hn.at[m, other], hr.at[m])
    save(hn, hn_o)
    for s, W in enumerate((WI0, WI1)):
        complete("I0" if s == 0 else "I1")
        save(W, (WI0_o, WI1_o)[s])
        for m in range(2):
            def up(i, _):
                cols = pl.ds(pl.multiple_of(i * 384, 128), 384)
                put = pl.ds(pl.multiple_of(i * 384 + D * s, 128), 384)
                u = dot(hn[m], W[:, cols])
                phi = 0.5 + 0.5 * lax.erf(u * (0.5 ** 0.5))
                g[pl.ds(TOK * m, TOK), put] = (u * phi).astype(BF)
                gp[pl.ds(TOK * m, TOK), put] = (phi + u * (jnp.exp(-0.5 * u * u) * 0.3989422804014327)).astype(BF)
                return 0

            lax.fori_loop(0, 3, up, 0)
            tick(3.3)
    save(g, g_o)
    save(gp, gp_o)
    for m in range(2):
        rows = pl.ds(pl.multiple_of(TOK * m + HALF * (1 - k), 16), HALF)
        arrive(df.at[rows], fr.at[m])
    save(df, df_o)
    for s, grad in enumerate((gb0, gb1)):
        for i in range(3):
            cols = pl.ds(384 * i, 384)
            fill_part(grad, g, df, cols, D * s, cols)
            tick(1.3)
        save(grad, (gb0_o, gb1_o)[s])
    for s, W in enumerate((WB0, WB1)):
        complete("B0" if s == 0 else "B1")
        save(W, (WB0_o, WB1_o)[s])
    for cp in saves:
        cp.wait()
    for wait in pend:
        wait()


def gather_forward(p, cot):
    S = jax.ShapeDtypeStruct
    dma = pltpu.SemaphoreType.DMA
    V, anyspace = pl.BlockSpec(memory_space=pltpu.VMEM), pl.BlockSpec(memory_space=pl.ANY)
    weights = [(D, 3 * QC), (QC, D), (D, D), (D, D), (D, D), (D, D)]
    kept = [((2, TOK, D), BF), ((2, TOK, QC), BF), ((2, KEYS, QC), BF), ((2, KEYS, QC), BF), ((2, TOK, 128), F32), ((2, TOK, QC), BF),
            ((2, HALF, D), F32), ((2, TOK, D), BF), ((2 * TOK, FH), BF), ((2 * TOK, FH), BF), ((2 * TOK, D), BF), ((D, D), BF), ((D, D), BF)]
    return pl.pallas_call(
        gather_forward_kernel,
        out_shape=[S(s, t) for s, t in kept] + [S(s, BF) for s in weights]
        + [S((8, 16, 144), BF), S((2, 2, HALF, KW), BF), S((2, TOK, 32), BF), S((144, 2 * QC), BF)],
        in_specs=[anyspace] * 7 + [V] * 5, out_specs=[anyspace] * 22 + [V],
        scratch_shapes=[pltpu.VMEM(s, BF) for s in weights] + [pltpu.VMEM(s, t) for s, t in kept]
        + [pltpu.VMEM((8, 16, 144), BF), pltpu.VMEM((4, 8, KW), F32), pltpu.VMEM((2, 2, HALF, 128), F32), pltpu.VMEM((2, TOK, 32), BF),
           pltpu.VMEM((128, 2 * QC), BF), pltpu.VMEM((7, 16, 2 * QC), BF), pltpu.VMEM((32, 2 * QC), BF), pltpu.VMEM((2, 2, HALF, KW), BF),
           pltpu.VMEM((HALF, KW), F32), pltpu.VMEM((2, TOK, QC), F32), pltpu.VMEM((2, HALF, D), BF), pltpu.VMEM((2, HALF, D), BF),
           pltpu.VMEM((2, HALF, D), BF), pltpu.VMEM((2, HALF, D), BF),
           dma((6, 16)), dma((6, 8)), dma((6, 8)), dma((6,)), dma((7,)), dma((7,)), dma((3,)), dma((3,)), dma((1,)), dma((1,)),
           dma((2,)), dma((2,)), dma((7,)), dma((7,)), dma((2, 2)), dma((2, 2)), dma((2,)), dma((2,)), dma((2,)), dma((2,)), dma((2,)), dma((2,)), dma((11,)), dma((22,))],
        compiler_params=pltpu.CompilerParams(collective_id=1, has_side_effects=True, vmem_limit_bytes=127 * 2 ** 19),
        name="gather_forward")(*p["raw"], p["lat"], cot, p["gains"], p["te"], p["seg_row"], p["seg_col"], p["base"])


def prologue(latents, segment_ids, time_embed, norm_gains, attn_in, time_in, rel_bias, out_proj, mlp_in, mlp_out, cotangent):
    c, b, y, k = place()

    def pick(v, axis):
        return lax.dynamic_index_in_dim(v, k, axis, keepdims=False)

    raw = (attn_in, time_in, mlp_in, jnp.pad(pick(out_proj.reshape(2, 72, D), 0), ((0, 8), (0, 0))), mlp_out)
    code = (segment_ids.reshape(2, HALF) + 2).astype(F32)
    seg_row = jnp.pad(code, ((0, 6), (80, KW - 80 - HALF)))
    seg_col = jnp.broadcast_to(code[..., None], (2, HALF, 128))
    te = jnp.pad(time_embed.reshape(10, D), ((0, 6), (0, 0))).reshape(16, 8, 144).transpose(1, 0, 2)
    bias = pick(rel_bias.reshape(25, 8, 2), 2)
    base = jnp.full((8, KW), NEG, F32)
    places = [80 + 34 * dr + dc for dr in range(-2, 3) for dc in range(-2, 3)]
    base = base.at[:, jnp.array(places)].set(bias.T)
    filled = (segment_ids.reshape(2, HALF, 1) >= 0).astype(F32)
    return dict(raw=raw, te=te, seg_row=seg_row, seg_col=seg_col, base=base, filled=filled, lat=latents.reshape(2, HALF, D), gains=norm_gains.T)


RSPEC = {"A": (144, 640, 640), "O": (80, 384, 384), "I0": (144, 384, 384), "I1": (144, 384, 384), "B0": (144, 384, 384), "B1": (144, 384, 384)}
KEEP = {"A": (36, 48, 4), "I0": (36, 48, 4), "I1": (36, 48, 4), "O": (36, 48, 2), "B0": (144, 144, 2), "B1": (144, 144, 2)}
ORDER = (1, 3, 2, 0)


def scatter_scratch(name):
    rows, wide, mid = RSPEC[name]
    slab = wide + mid
    dma = pltpu.SemaphoreType.DMA
    _, held, sources = KEEP[name]
    sends = {"A": 4, "I": 4, "O": 2, "B": 1}[name[0]]
    return [pltpu.VMEM((8 * rows, wide), BF), pltpu.VMEM((4 * rows, slab), BF), pltpu.VMEM((3 * rows, slab), BF),
            pltpu.VMEM((sends, held, slab), BF), pltpu.VMEM((sources, held, slab), BF),
            dma((4,)), dma((4,)), dma((8,)), dma((8,)), dma((3,)), dma((3,)), dma((4,)), dma((4,))]


N_SCATTER = 13


class Scatter:
    def __init__(self, name, grad, total, scratch, pend):
        self.name, self.grad, self.total, self.pend = name, grad, total, pend
        (self.yr, self.xr, self.zr, self.stage, self.fr, self.ys, self.yw, self.xs, self.xw, self.zs, self.zw, self.fs, self.fw) = scratch
        self.rows, self.wide, self.mid = RSPEC[name]
        self.c, self.b, self.y, self.k = place()
        self.z, self.x = self.c // 2, lax.rem(self.c, 2)
        y, w, l = self.y, self.wide, self.mid
        self.slab = pl.ds(pl.multiple_of(w * y, 128), w + l)
        self.mids = pl.ds(w, l)
        self.side = pl.ds(pl.multiple_of((w + l) * y, 128), w)
        self.away = pl.ds(pl.multiple_of((w + l) * (1 - y), 128), w)
        self.slab_mid = pl.ds(pl.multiple_of(w * (1 - y), 128), l)
        self.slab_side = pl.ds(pl.multiple_of(l * y, 128), w)
        self.xdev, self.ydev = {"canvas": self.c + 1 - 2 * self.x}, {"band": self.b + 2 - 4 * self.y}

    def at(self, group):
        return pl.ds(pl.multiple_of(group * self.rows, 16), self.rows)

    def pair(self, d):
        return pl.ds(pl.multiple_of(lax.rem(self.z + d, 4) * (2 * self.rows), 16), 2 * self.rows)

    def go(self, make):
        make().start()
        self.pend.append(make)

    def parts(self):
        return self.away, self.mids, self.side

    def group(self, d, x):
        return self.at(2 * lax.rem(self.z + d, 4) + x)

    def send_y(self):
        for d in ORDER:
            self.go(lambda d=d: remote(self.grad.at[self.pair(d), self.away], self.yr.at[self.pair(d)], self.ys.at[d], self.yw.at[d], self.ydev))

    def send_mid(self, steps=ORDER):
        for d in steps:
            self.go(lambda d=d: remote(self.grad.at[self.group(d, 1 - self.x), self.mids], self.xr.at[pl.ds(self.rows * d, self.rows), self.slab_mid],
                                       self.xs.at[d], self.xw.at[d], self.xdev))

    def side_x(self, d):
        rows2 = self.pair(d)
        pltpu.make_async_copy(self.yr.at[rows2], self.yr.at[rows2], self.yw.at[d]).wait()
        self.grad[rows2, self.side] += self.yr[rows2]
        self.go(lambda: remote(self.grad.at[self.group(d, 1 - self.x), self.side], self.xr.at[pl.ds(self.rows * d, self.rows), self.slab_side],
                               self.xs.at[4 + d], self.xw.at[4 + d], self.xdev))

    def sum_x(self, d):
        rows = pl.ds(self.rows * d, self.rows)
        for view, sem in ((self.xr.at[rows, self.slab_mid], d), (self.xr.at[rows, self.slab_side], 4 + d)):
            pltpu.make_async_copy(view, view, self.xw.at[sem]).wait()
        return self.grad[self.group(d, self.x), self.slab] + self.xr[rows]

    def send_z(self, d):
        self.grad[self.group(d, self.x), self.slab] = self.sum_x(d)
        self.go(lambda: remote(self.grad.at[self.group(d, self.x), self.slab], self.zr.at[pl.ds((3 - d) * self.rows, self.rows)], self.zs.at[d - 1],
                               self.zw.at[3 - d], {"canvas": 2 * lax.rem(self.z + d, 4) + self.x}))

    def dests(self):
        sources = KEEP[self.name][2]
        if self.name[0] == "B":
            return [(0, 2 * self.k + int(self.name[1]))]
        return [(i, 2 * self.k + i if sources == 2 else i) for i in range(sources)]

    def finish(self):
        acc = self.sum_x(0).astype(F32)
        for i in (2, 0, 1):
            rows = pl.ds(i * self.rows, self.rows)
            pltpu.make_async_copy(self.zr.at[rows], self.zr.at[rows], self.zw.at[i]).wait()
            acc = acc + self.zr[rows].astype(F32)
        n, held, sources = KEEP[self.name]
        slab = self.wide + self.mid
        if self.name[0] == "B":
            self.stage[0] = acc.astype(BF)
        else:
            self.total[0:self.rows, 0:slab] = acc
            for i in range(sources):
                self.stage[i, 0:n] = self.total[n * i:n * i + n, 0:slab].astype(BF)
                self.stage[i, n:held] = jnp.zeros((held - n, slab), BF)
        slot = self.b if sources == 4 else self.y
        for i, dest in self.dests():
            @pl.when(self.b == dest)
            def _():
                self.fr[slot] = self.stage[i]

            @pl.when(self.b != dest)
            def _():
                remote(self.stage.at[i], self.fr.at[slot], self.fs.at[i], self.fw.at[slot], {"band": dest}).start()

    def sent(self):
        for i, dest in self.dests():
            @pl.when(self.b != dest)
            def _():
                remote(self.stage.at[i], self.fr.at[0], self.fs.at[i], self.fw.at[0], {"band": dest}).wait_send()

    def collect(self, out):
        n, held, sources = KEEP[self.name]
        for i in range(sources):
            src = i if sources == 4 else 2 * i + self.y

            @pl.when(self.b != src)
            def _():
                pltpu.make_async_copy(self.fr.at[i], self.fr.at[i], self.fw.at[i]).wait()
        w, l = self.wide, self.mid
        for half in range(sources // 2):
            lo, hi = self.fr[half].astype(F32)[:n], self.fr[half + sources // 2].astype(F32)[:n]
            dst = out.at[half] if sources == 4 else out
            dst[:, 0:w] = lo[:, :w]
            dst[:, w:w + l] = lo[:, w:] + hi[:, :l]
            dst[:, w + l:] = hi[:, l:]


def everyone():
    c, b, y, k = place()
    return [{"band": lax.rem(b + d, 4)} for d in (1, 2, 3)] + [{"canvas": lax.rem(c + d, 8)} for d in range(1, 8)]


def fill_part(grad, left, right, cols, lefts, rights):
    def step(i, _):
        r = pl.multiple_of(i * 384, 128)
        grad[pl.ds(r, 384), cols] = dot_tn(left[:, pl.ds(r + lefts, 384)], right[:, rights]).astype(BF)
        return 0

    lax.fori_loop(0, grad.shape[0] // 384, step, 0)


def mlp_back_kernel(cot_in, filled, gains, WI0_in, WI1_in, WB0_in, WB1_in, hres, hn_in, g_in, gp, df_in, gb0, gb1,
                    out, dh, da, gain, out_b, grad_i0, grad_i1,
                    grad_b0, grad_b1, cot, WI0, WI1, WB0, WB1, hn, g, du, gi, x_send, x_recv, f_send, f_recv, dn, ds_, dr_, xs, xr, as_, ar, ls, gs, *scratch):
    c, b, y, k = place()
    sib = {"band": b + 1 - 2 * k}
    df = da
    loads = [pltpu.make_async_copy(src, dst, ls.at[i])
             for i, (src, dst) in enumerate(((gb0, grad_b0), (gb1, grad_b1), (WB0_in, WB0), (WB1_in, WB1), (g_in, g), (df_in, df), (gp, du), (hres, dh), (cot_in, cot), (hn_in, hn),
                                            (WI0_in, WI0), (WI1_in, WI1)))]
    for cp in loads:
        cp.start()
    greet([{"band": lax.rem(b + d, 4)} for d in (1, 2, 3)] + [{"canvas": c + 1 - 2 * lax.rem(c, 2)}] + [{"canvas": lax.rem(c + d, 8)} for d in (2, 4, 6)])
    pend = []
    rs = [Scatter("B0", grad_b0, None, scratch[:N_SCATTER], pend), Scatter("B1", grad_b1, None, scratch[N_SCATTER:], pend)]
    rs[1].fr, rs[1].fw = rs[0].fr, rs[0].fw

    def half(m, which):
        return pl.ds(pl.multiple_of(TOK * m + HALF * which, 16), HALF)

    for s in range(2):
        loads[s].wait()
        rs[s].send_y()
        if s == 0:
            rs[s].send_mid()
    for cp in loads[2:5]:
        cp.wait()
    for m in range(2):
        def down_other(i, _):
            cols = pl.ds(pl.multiple_of(i * 384, 128), 384)
            f_send[m, :, cols] = (dot(g[half(m, 1 - k), 0:D], WB0[:, cols]) + dot(g[half(m, 1 - k), D:], WB1[:, cols])).astype(BF)
            return 0

        lax.fori_loop(0, 3, down_other, 0)
        loads.append(remote(f_send.at[m], f_recv.at[m], ds_.at[m], dr_.at[m], sib))
        loads[-1].start()

        def down(i, _):
            cols = pl.ds(pl.multiple_of(i * 384, 128), 384)
            dn[m, :, cols] = dot(g[half(m, k), 0:D], WB0[:, cols]) + dot(g[half(m, k), D:], WB1[:, cols])
            return 0

        lax.fori_loop(0, 3, down, 0)

    def back_act(m, s):
        def step(i, _):
            r = pl.multiple_of(i * 384, 128)
            cols = pl.ds(pl.multiple_of(r + D * s, 128), 384)
            rows = pl.ds(TOK * m, TOK)
            du[rows, cols] = (dot_nt(df[rows], (WB0, WB1)[s][pl.ds(r, 384)]) * du[rows, cols].astype(F32)).astype(BF)
            return 0

        lax.fori_loop(0, 3, step, 0)

    rs[0].side_x(1)
    for cp in loads[5:12]:
        cp.wait()
    back_act(0, 0)
    rs[0].side_x(3)
    rs[0].send_z(1)
    for m in range(2):
        v = f_recv.at[m]
        pltpu.make_async_copy(v, v, dr_.at[m]).wait()
        out[m] = ((dh[m] + (dn[m] + v[...].astype(F32))) * filled[m]).astype(BF)
    back_act(1, 0)
    rs[0].side_x(2)
    rs[0].send_z(3)
    back_act(0, 1)
    rs[0].side_x(0)
    rs[1].send_mid((1, 3))
    rs[0].send_z(2)
    back_act(1, 1)
    rs[1].side_x(1)
    rs[1].send_mid((2,))
    saves = []
    for s in range(2):
        def step(i, _):
            r = pl.multiple_of(i * 384, 128)
            gi[s, pl.ds(r, 384)] = dot_tn(hn[:, pl.ds(r, 384)], du[:, D * s:D * s + D]).astype(BF)
            return 0

        lax.fori_loop(0, 3, step, 0)
        cp = pltpu.make_async_copy(gi.at[s], (grad_i0, grad_i1)[s], gs.at[s])
        cp.start()
        saves.append(cp)
        if s == 0:
            rs[1].side_x(3)
            rs[1].send_mid((0,))
            rs[1].send_z(1)
            rs[0].finish()
        else:
            rs[1].side_x(2)
            rs[1].send_z(3)

    for m in range(2):
        def hid(i, _):
            r = pl.multiple_of(i * 384, 128)
            rows = pl.ds(r, 384)
            v = dot_nt(du[half(m, 1 - k), 0:D], WI0[rows]) + dot_nt(du[half(m, 1 - k), D:], WI1[rows])
            x_send[m, :, rows] = v.astype(BF)
            return 0

        lax.fori_loop(0, 3, hid, 0)
        cp = remote(x_send.at[m], x_recv.at[m], xs.at[m], xr.at[m], sib)
        cp.start()
        loads.append(cp)

        def hid_own(i, _):
            r = pl.multiple_of(i * 384, 128)
            rows = pl.ds(r, 384)
            dn[m, :, rows] = dot_nt(du[half(m, k), 0:D], WI0[rows]) + dot_nt(du[half(m, k), D:], WI1[rows])
            return 0

        lax.fori_loop(0, 3, hid_own, 0)
        if m == 0:
            rs[1].side_x(0)
            rs[1].send_z(2)
    gain_two = jnp.zeros((1, D), F32)
    for m in range(2):
        pltpu.make_async_copy(x_recv.at[m], x_recv.at[m], xr.at[m]).wait()
        grad = dn[m] + x_recv[m].astype(F32)
        n, r = norm(dh[m])
        gain_two = gain_two + jnp.sum(grad * n, 0, keepdims=True)
        v = cot[m].astype(F32) * filled[m] + norm_back(n, r, grad * gains[1:2])
        dh[m] = v
        da[half(m, k)] = v.astype(BF)
        cp = remote(da.at[half(m, k)], da.at[half(m, k)], as_.at[m], ar.at[m], sib)
        cp.start()
        loads.append(cp)
    gain[...] = jnp.broadcast_to(gain_two, (8, D))
    for m in range(2):
        v = da.at[half(m, 1 - k)]
        pltpu.make_async_copy(v, v, ar.at[m]).wait()
    rs[1].finish()
    rs[0].collect(out_b)
    rs[0].sent()
    rs[1].sent()
    for cp in saves:
        cp.wait()
    for cp in loads[12:]:
        cp.wait_send()
    for make in pend:
        make().wait_send()


def mlp_back(*args):
    S = jax.ShapeDtypeStruct
    dma = pltpu.SemaphoreType.DMA
    V, anyspace = pl.BlockSpec(memory_space=pltpu.VMEM), pl.BlockSpec(memory_space=pl.ANY)
    return pl.pallas_call(
        mlp_back_kernel,
        out_shape=[S((2, HALF, D), BF), S((2, HALF, D), F32), S((2 * TOK, D), BF), S((8, D), F32), S((144, D), F32), S((D, D), BF), S((D, D), BF)],
        in_specs=[anyspace, V, V] + [anyspace] * 11, out_specs=[V] * 5 + [anyspace] * 2,
        scratch_shapes=[pltpu.VMEM((D, D), BF), pltpu.VMEM((D, D), BF), pltpu.VMEM((2, HALF, D), BF)] + [pltpu.VMEM((D, D), BF)] * 4
        + [pltpu.VMEM((2 * TOK, D), BF), pltpu.VMEM((2 * TOK, FH), BF), pltpu.VMEM((2 * TOK, FH), BF), pltpu.VMEM((2, D, D), BF),
                        pltpu.VMEM((2, HALF, D), BF), pltpu.VMEM((2, HALF, D), BF), pltpu.VMEM((2, HALF, D), BF), pltpu.VMEM((2, HALF, D), BF),
                        pltpu.VMEM((2, HALF, D), F32)]
        + [dma((2,))] * 6 + [dma((12,)), dma((2,))] + scatter_scratch("B0") + scatter_scratch("B1"),
        compiler_params=pltpu.CompilerParams(collective_id=2, has_side_effects=True, vmem_limit_bytes=127 * 2 ** 19),
        name="mlp_back")(*args)


def attn_back_kernel(WA, WO, ti, gains, lat, xn, q, kb, vb, lse, o, da, dh, mask, base, onehot, gain_two, te, gi0, gi1,
                     dlat, gt, small, out_o, out_a, out_i, out_t,
                     dt_all,
                     q_v, kb_v, vb_v, grad_o, grad_a, grad_i0, grad_i1, do, dqkv, rim, rim_in, tsum, tsum_in, gt_send, gt_in, x_send, x_recv, dbias, sm_send, sm_in, total,
                     ks, kr, ts, tr, ps, pr, us, ur, vs, vr, ls, xs, xr, ss, sr, bs, br, *scratch):
    c, b, y, k = place()
    sib, ynb = {"band": b + 1 - 2 * k}, {"band": b + 2 - 4 * y}
    peers = [lax.rem(c + d, 8) for d in range(1, 8)]
    pend, waits = [], iter(range(20))

    def load(src, dst):
        cp = pltpu.make_async_copy(src, dst, ls.at[next(waits)])
        cp.start()
        return cp

    loads_i = [load(gi0, grad_i0), load(gi1, grad_i1)]
    load_dh = load(dh, dlat)
    load_q = [load(q, q_v), load(kb, kb_v), load(vb, vb_v)]
    greet(everyone())
    n = N_SCATTER
    rs_o = Scatter("O", grad_o, total, scratch[:n], pend)
    rs_a = Scatter("A", grad_a, total, scratch[n:2 * n], pend)
    rs_i = [Scatter("I0", grad_i0, total, scratch[2 * n:3 * n], pend), Scatter("I1", grad_i1, total, scratch[3 * n:], pend)]

    def go(make):
        make().start()
        pend.append(make)

    def arrive(view, sem):
        pltpu.make_async_copy(view, view, sem).wait()

    slots = pl.ds(pl.multiple_of(16 * c, 16), 16)
    for s in range(2):
        loads_i[s].wait()
        rs_i[s].send_y()
        rs_i[s].send_mid()

    def first(o_v, da_v, wo_v):
        parts = [load(o, o_v), load(da, da_v), load(WO, wo_v)]
        for cp in parts:
            cp.wait()
        for i, cols in enumerate(rs_o.parts()):
            grad_o[:, cols] = dot_tn(o_v[...], da_v[:, cols]).astype(BF)
            if i == 0:
                rs_o.send_y()
            if i == 1:
                rs_o.send_mid()
        for m in range(2):
            do[m] = dot_nt(da_v[pl.ds(TOK * m, TOK)], wo_v[...]).astype(BF)

    pl.run_scoped(first, pltpu.VMEM((2 * TOK, QC), BF), pltpu.VMEM((2 * TOK, D), BF), pltpu.VMEM((QC, D), BF))

    def second(dqf, dkf, dvf, toep, dsum):
        dqf[...] = jnp.zeros_like(dqf)
        dkf[...] = jnp.zeros_like(dkf)
        dvf[...] = jnp.zeros_like(dvf)
        for cp in load_q:
            cp.wait()

        def head(h, _):
            win, hm = head_window(h)
            toep[...] = toeplitz(base, h)
            dsum[...] = jnp.zeros_like(dsum)
            lane_h = lax.broadcasted_iota(jnp.int32, (1, 128), 1) == h

            def tile(t, _):
                m, j = t // 2, lax.rem(t, 2)
                rows = pl.ds(pl.multiple_of(HALF * j, 16), HALF)
                krows = pl.ds(pl.multiple_of(HALF * j, 16), KW)
                qm, dm = q_v[m, rows, win] * hm, do[m, rows, win] * hm
                kw = kb_v[m, krows, win]
                level = jnp.sum(jnp.where(lane_h, lse[m, rows], 0.0), -1, keepdims=True)
                p = jnp.exp(dot_nt(qm, kw) * SCALE + (toep[...] + mask[m, j]) - level)
                dp = dot_nt(dm, vb_v[m, krows, win])
                delta = jnp.sum(p * dp, -1, keepdims=True)
                ds = (p * (dp - delta)).astype(BF)
                dsum[...] += ds.astype(F32)
                dqf[m, rows, win] += dot(ds, kw * hm)
                dkf[m, krows, win] += dot_tn(ds, qm)
                dvf[m, krows, win] += dot_tn(p.astype(BF), dm)
                return 0

            lax.fori_loop(0, 4, tile, 0)
            strip = dsum[0:8]
            for r in range(8, HALF, 8):
                strip = strip + pltpu.roll(dsum[r:r + 8], KW - r, 1)
            line = strip[0:1]
            for r in range(1, 8):
                line = line + pltpu.roll(strip, KW - r, 1)[r:r + 1]
            dbias[pl.ds(h, 1)] = line
            return 0

        for i in range(4):
            lax.fori_loop(2 * i, 2 * i + 2, head, 0)
            if i == 0:
                for d in (1, 3, 2):
                    rs_i[0].side_x(d)
            elif i == 1:
                rs_i[0].side_x(0)
                for d in (1, 3, 2):
                    rs_i[0].send_z(d)
                rs_i[1].side_x(1)
            elif i == 2:
                for d in (3, 2, 0):
                    rs_i[1].side_x(d)
                rs_i[1].send_z(1)
        away = pl.ds(pl.multiple_of(624 * (1 - y), 16), 80)
        edge = pl.ds(pl.multiple_of(544 - 464 * y, 16), 80)
        for m in range(2):
            rim[m, 0] = (dkf[m, away] * SCALE).astype(BF)
            rim[m, 1] = dvf[m, away].astype(BF)
            go(lambda m=m: remote(rim.at[m], rim_in.at[m], ks.at[m], kr.at[m], ynb))
        for m in range(2):
            tok = pl.ds(TOK * m, TOK)
            dqkv[tok, 0:QC] = (dqf[m] * SCALE).astype(BF)
        for d in ORDER:
            rs_o.side_x(d)
        rs_i[1].send_z(3)
        rs_i[1].send_z(2)
        for m in range(2):
            arrive(rim_in.at[m], kr.at[m])
            tok = pl.ds(TOK * m, TOK)
            dkf[m, edge] += rim_in[m, 0].astype(F32) * (1.0 / SCALE)
            dvf[m, edge] += rim_in[m, 1].astype(F32)
            dqkv[tok, QC:2 * QC] = (dkf[m, 80:624] * SCALE).astype(BF)
            dqkv[tok, 2 * QC:] = dvf[m, 80:624].astype(BF)

    pl.run_scoped(second, pltpu.VMEM((2, TOK, QC), F32), pltpu.VMEM((2, KEYS, QC), F32), pltpu.VMEM((2, KEYS, QC), F32),
                  pltpu.VMEM((HALF, KW), F32), pltpu.VMEM((HALF, KW), F32))

    def third(xn_v, wa_v, dn):
        loads = [load(xn, xn_v), load(WA, wa_v)]
        tq = dot_tn(onehot[0], dqkv[0:TOK, 0:QC]) + dot_tn(onehot[1], dqkv[TOK:, 0:QC])
        tv = dot_tn(onehot[0], dqkv[0:TOK, 2 * QC:]) + dot_tn(onehot[1], dqkv[TOK:, 2 * QC:])
        tsum[:, 0:QC] = tq[0:16].astype(BF)
        tsum[:, QC:] = tv[0:16].astype(BF)
        go(lambda: remote(tsum, tsum_in, ts.at[0], tr.at[0], ynb))
        loads[0].wait()
        for i, cols in enumerate(rs_a.parts()):
            fill_part(grad_a, xn_v, dqkv, cols, 0, cols)
            if i == 0:
                rs_a.send_y()
                arrive(tsum_in, tr.at[0])
                dt_all[k, slots] = (tsum[...].astype(F32) + tsum_in[...].astype(F32)).astype(BF)
                for n, p in enumerate(peers):
                    go(lambda n=n, p=p: remote(dt_all.at[k, slots], dt_all.at[k, slots], ps.at[n], pr.at[6 - n], {"canvas": p}))
            if i == 1:
                rs_a.send_mid((1, 3))
        for d in (1, 3, 2):
            rs_o.send_z(d)
        rs_i[0].finish()
        loads[1].wait()
        for m in range(2):
            rows = pl.ds(pl.multiple_of(TOK * m + HALF * (1 - k), 16), HALF)
            rows_own = pl.ds(pl.multiple_of(TOK * m + HALF * k, 16), HALF)

            def back(n, _):
                cols = pl.ds(pl.multiple_of(n * 384, 128), 384)
                x_send[m, :, cols] = dot_nt(dqkv[rows], wa_v[cols]).astype(BF)
                return 0

            lax.fori_loop(0, 3, back, 0)
            go(lambda m=m: remote(x_send.at[m], x_recv.at[m], xs.at[m], xr.at[m], sib))

            def back_own(n, _):
                cols = pl.ds(pl.multiple_of(n * 384, 128), 384)
                dn[m, :, cols] = dot_nt(dqkv[rows_own], wa_v[cols])
                return 0

            lax.fori_loop(0, 3, back_own, 0)
        rs_i[1].finish()
        rs_a.side_x(1)
        rs_a.send_mid((2,))
        for n in range(7):
            arrive(dt_all.at[k, pl.ds(pl.multiple_of(16 * lax.rem(c + n + 1, 8), 16), 16)], pr.at[n])
        go(lambda: remote(dt_all.at[k], dt_all.at[k], us.at[0], ur.at[0], sib))
        gt_send[...] = dot_nt(dt_all[k], ti[...])
        go(lambda: remote(gt_send, gt_in, us.at[1], ur.at[1], sib))
        rs_a.side_x(3)
        rs_a.send_mid((0,))
        rs_a.send_z(1)
        load_dh.wait()
        gain_one = jnp.zeros((1, D), F32)
        for m in range(2):
            arrive(x_recv.at[m], xr.at[m])
            grad = dn[m] + x_recv[m].astype(F32)
            n, r = norm(lat[m].astype(F32))
            gain_one = gain_one + jnp.sum(grad * n, 0, keepdims=True)
            dlat[m] = dlat[m] + norm_back(n, r, grad * gains[0:1])
            if m == 0:
                rs_a.side_x(2)
                rs_a.send_z(3)
        first_row = lax.broadcasted_iota(jnp.int32, (8, 1), 0) == 0
        both = jnp.where(first_row, jnp.broadcast_to(gain_one, (8, D)), gain_two[...])
        for p in range(8):
            sm_send[p, 0:8] = dbias[...]
            sm_send[p, 8:16] = (pltpu.roll(both, D - 144 * p, 1) if p else both)[:, 0:KW]

    pl.run_scoped(third, pltpu.VMEM((2 * TOK, D), BF), pltpu.VMEM((D, 3 * QC), BF), pltpu.VMEM((2, HALF, D), F32))
    for n, p in enumerate(peers):
        go(lambda n=n, p=p: remote(sm_send.at[p], sm_in.at[6 - n], ss.at[n], sr.at[6 - n], {"canvas": p}))
    rs_o.finish()
    arrive(gt_in, ur.at[1])
    gt_in[...] = gt_in[...] + gt_send[...]
    for n, p in enumerate(peers):
        go(lambda n=n, p=p: remote(gt_in.at[pl.ds(pl.multiple_of(16 * p, 16), 16)], gt.at[c], vs.at[n], vr.at[6 - n], {"canvas": p}))
    gt[c] = gt_in[pl.ds(pl.multiple_of(16 * c, 16), 16)]
    rs_a.side_x(0)
    rs_a.send_z(2)
    acc = sm_send[c]
    for n in range(7):
        arrive(sm_in.at[n], sr.at[n])
        acc = acc + sm_in[n]
    small[b] = acc
    for i in range(3):
        go(lambda i=i: remote(small.at[b], small.at[b], bs.at[i], br.at[2 - i], {"band": lax.rem(b + i + 1, 4)}))
    def last(buf_a, buf_i, buf_t):
        for s in range(2):
            rs_i[s].collect(buf_i.at[s])
            for half in range(2):
                for n in range(8):
                    at = 576 * n + 288 * half + 144 * s
                    out_i[:, at:at + 144] = buf_i[s, half, :, 144 * n:144 * n + 144]
        rs_o.collect(out_o)
        for n in range(7):
            arrive(gt.at[lax.rem(c + n + 1, 8)], vr.at[n])
        arrive(dt_all.at[1 - k], ur.at[0])
        slots_all = te[...].reshape(128, 144)
        for half in range(2):
            total[...] = dot_tn(slots_all, dt_all[half])
            for i in range(4):
                @pl.when(b == i)
                def _():
                    buf_t[...] = total[36 * i:36 * i + 36]

            for t in range(2):
                for i in range(8):
                    at = D * t + 144 * i + 72 * half
                    out_t[:, at:at + 72] = buf_t[:, QC * t + 80 * i:QC * t + 80 * i + 72]
        for i in range(3):
            arrive(small.at[lax.rem(b + i + 1, 4)], br.at[i])
        rs_a.finish()
        rs_a.collect(buf_a)
        for half in range(2):
            for t in range(3):
                for i in range(8):
                    at = D * t + 144 * i + 72 * half
                    out_a[:, at:at + 72] = buf_a[half, :, QC * t + 80 * i:QC * t + 80 * i + 72]

    pl.run_scoped(last, pltpu.VMEM((2, 36, 3 * QC), F32), pltpu.VMEM((2, 2, 36, D), F32), pltpu.VMEM((36, 2 * QC), F32))
    for rs in (rs_o, rs_a, *rs_i):
        rs.sent()
    for make in pend:
        make().wait_send()


def attn_back(*args):
    S = jax.ShapeDtypeStruct
    dma = pltpu.SemaphoreType.DMA
    V, anyspace = pl.BlockSpec(memory_space=pltpu.VMEM), pl.BlockSpec(memory_space=pl.ANY)
    return pl.pallas_call(
        attn_back_kernel,
        out_shape=[S((2, HALF, D), F32), S((8, 16, 144), F32), S((4, 16, KW), F32), S((36, D), F32), S((36, 3 * D), F32), S((36, 2 * FH), F32), S((36, 2 * D), F32)],
        in_specs=[anyspace, anyspace, V, V, V] + [anyspace] * 4 + [V] + [anyspace] * 3 + [V] * 5 + [anyspace] * 2, out_specs=[V] * 7,
        scratch_shapes=[pltpu.VMEM((2, 128, 2 * QC), BF),
                        pltpu.VMEM((2, TOK, QC), BF), pltpu.VMEM((2, KEYS, QC), BF), pltpu.VMEM((2, KEYS, QC), BF),
                        pltpu.VMEM((QC, D), BF), pltpu.VMEM((D, 3 * QC), BF), pltpu.VMEM((D, D), BF), pltpu.VMEM((D, D), BF), pltpu.VMEM((2, TOK, QC), BF),
                        pltpu.VMEM((2 * TOK, 3 * QC), BF),
                        pltpu.VMEM((2, 2, 80, QC), BF), pltpu.VMEM((2, 2, 80, QC), BF), pltpu.VMEM((16, 2 * QC), BF), pltpu.VMEM((16, 2 * QC), BF),
                        pltpu.VMEM((128, 144), F32), pltpu.VMEM((128, 144), F32),
                        pltpu.VMEM((2, HALF, D), BF), pltpu.VMEM((2, HALF, D), BF), pltpu.VMEM((8, KW), F32), pltpu.VMEM((8, 16, KW), F32), pltpu.VMEM((7, 16, KW), F32),
                        pltpu.VMEM((144, 1280), F32),
                        dma((2,)), dma((2,)), dma((1,)), dma((1,)), dma((7,)), dma((7,)), dma((2,)), dma((2,)), dma((7,)), dma((7,)), dma((20,)), dma((2,)), dma((2,)),
                        dma((7,)), dma((7,)), dma((3,)), dma((3,))]
        + scatter_scratch("O") + scatter_scratch("A") + scatter_scratch("I0") + scatter_scratch("I1"),
        compiler_params=pltpu.CompilerParams(collective_id=3, has_side_effects=True, vmem_limit_bytes=127 * 2 ** 19),
        name="attn_back")(*args)


def local_fast(*args):
    p = prologue(*args)
    c, b, y, k = place()
    cot = args[10].reshape(2, HALF, D)
    (xn, q, kb, vb, lse, o, hres, hn, g, gp, df, gb0, gb1, WA, WO, WI0, WI1, WB0, WB1, te_all, mask, onehot, ti) = gather_forward(p, cot)
    out, dh, da, gain_two, out_b, gi0, gi1 = mlp_back(cot, p["filled"], p["gains"], WI0, WI1, WB0, WB1, hres, hn.reshape(2 * TOK, D), g, gp, df, gb0, gb1)
    dlat, gt, small, grad_out, grad_a, grad_i, grad_time_in = attn_back(
        WA, WO, ti, p["gains"], p["lat"], xn.reshape(2 * TOK, D), q, kb, vb, lse, o.reshape(2 * TOK, QC), da, dh,
        mask, p["base"], onehot, gain_two, te_all, gi0, gi1)
    shape = (2, 1, 8, 34, D)
    places = [80 + 34 * dr + dc for dr in range(-2, 3) for dc in range(-2, 3)]
    bias = small[0:2, 0:8] + small[2:4, 0:8]
    grad_bias = bias[:, :, jnp.array(places)].transpose(2, 1, 0).reshape(25, 16)
    mine = lax.dynamic_slice_in_dim(small[:, 8:10, 0:144].sum(0), 36 * b, 36, 1)
    grad_time = gt.transpose(1, 0, 2).reshape(16, D)[:10].reshape(2, 1, 5, D)
    return (out.reshape(shape), dlat.reshape(shape), grad_time, mine.T, grad_a, grad_time_in, grad_bias, grad_out, grad_i, out_b)


def solution(mesh):
    return jax.shard_map(
        local_fast if mesh.shape["canvas"] == 8 and mesh.shape["band"] == 4 else local,
        mesh=mesh,
        in_specs=(
            P(None, "canvas", "band", None, None),
            P(None, "canvas", "band", None),
            P(None, "canvas", None, None),
            P(),
            P("canvas", None),
            P("canvas", None),
            P(),
            P("canvas", None),
            P("canvas", None),
            P("canvas", None),
            P(None, "canvas", "band", None, None),
        ),
        out_specs=(
            P(None, "canvas", "band", None, None),
            P(None, "canvas", "band", None, None),
            P(None, "canvas", None, None),
            P(("canvas", "band"), None),
            P(("canvas", "band"), None),
            P(("canvas", "band"), None),
            P(),
            P(("canvas", "band"), None),
            P(("canvas", "band"), None),
            P(("canvas", "band"), None),
        ),
        check_vma=False,
    )
```
